32 devices in a mesh: parts: 2 (over x), tile: 16 (over z, y, core).
Axes of the slice: x: 2, y: 2, z: 4, core: 2. Of those that a mesh axis runs over, the one named last changes fastest.
Arguments:
- visibility: float32 [2048, 2, 128], P(('parts', 'tile')), parts along dimension 0, may hold values from -0.5 to 0.5
- coords: float32 [2048, 3, 128], P(('parts', 'tile')), parts along dimension 0, may hold values from -8 to 8
- block_owner: int32 [2048, 1], P(('parts', 'tile')), parts along dimension 0, may hold values from 0 to 15; in each aligned block of 64 rows (0 to 63, 64 to 127, ...) at most 8 rows name the same one
- block_row: int32 [2048], P(('parts', 'tile')), parts along dimension 0, may hold values from 0 to 96, as said below
- block_col: int32 [2048], P(('parts', 'tile')), parts along dimension 0, may hold values from 0 to 2016
- stations: int32 [2048, 2], P(('parts', 'tile')), parts along dimension 0, may hold values from 0 to 511
- block_count: int32 [32], P(('parts', 'tile')), parts along dimension 0, may hold values from 32 to 64, as said below
- beam_terms: float32 [512, 2, 1024], replicated, may hold values from -4 to 4
Outputs:
- spectrum: float32 [2, 256, 32768], P(None, ('parts', 'tile')), parts along dimension 1
The draws below stay inside these ranges and needn't reach their ends.
There are 2 independent parts, one for each index of `parts`. The reference program is written for one: setup_inputs(seed, part) draws one part's arguments, and reference() takes and returns one part's arrays. A program takes and returns all parts, laid end to end along the dimension named above; an argument that names none is the same for every part. Nothing has to cross between parts.
Inputs may be any that keep to these rules, and one draw needn't show every extreme that they name: `block_owner`: among the 64 block slots of one device, at most 8 name the same owner, and every owner is named by some slot. `block_count`: some device's count is 64 in every draw. Among the 64 block slots of one device, at most 5 have the same block_row div 8.
All inputs are finite; a program needn't handle non-finite values.
Results may differ from the reference program's by a relative error of at most 0.0003.
Values sent between devices are 32-bit elements; how exact they have to be, the bound alone decides.
No kernel may reach another device: no remote copies, remote signals or barrier semaphores. Data moves between devices by JAX's collectives and lax.ppermute only.
A program may use at most 64 MiB of HBM per device.

```python
import math
import jax
import jax.numpy as jnp
import numpy as np
from jax import lax

VROWS = 128
SUB = 32
NG = 32768
STATIONS = 512
BLK_DEV = 64
ROWS_DEV = 8
OWNERS = 16
BLOCKS = 1024
CAP = 8
TILE_COLS = 2048
U_ROWS = 128


def draw_block_count(key, part):
    key = jax.random.fold_in(key, 11)
    key_counts, key_chosen = jax.random.split(key)
    counts = jax.random.randint(key_counts, (OWNERS,), BLK_DEV // 2, BLK_DEV + 1)
    chosen = jax.random.randint(key_chosen, (), 0, OWNERS)
    return jnp.where(jnp.arange(OWNERS) == chosen, BLK_DEV, counts).astype(jnp.int32)


def draw_block_row(key, part):
    key = jax.random.fold_in(key, 23)
    start_bands = (U_ROWS - SUB) // ROWS_DEV + 1
    numbers = jnp.arange(BLK_DEV)
    base = numbers * start_bands // BLK_DEV
    base = jnp.where(numbers == BLK_DEV - 1, start_bands - 1, base)
    device_keys = jax.random.split(key, OWNERS)

    def one_device(device_key):
        key_order, key_offset = jax.random.split(device_key)
        order = jax.random.permutation(key_order, BLK_DEV)
        offset = jax.random.randint(key_offset, (BLK_DEV,), 0, ROWS_DEV)
        offset = jnp.where(numbers == 0, 0, offset)
        rows = jnp.minimum(base * ROWS_DEV + offset, U_ROWS - SUB)
        rows = jnp.where(numbers == BLK_DEV - 1, U_ROWS - SUB, rows)
        return rows[order]
    return jax.vmap(one_device)(device_keys).reshape(-1).astype(jnp.int32)


def plant(values, key, smallest, top_value):
    index_at = [jax.random.randint(jax.random.fold_in(key, axis), (), 0, length) for axis, length in enumerate(values.shape)]
    longest = values.shape.index(max(values.shape))
    beside = index_at[:longest] + [(index_at[longest] + 1) % values.shape[longest]] + index_at[longest + 1:]
    return values.at[tuple(index_at)].set(smallest).at[tuple(beside)].set(top_value)


def block_levels(key, extent, cuts, low, high):
    def one(dim, shards_of):
        draws = jax.random.uniform(jax.random.fold_in(jax.random.fold_in(key, 6), dim), (shards_of,), jnp.float32, low / len(cuts), high / len(cuts))
        return jnp.repeat(jnp.exp(draws), extent[dim] // shards_of).reshape((-1,) + (1,) * (len(extent) - dim - 1))

    factor_of = one(*cuts[0])
    for cut in cuts[1:]:
        factor_of = factor_of * one(*cut)
    return factor_of


def shared_out(rng, own, number, rows, count, top, reach, skew):
    order = jax.random.permutation(rng, count)
    heavy_load, usual = load_shares(count, rows * top, reach, skew, True), load_shares(count, rows * top, reach, skew, False)
    places = jnp.arange(count)

    def named(lengths, turn):
        used = int((lengths > 0).sum())
        fixed = max(1, used // 4)
        shifted = fixed + (places - fixed + turn * (used - fixed)) % max(1, count - fixed)
        return jnp.zeros((count,), jnp.int32).at[order[jnp.where(places < fixed, places, shifted)]].set(jnp.asarray(lengths, jnp.int32))

    lengths = jnp.where(number % 4 == 0, named(heavy_load, number // 4), named(usual, number - number // 4 - 1))
    mixed = jax.random.permutation(jax.random.fold_in(own, 3), count)
    source_of, receiver = mixed[0:count // 2 * 2:2], mixed[1:count // 2 * 2:2]
    room = jnp.minimum(lengths[source_of] - 1, reach - lengths[receiver]) // 2
    room = jnp.where((source_of == order[0]) | (receiver == order[0]) | (lengths[receiver] == 0), 0, jnp.maximum(room, 0))
    shifted = jax.random.randint(jax.random.fold_in(own, 4), (count // 2,), 0, 1 << 20) % (room + 1)
    lengths = lengths.at[source_of].add(-shifted).at[receiver].add(shifted)
    labels = jnp.searchsorted(jnp.cumsum(lengths), jnp.arange(rows * top), side="right").astype(jnp.int32)
    table = labels.reshape(top, rows).T
    table = table[jax.random.permutation(jax.random.fold_in(own, 1), rows)]
    turn = jax.random.randint(jax.random.fold_in(own, 2), (rows, 1), 0, top)
    return jnp.take_along_axis(table, (jnp.arange(top)[None, :] + turn) % top, axis=1)


def load_shares(amount, total, bound, skew, full):
    weights = [(1 << 20) // math.isqrt(standing ** skew) + 1 for standing in range(1, amount + 1)]
    largest = bound if full else min(bound, max(-(-total // amount), total * weights[0] // sum(weights)))
    least = 1 if total - largest >= amount - 1 else 0
    given, rest = [largest] + [least] * (amount - 1), total - largest - least * (amount - 1)
    while rest > 0:
        candidates = [i for i in range(1, amount) if given[i] < largest] or [i for i in range(1, amount) if given[i] < bound]
        whole, remaining = sum([weights[i] for i in candidates]), rest
        for i in candidates:
            extra = min(bound - given[i], max(1, remaining * weights[i] // whole), rest)
            given[i] = given[i] + extra
            rest = rest - extra
    return np.array(given)


def gaussian(stream_key, shape, spread, reach, shards=(), dtype=jnp.bfloat16):
    drawn = jax.random.normal(stream_key, shape, jnp.float32) * spread
    if len(shards) > 0:
        drawn = block_levels(stream_key, shape, shards, -0.22, 0.18) * drawn
    return jnp.clip(drawn, min=-reach, max=reach).astype(dtype)


def setup_inputs(seed: int = 0, part: int = 0) -> dict:
    splits = jax.random.split(jax.random.key(seed), 9)
    part_keys = jax.random.split(jax.random.fold_in(splits[8], part), 9)
    visibility = gaussian(part_keys[0], (BLOCKS, 2, VROWS), 0.09, 0.5, ((0, 16),), jnp.float32)
    coords = jnp.clip(jax.random.uniform(part_keys[1], (BLOCKS, 3, VROWS), jnp.float32, -8.0, 8.0) * block_levels(part_keys[1], (BLOCKS, 3, VROWS), ((0, 16),), -0.4, 0.0), -8.0, 8.0)
    block_owner_keys = jax.random.split(jax.random.fold_in(part_keys[2], 1), BLOCKS // BLK_DEV)
    block_owner_turns = jax.random.permutation(jax.random.fold_in(part_keys[2], 3), BLOCKS // BLK_DEV)
    block_owner = jax.vmap(lambda own, number: shared_out(jax.random.fold_in(part_keys[2], 2), own, number, BLK_DEV, OWNERS, 1, CAP, 2))(block_owner_keys, block_owner_turns).reshape((BLOCKS, 1))
    block_row = draw_block_row(jax.random.fold_in(jax.random.fold_in(splits[8], part), 71), part)
    block_col = plant(jax.random.randint(part_keys[4], (BLOCKS,), 0, TILE_COLS - SUB + 1), jax.random.fold_in(part_keys[4], 1), 0, TILE_COLS - SUB).astype(jnp.int32)
    stations = plant(jax.random.randint(part_keys[5], (BLOCKS, 2), 0, STATIONS), jax.random.fold_in(part_keys[5], 1), 0, STATIONS - 1).astype(jnp.int32)
    block_count = draw_block_count(jax.random.fold_in(jax.random.fold_in(splits[8], part), 71), part)
    beam_terms = gaussian(splits[7], (STATIONS, 2, SUB * SUB), 0.7, 4.0, (), jnp.float32)
    return {"visibility": visibility, "coords": coords, "block_owner": block_owner, "block_row": block_row, "block_col": block_col, "stations": stations, "block_count": block_count, "beam_terms": beam_terms}


highest = lax.Precision.HIGHEST

def pixel_tables():
    position = jnp.arange(SUB * SUB)
    row_pos = ((position // SUB).astype(jnp.float32) - SUB // 2) / SUB
    col_pos = ((position % SUB).astype(jnp.float32) - SUB // 2) / SUB
    depth = row_pos * row_pos + col_pos * col_pos
    tapering = (1.0 - 2.0 * row_pos * row_pos) * (1.0 - 2.0 * col_pos * col_pos)
    return (jnp.stack([row_pos, col_pos, depth]), tapering)

def sky_images(visibility, coords, station_one, station_two, beam_terms):
    pixel_table, tapering = pixel_tables()
    phase = 2.0 * math.pi * jnp.einsum('gck,cp->gkp', coords, pixel_table, precision=highest)
    cosine = jnp.cos(phase)
    sine = jnp.sin(phase)
    vis_re = visibility[:, 0]
    vis_im = visibility[:, 1]
    sum_re = jnp.einsum('gk,gkp->gp', vis_re, cosine, precision=highest) - jnp.einsum('gk,gkp->gp', vis_im, sine, precision=highest)
    sum_im = jnp.einsum('gk,gkp->gp', vis_re, sine, precision=highest) + jnp.einsum('gk,gkp->gp', vis_im, cosine, precision=highest)
    beam_one = beam_terms[station_one]
    beam_two = beam_terms[station_two]
    beam_re = beam_one[:, 0] * beam_two[:, 0] + beam_one[:, 1] * beam_two[:, 1]
    beam_im = beam_one[:, 1] * beam_two[:, 0] - beam_one[:, 0] * beam_two[:, 1]
    sky_re = tapering * (beam_re * sum_re - beam_im * sum_im)
    sky_im = tapering * (beam_re * sum_im + beam_im * sum_re)
    return (sky_re, sky_im)

def group_subgrids(inputs, beam_terms):
    visibility, coords, station_one, station_two = inputs
    sky_re, sky_im = sky_images(visibility, coords, station_one, station_two, beam_terms)
    sky = (sky_re + 1j * sky_im).reshape(-1, SUB, SUB)
    cells = jnp.fft.fft2(sky, axes=(1, 2)) / SUB
    cells = cells.reshape(-1, SUB * SUB)
    return jnp.stack([jnp.real(cells), jnp.imag(cells)], axis=1).astype(jnp.float32)

def reference(visibility, coords, block_owner, block_row, block_col, stations, block_count, beam_terms):
    total = visibility.shape[0]
    group_rows = 8

    def one_group(inputs):
        return group_subgrids(inputs, beam_terms)
    stacked = lax.map(one_group, (visibility.reshape(-1, group_rows, 2, VROWS), coords.reshape(-1, group_rows, 3, VROWS), stations[:, 0].reshape(-1, group_rows), stations[:, 1].reshape(-1, group_rows)))
    subgrids = stacked.reshape(total, 2, SUB * SUB)
    numbers = jnp.arange(total).astype(jnp.int32)
    is_live = numbers % BLK_DEV < block_count[numbers // BLK_DEV]
    subgrids = jnp.where(is_live[:, None, None], subgrids, jnp.zeros_like(subgrids))
    columns = (block_owner[:, 0] * TILE_COLS + block_col).astype(jnp.int32)
    rows = block_row.astype(jnp.int32)
    anchor = jnp.zeros((), jnp.int32)

    def place(number, grid):
        subgrid = subgrids[number].reshape(2, SUB, SUB)
        offset = (anchor, rows[number], columns[number])
        current = lax.dynamic_slice(grid, offset, (2, SUB, SUB))
        return lax.dynamic_update_slice(grid, current + subgrid, offset)
    grid = lax.fori_loop(0, total, place, jnp.zeros((2, U_ROWS, NG), jnp.float32))
    band = grid[0] + 1j * grid[1]
    transformed = jnp.fft.fft(band, axis=1) / math.sqrt(NG)
    return jnp.stack([jnp.real(transformed), jnp.imag(transformed)]).astype(jnp.float32)
```

```python
import functools
import math

import jax
import jax.numpy as jnp
import ml_dtypes
import numpy as np
from jax import lax
from jax.experimental import pallas as pl
from jax.experimental.pallas import tpu as pltpu
from jax.sharding import PartitionSpec as P

VROWS = 128
SUB = 32
NG = 32768
ROWS_DEV = 8
LEAD = 256
TAIL = 128
GROUP = 8

SIN_TERMS = (4.442882920, -7.308245680, 3.606354030, -0.846110410, 0.109822040)
COS_TERMS = (1.414213500, -6.978850910, 5.739459580, -1.883552820, 0.310677860)


def halves(table):
    table = np.round(table, 12).astype(np.float32)
    high = table.astype(ml_dtypes.bfloat16)
    low = (table - high.astype(np.float32)).astype(ml_dtypes.bfloat16)
    return high, low


def root(numbers, length):
    angle = 2.0 * np.pi / length * (numbers % length)
    return np.cos(angle), -np.sin(angle)


def complex_left(re, im):
    return np.block([[re, -im], [im, re]])


@functools.cache
def image_tables():
    eight = np.arange(8)
    re, im = root(np.outer(eight, eight), 8)
    left = complex_left(np.kron(np.eye(16), re), np.kron(np.eye(16), im))
    lane = np.arange(128)
    twist = root(np.outer(eight, lane // SUB), SUB)
    four = 8 * np.outer(lane // SUB, lane // SUB) + np.outer(lane % SUB, lane % SUB)
    re, im = root(four, SUB)
    right = complex_left(re, im).T
    row_pos = ((4 * eight[:, None] + lane[None, :] // SUB) - SUB // 2) / SUB
    col_pos = np.broadcast_to((lane[None, :] % SUB - SUB // 2) / SUB, (8, 128))
    taper = (1 - 2 * row_pos**2) * (1 - 2 * col_pos**2) / SUB
    small = np.stack([taper, np.round(twist[0], 12), np.round(twist[1], 12)]).astype(np.float32)
    return (*halves(left), *halves(right), small)


@functools.cache
def row_tables():
    lead, tail = np.arange(LEAD), np.arange(TAIL)
    first = complex_left(*root(np.outer(lead, lead), LEAD))
    twist = np.stack(root(np.outer(lead, tail), NG)) / math.sqrt(NG)
    second = complex_left(*root(np.outer(tail, tail), TAIL))
    return (*halves(first), *halves(second), np.round(twist, 12).astype(np.float32))


def split(value):
    high = value.astype(jnp.bfloat16)
    return high, (value - high.astype(jnp.float32)).astype(jnp.bfloat16)


def dot(left, right, transposed=False):
    dims = (((1,), (1 if transposed else 0,)), ((), ()))
    return lax.dot_general(left, right, dims, preferred_element_type=jnp.float32)


def polynomial(terms, z):
    value = z * terms[-1] + terms[-2]
    for term in terms[-3::-1]:
        value = value * z + term
    return value


def cos_sin(turns):
    whole = (turns + 12582912.0) - 12582912.0
    t = turns - whole
    z = t * t
    half_sin = t * polynomial(SIN_TERMS, z)
    half_cos = polynomial(COS_TERMS, z)
    return 1.0 - half_sin * half_sin, half_sin * half_cos


def send_layout(per_device, owners):
    cap = -(-per_device // (owners - SUB // ROWS_DEV + 1))
    tiles = 2 * cap + (2 * cap + 1 + 3) // 4
    return cap, tiles


def image_kernel(
    cap,
    tile_cols,
    owner_s,
    row_s,
    col_s,
    station_s,
    count_s,
    vis,
    coords,
    beams,
    left_hi,
    left_lo,
    right_hi,
    right_lo,
    small,
    out,
    beam_buf,
    sky,
    cells,
    ranks,
    sems,
):
    per_device = vis.shape[0] // 2
    owners = out.shape[0]
    live = count_s[0]
    groups = (live + GROUP - 1) // GROUP

    @pl.loop(0, groups)
    def _(g):
        for j in range(GROUP):
            n = g * GROUP + j
            for side in range(2):
                pltpu.make_async_copy(
                    beams.at[station_s[side, n]], beam_buf.at[2 * n + side], sems.at[g]
                ).start()

    out[...] = jnp.zeros_like(out)
    sky[...] = jnp.zeros_like(sky)

    @pl.loop(0, owners)
    def _(b):
        ranks[b] = 0

    taper = small[0]
    twist_re = jnp.concatenate([small[1]] * 16, axis=0)
    twist_im = jnp.concatenate([small[2]] * 16, axis=0)
    number = lax.broadcasted_iota(jnp.int32, (SUB, VROWS), 0)
    l_row = (4 * (number % 8) + number // 8 - SUB // 2).astype(jnp.float32) / SUB
    l_col = (number - SUB // 2).astype(jnp.float32) / SUB
    d_row = l_row * l_row
    d_col = l_col * l_col
    sublane = lax.broadcasted_iota(jnp.int32, (8, 128), 0)
    lane = lax.broadcasted_iota(jnp.int32, (8, 128), 1)
    lane_group = lane // SUB

    @pl.loop(0, groups)
    def _(g):
        waited = beam_buf.at[pl.ds(g * 2 * GROUP, 2 * GROUP)]
        pltpu.make_async_copy(beams.at[pl.ds(0, 2 * GROUP)], waited, sems.at[g]).wait()
        for quad in range(GROUP // 4):
            x_hi, x_lo, columns = [], [], []
            for j in range(4):
                n = g * GROUP + quad * 4 + j
                u = coords[0, pl.ds(n, 1), :]
                v = coords[1, pl.ds(n, 1), :]
                w = coords[2, pl.ds(n, 1), :]
                vis_re = vis[pl.ds(2 * n, 1), :]
                vis_im = vis[pl.ds(2 * n + 1, 1), :]
                cos_row, sin_row = cos_sin(u * l_row + w * d_row)
                cos_col, sin_col = cos_sin(v * l_col + w * d_col)
                x = jnp.concatenate(
                    [
                        vis_re * cos_row - vis_im * sin_row,
                        vis_re * sin_row + vis_im * cos_row,
                    ],
                    axis=1,
                )
                hi, lo = split(x)
                x_hi.append(hi)
                x_lo.append(lo)
                columns.append(split(cos_col) + split(sin_col))
            c_hi, c_lo, s_hi, s_lo = zip(*columns)

            def matrix(c, s):
                real = [jnp.concatenate([a, -b], axis=1) for a, b in zip(c, s)]
                imag = [jnp.concatenate([b, a], axis=1) for a, b in zip(c, s)]
                return jnp.concatenate(real + imag, axis=0)

            lhs = jnp.concatenate(x_hi + x_lo, axis=0)
            both = dot(lhs, matrix(c_hi, s_hi), True)
            sums = both[:128] + both[128:] + dot(lhs[:128], matrix(c_lo, s_lo), True)
            for j in range(4):
                n = g * GROUP + quad * 4 + j
                flat = []
                for c in range(2):
                    value = None
                    for i in range(4):
                        piece = sums[32 * j + 8 * i : 32 * j + 8 * i + 8, 128 * c : 128 * c + 128]
                        if i != j:
                            piece = pltpu.roll(piece, (SUB * (i - j)) % 128, 1)
                        value = piece if value is None else jnp.where(lane_group == i, piece, value)
                    flat.append(value)
                one_re = beam_buf[2 * n, pl.ds(0, 8, stride=2), :]
                one_im = beam_buf[2 * n, pl.ds(1, 8, stride=2), :]
                two_re = beam_buf[2 * n + 1, pl.ds(0, 8, stride=2), :]
                two_im = beam_buf[2 * n + 1, pl.ds(1, 8, stride=2), :]
                beam_re = taper * (one_re * two_re + one_im * two_im)
                beam_im = taper * (one_im * two_re - one_re * two_im)
                sky_re = beam_re * flat[0] - beam_im * flat[1]
                sky_im = beam_re * flat[1] + beam_im * flat[0]
                in_use = n < live
                place = pl.multiple_of((g % 2) * 64 + (quad * 4 + j) * 8, 8)
                sky[g // 2, pl.ds(place, 8), :] = jnp.where(in_use, sky_re, 0.0)
                sky[g // 2, pl.ds(place + 128, 8), :] = jnp.where(in_use, sky_im, 0.0)

    for half in range(per_device // 32):

        @pl.when(live > 32 * half)
        def _():
            value = jnp.concatenate([sky[2 * half], sky[2 * half + 1]], axis=1)
            hi, lo = split(value)
            z = dot(left_hi[...], hi) + dot(left_lo[...], hi) + dot(left_hi[...], lo)
            rows = []
            for k in range(2):
                z_re = z[:128, 128 * k : 128 * k + 128]
                z_im = z[128:, 128 * k : 128 * k + 128]
                y_re = z_re * twist_re - z_im * twist_im
                y_im = z_re * twist_im + z_im * twist_re
                rows.append(jnp.concatenate([y_re, y_im], axis=1))
            hi, lo = split(jnp.concatenate(rows, axis=0))
            cells[256 * half : 256 * half + 256, :] = (
                dot(hi, right_hi[...]) + dot(lo, right_hi[...]) + dot(hi, right_lo[...])
            )

    label_tile = 2 * cap + (2 * cap) // 4
    label_lane = SUB * ((2 * cap) % 4)

    @pl.loop(0, groups)
    def _(g):
        for j in range(GROUP):
            n = g * GROUP + j
            band = row_s[n] // ROWS_DEV
            shift = row_s[n] % ROWS_DEV
            rank = ranks[band]
            ranks[band] = rank + 1
            place = pl.multiple_of(n * 8, 8)
            late = sublane < shift
            last = jnp.minimum(band + 4, owners - 1)
            for c in range(2):
                value = cells[pl.ds(place, 8), 128 * c : 128 * c + 128]
                value = pltpu.roll(value, shift, 0)
                next_value = pltpu.roll(value, SUB, 1)
                spread = jnp.where(late, jnp.where(lane_group == 0, 0.0, next_value), value)
                tile = 2 * rank + c
                for o in range(4):
                    pltpu.store(out.at[band + o, tile], spread, mask=lane_group == o)
                part = tile % 4
                tail = pltpu.roll(value, SUB * (part + 1), 1)
                pltpu.store(
                    out.at[last, 2 * cap + tile // 4], tail, mask=late & (lane_group == part)
                )
            column = jnp.full((8, 128), owner_s[n] * tile_cols + col_s[n], jnp.float32)
            for o in range(5):
                here = (sublane == 0) & (lane == label_lane + o * cap + rank)
                if o == 4:
                    here = here & (sublane < shift)
                target = last if o == 4 else band + o
                pltpu.store(out.at[target, label_tile], column, mask=here)


def row_kernel(
    cap,
    received,
    first_hi,
    first_lo,
    second_hi,
    second_lo,
    twist,
    out,
    grid,
    label_v,
    label_s,
    sem,
):
    sources = received.shape[0]
    label_tile = 2 * cap + (2 * cap) // 4
    label_lane = SUB * ((2 * cap) % 4)
    label_v[...] = received[:, label_tile, 0, :].astype(jnp.int32)
    copy = pltpu.make_async_copy(label_v, label_s, sem)
    copy.start()
    grid[...] = jnp.zeros_like(grid)
    lane = lax.broadcasted_iota(jnp.int32, (8, 128), 1)
    copy.wait()

    @pl.loop(0, sources)
    def _(source):
        for i in range(cap):
            for o in range(5):
                column = label_s[source, label_lane + o * cap + i]
                tile = column // 128
                offset = column % 128
                here = pl.multiple_of(tile * 8, 8)
                place = lane - offset
                inside = (place >= 0) & (place < SUB)
                beyond = place < SUB - 128
                for c in range(2):
                    if o < 4:
                        value, part = received[source, 2 * i + c], o
                    else:
                        value = received[source, 2 * cap + (2 * i + c) // 4]
                        part = (2 * i + c) % 4
                    value = pltpu.roll(value, (offset + 128 - SUB * part) % 128, 1)
                    grid[c, pl.ds(here, 8), :] += jnp.where(inside, value, 0.0)
                    grid[c, pl.ds(here + 8, 8), :] += jnp.where(beyond, value, 0.0)

    @pl.loop(0, ROWS_DEV // 2)
    def _(pair):
        row = pair * 2
        columns = []
        for k in range(2):
            columns.append(
                jnp.concatenate(
                    [grid[c, pl.ds(row + k, LEAD, stride=ROWS_DEV), :] for c in range(2)], axis=0
                )
            )
        hi, lo = split(jnp.concatenate(columns, axis=1))
        a = dot(first_hi[...], hi) + dot(first_lo[...], hi) + dot(first_hi[...], lo)
        for k in range(2):
            a_re = a[:LEAD, 128 * k : 128 * k + 128]
            a_im = a[LEAD:, 128 * k : 128 * k + 128]
            b_re = a_re * twist[0] - a_im * twist[1]
            b_im = a_re * twist[1] + a_im * twist[0]
            hi, lo = split(jnp.concatenate([b_re, b_im], axis=1))
            result = (
                dot(second_hi[...], hi, True)
                + dot(second_lo[...], hi, True)
                + dot(second_hi[...], lo, True)
            )
            for c in range(2):
                for h in range(2):
                    out[c, pl.ds(h * 8 + row + k, TAIL, stride=16), :] = result[
                        128 * c : 128 * c + 128, 128 * h : 128 * h + 128
                    ]


def shards(
    visibility, coords, block_owner, block_row, block_col, stations, block_count, beam_terms
):
    owners = lax.axis_size("tile")
    per_device = visibility.shape[0]
    tile_cols = NG // owners
    cap, tiles = send_layout(per_device, owners)
    stations_all = beam_terms.shape[0]
    smem = pl.BlockSpec(memory_space=pltpu.SMEM)
    vmem = pl.BlockSpec(memory_space=pltpu.VMEM)
    beams = (
        beam_terms.reshape(stations_all, 2, 8, 128)
        .transpose(0, 2, 1, 3)
        .reshape(stations_all, 16, 128)
    )
    sent = pl.pallas_call(
        functools.partial(image_kernel, cap, tile_cols),
        out_shape=jax.ShapeDtypeStruct((owners, tiles, 8, 128), jnp.float32),
        in_specs=[smem] * 5 + [vmem] * 2 + [pl.BlockSpec(memory_space=pl.ANY)] + [vmem] * 5,
        out_specs=vmem,
        scratch_shapes=[
            pltpu.VMEM((2 * per_device, 16, 128), jnp.float32),
            pltpu.VMEM((per_device // 16, 256, 128), jnp.float32),
            pltpu.VMEM((per_device * 8, 256), jnp.float32),
            pltpu.SMEM((owners,), jnp.int32),
            pltpu.SemaphoreType.DMA((per_device // GROUP,)),
        ],
        compiler_params=pltpu.CompilerParams(vmem_limit_bytes=24 * 1024 * 1024),
        name="image",
    )(
        block_owner.reshape(per_device),
        block_row,
        block_col,
        stations.T,
        block_count,
        visibility.reshape(per_device * 2, VROWS),
        coords.transpose(1, 0, 2),
        beams,
        *image_tables(),
    )
    received = lax.all_to_all(sent, "tile", split_axis=0, concat_axis=0, tiled=True)
    result = pl.pallas_call(
        functools.partial(row_kernel, cap),
        out_shape=jax.ShapeDtypeStruct((2, LEAD * ROWS_DEV, TAIL), jnp.float32),
        in_specs=[vmem] * 6,
        out_specs=vmem,
        scratch_shapes=[
            pltpu.VMEM((2, (LEAD + 1) * ROWS_DEV, TAIL), jnp.float32),
            pltpu.VMEM((owners, 128), jnp.int32),
            pltpu.SMEM((owners, 128), jnp.int32),
            pltpu.SemaphoreType.DMA,
        ],
        compiler_params=pltpu.CompilerParams(vmem_limit_bytes=24 * 1024 * 1024),
        name="rows",
    )(received, *row_tables())
    return (
        result.reshape(2, LEAD, ROWS_DEV, TAIL).transpose(0, 2, 1, 3).reshape(2, ROWS_DEV, NG)
    )


def solution(mesh):
    placed = (
        P(("parts", "tile"), None, None),
        P(("parts", "tile"), None, None),
        P(("parts", "tile"), None),
        P(("parts", "tile")),
        P(("parts", "tile")),
        P(("parts", "tile"), None),
        P(("parts", "tile")),
        P(),
    )
    return jax.shard_map(
        shards,
        mesh=mesh,
        in_specs=placed,
        out_specs=P(None, ("parts", "tile"), None),
        check_vma=False,
    )
```

```python
import functools
import math

import jax
import jax.numpy as jnp
import ml_dtypes
import numpy as np
from jax import lax
from jax.experimental import pallas as pl
from jax.experimental.pallas import tpu as pltpu
from jax.sharding import PartitionSpec as P

VROWS = 128
SUB = 32
NG = 32768
ROWS_DEV = 8
LEAD = 256
TAIL = 128
GROUP = 8

SIN_TERMS = (4.442882920, -7.308245680, 3.606354030, -0.846110410, 0.109822040)
COS_TERMS = (1.414213500, -6.978850910, 5.739459580, -1.883552820, 0.310677860)


def halves(table):
    table = np.round(table, 12).astype(np.float32)
    high = table.astype(ml_dtypes.bfloat16)
    low = (table - high.astype(np.float32)).astype(ml_dtypes.bfloat16)
    return high, low


def root(numbers, length):
    angle = 2.0 * np.pi / length * (numbers % length)
    return np.cos(angle), -np.sin(angle)


def complex_left(re, im):
    return np.block([[re, -im], [im, re]])


@functools.cache
def image_tables():
    eight = np.arange(8)
    re, im = root(np.outer(eight, eight), 8)
    left = complex_left(np.kron(np.eye(16), re), np.kron(np.eye(16), im))
    lane = np.arange(128)
    twist = root(np.outer(eight, lane // SUB), SUB)
    four = 8 * np.outer(lane // SUB, lane // SUB) + np.outer(lane % SUB, lane % SUB)
    re, im = root(four, SUB)
    right = complex_left(re, im).T
    row_pos = ((4 * eight[:, None] + lane[None, :] // SUB) - SUB // 2) / SUB
    col_pos = np.broadcast_to((lane[None, :] % SUB - SUB // 2) / SUB, (8, 128))
    taper = (1 - 2 * row_pos**2) * (1 - 2 * col_pos**2) / SUB
    small = np.stack([taper, np.round(twist[0], 12), np.round(twist[1], 12)]).astype(np.float32)
    return (*halves(left), *halves(right), small)


@functools.cache
def row_tables():
    lead, tail = np.arange(LEAD), np.arange(TAIL)
    first = complex_left(*root(np.outer(lead, lead), LEAD))
    twist = np.stack(root(np.outer(lead, tail), NG)) / math.sqrt(NG)
    second = complex_left(*root(np.outer(tail, tail), TAIL))
    return (*halves(first), *halves(second), np.round(twist, 12).astype(np.float32))


def split(value):
    high = value.astype(jnp.bfloat16)
    return high, (value - high.astype(jnp.float32)).astype(jnp.bfloat16)


def dot(left, right, transposed=False):
    dims = (((1,), (1 if transposed else 0,)), ((), ()))
    return lax.dot_general(left, right, dims, preferred_element_type=jnp.float32)


def polynomial(terms, z):
    value = z * terms[-1] + terms[-2]
    for term in terms[-3::-1]:
        value = value * z + term
    return value


def cos_sin(turns):
    whole = (turns + 12582912.0) - 12582912.0
    t = turns - whole
    z = t * t
    half_sin = t * polynomial(SIN_TERMS, z)
    half_cos = polynomial(COS_TERMS, z)
    return 1.0 - half_sin * half_sin, half_sin * half_cos


def send_layout(per_device, owners):
    cap = -(-per_device // (owners - SUB // ROWS_DEV + 1))
    tiles = 2 * cap + (2 * cap + 1 + 3) // 4
    return cap, tiles


def image_kernel(
    cap,
    tile_cols,
    *refs,
):
    count_s, beams, args, out, copied = refs[0], refs[1], refs[2:13], refs[13], refs[14:25]
    beam_buf, sky, cells, ranks, sems, arg_sems = refs[25:]
    copies = [
        pltpu.make_async_copy(arg, held, arg_sems.at[k])
        for k, (arg, held) in enumerate(zip(args, copied))
    ]
    for copy in copies:
        copy.start()
    owner_s, row_s, col_s, station_s, vis, coords = copied[:6]
    left_hi, left_lo, right_hi, right_lo, small = copied[6:]
    per_device = vis.shape[0] // 2
    owners = out.shape[0]
    copies[3].wait()
    live = count_s[0]
    groups = (live + GROUP - 1) // GROUP

    @pl.loop(0, groups)
    def _(g):
        for j in range(GROUP):
            n = g * GROUP + j
            for side in range(2):
                pltpu.make_async_copy(
                    beams.at[station_s[side, n]], beam_buf.at[2 * n + side], sems.at[g]
                ).start()

    out[...] = jnp.zeros_like(out)
    sky[...] = jnp.zeros_like(sky)

    @pl.loop(0, owners)
    def _(b):
        ranks[b] = 0

    copies[4].wait()
    copies[5].wait()
    copies[10].wait()
    taper = small[0]
    twist_re = jnp.concatenate([small[1]] * 16, axis=0)
    twist_im = jnp.concatenate([small[2]] * 16, axis=0)
    number = lax.broadcasted_iota(jnp.int32, (SUB, VROWS), 0)
    l_row = (4 * (number % 8) + number // 8 - SUB // 2).astype(jnp.float32) / SUB
    l_col = (number - SUB // 2).astype(jnp.float32) / SUB
    d_row = l_row * l_row
    d_col = l_col * l_col
    sublane = lax.broadcasted_iota(jnp.int32, (8, 128), 0)
    lane = lax.broadcasted_iota(jnp.int32, (8, 128), 1)
    lane_group = lane // SUB

    @pl.loop(0, groups)
    def _(g):
        waited = beam_buf.at[pl.ds(g * 2 * GROUP, 2 * GROUP)]
        pltpu.make_async_copy(beams.at[pl.ds(0, 2 * GROUP)], waited, sems.at[g]).wait()
        for quad in range(GROUP // 4):
            x_hi, x_lo, columns = [], [], []
            for j in range(4):
                n = g * GROUP + quad * 4 + j
                u = coords[0, pl.ds(n, 1), :]
                v = coords[1, pl.ds(n, 1), :]
                w = coords[2, pl.ds(n, 1), :]
                vis_re = vis[pl.ds(2 * n, 1), :]
                vis_im = vis[pl.ds(2 * n + 1, 1), :]
                cos_row, sin_row = cos_sin(u * l_row + w * d_row)
                cos_col, sin_col = cos_sin(v * l_col + w * d_col)
                x = jnp.concatenate(
                    [
                        vis_re * cos_row - vis_im * sin_row,
                        vis_re * sin_row + vis_im * cos_row,
                    ],
                    axis=1,
                )
                hi, lo = split(x)
                x_hi.append(hi)
                x_lo.append(lo)
                columns.append(split(cos_col) + split(sin_col))
            c_hi, c_lo, s_hi, s_lo = zip(*columns)

            def matrix(c, s):
                real = [jnp.concatenate([a, -b], axis=1) for a, b in zip(c, s)]
                imag = [jnp.concatenate([b, a], axis=1) for a, b in zip(c, s)]
                return jnp.concatenate(real + imag, axis=0)

            lhs = jnp.concatenate(x_hi + x_lo, axis=0)
            both = dot(lhs, matrix(c_hi, s_hi), True)
            sums = both[:128] + both[128:] + dot(lhs[:128], matrix(c_lo, s_lo), True)
            for j in range(4):
                n = g * GROUP + quad * 4 + j
                flat = []
                for c in range(2):
                    value = None
                    for i in range(4):
                        piece = sums[32 * j + 8 * i : 32 * j + 8 * i + 8, 128 * c : 128 * c + 128]
                        if i != j:
                            piece = pltpu.roll(piece, (SUB * (i - j)) % 128, 1)
                        value = piece if value is None else jnp.where(lane_group == i, piece, value)
                    flat.append(value)
                one_re = beam_buf[2 * n, pl.ds(0, 8, stride=2), :]
                one_im = beam_buf[2 * n, pl.ds(1, 8, stride=2), :]
                two_re = beam_buf[2 * n + 1, pl.ds(0, 8, stride=2), :]
                two_im = beam_buf[2 * n + 1, pl.ds(1, 8, stride=2), :]
                beam_re = taper * (one_re * two_re + one_im * two_im)
                beam_im = taper * (one_im * two_re - one_re * two_im)
                sky_re = beam_re * flat[0] - beam_im * flat[1]
                sky_im = beam_re * flat[1] + beam_im * flat[0]
                in_use = n < live
                place = pl.multiple_of((g % 2) * 64 + (quad * 4 + j) * 8, 8)
                sky[g // 2, pl.ds(place, 8), :] = jnp.where(in_use, sky_re, 0.0)
                sky[g // 2, pl.ds(place + 128, 8), :] = jnp.where(in_use, sky_im, 0.0)

    for copy in copies[6:10] + copies[:3]:
        copy.wait()
    for half in range(per_device // 32):

        @pl.when(live > 32 * half)
        def _():
            value = jnp.concatenate([sky[2 * half], sky[2 * half + 1]], axis=1)
            hi, lo = split(value)
            z = dot(left_hi[...], hi) + dot(left_lo[...], hi) + dot(left_hi[...], lo)
            rows = []
            for k in range(2):
                z_re = z[:128, 128 * k : 128 * k + 128]
                z_im = z[128:, 128 * k : 128 * k + 128]
                y_re = z_re * twist_re - z_im * twist_im
                y_im = z_re * twist_im + z_im * twist_re
                rows.append(jnp.concatenate([y_re, y_im], axis=1))
            hi, lo = split(jnp.concatenate(rows, axis=0))
            cells[256 * half : 256 * half + 256, :] = (
                dot(hi, right_hi[...]) + dot(lo, right_hi[...]) + dot(hi, right_lo[...])
            )

    label_tile = 2 * cap + (2 * cap) // 4
    label_lane = SUB * ((2 * cap) % 4)

    @pl.loop(0, groups)
    def _(g):
        for j in range(GROUP):
            n = g * GROUP + j
            band = row_s[n] // ROWS_DEV
            shift = row_s[n] % ROWS_DEV
            rank = ranks[band]
            ranks[band] = rank + 1
            place = pl.multiple_of(n * 8, 8)
            late = sublane < shift
            last = jnp.minimum(band + 4, owners - 1)
            for c in range(2):
                value = cells[pl.ds(place, 8), 128 * c : 128 * c + 128]
                value = pltpu.roll(value, shift, 0)
                next_value = pltpu.roll(value, SUB, 1)
                spread = jnp.where(late, jnp.where(lane_group == 0, 0.0, next_value), value)
                tile = 2 * rank + c
                for o in range(4):
                    pltpu.store(out.at[band + o, tile], spread, mask=lane_group == o)
                part = tile % 4
                tail = pltpu.roll(value, SUB * (part + 1), 1)
                pltpu.store(
                    out.at[last, 2 * cap + tile // 4], tail, mask=late & (lane_group == part)
                )
            column = jnp.full((8, 128), owner_s[n] * tile_cols + col_s[n], jnp.float32)
            for o in range(5):
                here = (sublane == 0) & (lane == label_lane + o * cap + rank)
                if o == 4:
                    here = here & (sublane < shift)
                target = last if o == 4 else band + o
                pltpu.store(out.at[target, label_tile], column, mask=here)


def row_kernel(
    cap,
    received,
    first_hi,
    first_lo,
    second_hi,
    second_lo,
    twist,
    out,
    grid,
    label_v,
    label_s,
    sem,
):
    sources = received.shape[0]
    label_tile = 2 * cap + (2 * cap) // 4
    label_lane = SUB * ((2 * cap) % 4)
    label_v[...] = received[:, label_tile, 0, :].astype(jnp.int32)
    copy = pltpu.make_async_copy(label_v, label_s, sem)
    copy.start()
    grid[...] = jnp.zeros_like(grid)
    lane = lax.broadcasted_iota(jnp.int32, (8, 128), 1)
    copy.wait()

    @pl.loop(0, sources)
    def _(source):
        for i in range(cap):
            for o in range(5):
                column = label_s[source, label_lane + o * cap + i]
                tile = column // 128
                offset = column % 128
                here = pl.multiple_of(tile * 8, 8)
                place = lane - offset
                inside = (place >= 0) & (place < SUB)
                beyond = place < SUB - 128
                for c in range(2):
                    if o < 4:
                        value, part = received[source, 2 * i + c], o
                    else:
                        value = received[source, 2 * cap + (2 * i + c) // 4]
                        part = (2 * i + c) % 4
                    value = pltpu.roll(value, (offset + 128 - SUB * part) % 128, 1)
                    grid[c, pl.ds(here, 8), :] += jnp.where(inside, value, 0.0)
                    grid[c, pl.ds(here + 8, 8), :] += jnp.where(beyond, value, 0.0)

    @pl.loop(0, ROWS_DEV // 2)
    def _(pair):
        row = pair * 2
        columns = []
        for k in range(2):
            columns.append(
                jnp.concatenate(
                    [grid[c, pl.ds(row + k, LEAD, stride=ROWS_DEV), :] for c in range(2)], axis=0
                )
            )
        hi, lo = split(jnp.concatenate(columns, axis=1))
        a = dot(first_hi[...], hi) + dot(first_lo[...], hi) + dot(first_hi[...], lo)
        for k in range(2):
            a_re = a[:LEAD, 128 * k : 128 * k + 128]
            a_im = a[LEAD:, 128 * k : 128 * k + 128]
            b_re = a_re * twist[0] - a_im * twist[1]
            b_im = a_re * twist[1] + a_im * twist[0]
            hi, lo = split(jnp.concatenate([b_re, b_im], axis=1))
            result = (
                dot(second_hi[...], hi, True)
                + dot(second_lo[...], hi, True)
                + dot(second_hi[...], lo, True)
            )
            for c in range(2):
                for h in range(2):
                    out[c, pl.ds(h * 8 + row + k, TAIL, stride=16), :] = result[
                        128 * c : 128 * c + 128, 128 * h : 128 * h + 128
                    ]


def shards(
    visibility, coords, block_owner, block_row, block_col, stations, block_count, beam_terms
):
    owners = lax.axis_size("tile")
    per_device = visibility.shape[0]
    tile_cols = NG // owners
    cap, tiles = send_layout(per_device, owners)
    stations_all = beam_terms.shape[0]
    vmem = pl.BlockSpec(memory_space=pltpu.VMEM)
    beams = (
        beam_terms.reshape(stations_all, 2, 8, 128)
        .transpose(0, 2, 1, 3)
        .reshape(stations_all, 16, 128)
    )
    labels = (
        block_owner.reshape(per_device),
        block_row,
        block_col,
        stations.T,
    )
    values = (
        visibility.reshape(per_device * 2, VROWS),
        coords.transpose(1, 0, 2),
        *image_tables(),
    )
    hbm = pl.BlockSpec(memory_space=pltpu.HBM)
    sent = pl.pallas_call(
        functools.partial(image_kernel, cap, tile_cols),
        out_shape=jax.ShapeDtypeStruct((owners, tiles, 8, 128), jnp.float32),
        in_specs=[pl.BlockSpec(memory_space=pltpu.SMEM)] + [hbm] * (1 + len(labels) + len(values)),
        out_specs=vmem,
        scratch_shapes=[
            *(pltpu.SMEM(label.shape, label.dtype) for label in labels),
            *(pltpu.VMEM(value.shape, value.dtype) for value in values),
            pltpu.VMEM((2 * per_device, 16, 128), jnp.float32),
            pltpu.VMEM((per_device // 16, 256, 128), jnp.float32),
            pltpu.VMEM((per_device * 8, 256), jnp.float32),
            pltpu.SMEM((owners,), jnp.int32),
            pltpu.SemaphoreType.DMA((per_device // GROUP,)),
            pltpu.SemaphoreType.DMA((len(labels) + len(values),)),
        ],
        compiler_params=pltpu.CompilerParams(vmem_limit_bytes=24 * 1024 * 1024),
        name="image",
    )(
        block_count,
        *(pltpu.with_memory_space_constraint(x, pltpu.HBM) for x in (beams, *labels, *values)),
    )
    received = lax.all_to_all(sent, "tile", split_axis=0, concat_axis=0, tiled=True)
    result = pl.pallas_call(
        functools.partial(row_kernel, cap),
        out_shape=jax.ShapeDtypeStruct((2, LEAD * ROWS_DEV, TAIL), jnp.float32),
        in_specs=[vmem] * 6,
        out_specs=vmem,
        scratch_shapes=[
            pltpu.VMEM((2, (LEAD + 1) * ROWS_DEV, TAIL), jnp.float32),
            pltpu.VMEM((owners, 128), jnp.int32),
            pltpu.SMEM((owners, 128), jnp.int32),
            pltpu.SemaphoreType.DMA,
        ],
        compiler_params=pltpu.CompilerParams(vmem_limit_bytes=24 * 1024 * 1024),
        name="rows",
    )(received, *row_tables())
    return (
        result.reshape(2, LEAD, ROWS_DEV, TAIL).transpose(0, 2, 1, 3).reshape(2, ROWS_DEV, NG)
    )


def solution(mesh):
    placed = (
        P(("parts", "tile"), None, None),
        P(("parts", "tile"), None, None),
        P(("parts", "tile"), None),
        P(("parts", "tile")),
        P(("parts", "tile")),
        P(("parts", "tile"), None),
        P(("parts", "tile")),
        P(),
    )
    return jax.shard_map(
        shards,
        mesh=mesh,
        in_specs=placed,
        out_specs=P(None, ("parts", "tile"), None),
        check_vma=False,
    )
```

```python
import functools
import math

import jax
import jax.numpy as jnp
import ml_dtypes
import numpy as np
from jax import lax
from jax.experimental import pallas as pl
from jax.experimental.pallas import tpu as pltpu
from jax.sharding import PartitionSpec as P

VROWS = 128
SUB = 32
NG = 32768
ROWS_DEV = 8
LEAD = 256
TAIL = 128
GROUP = 8

SIN_TERMS = (4.442882920, -7.308245680, 3.606354030, -0.846110410, 0.109822040)
COS_TERMS = (1.414213500, -6.978850910, 5.739459580, -1.883552820, 0.310677860)


def halves(table):
    table = np.round(table, 12).astype(np.float32)
    high = table.astype(ml_dtypes.bfloat16)
    low = (table - high.astype(np.float32)).astype(ml_dtypes.bfloat16)
    return high, low


def root(numbers, length):
    angle = 2.0 * np.pi / length * (numbers % length)
    return np.cos(angle), -np.sin(angle)


def complex_left(re, im):
    return np.block([[re, -im], [im, re]])


@functools.cache
def image_tables():
    eight = np.arange(8)
    re, im = root(np.outer(eight, eight), 8)
    left = complex_left(np.kron(np.eye(16), re), np.kron(np.eye(16), im))
    lane = np.arange(128)
    twist = root(np.outer(eight, lane // SUB), SUB)
    four = 8 * np.outer(lane // SUB, lane // SUB) + np.outer(lane % SUB, lane % SUB)
    re, im = root(four, SUB)
    right = complex_left(re, im).T
    row_pos = ((4 * eight[:, None] + lane[None, :] // SUB) - SUB // 2) / SUB
    col_pos = np.broadcast_to((lane[None, :] % SUB - SUB // 2) / SUB, (8, 128))
    taper = (1 - 2 * row_pos**2) * (1 - 2 * col_pos**2) / SUB
    small = np.stack([taper, np.round(twist[0], 12), np.round(twist[1], 12)]).astype(np.float32)
    return (*halves(left), *halves(right), small)


@functools.cache
def row_tables():
    lead, tail = np.arange(LEAD), np.arange(TAIL)
    first = complex_left(*root(np.outer(lead, lead), LEAD))
    twist = np.stack(root(np.outer(lead, tail), NG)) / math.sqrt(NG)
    second = complex_left(*root(np.outer(tail, tail), TAIL))
    return (*halves(first), *halves(second), np.round(twist, 12).astype(np.float32))


def split(value):
    high = value.astype(jnp.bfloat16)
    return high, (value - high.astype(jnp.float32)).astype(jnp.bfloat16)


def dot(left, right, transposed=False):
    dims = (((1,), (1 if transposed else 0,)), ((), ()))
    return lax.dot_general(left, right, dims, preferred_element_type=jnp.float32)


def polynomial(terms, z):
    value = z * terms[-1] + terms[-2]
    for term in terms[-3::-1]:
        value = value * z + term
    return value


def cos_sin(turns):
    whole = (turns + 12582912.0) - 12582912.0
    t = turns - whole
    z = t * t
    half_sin = t * polynomial(SIN_TERMS, z)
    half_cos = polynomial(COS_TERMS, z)
    return 1.0 - half_sin * half_sin, half_sin * half_cos


def send_layout(per_device, owners):
    cap = -(-per_device // (owners - SUB // ROWS_DEV + 1))
    tiles = 2 * cap + (2 * cap + 1 + 3) // 4
    return cap, tiles


def image_kernel(
    cap,
    tile_cols,
    *refs,
):
    me = lax.axis_index("tile")
    owners = lax.axis_size("tile")
    count_s, beams, args, refs = refs[0], refs[1], refs[2:13], refs[13:]
    slots, copied = refs[:owners], refs[owners : owners + 11]
    out, beam_buf, sky, cells, ranks, sems, arg_sems = refs[owners + 11 :]
    copies = [
        pltpu.make_async_copy(arg, held, arg_sems.at[k])
        for k, (arg, held) in enumerate(zip(args, copied))
    ]
    for copy in copies:
        copy.start()
    owner_s, row_s, col_s, station_s, vis, coords = copied[:6]
    left_hi, left_lo, right_hi, right_lo, small = copied[6:]
    per_device = vis.shape[0] // 2
    copies[3].wait()
    live = count_s[0]
    groups = (live + GROUP - 1) // GROUP

    @pl.loop(0, groups)
    def _(g):
        for j in range(GROUP):
            n = g * GROUP + j
            for side in range(2):
                pltpu.make_async_copy(
                    beams.at[station_s[side, n]], beam_buf.at[2 * n + side], sems.at[g]
                ).start()

    out[...] = jnp.zeros_like(out)
    sky[...] = jnp.zeros_like(sky)

    @pl.loop(0, owners)
    def _(b):
        ranks[b] = 0

    copies[4].wait()
    copies[5].wait()
    copies[10].wait()
    taper = small[0]
    twist_re = jnp.concatenate([small[1]] * 16, axis=0)
    twist_im = jnp.concatenate([small[2]] * 16, axis=0)
    number = lax.broadcasted_iota(jnp.int32, (SUB, VROWS), 0)
    l_row = (4 * (number % 8) + number // 8 - SUB // 2).astype(jnp.float32) / SUB
    l_col = (number - SUB // 2).astype(jnp.float32) / SUB
    d_row = l_row * l_row
    d_col = l_col * l_col
    sublane = lax.broadcasted_iota(jnp.int32, (8, 128), 0)
    lane = lax.broadcasted_iota(jnp.int32, (8, 128), 1)
    lane_group = lane // SUB

    @pl.loop(0, groups)
    def _(g):
        waited = beam_buf.at[pl.ds(g * 2 * GROUP, 2 * GROUP)]
        pltpu.make_async_copy(beams.at[pl.ds(0, 2 * GROUP)], waited, sems.at[g]).wait()
        for quad in range(GROUP // 4):
            x_hi, x_lo, columns = [], [], []
            for j in range(4):
                n = g * GROUP + quad * 4 + j
                u = coords[0, pl.ds(n, 1), :]
                v = coords[1, pl.ds(n, 1), :]
                w = coords[2, pl.ds(n, 1), :]
                vis_re = vis[pl.ds(2 * n, 1), :]
                vis_im = vis[pl.ds(2 * n + 1, 1), :]
                cos_row, sin_row = cos_sin(u * l_row + w * d_row)
                cos_col, sin_col = cos_sin(v * l_col + w * d_col)
                x = jnp.concatenate(
                    [
                        vis_re * cos_row - vis_im * sin_row,
                        vis_re * sin_row + vis_im * cos_row,
                    ],
                    axis=1,
                )
                hi, lo = split(x)
                x_hi.append(hi)
                x_lo.append(lo)
                columns.append(split(cos_col) + split(sin_col))
            c_hi, c_lo, s_hi, s_lo = zip(*columns)

            def matrix(c, s):
                real = [jnp.concatenate([a, -b], axis=1) for a, b in zip(c, s)]
                imag = [jnp.concatenate([b, a], axis=1) for a, b in zip(c, s)]
                return jnp.concatenate(real + imag, axis=0)

            lhs = jnp.concatenate(x_hi + x_lo, axis=0)
            both = dot(lhs, matrix(c_hi, s_hi), True)
            sums = both[:128] + both[128:] + dot(lhs[:128], matrix(c_lo, s_lo), True)
            for j in range(4):
                n = g * GROUP + quad * 4 + j
                flat = []
                for c in range(2):
                    value = None
                    for i in range(4):
                        piece = sums[32 * j + 8 * i : 32 * j + 8 * i + 8, 128 * c : 128 * c + 128]
                        if i != j:
                            piece = pltpu.roll(piece, (SUB * (i - j)) % 128, 1)
                        value = piece if value is None else jnp.where(lane_group == i, piece, value)
                    flat.append(value)
                one_re = beam_buf[2 * n, pl.ds(0, 8, stride=2), :]
                one_im = beam_buf[2 * n, pl.ds(1, 8, stride=2), :]
                two_re = beam_buf[2 * n + 1, pl.ds(0, 8, stride=2), :]
                two_im = beam_buf[2 * n + 1, pl.ds(1, 8, stride=2), :]
                beam_re = taper * (one_re * two_re + one_im * two_im)
                beam_im = taper * (one_im * two_re - one_re * two_im)
                sky_re = beam_re * flat[0] - beam_im * flat[1]
                sky_im = beam_re * flat[1] + beam_im * flat[0]
                in_use = n < live
                place = pl.multiple_of((g % 2) * 64 + (quad * 4 + j) * 8, 8)
                sky[g // 2, pl.ds(place, 8), :] = jnp.where(in_use, sky_re, 0.0)
                sky[g // 2, pl.ds(place + 128, 8), :] = jnp.where(in_use, sky_im, 0.0)

    for copy in copies[6:10] + copies[:3]:
        copy.wait()
    for half in range(per_device // 32):

        @pl.when(live > 32 * half)
        def _():
            value = jnp.concatenate([sky[2 * half], sky[2 * half + 1]], axis=1)
            hi, lo = split(value)
            z = dot(left_hi[...], hi) + dot(left_lo[...], hi) + dot(left_hi[...], lo)
            rows = []
            for k in range(2):
                z_re = z[:128, 128 * k : 128 * k + 128]
                z_im = z[128:, 128 * k : 128 * k + 128]
                y_re = z_re * twist_re - z_im * twist_im
                y_im = z_re * twist_im + z_im * twist_re
                rows.append(jnp.concatenate([y_re, y_im], axis=1))
            hi, lo = split(jnp.concatenate(rows, axis=0))
            cells[256 * half : 256 * half + 256, :] = (
                dot(hi, right_hi[...]) + dot(lo, right_hi[...]) + dot(hi, right_lo[...])
            )

    label_tile = 2 * cap + (2 * cap) // 4
    label_lane = SUB * ((2 * cap) % 4)

    @pl.loop(0, groups)
    def _(g):
        for j in range(GROUP):
            n = g * GROUP + j
            band = row_s[n] // ROWS_DEV
            shift = row_s[n] % ROWS_DEV
            rank = ranks[band]
            ranks[band] = rank + 1
            place = pl.multiple_of(n * 8, 8)
            late = sublane < shift
            last = jnp.minimum(band + 4, owners - 1)
            for c in range(2):
                value = cells[pl.ds(place, 8), 128 * c : 128 * c + 128]
                value = pltpu.roll(value, shift, 0)
                next_value = pltpu.roll(value, SUB, 1)
                spread = jnp.where(late, jnp.where(lane_group == 0, 0.0, next_value), value)
                tile = 2 * rank + c
                for o in range(4):
                    pltpu.store(out.at[(band + o) ^ me, tile], spread, mask=lane_group == o)
                part = tile % 4
                tail = pltpu.roll(value, SUB * (part + 1), 1)
                pltpu.store(
                    out.at[last ^ me, 2 * cap + tile // 4], tail, mask=late & (lane_group == part)
                )
            column = jnp.full((8, 128), owner_s[n] * tile_cols + col_s[n], jnp.float32)
            for o in range(5):
                here = (sublane == 0) & (lane == label_lane + o * cap + rank)
                if o == 4:
                    here = here & (sublane < shift)
                target = last if o == 4 else band + o
                pltpu.store(out.at[target ^ me, label_tile], column, mask=here)

    for k, slot in enumerate(slots):
        slot[...] = out[k]


def row_kernel(
    cap,
    first_hi,
    first_lo,
    second_hi,
    second_lo,
    twist,
    *refs,
):
    sources = lax.axis_size("tile")
    slots = refs[:sources]
    out, received, grid, label_v, label_s, sem = refs[sources:]
    for k, slot in enumerate(slots):
        received[k] = slot[...]
    label_tile = 2 * cap + (2 * cap) // 4
    label_lane = SUB * ((2 * cap) % 4)
    label_v[...] = received[:, label_tile, 0, :].astype(jnp.int32)
    copy = pltpu.make_async_copy(label_v, label_s, sem)
    copy.start()
    grid[...] = jnp.zeros_like(grid)
    lane = lax.broadcasted_iota(jnp.int32, (8, 128), 1)
    copy.wait()

    @pl.loop(0, sources)
    def _(source):
        for i in range(cap):
            for o in range(5):
                column = label_s[source, label_lane + o * cap + i]
                tile = column // 128
                offset = column % 128
                here = pl.multiple_of(tile * 8, 8)
                place = lane - offset
                inside = (place >= 0) & (place < SUB)
                beyond = place < SUB - 128
                for c in range(2):
                    if o < 4:
                        value, part = received[source, 2 * i + c], o
                    else:
                        value = received[source, 2 * cap + (2 * i + c) // 4]
                        part = (2 * i + c) % 4
                    value = pltpu.roll(value, (offset + 128 - SUB * part) % 128, 1)
                    grid[c, pl.ds(here, 8), :] += jnp.where(inside, value, 0.0)
                    grid[c, pl.ds(here + 8, 8), :] += jnp.where(beyond, value, 0.0)

    @pl.loop(0, ROWS_DEV // 2)
    def _(pair):
        row = pair * 2
        columns = []
        for k in range(2):
            columns.append(
                jnp.concatenate(
                    [grid[c, pl.ds(row + k, LEAD, stride=ROWS_DEV), :] for c in range(2)], axis=0
                )
            )
        hi, lo = split(jnp.concatenate(columns, axis=1))
        a = dot(first_hi[...], hi) + dot(first_lo[...], hi) + dot(first_hi[...], lo)
        for k in range(2):
            a_re = a[:LEAD, 128 * k : 128 * k + 128]
            a_im = a[LEAD:, 128 * k : 128 * k + 128]
            b_re = a_re * twist[0] - a_im * twist[1]
            b_im = a_re * twist[1] + a_im * twist[0]
            hi, lo = split(jnp.concatenate([b_re, b_im], axis=1))
            result = (
                dot(second_hi[...], hi, True)
                + dot(second_lo[...], hi, True)
                + dot(second_hi[...], lo, True)
            )
            for c in range(2):
                for h in range(2):
                    out[c, pl.ds(h * 8 + row + k, TAIL, stride=16), :] = result[
                        128 * c : 128 * c + 128, 128 * h : 128 * h + 128
                    ]


def shards(
    visibility, coords, block_owner, block_row, block_col, stations, block_count, beam_terms
):
    owners = lax.axis_size("tile")
    per_device = visibility.shape[0]
    tile_cols = NG // owners
    cap, tiles = send_layout(per_device, owners)
    stations_all = beam_terms.shape[0]
    vmem = pl.BlockSpec(memory_space=pltpu.VMEM)
    beams = (
        beam_terms.reshape(stations_all, 2, 8, 128)
        .transpose(0, 2, 1, 3)
        .reshape(stations_all, 16, 128)
    )
    labels = (
        block_owner.reshape(per_device),
        block_row,
        block_col,
        stations.T,
    )
    values = (
        visibility.reshape(per_device * 2, VROWS),
        coords.transpose(1, 0, 2),
        *image_tables(),
    )
    hbm = pl.BlockSpec(memory_space=pltpu.HBM)
    sent = pl.pallas_call(
        functools.partial(image_kernel, cap, tile_cols),
        out_shape=[jax.ShapeDtypeStruct((tiles, 8, 128), jnp.float32)] * owners,
        in_specs=[pl.BlockSpec(memory_space=pltpu.SMEM)] + [hbm] * (1 + len(labels) + len(values)),
        out_specs=[vmem] * owners,
        scratch_shapes=[
            *(pltpu.SMEM(label.shape, label.dtype) for label in labels),
            *(pltpu.VMEM(value.shape, value.dtype) for value in values),
            pltpu.VMEM((owners, tiles, 8, 128), jnp.float32),
            pltpu.VMEM((2 * per_device, 16, 128), jnp.float32),
            pltpu.VMEM((per_device // 16, 256, 128), jnp.float32),
            pltpu.VMEM((per_device * 8, 256), jnp.float32),
            pltpu.SMEM((owners,), jnp.int32),
            pltpu.SemaphoreType.DMA((per_device // GROUP,)),
            pltpu.SemaphoreType.DMA((len(labels) + len(values),)),
        ],
        compiler_params=pltpu.CompilerParams(vmem_limit_bytes=24 * 1024 * 1024),
        name="image",
    )(
        block_count,
        *(pltpu.with_memory_space_constraint(x, pltpu.HBM) for x in (beams, *labels, *values)),
    )
    received = list(sent)
    for k in range(owners - 1, 0, -1):
        received[k] = lax.ppermute(
            sent[k], "tile", [(source, source ^ k) for source in range(owners)]
        )
    result = pl.pallas_call(
        functools.partial(row_kernel, cap),
        out_shape=jax.ShapeDtypeStruct((2, LEAD * ROWS_DEV, TAIL), jnp.float32),
        in_specs=[vmem] * (5 + owners),
        out_specs=vmem,
        scratch_shapes=[
            pltpu.VMEM((owners, tiles, 8, 128), jnp.float32),
            pltpu.VMEM((2, (LEAD + 1) * ROWS_DEV, TAIL), jnp.float32),
            pltpu.VMEM((owners, 128), jnp.int32),
            pltpu.SMEM((owners, 128), jnp.int32),
            pltpu.SemaphoreType.DMA,
        ],
        compiler_params=pltpu.CompilerParams(vmem_limit_bytes=24 * 1024 * 1024),
        name="rows",
    )(*row_tables(), *received)
    return (
        result.reshape(2, LEAD, ROWS_DEV, TAIL).transpose(0, 2, 1, 3).reshape(2, ROWS_DEV, NG)
    )


def solution(mesh):
    placed = (
        P(("parts", "tile"), None, None),
        P(("parts", "tile"), None, None),
        P(("parts", "tile"), None),
        P(("parts", "tile")),
        P(("parts", "tile")),
        P(("parts", "tile"), None),
        P(("parts", "tile")),
        P(),
    )
    return jax.shard_map(
        shards,
        mesh=mesh,
        in_specs=placed,
        out_specs=P(None, ("parts", "tile"), None),
        check_vma=False,
    )
```

```python
import functools
import math

import jax
import jax.numpy as jnp
import ml_dtypes
import numpy as np
from jax import lax
from jax.experimental import pallas as pl
from jax.experimental.pallas import tpu as pltpu
from jax.sharding import PartitionSpec as P

VROWS = 128
SUB = 32
NG = 32768
ROWS_DEV = 8
LEAD = 256
TAIL = 128
GROUP = 8

SIN_TERMS = (4.442882920, -7.308245680, 3.606354030, -0.846110410, 0.109822040)
COS_TERMS = (1.414213500, -6.978850910, 5.739459580, -1.883552820, 0.310677860)


def halves(table):
    table = np.round(table, 12).astype(np.float32)
    high = table.astype(ml_dtypes.bfloat16)
    low = (table - high.astype(np.float32)).astype(ml_dtypes.bfloat16)
    return high, low


def root(numbers, length):
    angle = 2.0 * np.pi / length * (numbers % length)
    return np.cos(angle), -np.sin(angle)


def complex_left(re, im):
    return np.block([[re, -im], [im, re]])


@functools.cache
def image_tables():
    eight = np.arange(8)
    re, im = root(np.outer(eight, eight), 8)
    left = complex_left(np.kron(np.eye(16), re), np.kron(np.eye(16), im))
    lane = np.arange(128)
    twist = root(np.outer(eight, lane // SUB), SUB)
    four = 8 * np.outer(lane // SUB, lane // SUB) + np.outer(lane % SUB, lane % SUB)
    re, im = root(four, SUB)
    right = complex_left(re, im).T
    row_pos = ((4 * eight[:, None] + lane[None, :] // SUB) - SUB // 2) / SUB
    col_pos = np.broadcast_to((lane[None, :] % SUB - SUB // 2) / SUB, (8, 128))
    taper = (1 - 2 * row_pos**2) * (1 - 2 * col_pos**2) / SUB
    small = np.stack([taper, np.round(twist[0], 12), np.round(twist[1], 12)]).astype(np.float32)
    return (*halves(left), *halves(right), small)


@functools.cache
def row_tables():
    lead, tail = np.arange(LEAD), np.arange(TAIL)
    first = complex_left(*root(np.outer(lead, lead), LEAD))
    twist = np.stack(root(np.outer(lead, tail), NG)) / math.sqrt(NG)
    second = complex_left(*root(np.outer(tail, tail), TAIL))
    return (*halves(first), *halves(second), np.round(twist, 12).astype(np.float32))


def split(value):
    high = value.astype(jnp.bfloat16)
    return high, (value - high.astype(jnp.float32)).astype(jnp.bfloat16)


def dot(left, right, transposed=False):
    dims = (((1,), (1 if transposed else 0,)), ((), ()))
    return lax.dot_general(left, right, dims, preferred_element_type=jnp.float32)


def polynomial(terms, z):
    value = z * terms[-1] + terms[-2]
    for term in terms[-3::-1]:
        value = value * z + term
    return value


def cos_sin(turns):
    whole = (turns + 12582912.0) - 12582912.0
    t = turns - whole
    z = t * t
    half_sin = t * polynomial(SIN_TERMS, z)
    half_cos = polynomial(COS_TERMS, z)
    return 1.0 - half_sin * half_sin, half_sin * half_cos


def send_layout(per_device, owners):
    cap = -(-per_device // (owners - SUB // ROWS_DEV + 1))
    tiles = 2 * cap + (2 * cap + 1 + 3) // 4
    return cap, tiles


def image_kernel(
    cap,
    tile_cols,
    *refs,
):
    count_s, beams, args, out, copied = refs[0], refs[1], refs[2:13], refs[13], refs[14:25]
    beam_buf, sky, cells, ranks, sems, arg_sems = refs[25:]
    copies = [
        pltpu.make_async_copy(arg, held, arg_sems.at[k])
        for k, (arg, held) in enumerate(zip(args, copied))
    ]
    for copy in copies:
        copy.start()
    owner_s, row_s, col_s, station_s, vis, coords = copied[:6]
    left_hi, left_lo, right_hi, right_lo, small = copied[6:]
    per_device = vis.shape[0] // 2
    owners = out.shape[0]
    out[...] = jnp.zeros_like(out)
    sky[...] = jnp.zeros_like(sky)
    for b in range(owners):
        ranks[b] = 0
    copies[3].wait()
    live = count_s[0]
    groups = (live + GROUP - 1) // GROUP

    @pl.loop(0, groups)
    def _(g):
        for j in range(GROUP):
            n = g * GROUP + j
            for side in range(2):
                pltpu.make_async_copy(
                    beams.at[station_s[side, n]], beam_buf.at[2 * n + side], sems.at[g]
                ).start()

    copies[4].wait()
    copies[5].wait()
    copies[10].wait()
    taper = small[0]
    twist_re = jnp.concatenate([small[1]] * 16, axis=0)
    twist_im = jnp.concatenate([small[2]] * 16, axis=0)
    number = lax.broadcasted_iota(jnp.int32, (SUB, VROWS), 0)
    l_row = (4 * (number % 8) + number // 8 - SUB // 2).astype(jnp.float32) / SUB
    l_col = (number - SUB // 2).astype(jnp.float32) / SUB
    d_row = l_row * l_row
    d_col = l_col * l_col
    sublane = lax.broadcasted_iota(jnp.int32, (8, 128), 0)
    lane = lax.broadcasted_iota(jnp.int32, (8, 128), 1)
    lane_group = lane // SUB

    @pl.loop(0, groups)
    def _(g):
        waited = beam_buf.at[pl.ds(g * 2 * GROUP, 2 * GROUP)]
        pltpu.make_async_copy(beams.at[pl.ds(0, 2 * GROUP)], waited, sems.at[g]).wait()
        for quad in range(GROUP // 4):
            x_hi, x_lo, columns = [], [], []
            for j in range(4):
                n = g * GROUP + quad * 4 + j
                u = coords[0, pl.ds(n, 1), :]
                v = coords[1, pl.ds(n, 1), :]
                w = coords[2, pl.ds(n, 1), :]
                vis_re = vis[pl.ds(2 * n, 1), :]
                vis_im = vis[pl.ds(2 * n + 1, 1), :]
                cos_row, sin_row = cos_sin(u * l_row + w * d_row)
                cos_col, sin_col = cos_sin(v * l_col + w * d_col)
                x = jnp.concatenate(
                    [
                        vis_re * cos_row - vis_im * sin_row,
                        vis_re * sin_row + vis_im * cos_row,
                    ],
                    axis=1,
                )
                hi, lo = split(x)
                x_hi.append(hi)
                x_lo.append(lo)
                columns.append(split(cos_col) + split(sin_col))
            c_hi, c_lo, s_hi, s_lo = zip(*columns)

            def matrix(c, s):
                real = [jnp.concatenate([a, -b], axis=1) for a, b in zip(c, s)]
                imag = [jnp.concatenate([b, a], axis=1) for a, b in zip(c, s)]
                return jnp.concatenate(real + imag, axis=0)

            lhs = jnp.concatenate(x_hi + x_lo, axis=0)
            both = dot(lhs, matrix(c_hi, s_hi), True)
            sums = both[:128] + both[128:] + dot(lhs[:128], matrix(c_lo, s_lo), True)
            for j in range(4):
                n = g * GROUP + quad * 4 + j
                flat = []
                for c in range(2):
                    value = None
                    for i in range(4):
                        piece = sums[32 * j + 8 * i : 32 * j + 8 * i + 8, 128 * c : 128 * c + 128]
                        if i != j:
                            piece = pltpu.roll(piece, (SUB * (i - j)) % 128, 1)
                        value = piece if value is None else jnp.where(lane_group == i, piece, value)
                    flat.append(value)
                one_re = beam_buf[2 * n, pl.ds(0, 8, stride=2), :]
                one_im = beam_buf[2 * n, pl.ds(1, 8, stride=2), :]
                two_re = beam_buf[2 * n + 1, pl.ds(0, 8, stride=2), :]
                two_im = beam_buf[2 * n + 1, pl.ds(1, 8, stride=2), :]
                beam_re = taper * (one_re * two_re + one_im * two_im)
                beam_im = taper * (one_im * two_re - one_re * two_im)
                sky_re = beam_re * flat[0] - beam_im * flat[1]
                sky_im = beam_re * flat[1] + beam_im * flat[0]
                in_use = n < live
                place = pl.multiple_of((g % 2) * 64 + (quad * 4 + j) * 8, 8)
                sky[g // 2, pl.ds(place, 8), :] = jnp.where(in_use, sky_re, 0.0)
                sky[g // 2, pl.ds(place + 128, 8), :] = jnp.where(in_use, sky_im, 0.0)

    for copy in copies[6:10] + copies[:3]:
        copy.wait()
    for half in range(per_device // 32):

        @pl.when(live > 32 * half)
        def _():
            value = jnp.concatenate([sky[2 * half], sky[2 * half + 1]], axis=1)
            hi, lo = split(value)
            z = dot(left_hi[...], hi) + dot(left_lo[...], hi) + dot(left_hi[...], lo)
            rows = []
            for k in range(2):
                z_re = z[:128, 128 * k : 128 * k + 128]
                z_im = z[128:, 128 * k : 128 * k + 128]
                y_re = z_re * twist_re - z_im * twist_im
                y_im = z_re * twist_im + z_im * twist_re
                rows.append(jnp.concatenate([y_re, y_im], axis=1))
            hi, lo = split(jnp.concatenate(rows, axis=0))
            cells[256 * half : 256 * half + 256, :] = (
                dot(hi, right_hi[...]) + dot(lo, right_hi[...]) + dot(hi, right_lo[...])
            )

    label_tile = 2 * cap + (2 * cap) // 4
    label_lane = SUB * ((2 * cap) % 4)

    @pl.loop(0, groups)
    def _(g):
        for j in range(GROUP):
            n = g * GROUP + j
            band = row_s[n] // ROWS_DEV
            shift = row_s[n] % ROWS_DEV
            rank = ranks[band]
            ranks[band] = rank + 1
            place = pl.multiple_of(n * 8, 8)
            late = sublane < shift
            last = jnp.minimum(band + 4, owners - 1)
            for c in range(2):
                value = cells[pl.ds(place, 8), 128 * c : 128 * c + 128]
                value = pltpu.roll(value, shift, 0)
                next_value = pltpu.roll(value, SUB, 1)
                spread = jnp.where(late, jnp.where(lane_group == 0, 0.0, next_value), value)
                tile = 2 * rank + c
                for o in range(4):
                    pltpu.store(out.at[band + o, tile], spread, mask=lane_group == o)
                part = tile % 4
                tail = pltpu.roll(value, SUB * (part + 1), 1)
                pltpu.store(
                    out.at[last, 2 * cap + tile // 4], tail, mask=late & (lane_group == part)
                )
            column = jnp.full((8, 128), owner_s[n] * tile_cols + col_s[n], jnp.float32)
            for o in range(5):
                here = (sublane == 0) & (lane == label_lane + o * cap + rank)
                if o == 4:
                    here = here & (sublane < shift)
                target = last if o == 4 else band + o
                pltpu.store(out.at[target, label_tile], column, mask=here)


def row_kernel(
    cap,
    received,
    first_hi,
    first_lo,
    second_hi,
    second_lo,
    twist,
    out,
    *scratch,
):
    grids, (label_v, label_s, sem) = scratch[:4], scratch[4:]
    sources = received.shape[0]
    label_tile = 2 * cap + (2 * cap) // 4
    label_lane = SUB * ((2 * cap) % 4)
    label_v[...] = received[:, label_tile, 0, :].astype(jnp.int32)
    copy = pltpu.make_async_copy(label_v, label_s, sem)
    copy.start()
    for grid in grids:
        grid[...] = jnp.zeros_like(grid)
    lane = lax.broadcasted_iota(jnp.int32, (8, 128), 1)
    copy.wait()

    @pl.loop(0, sources // 2)
    def _(pair):
        for i in range(cap):
            for o in range(5):
                for odd in range(2):
                    source = 2 * pair + odd
                    column = label_s[source, label_lane + o * cap + i]
                    offset = column % 128
                    here = pl.multiple_of((column // 128) * 8, 8)
                    place = lane - offset
                    inside = (place >= 0) & (place < SUB)
                    beyond = place < SUB - 128
                    added = []
                    for c in range(2):
                        if o < 4:
                            value, part = received[source, 2 * i + c], o
                        else:
                            value = received[source, 2 * cap + (2 * i + c) // 4]
                            part = (2 * i + c) % 4
                        value = pltpu.roll(value, (offset + 128 - SUB * part) % 128, 1)
                        added.append(jnp.where(inside, value, 0.0))
                        added.append(jnp.where(beyond, value, 0.0))
                    held = [
                        grids[2 * odd + c][pl.ds(here + 8 * k, 8), :]
                        for c in range(2)
                        for k in range(2)
                    ]
                    for c in range(2):
                        for k in range(2):
                            grids[2 * odd + c][pl.ds(here + 8 * k, 8), :] = (
                                held[2 * c + k] + added[2 * c + k]
                            )

    @pl.loop(0, ROWS_DEV // 2)
    def _(pair):
        row = pair * 2
        columns = []
        for k in range(2):
            rows = pl.ds(row + k, LEAD, stride=ROWS_DEV)
            columns.append(
                jnp.concatenate([grids[c][rows, :] + grids[2 + c][rows, :] for c in range(2)], 0)
            )
        hi, lo = split(jnp.concatenate(columns, axis=1))
        first = jnp.concatenate([first_hi[...], first_lo[...], first_hi[...]], axis=1)
        a = dot(first, jnp.concatenate([hi, hi, lo], axis=0))
        for k in range(2):
            a_re = a[:LEAD, 128 * k : 128 * k + 128]
            a_im = a[LEAD:, 128 * k : 128 * k + 128]
            b_re = a_re * twist[0] - a_im * twist[1]
            b_im = a_re * twist[1] + a_im * twist[0]
            hi, lo = split(jnp.concatenate([b_re, b_im], axis=1))
            second = jnp.concatenate([second_hi[...], second_lo[...], second_hi[...]], axis=1)
            result = dot(second, jnp.concatenate([hi, hi, lo], axis=1), True)
            for c in range(2):
                for h in range(2):
                    out[c, pl.ds(h * 8 + row + k, TAIL, stride=16), :] = result[
                        128 * c : 128 * c + 128, 128 * h : 128 * h + 128
                    ]


def shards(
    visibility, coords, block_owner, block_row, block_col, stations, block_count, beam_terms
):
    owners = lax.axis_size("tile")
    per_device = visibility.shape[0]
    tile_cols = NG // owners
    cap, tiles = send_layout(per_device, owners)
    stations_all = beam_terms.shape[0]
    vmem = pl.BlockSpec(memory_space=pltpu.VMEM)
    beams = (
        beam_terms.reshape(stations_all, 2, 8, 128)
        .transpose(0, 2, 1, 3)
        .reshape(stations_all, 16, 128)
    )
    labels = (
        block_owner.reshape(per_device),
        block_row,
        block_col,
        stations.T,
    )
    values = (
        visibility.reshape(per_device * 2, VROWS),
        coords.transpose(1, 0, 2),
        *image_tables(),
    )
    hbm = pl.BlockSpec(memory_space=pltpu.HBM)
    sent = pl.pallas_call(
        functools.partial(image_kernel, cap, tile_cols),
        out_shape=jax.ShapeDtypeStruct((owners, tiles, 8, 128), jnp.float32),
        in_specs=[pl.BlockSpec(memory_space=pltpu.SMEM)] + [hbm] * (1 + len(labels) + len(values)),
        out_specs=vmem,
        scratch_shapes=[
            *(pltpu.SMEM(label.shape, label.dtype) for label in labels),
            *(pltpu.VMEM(value.shape, value.dtype) for value in values),
            pltpu.VMEM((2 * per_device, 16, 128), jnp.float32),
            pltpu.VMEM((per_device // 16, 256, 128), jnp.float32),
            pltpu.VMEM((per_device * 8, 256), jnp.float32),
            pltpu.SMEM((owners,), jnp.int32),
            pltpu.SemaphoreType.DMA((per_device // GROUP,)),
            pltpu.SemaphoreType.DMA((len(labels) + len(values),)),
        ],
        compiler_params=pltpu.CompilerParams(vmem_limit_bytes=24 * 1024 * 1024),
        name="image",
    )(
        block_count,
        *(pltpu.with_memory_space_constraint(x, pltpu.HBM) for x in (beams, *labels, *values)),
    )
    received = lax.all_to_all(sent, "tile", split_axis=0, concat_axis=0, tiled=True)
    result = pl.pallas_call(
        functools.partial(row_kernel, cap),
        out_shape=jax.ShapeDtypeStruct((2, LEAD * ROWS_DEV, TAIL), jnp.float32),
        in_specs=[vmem] * 6,
        out_specs=vmem,
        scratch_shapes=[
            *(pltpu.VMEM(((LEAD + 1) * ROWS_DEV, TAIL), jnp.float32) for _ in range(4)),
            pltpu.VMEM((owners, 128), jnp.int32),
            pltpu.SMEM((owners, 128), jnp.int32),
            pltpu.SemaphoreType.DMA,
        ],
        compiler_params=pltpu.CompilerParams(vmem_limit_bytes=24 * 1024 * 1024),
        name="rows",
    )(received, *row_tables())
    return (
        result.reshape(2, LEAD, ROWS_DEV, TAIL).transpose(0, 2, 1, 3).reshape(2, ROWS_DEV, NG)
    )


def solution(mesh):
    placed = (
        P(("parts", "tile"), None, None),
        P(("parts", "tile"), None, None),
        P(("parts", "tile"), None),
        P(("parts", "tile")),
        P(("parts", "tile")),
        P(("parts", "tile"), None),
        P(("parts", "tile")),
        P(),
    )
    return jax.shard_map(
        shards,
        mesh=mesh,
        in_specs=placed,
        out_specs=P(None, ("parts", "tile"), None),
        check_vma=False,
    )
```

```python
import functools
import math

import jax
import jax.numpy as jnp
import ml_dtypes
import numpy as np
from jax import lax
from jax.experimental import pallas as pl
from jax.experimental.pallas import tpu as pltpu
from jax.sharding import PartitionSpec as P

VROWS = 128
SUB = 32
NG = 32768
ROWS_DEV = 8
LEAD = 256
TAIL = 128
GROUP = 8

SIN_TERMS = (4.442882920, -7.308245680, 3.606354030, -0.846110410, 0.109822040)
COS_TERMS = (1.414213500, -6.978850910, 5.739459580, -1.883552820, 0.310677860)


def halves(table):
    table = np.round(table, 12).astype(np.float32)
    high = table.astype(ml_dtypes.bfloat16)
    low = (table - high.astype(np.float32)).astype(ml_dtypes.bfloat16)
    return high, low


def root(numbers, length):
    angle = 2.0 * np.pi / length * (numbers % length)
    return np.cos(angle), -np.sin(angle)


def complex_left(re, im):
    return np.block([[re, -im], [im, re]])


@functools.cache
def image_tables():
    eight = np.arange(8)
    re, im = root(np.outer(eight, eight), 8)
    left = complex_left(np.kron(np.eye(16), re), np.kron(np.eye(16), im))
    lane = np.arange(128)
    twist = root(np.outer(eight, lane // SUB), SUB)
    four = 8 * np.outer(lane // SUB, lane // SUB) + np.outer(lane % SUB, lane % SUB)
    re, im = root(four, SUB)
    right = complex_left(re, im).T
    row_pos = ((4 * eight[:, None] + lane[None, :] // SUB) - SUB // 2) / SUB
    col_pos = np.broadcast_to((lane[None, :] % SUB - SUB // 2) / SUB, (8, 128))
    taper = (1 - 2 * row_pos**2) * (1 - 2 * col_pos**2) / SUB
    small = np.stack([taper, np.round(twist[0], 12), np.round(twist[1], 12)]).astype(np.float32)
    return (*halves(left), *halves(right), small)


@functools.cache
def row_tables():
    lead, tail = np.arange(LEAD), np.arange(TAIL)
    even = complex_left(*root(np.outer(tail, tail), TAIL))
    odd = complex_left(*root(np.outer(tail, 2 * tail + 1), LEAD))
    twist = np.stack(root(np.outer(lead, tail), NG)) / math.sqrt(NG)
    first = np.stack(halves(even) + halves(odd))
    return first, np.stack(halves(even)), np.round(twist, 12).astype(np.float32)


def split(value):
    high = value.astype(jnp.bfloat16)
    return high, (value - high.astype(jnp.float32)).astype(jnp.bfloat16)


def dot(left, right, transposed=False):
    dims = (((1,), (1 if transposed else 0,)), ((), ()))
    return lax.dot_general(left, right, dims, preferred_element_type=jnp.float32)


def polynomial(terms, z):
    value = z * terms[-1] + terms[-2]
    for term in terms[-3::-1]:
        value = value * z + term
    return value


def cos_sin(turns):
    whole = (turns + 12582912.0) - 12582912.0
    t = turns - whole
    z = t * t
    half_sin = t * polynomial(SIN_TERMS, z)
    half_cos = polynomial(COS_TERMS, z)
    return 1.0 - half_sin * half_sin, half_sin * half_cos


def send_layout(per_device, owners):
    cap = -(-per_device // (owners - SUB // ROWS_DEV + 1))
    tiles = 2 * cap + (2 * cap + 1 + 3) // 4
    return cap, tiles


def image_kernel(
    cap,
    tile_cols,
    *refs,
):
    count_s, beams, args, out, copied = refs[0], refs[1], refs[2:13], refs[13], refs[14:25]
    beam_buf, sky, cells, ranks, sems, arg_sems = refs[25:]
    copies = [
        pltpu.make_async_copy(arg, held, arg_sems.at[k])
        for k, (arg, held) in enumerate(zip(args, copied))
    ]
    for copy in copies:
        copy.start()
    owner_s, row_s, col_s, station_s, vis, coords = copied[:6]
    left_hi, left_lo, right_hi, right_lo, small = copied[6:]
    per_device = vis.shape[0] // 2
    owners = out.shape[0]
    out[...] = jnp.zeros_like(out)
    sky[...] = jnp.zeros_like(sky)
    for b in range(owners):
        ranks[b] = 0
    copies[3].wait()
    live = count_s[0]
    groups = (live + GROUP - 1) // GROUP

    @pl.loop(0, groups)
    def _(g):
        for j in range(GROUP):
            n = g * GROUP + j
            for side in range(2):
                pltpu.make_async_copy(
                    beams.at[station_s[side, n]], beam_buf.at[2 * n + side], sems.at[g]
                ).start()

    copies[4].wait()
    copies[5].wait()
    copies[10].wait()
    taper = small[0]
    twist_re = jnp.concatenate([small[1]] * 16, axis=0)
    twist_im = jnp.concatenate([small[2]] * 16, axis=0)
    number = lax.broadcasted_iota(jnp.int32, (SUB, VROWS), 0)
    l_row = (4 * (number % 8) + number // 8 - SUB // 2).astype(jnp.float32) / SUB
    l_col = (number - SUB // 2).astype(jnp.float32) / SUB
    d_row = l_row * l_row
    d_col = l_col * l_col
    sublane = lax.broadcasted_iota(jnp.int32, (8, 128), 0)
    lane = lax.broadcasted_iota(jnp.int32, (8, 128), 1)
    lane_group = lane // SUB

    @pl.loop(0, groups)
    def _(g):
        waited = beam_buf.at[pl.ds(g * 2 * GROUP, 2 * GROUP)]
        pltpu.make_async_copy(beams.at[pl.ds(0, 2 * GROUP)], waited, sems.at[g]).wait()
        for quad in range(GROUP // 4):
            x_hi, x_lo, columns = [], [], []
            for j in range(4):
                n = g * GROUP + quad * 4 + j
                u = coords[0, pl.ds(n, 1), :]
                v = coords[1, pl.ds(n, 1), :]
                w = coords[2, pl.ds(n, 1), :]
                vis_re = vis[pl.ds(2 * n, 1), :]
                vis_im = vis[pl.ds(2 * n + 1, 1), :]
                cos_row, sin_row = cos_sin(u * l_row + w * d_row)
                cos_col, sin_col = cos_sin(v * l_col + w * d_col)
                x = jnp.concatenate(
                    [
                        vis_re * cos_row - vis_im * sin_row,
                        vis_re * sin_row + vis_im * cos_row,
                    ],
                    axis=1,
                )
                hi, lo = split(x)
                x_hi.append(hi)
                x_lo.append(lo)
                columns.append(split(cos_col) + split(sin_col))
            c_hi, c_lo, s_hi, s_lo = zip(*columns)

            def matrix(c, s):
                real = [jnp.concatenate([a, -b], axis=1) for a, b in zip(c, s)]
                imag = [jnp.concatenate([b, a], axis=1) for a, b in zip(c, s)]
                return jnp.concatenate(real + imag, axis=0)

            lhs = jnp.concatenate(x_hi + x_lo, axis=0)
            both = dot(lhs, matrix(c_hi, s_hi), True)
            sums = both[:128] + both[128:] + dot(lhs[:128], matrix(c_lo, s_lo), True)
            for j in range(4):
                n = g * GROUP + quad * 4 + j
                flat = []
                for c in range(2):
                    value = None
                    for i in range(4):
                        piece = sums[32 * j + 8 * i : 32 * j + 8 * i + 8, 128 * c : 128 * c + 128]
                        if i != j:
                            piece = pltpu.roll(piece, (SUB * (i - j)) % 128, 1)
                        value = piece if value is None else jnp.where(lane_group == i, piece, value)
                    flat.append(value)
                one_re = beam_buf[2 * n, pl.ds(0, 8, stride=2), :]
                one_im = beam_buf[2 * n, pl.ds(1, 8, stride=2), :]
                two_re = beam_buf[2 * n + 1, pl.ds(0, 8, stride=2), :]
                two_im = beam_buf[2 * n + 1, pl.ds(1, 8, stride=2), :]
                beam_re = taper * (one_re * two_re + one_im * two_im)
                beam_im = taper * (one_im * two_re - one_re * two_im)
                sky_re = beam_re * flat[0] - beam_im * flat[1]
                sky_im = beam_re * flat[1] + beam_im * flat[0]
                in_use = n < live
                place = pl.multiple_of((g % 2) * 64 + (quad * 4 + j) * 8, 8)
                sky[g // 2, pl.ds(place, 8), :] = jnp.where(in_use, sky_re, 0.0)
                sky[g // 2, pl.ds(place + 128, 8), :] = jnp.where(in_use, sky_im, 0.0)

    for copy in copies[6:10] + copies[:3]:
        copy.wait()
    for half in range(per_device // 32):

        @pl.when(live > 32 * half)
        def _():
            value = jnp.concatenate([sky[2 * half], sky[2 * half + 1]], axis=1)
            hi, lo = split(value)
            z = dot(left_hi[...], hi) + dot(left_lo[...], hi) + dot(left_hi[...], lo)
            rows = []
            for k in range(2):
                z_re = z[:128, 128 * k : 128 * k + 128]
                z_im = z[128:, 128 * k : 128 * k + 128]
                y_re = z_re * twist_re - z_im * twist_im
                y_im = z_re * twist_im + z_im * twist_re
                rows.append(jnp.concatenate([y_re, y_im], axis=1))
            hi, lo = split(jnp.concatenate(rows, axis=0))
            cells[256 * half : 256 * half + 256, :] = (
                dot(hi, right_hi[...]) + dot(lo, right_hi[...]) + dot(hi, right_lo[...])
            )

    label_tile = 2 * cap + (2 * cap) // 4
    label_lane = SUB * ((2 * cap) % 4)

    @pl.loop(0, groups)
    def _(g):
        for j in range(GROUP):
            n = g * GROUP + j
            band = row_s[n] // ROWS_DEV
            shift = row_s[n] % ROWS_DEV
            rank = ranks[band]
            ranks[band] = rank + 1
            place = pl.multiple_of(n * 8, 8)
            late = sublane < shift
            last = jnp.minimum(band + 4, owners - 1)
            for c in range(2):
                value = cells[pl.ds(place, 8), 128 * c : 128 * c + 128]
                value = pltpu.roll(value, shift, 0)
                next_value = pltpu.roll(value, SUB, 1)
                spread = jnp.where(late, jnp.where(lane_group == 0, 0.0, next_value), value)
                tile = 2 * rank + c
                for o in range(4):
                    pltpu.store(out.at[band + o, tile], spread, mask=lane_group == o)
                part = tile % 4
                tail = pltpu.roll(value, SUB * (part + 1), 1)
                pltpu.store(
                    out.at[last, 2 * cap + tile // 4], tail, mask=late & (lane_group == part)
                )
            column = jnp.full((8, 128), owner_s[n] * tile_cols + col_s[n], jnp.float32)
            for o in range(5):
                here = (sublane == 0) & (lane == label_lane + o * cap + rank)
                if o == 4:
                    here = here & (sublane < shift)
                target = last if o == 4 else band + o
                pltpu.store(out.at[target, label_tile], column, mask=here)


def row_kernel(
    cap,
    received,
    first,
    second,
    twist,
    out,
    *scratch,
):
    grids, (label_v, label_s, sem) = scratch[:2], scratch[2:]
    sources = received.shape[0]
    label_tile = 2 * cap + (2 * cap) // 4
    label_lane = SUB * ((2 * cap) % 4)
    label_v[...] = received[:, label_tile, 0, :].astype(jnp.int32)
    copy = pltpu.make_async_copy(label_v, label_s, sem)
    copy.start()
    for grid in grids:
        grid[...] = jnp.zeros_like(grid)
    lane = lax.broadcasted_iota(jnp.int32, (8, 128), 1)
    copy.wait()

    @pl.loop(0, sources)
    def _(source):
        for i in range(cap):
            for o in range(5):
                column = label_s[source, label_lane + o * cap + i]
                offset = column % 128
                here = pl.multiple_of((column // 128) * 8, 8)
                place = lane - offset
                inside = (place >= 0) & (place < SUB)
                beyond = place < SUB - 128
                added = []
                for c in range(2):
                    if o < 4:
                        value, part = received[source, 2 * i + c], o
                    else:
                        value = received[source, 2 * cap + (2 * i + c) // 4]
                        part = (2 * i + c) % 4
                    value = pltpu.roll(value, (offset + 128 - SUB * part) % 128, 1)
                    added.append(jnp.where(inside, value, 0.0))
                    added.append(jnp.where(beyond, value, 0.0))
                held = [
                    grids[c][pl.ds(here + 8 * k, 8), :] for c in range(2) for k in range(2)
                ]
                for c in range(2):
                    for k in range(2):
                        grids[c][pl.ds(here + 8 * k, 8), :] = held[2 * c + k] + added[2 * c + k]

    @pl.loop(0, ROWS_DEV // 2)
    def _(pair):
        row = pair * 2
        halves_of = []
        for e in range(2):
            rows = [pl.ds(ROWS_DEV * e + row + k, TAIL, stride=2 * ROWS_DEV) for k in range(2)]
            value = jnp.concatenate(
                [jnp.concatenate([grids[c][at, :] for at in rows], axis=1) for c in range(2)], 0
            )
            hi, lo = split(value)
            table_hi, table_lo = first[2 * e], first[2 * e + 1]
            table = jnp.concatenate([table_hi, table_lo, table_hi], axis=1)
            halves_of.append(dot(table, jnp.concatenate([hi, hi, lo], axis=0)))
        low, high = halves_of[0] + halves_of[1], halves_of[0] - halves_of[1]
        for k in range(2):
            b = []
            for e, a in enumerate((low, high)):
                a_re = a[:TAIL, 128 * k : 128 * k + 128]
                a_im = a[TAIL:, 128 * k : 128 * k + 128]
                turn_re = twist[0, TAIL * e : TAIL * e + TAIL]
                turn_im = twist[1, TAIL * e : TAIL * e + TAIL]
                b.append(
                    jnp.concatenate(
                        [a_re * turn_re - a_im * turn_im, a_re * turn_im + a_im * turn_re], axis=1
                    )
                )
            hi, lo = split(jnp.concatenate(b, axis=0))
            table = jnp.concatenate([second[0], second[1], second[0]], axis=1)
            result = dot(table, jnp.concatenate([hi, hi, lo], axis=1), True)
            for c in range(2):
                for h in range(2):
                    out[c, pl.ds(h * 8 + row + k, TAIL, stride=16), :] = result[
                        128 * c : 128 * c + 128, 128 * h : 128 * h + 128
                    ]


def shards(
    visibility, coords, block_owner, block_row, block_col, stations, block_count, beam_terms
):
    owners = lax.axis_size("tile")
    per_device = visibility.shape[0]
    tile_cols = NG // owners
    cap, tiles = send_layout(per_device, owners)
    stations_all = beam_terms.shape[0]
    vmem = pl.BlockSpec(memory_space=pltpu.VMEM)
    beams = (
        beam_terms.reshape(stations_all, 2, 8, 128)
        .transpose(0, 2, 1, 3)
        .reshape(stations_all, 16, 128)
    )
    labels = (
        block_owner.reshape(per_device),
        block_row,
        block_col,
        stations.T,
    )
    values = (
        visibility.reshape(per_device * 2, VROWS),
        coords.transpose(1, 0, 2),
        *image_tables(),
    )
    hbm = pl.BlockSpec(memory_space=pltpu.HBM)
    sent = pl.pallas_call(
        functools.partial(image_kernel, cap, tile_cols),
        out_shape=jax.ShapeDtypeStruct((owners, tiles, 8, 128), jnp.float32),
        in_specs=[pl.BlockSpec(memory_space=pltpu.SMEM)] + [hbm] * (1 + len(labels) + len(values)),
        out_specs=vmem,
        scratch_shapes=[
            *(pltpu.SMEM(label.shape, label.dtype) for label in labels),
            *(pltpu.VMEM(value.shape, value.dtype) for value in values),
            pltpu.VMEM((2 * per_device, 16, 128), jnp.float32),
            pltpu.VMEM((per_device // 16, 256, 128), jnp.float32),
            pltpu.VMEM((per_device * 8, 256), jnp.float32),
            pltpu.SMEM((owners,), jnp.int32),
            pltpu.SemaphoreType.DMA((per_device // GROUP,)),
            pltpu.SemaphoreType.DMA((len(labels) + len(values),)),
        ],
        compiler_params=pltpu.CompilerParams(vmem_limit_bytes=24 * 1024 * 1024),
        name="image",
    )(
        block_count,
        *(pltpu.with_memory_space_constraint(x, pltpu.HBM) for x in (beams, *labels, *values)),
    )
    received = lax.all_to_all(sent, "tile", split_axis=0, concat_axis=0, tiled=True)
    result = pl.pallas_call(
        functools.partial(row_kernel, cap),
        out_shape=jax.ShapeDtypeStruct((2, LEAD * ROWS_DEV, TAIL), jnp.float32),
        in_specs=[vmem] * 4,
        out_specs=vmem,
        scratch_shapes=[
            *(pltpu.VMEM(((LEAD + 1) * ROWS_DEV, TAIL), jnp.float32) for _ in range(2)),
            pltpu.VMEM((owners, 128), jnp.int32),
            pltpu.SMEM((owners, 128), jnp.int32),
            pltpu.SemaphoreType.DMA,
        ],
        compiler_params=pltpu.CompilerParams(vmem_limit_bytes=24 * 1024 * 1024),
        name="rows",
    )(received, *row_tables())
    return (
        result.reshape(2, LEAD, ROWS_DEV, TAIL).transpose(0, 2, 1, 3).reshape(2, ROWS_DEV, NG)
    )


def solution(mesh):
    placed = (
        P(("parts", "tile"), None, None),
        P(("parts", "tile"), None, None),
        P(("parts", "tile"), None),
        P(("parts", "tile")),
        P(("parts", "tile")),
        P(("parts", "tile"), None),
        P(("parts", "tile")),
        P(),
    )
    return jax.shard_map(
        shards,
        mesh=mesh,
        in_specs=placed,
        out_specs=P(None, ("parts", "tile"), None),
        check_vma=False,
    )
```

```python
import functools
import math

import jax
import jax.numpy as jnp
import ml_dtypes
import numpy as np
from jax import lax
from jax.experimental import pallas as pl
from jax.experimental.pallas import tpu as pltpu
from jax.sharding import PartitionSpec as P

VROWS = 128
SUB = 32
NG = 32768
ROWS_DEV = 8
LEAD = 256
TAIL = 128
GROUP = 8

SIN_TERMS = (4.442882920, -7.308245680, 3.606354030, -0.846110410, 0.109822040)
COS_TERMS = (1.414213500, -6.978850910, 5.739459580, -1.883552820, 0.310677860)


def halves(table):
    table = np.round(table, 12).astype(np.float32)
    high = table.astype(ml_dtypes.bfloat16)
    low = (table - high.astype(np.float32)).astype(ml_dtypes.bfloat16)
    return high, low


def root(numbers, length):
    angle = 2.0 * np.pi / length * (numbers % length)
    return np.cos(angle), -np.sin(angle)


def complex_left(re, im):
    return np.block([[re, -im], [im, re]])


@functools.cache
def image_tables():
    eight = np.arange(8)
    re, im = root(np.outer(eight, eight), 8)
    left = complex_left(np.kron(np.eye(16), re), np.kron(np.eye(16), im))
    lane = np.arange(128)
    twist = root(np.outer(eight, lane // SUB), SUB)
    four = 8 * np.outer(lane // SUB, lane // SUB) + np.outer(lane % SUB, lane % SUB)
    re, im = root(four, SUB)
    right = complex_left(re, im).T
    row_pos = ((4 * eight[:, None] + lane[None, :] // SUB) - SUB // 2) / SUB
    col_pos = np.broadcast_to((lane[None, :] % SUB - SUB // 2) / SUB, (8, 128))
    taper = (1 - 2 * row_pos**2) * (1 - 2 * col_pos**2) / SUB
    small = np.stack([taper, np.round(twist[0], 12), np.round(twist[1], 12)]).astype(np.float32)
    return (*halves(left), *halves(right), small)


@functools.cache
def row_tables():
    lead, tail = np.arange(LEAD), np.arange(TAIL)
    even = complex_left(*root(np.outer(tail, tail), TAIL))
    odd = complex_left(*root(np.outer(tail, 2 * tail + 1), LEAD))
    twist = np.stack(root(np.outer(lead, tail), NG)) / math.sqrt(NG)
    first = np.stack(halves(even) + halves(odd))
    return first, np.stack(halves(even)), np.round(twist, 12).astype(np.float32)


def split(value):
    high = value.astype(jnp.bfloat16)
    return high, (value - high.astype(jnp.float32)).astype(jnp.bfloat16)


def dot(left, right, transposed=False):
    dims = (((1,), (1 if transposed else 0,)), ((), ()))
    return lax.dot_general(left, right, dims, preferred_element_type=jnp.float32)


def polynomial(terms, z):
    value = z * terms[-1] + terms[-2]
    for term in terms[-3::-1]:
        value = value * z + term
    return value


def cos_sin(turns):
    whole = (turns + 12582912.0) - 12582912.0
    t = turns - whole
    z = t * t
    half_sin = t * polynomial(SIN_TERMS, z)
    half_cos = polynomial(COS_TERMS, z)
    return 1.0 - half_sin * half_sin, half_sin * half_cos


def send_layout(per_device, owners):
    cap = -(-per_device // (owners - SUB // ROWS_DEV + 1))
    tiles = 2 * cap + (2 * cap + 1 + 3) // 4
    return cap, tiles


def image_kernel(
    cap,
    tile_cols,
    *refs,
):
    count_s, beams, args, out, copied = refs[0], refs[1], refs[2:13], refs[13], refs[14:25]
    beam_buf, sky, cells, ranks, sems, arg_sems = refs[25:]
    copies = [
        pltpu.make_async_copy(arg, held, arg_sems.at[k])
        for k, (arg, held) in enumerate(zip(args, copied))
    ]
    for copy in copies:
        copy.start()
    owner_s, row_s, col_s, station_s, vis, coords = copied[:6]
    left_hi, left_lo, right_hi, right_lo, small = copied[6:]
    per_device = vis.shape[0] // 2
    owners = out.shape[0]
    out[...] = jnp.zeros_like(out)
    sky[...] = jnp.zeros_like(sky)
    for b in range(owners):
        ranks[b] = 0
    copies[3].wait()
    live = count_s[0]
    groups = (live + GROUP - 1) >> 3

    @pl.loop(0, groups)
    def _(g):
        for j in range(GROUP):
            n = g * GROUP + j
            for side in range(2):
                pltpu.make_async_copy(
                    beams.at[station_s[side, n]], beam_buf.at[2 * n + side], sems.at[g]
                ).start()

    copies[4].wait()
    copies[5].wait()
    copies[10].wait()
    taper = small[0]
    twist_re = jnp.concatenate([small[1]] * 16, axis=0)
    twist_im = jnp.concatenate([small[2]] * 16, axis=0)
    number = lax.broadcasted_iota(jnp.int32, (SUB, VROWS), 0)
    l_row = (4 * (number % 8) + number // 8 - SUB // 2).astype(jnp.float32) / SUB
    l_col = (number - SUB // 2).astype(jnp.float32) / SUB
    d_row = l_row * l_row
    d_col = l_col * l_col
    sublane = lax.broadcasted_iota(jnp.int32, (8, 128), 0)
    lane = lax.broadcasted_iota(jnp.int32, (8, 128), 1)
    lane_group = lane // SUB

    @pl.loop(0, groups)
    def _(g):
        waited = beam_buf.at[pl.ds(g * 2 * GROUP, 2 * GROUP)]
        pltpu.make_async_copy(beams.at[pl.ds(0, 2 * GROUP)], waited, sems.at[g]).wait()
        for quad in range(GROUP // 4):
            x_hi, x_lo, columns = [], [], []
            for j in range(4):
                n = g * GROUP + quad * 4 + j
                u = coords[0, pl.ds(n, 1), :]
                v = coords[1, pl.ds(n, 1), :]
                w = coords[2, pl.ds(n, 1), :]
                vis_re = vis[pl.ds(2 * n, 1), :]
                vis_im = vis[pl.ds(2 * n + 1, 1), :]
                cos_row, sin_row = cos_sin(u * l_row + w * d_row)
                cos_col, sin_col = cos_sin(v * l_col + w * d_col)
                x = jnp.concatenate(
                    [
                        vis_re * cos_row - vis_im * sin_row,
                        vis_re * sin_row + vis_im * cos_row,
                    ],
                    axis=1,
                )
                hi, lo = split(x)
                x_hi.append(hi)
                x_lo.append(lo)
                columns.append(split(cos_col) + split(sin_col))
            c_hi, c_lo, s_hi, s_lo = zip(*columns)

            def matrix(c, s):
                real = [jnp.concatenate([a, -b], axis=1) for a, b in zip(c, s)]
                imag = [jnp.concatenate([b, a], axis=1) for a, b in zip(c, s)]
                return jnp.concatenate(real + imag, axis=0)

            lhs = jnp.concatenate(x_hi + x_lo, axis=0)
            both = dot(lhs, matrix(c_hi, s_hi), True)
            sums = both[:128] + both[128:] + dot(lhs[:128], matrix(c_lo, s_lo), True)
            for j in range(4):
                n = g * GROUP + quad * 4 + j
                flat = []
                for c in range(2):
                    value = None
                    for i in range(4):
                        piece = sums[32 * j + 8 * i : 32 * j + 8 * i + 8, 128 * c : 128 * c + 128]
                        if i != j:
                            piece = pltpu.roll(piece, (SUB * (i - j)) % 128, 1)
                        value = piece if value is None else jnp.where(lane_group == i, piece, value)
                    flat.append(value)
                one_re = beam_buf[2 * n, pl.ds(0, 8, stride=2), :]
                one_im = beam_buf[2 * n, pl.ds(1, 8, stride=2), :]
                two_re = beam_buf[2 * n + 1, pl.ds(0, 8, stride=2), :]
                two_im = beam_buf[2 * n + 1, pl.ds(1, 8, stride=2), :]
                beam_re = taper * (one_re * two_re + one_im * two_im)
                beam_im = taper * (one_im * two_re - one_re * two_im)
                sky_re = beam_re * flat[0] - beam_im * flat[1]
                sky_im = beam_re * flat[1] + beam_im * flat[0]
                in_use = n < live
                place = pl.multiple_of((g & 1) * 64 + (quad * 4 + j) * 8, 8)
                sky[g >> 1, pl.ds(place, 8), :] = jnp.where(in_use, sky_re, 0.0)
                sky[g >> 1, pl.ds(place + 128, 8), :] = jnp.where(in_use, sky_im, 0.0)

    for copy in copies[6:10] + copies[:3]:
        copy.wait()
    for half in range(per_device // 32):

        @pl.when(live > 32 * half)
        def _():
            value = jnp.concatenate([sky[2 * half], sky[2 * half + 1]], axis=1)
            hi, lo = split(value)
            z = dot(left_hi[...], hi) + dot(left_lo[...], hi) + dot(left_hi[...], lo)
            rows = []
            for k in range(2):
                z_re = z[:128, 128 * k : 128 * k + 128]
                z_im = z[128:, 128 * k : 128 * k + 128]
                y_re = z_re * twist_re - z_im * twist_im
                y_im = z_re * twist_im + z_im * twist_re
                rows.append(jnp.concatenate([y_re, y_im], axis=1))
            hi, lo = split(jnp.concatenate(rows, axis=0))
            cells[256 * half : 256 * half + 256, :] = (
                dot(hi, right_hi[...]) + dot(lo, right_hi[...]) + dot(hi, right_lo[...])
            )

    label_tile = 2 * cap + (2 * cap) // 4
    label_lane = SUB * ((2 * cap) % 4)

    @pl.loop(0, groups)
    def _(g):
        for j in range(GROUP):
            n = g * GROUP + j
            band = row_s[n] >> 3
            shift = row_s[n] & 7
            rank = ranks[band]
            ranks[band] = rank + 1
            place = pl.multiple_of(n * 8, 8)
            late = sublane < shift
            last = jnp.minimum(band + 4, owners - 1)
            for c in range(2):
                value = cells[pl.ds(place, 8), 128 * c : 128 * c + 128]
                value = pltpu.roll(value, shift, 0)
                next_value = pltpu.roll(value, SUB, 1)
                spread = jnp.where(late, jnp.where(lane_group == 0, 0.0, next_value), value)
                tile = 2 * rank + c
                for o in range(4):
                    pltpu.store(out.at[band + o, tile], spread, mask=lane_group == o)
                part = tile & 3
                tail = pltpu.roll(value, SUB * (part + 1), 1)
                pltpu.store(
                    out.at[last, 2 * cap + (tile >> 2)], tail, mask=late & (lane_group == part)
                )
            column = jnp.full((8, 128), owner_s[n] * tile_cols + col_s[n], jnp.float32)
            for o in range(5):
                here = (sublane == 0) & (lane == label_lane + o * cap + rank)
                if o == 4:
                    here = here & (sublane < shift)
                target = last if o == 4 else band + o
                pltpu.store(out.at[target, label_tile], column, mask=here)


def row_kernel(
    cap,
    received,
    first,
    second,
    twist,
    out,
    *scratch,
):
    grids, (label_v, label_s, sem) = scratch[:2], scratch[2:]
    sources = received.shape[0]
    label_tile = 2 * cap + (2 * cap) // 4
    label_lane = SUB * ((2 * cap) % 4)
    label_v[...] = received[:, label_tile, 0, :].astype(jnp.int32)
    copy = pltpu.make_async_copy(label_v, label_s, sem)
    copy.start()
    for grid in grids:
        grid[...] = jnp.zeros_like(grid)
    lane = lax.broadcasted_iota(jnp.int32, (8, 128), 1)
    copy.wait()

    @pl.loop(0, sources)
    def _(source):
        for i in range(cap):
            for o in range(5):
                column = label_s[source, label_lane + o * cap + i]
                offset = column & 127
                here = pl.multiple_of((column >> 7) * 8, 8)
                place = lane - offset
                inside = (place >= 0) & (place < SUB)
                beyond = place < SUB - 128
                added = []
                for c in range(2):
                    if o < 4:
                        value, part = received[source, 2 * i + c], o
                    else:
                        value = received[source, 2 * cap + (2 * i + c) // 4]
                        part = (2 * i + c) % 4
                    value = pltpu.roll(value, (offset - SUB * part) & 127, 1)
                    added.append(jnp.where(inside, value, 0.0))
                    added.append(jnp.where(beyond, value, 0.0))
                held = [
                    grids[c][pl.ds(here + 8 * k, 8), :] for c in range(2) for k in range(2)
                ]
                for c in range(2):
                    for k in range(2):
                        grids[c][pl.ds(here + 8 * k, 8), :] = held[2 * c + k] + added[2 * c + k]

    @pl.loop(0, ROWS_DEV // 2)
    def _(pair):
        row = pair * 2
        halves_of = []
        for e in range(2):
            rows = [pl.ds(ROWS_DEV * e + row + k, TAIL, stride=2 * ROWS_DEV) for k in range(2)]
            value = jnp.concatenate(
                [jnp.concatenate([grids[c][at, :] for at in rows], axis=1) for c in range(2)], 0
            )
            hi, lo = split(value)
            table_hi, table_lo = first[2 * e], first[2 * e + 1]
            table = jnp.concatenate([table_hi, table_lo, table_hi], axis=1)
            halves_of.append(dot(table, jnp.concatenate([hi, hi, lo], axis=0)))
        low, high = halves_of[0] + halves_of[1], halves_of[0] - halves_of[1]
        for k in range(2):
            b = []
            for e, a in enumerate((low, high)):
                a_re = a[:TAIL, 128 * k : 128 * k + 128]
                a_im = a[TAIL:, 128 * k : 128 * k + 128]
                turn_re = twist[0, TAIL * e : TAIL * e + TAIL]
                turn_im = twist[1, TAIL * e : TAIL * e + TAIL]
                b.append(
                    jnp.concatenate(
                        [a_re * turn_re - a_im * turn_im, a_re * turn_im + a_im * turn_re], axis=1
                    )
                )
            hi, lo = split(jnp.concatenate(b, axis=0))
            table = jnp.concatenate([second[0], second[1], second[0]], axis=1)
            result = dot(table, jnp.concatenate([hi, hi, lo], axis=1), True)
            for c in range(2):
                for h in range(2):
                    out[c, pl.ds(h * 8 + row + k, TAIL, stride=16), :] = result[
                        128 * c : 128 * c + 128, 128 * h : 128 * h + 128
                    ]


def shards(
    visibility, coords, block_owner, block_row, block_col, stations, block_count, beam_terms
):
    owners = lax.axis_size("tile")
    per_device = visibility.shape[0]
    tile_cols = NG // owners
    cap, tiles = send_layout(per_device, owners)
    stations_all = beam_terms.shape[0]
    vmem = pl.BlockSpec(memory_space=pltpu.VMEM)
    beams = (
        beam_terms.reshape(stations_all, 2, 8, 128)
        .transpose(0, 2, 1, 3)
        .reshape(stations_all, 16, 128)
    )
    labels = (
        block_owner.reshape(per_device),
        block_row,
        block_col,
        stations.T,
    )
    values = (
        visibility.reshape(per_device * 2, VROWS),
        coords.transpose(1, 0, 2),
        *image_tables(),
    )
    hbm = pl.BlockSpec(memory_space=pltpu.HBM)
    sent = pl.pallas_call(
        functools.partial(image_kernel, cap, tile_cols),
        out_shape=jax.ShapeDtypeStruct((owners, tiles, 8, 128), jnp.float32),
        in_specs=[pl.BlockSpec(memory_space=pltpu.SMEM)] + [hbm] * (1 + len(labels) + len(values)),
        out_specs=vmem,
        scratch_shapes=[
            *(pltpu.SMEM(label.shape, label.dtype) for label in labels),
            *(pltpu.VMEM(value.shape, value.dtype) for value in values),
            pltpu.VMEM((2 * per_device, 16, 128), jnp.float32),
            pltpu.VMEM((per_device // 16, 256, 128), jnp.float32),
            pltpu.VMEM((per_device * 8, 256), jnp.float32),
            pltpu.SMEM((owners,), jnp.int32),
            pltpu.SemaphoreType.DMA((per_device // GROUP,)),
            pltpu.SemaphoreType.DMA((len(labels) + len(values),)),
        ],
        compiler_params=pltpu.CompilerParams(vmem_limit_bytes=24 * 1024 * 1024),
        name="image",
    )(
        block_count,
        *(pltpu.with_memory_space_constraint(x, pltpu.HBM) for x in (beams, *labels, *values)),
    )
    received = lax.all_to_all(sent, "tile", split_axis=0, concat_axis=0, tiled=True)
    result = pl.pallas_call(
        functools.partial(row_kernel, cap),
        out_shape=jax.ShapeDtypeStruct((2, LEAD * ROWS_DEV, TAIL), jnp.float32),
        in_specs=[vmem] * 4,
        out_specs=vmem,
        scratch_shapes=[
            *(pltpu.VMEM(((LEAD + 1) * ROWS_DEV, TAIL), jnp.float32) for _ in range(2)),
            pltpu.VMEM((owners, 128), jnp.int32),
            pltpu.SMEM((owners, 128), jnp.int32),
            pltpu.SemaphoreType.DMA,
        ],
        compiler_params=pltpu.CompilerParams(vmem_limit_bytes=24 * 1024 * 1024),
        name="rows",
    )(received, *row_tables())
    return (
        result.reshape(2, LEAD, ROWS_DEV, TAIL).transpose(0, 2, 1, 3).reshape(2, ROWS_DEV, NG)
    )


def solution(mesh):
    placed = (
        P(("parts", "tile"), None, None),
        P(("parts", "tile"), None, None),
        P(("parts", "tile"), None),
        P(("parts", "tile")),
        P(("parts", "tile")),
        P(("parts", "tile"), None),
        P(("parts", "tile")),
        P(),
    )
    return jax.shard_map(
        shards,
        mesh=mesh,
        in_specs=placed,
        out_specs=P(None, ("parts", "tile"), None),
        check_vma=False,
    )
```

```python
import functools
import math

import jax
import jax.numpy as jnp
import ml_dtypes
import numpy as np
from jax import lax
from jax.experimental import pallas as pl
from jax.experimental.pallas import tpu as pltpu
from jax.sharding import PartitionSpec as P

VROWS = 128
SUB = 32
NG = 32768
ROWS_DEV = 8
LEAD = 256
TAIL = 128
GROUP = 8

SIN_TERMS = (4.442882920, -7.308245680, 3.606354030, -0.846110410, 0.109822040)
COS_TERMS = (1.414213500, -6.978850910, 5.739459580, -1.883552820, 0.310677860)


def halves(table):
    table = np.round(table, 12).astype(np.float32)
    high = table.astype(ml_dtypes.bfloat16)
    low = (table - high.astype(np.float32)).astype(ml_dtypes.bfloat16)
    return high, low


def root(numbers, length):
    angle = 2.0 * np.pi / length * (numbers % length)
    return np.cos(angle), -np.sin(angle)


def complex_left(re, im):
    return np.block([[re, -im], [im, re]])


@functools.cache
def image_tables():
    eight = np.arange(8)
    re, im = root(np.outer(eight, eight), 8)
    left = complex_left(np.kron(np.eye(GROUP), re), np.kron(np.eye(GROUP), im))
    lane = np.arange(128)
    twist = root(np.outer(eight, lane // SUB), SUB)
    four = 8 * np.outer(lane // SUB, lane // SUB) + np.outer(lane % SUB, lane % SUB)
    re, im = root(four, SUB)
    right = complex_left(re, im).T
    row_pos = ((4 * eight[:, None] + lane[None, :] // SUB) - SUB // 2) / SUB
    col_pos = np.broadcast_to((lane[None, :] % SUB - SUB // 2) / SUB, (8, 128))
    taper = (1 - 2 * row_pos**2) * (1 - 2 * col_pos**2) / SUB
    small = np.stack([taper, np.round(twist[0], 12), np.round(twist[1], 12)]).astype(np.float32)
    return (*halves(left), *halves(right), small)


@functools.cache
def row_tables():
    lead, tail = np.arange(LEAD), np.arange(TAIL)
    even = complex_left(*root(np.outer(tail, tail), TAIL))
    odd = complex_left(*root(np.outer(tail, 2 * tail + 1), LEAD))
    twist = np.stack(root(np.outer(lead, tail), NG)) / math.sqrt(NG)
    first = np.stack(halves(even) + halves(odd))
    return first, np.stack(halves(even)), np.round(twist, 12).astype(np.float32)


def split(value):
    high = value.astype(jnp.bfloat16)
    return high, (value - high.astype(jnp.float32)).astype(jnp.bfloat16)


def dot(left, right, transposed=False):
    dims = (((1,), (1 if transposed else 0,)), ((), ()))
    return lax.dot_general(left, right, dims, preferred_element_type=jnp.float32)


def polynomial(terms, z):
    value = z * terms[-1] + terms[-2]
    for term in terms[-3::-1]:
        value = value * z + term
    return value


def cos_sin(turns):
    whole = (turns + 12582912.0) - 12582912.0
    t = turns - whole
    z = t * t
    half_sin = t * polynomial(SIN_TERMS, z)
    half_cos = polynomial(COS_TERMS, z)
    return 1.0 - half_sin * half_sin, half_sin * half_cos


def send_layout(per_device, owners):
    cap = -(-per_device // (owners - SUB // ROWS_DEV + 1))
    tiles = 2 * cap + (2 * cap + 1 + 3) // 4
    return cap, tiles


def image_kernel(
    cap,
    tile_cols,
    *refs,
):
    count_s, beams, args, out, copied = refs[0], refs[1], refs[2:13], refs[13], refs[14:25]
    beam_buf, sky, ranks, sems, arg_sems = refs[25:]
    copies = [
        pltpu.make_async_copy(arg, held, arg_sems.at[k])
        for k, (arg, held) in enumerate(zip(args, copied))
    ]
    for copy in copies:
        copy.start()
    owner_s, row_s, col_s, station_s, vis, coords = copied[:6]
    left_hi, left_lo, right_hi, right_lo, small = copied[6:]
    per_device = vis.shape[0] // 2
    owners = out.shape[0]
    out[...] = jnp.zeros_like(out)
    sky[...] = jnp.zeros_like(sky)
    for b in range(owners):
        ranks[b] = 0
    copies[3].wait()
    live = count_s[0]
    groups = (live + GROUP - 1) >> 3

    def fetch_beams(g):
        for j in range(GROUP):
            n = jnp.minimum(g, per_device // GROUP - 1) * GROUP + j
            for side in range(2):
                pltpu.make_async_copy(
                    beams.at[station_s[side, n]],
                    beam_buf.at[2 * (g * GROUP + j) + side],
                    sems.at[g],
                ).start()

    def await_beams(g):
        waited = beam_buf.at[pl.ds(g * 2 * GROUP, 2 * GROUP)]
        pltpu.make_async_copy(beams.at[pl.ds(0, 2 * GROUP)], waited, sems.at[g]).wait()

    for g in range(3):
        fetch_beams(g)
    copies[4].wait()
    copies[5].wait()
    copies[10].wait()
    taper = small[0]
    twist_re = jnp.concatenate([small[1]] * GROUP, axis=0)
    twist_im = jnp.concatenate([small[2]] * GROUP, axis=0)
    number = lax.broadcasted_iota(jnp.int32, (SUB, VROWS), 0)
    l_row = (4 * (number % 8) + number // 8 - SUB // 2).astype(jnp.float32) / SUB
    l_col = (number - SUB // 2).astype(jnp.float32) / SUB
    d_row = l_row * l_row
    d_col = l_col * l_col
    sublane = lax.broadcasted_iota(jnp.int32, (8, 128), 0)
    lane = lax.broadcasted_iota(jnp.int32, (8, 128), 1)
    lane_group = lane // SUB

    def images(g):
        for quad in range(GROUP // 4):
            x_hi, x_lo, columns = [], [], []
            for j in range(4):
                n = g * GROUP + quad * 4 + j
                u = coords[0, pl.ds(n, 1), :]
                v = coords[1, pl.ds(n, 1), :]
                w = coords[2, pl.ds(n, 1), :]
                vis_re = vis[pl.ds(2 * n, 1), :]
                vis_im = vis[pl.ds(2 * n + 1, 1), :]
                cos_row, sin_row = cos_sin(u * l_row + w * d_row)
                cos_col, sin_col = cos_sin(v * l_col + w * d_col)
                x = jnp.concatenate(
                    [
                        vis_re * cos_row - vis_im * sin_row,
                        vis_re * sin_row + vis_im * cos_row,
                    ],
                    axis=1,
                )
                hi, lo = split(x)
                x_hi.append(hi)
                x_lo.append(lo)
                columns.append(split(cos_col) + split(sin_col))
            c_hi, c_lo, s_hi, s_lo = zip(*columns)

            def matrix(c, s):
                real = [jnp.concatenate([a, -b], axis=1) for a, b in zip(c, s)]
                imag = [jnp.concatenate([b, a], axis=1) for a, b in zip(c, s)]
                return jnp.concatenate(real + imag, axis=0)

            lhs = jnp.concatenate(x_hi + x_lo, axis=0)
            both = dot(lhs, matrix(c_hi, s_hi), True)
            sums = both[:128] + both[128:] + dot(lhs[:128], matrix(c_lo, s_lo), True)
            for j in range(4):
                n = g * GROUP + quad * 4 + j
                flat = []
                for c in range(2):
                    value = None
                    for i in range(4):
                        piece = sums[32 * j + 8 * i : 32 * j + 8 * i + 8, 128 * c : 128 * c + 128]
                        if i != j:
                            piece = pltpu.roll(piece, (SUB * (i - j)) % 128, 1)
                        value = piece if value is None else jnp.where(lane_group == i, piece, value)
                    flat.append(value)
                one_re = beam_buf[2 * n, pl.ds(0, 8, stride=2), :]
                one_im = beam_buf[2 * n, pl.ds(1, 8, stride=2), :]
                two_re = beam_buf[2 * n + 1, pl.ds(0, 8, stride=2), :]
                two_im = beam_buf[2 * n + 1, pl.ds(1, 8, stride=2), :]
                beam_re = taper * (one_re * two_re + one_im * two_im)
                beam_im = taper * (one_im * two_re - one_re * two_im)
                sky_re = beam_re * flat[0] - beam_im * flat[1]
                sky_im = beam_re * flat[1] + beam_im * flat[0]
                in_use = n < live
                place = (quad * 4 + j) * 8
                sky[g & 1, place : place + 8, :] = jnp.where(in_use, sky_re, 0.0)
                sky[g & 1, place + 64 : place + 72, :] = jnp.where(in_use, sky_im, 0.0)

    label_tile = 2 * cap + (2 * cap) // 4
    label_lane = SUB * ((2 * cap) % 4)

    def cells(g):
        hi, lo = split(sky[g & 1])
        left = jnp.concatenate([left_hi[...], left_lo[...], left_hi[...]], axis=1)
        z = dot(left, jnp.concatenate([hi, hi, lo], axis=0))
        z_re, z_im = z[:64], z[64:]
        y_re = z_re * twist_re - z_im * twist_im
        y_im = z_re * twist_im + z_im * twist_re
        hi, lo = split(jnp.concatenate([y_re, y_im], axis=1))
        right = jnp.concatenate([right_hi[...], right_hi[...], right_lo[...]], axis=0)
        result = dot(jnp.concatenate([hi, lo, hi], axis=1), right)
        for j in range(GROUP):
            n = g * GROUP + j
            band = row_s[n] >> 3
            shift = row_s[n] & 7
            rank = ranks[band]
            ranks[band] = rank + 1
            late = sublane < shift
            last = jnp.minimum(band + 4, owners - 1)
            for c in range(2):
                value = result[8 * j : 8 * j + 8, 128 * c : 128 * c + 128]
                value = pltpu.roll(value, shift, 0)
                next_value = pltpu.roll(value, SUB, 1)
                spread = jnp.where(late, jnp.where(lane_group == 0, 0.0, next_value), value)
                tile = 2 * rank + c
                for o in range(4):
                    pltpu.store(out.at[band + o, tile], spread, mask=lane_group == o)
                part = tile & 3
                tail = pltpu.roll(value, SUB * (part + 1), 1)
                pltpu.store(
                    out.at[last, 2 * cap + (tile >> 2)], tail, mask=late & (lane_group == part)
                )
            column = jnp.full((8, 128), owner_s[n] * tile_cols + col_s[n], jnp.float32)
            for o in range(5):
                here = (sublane == 0) & (lane == label_lane + o * cap + rank)
                if o == 4:
                    here = here & (sublane < shift)
                target = last if o == 4 else band + o
                pltpu.store(out.at[target, label_tile], column, mask=here)

    await_beams(0)
    images(0)
    for copy in copies[6:10] + copies[:3]:
        copy.wait()

    @pl.loop(1, groups)
    def _(g):
        await_beams(g)
        fetch_beams(g + 2)
        cells(g - 1)
        images(g)

    cells(groups - 1)
    await_beams(groups)
    await_beams(groups + 1)


def row_kernel(
    cap,
    received,
    first,
    second,
    twist,
    out,
    *scratch,
):
    grids, (label_v, label_s, sem) = scratch[:2], scratch[2:]
    sources = received.shape[0]
    label_tile = 2 * cap + (2 * cap) // 4
    label_lane = SUB * ((2 * cap) % 4)
    label_v[...] = received[:, label_tile, 0, :].astype(jnp.int32)
    copy = pltpu.make_async_copy(label_v, label_s, sem)
    copy.start()
    for grid in grids:
        grid[...] = jnp.zeros_like(grid)
    lane = lax.broadcasted_iota(jnp.int32, (8, 128), 1)
    copy.wait()

    @pl.loop(0, sources)
    def _(source):
        for i in range(cap):
            for o in range(5):
                column = label_s[source, label_lane + o * cap + i]
                offset = column & 127
                here = pl.multiple_of((column >> 7) * 8, 8)
                place = lane - offset
                inside = (place >= 0) & (place < SUB)
                beyond = place < SUB - 128
                added = []
                for c in range(2):
                    if o < 4:
                        value, part = received[source, 2 * i + c], o
                    else:
                        value = received[source, 2 * cap + (2 * i + c) // 4]
                        part = (2 * i + c) % 4
                    value = pltpu.roll(value, (offset - SUB * part) & 127, 1)
                    added.append(jnp.where(inside, value, 0.0))
                    added.append(jnp.where(beyond, value, 0.0))
                held = [
                    grids[c][pl.ds(here + 8 * k, 8), :] for c in range(2) for k in range(2)
                ]
                for c in range(2):
                    for k in range(2):
                        grids[c][pl.ds(here + 8 * k, 8), :] = held[2 * c + k] + added[2 * c + k]

    for row in range(0, ROWS_DEV, 2):
        halves_of = []
        for e in range(2):
            rows = [pl.ds(ROWS_DEV * e + row + k, TAIL, stride=2 * ROWS_DEV) for k in range(2)]
            value = jnp.concatenate(
                [jnp.concatenate([grids[c][at, :] for at in rows], axis=1) for c in range(2)], 0
            )
            hi, lo = split(value)
            table_hi, table_lo = first[2 * e], first[2 * e + 1]
            table = jnp.concatenate([table_hi, table_lo, table_hi], axis=1)
            halves_of.append(dot(table, jnp.concatenate([hi, hi, lo], axis=0)))
        low, high = halves_of[0] + halves_of[1], halves_of[0] - halves_of[1]
        for k in range(2):
            b = []
            for e, a in enumerate((low, high)):
                a_re = a[:TAIL, 128 * k : 128 * k + 128]
                a_im = a[TAIL:, 128 * k : 128 * k + 128]
                turn_re = twist[0, TAIL * e : TAIL * e + TAIL]
                turn_im = twist[1, TAIL * e : TAIL * e + TAIL]
                b.append(
                    jnp.concatenate(
                        [a_re * turn_re - a_im * turn_im, a_re * turn_im + a_im * turn_re], axis=1
                    )
                )
            hi, lo = split(jnp.concatenate(b, axis=0))
            table = jnp.concatenate([second[0], second[1], second[0]], axis=1)
            result = dot(table, jnp.concatenate([hi, hi, lo], axis=1), True)
            for c in range(2):
                for h in range(2):
                    out[c, pl.ds(h * 8 + row + k, TAIL, stride=16), :] = result[
                        128 * c : 128 * c + 128, 128 * h : 128 * h + 128
                    ]


def shards(
    visibility, coords, block_owner, block_row, block_col, stations, block_count, beam_terms
):
    owners = lax.axis_size("tile")
    per_device = visibility.shape[0]
    tile_cols = NG // owners
    cap, tiles = send_layout(per_device, owners)
    stations_all = beam_terms.shape[0]
    vmem = pl.BlockSpec(memory_space=pltpu.VMEM)
    beams = (
        beam_terms.reshape(stations_all, 2, 8, 128)
        .transpose(0, 2, 1, 3)
        .reshape(stations_all, 16, 128)
    )
    labels = (
        block_owner.reshape(per_device),
        block_row,
        block_col,
        stations.T,
    )
    values = (
        visibility.reshape(per_device * 2, VROWS),
        coords.transpose(1, 0, 2),
        *image_tables(),
    )
    hbm = pl.BlockSpec(memory_space=pltpu.HBM)
    sent = pl.pallas_call(
        functools.partial(image_kernel, cap, tile_cols),
        out_shape=jax.ShapeDtypeStruct((owners, tiles, 8, 128), jnp.float32),
        in_specs=[pl.BlockSpec(memory_space=pltpu.SMEM)] + [hbm] * (1 + len(labels) + len(values)),
        out_specs=vmem,
        scratch_shapes=[
            *(pltpu.SMEM(label.shape, label.dtype) for label in labels),
            *(pltpu.VMEM(value.shape, value.dtype) for value in values),
            pltpu.VMEM((2 * (per_device + 2 * GROUP), 16, 128), jnp.float32),
            pltpu.VMEM((2, 128, 128), jnp.float32),
            pltpu.SMEM((owners,), jnp.int32),
            pltpu.SemaphoreType.DMA((per_device // GROUP + 2,)),
            pltpu.SemaphoreType.DMA((len(labels) + len(values),)),
        ],
        compiler_params=pltpu.CompilerParams(vmem_limit_bytes=24 * 1024 * 1024),
        name="image",
    )(
        block_count,
        *(pltpu.with_memory_space_constraint(x, pltpu.HBM) for x in (beams, *labels, *values)),
    )
    received = lax.all_to_all(sent, "tile", split_axis=0, concat_axis=0, tiled=True)
    result = pl.pallas_call(
        functools.partial(row_kernel, cap),
        out_shape=jax.ShapeDtypeStruct((2, LEAD * ROWS_DEV, TAIL), jnp.float32),
        in_specs=[vmem] * 4,
        out_specs=vmem,
        scratch_shapes=[
            *(pltpu.VMEM(((LEAD + 1) * ROWS_DEV, TAIL), jnp.float32) for _ in range(2)),
            pltpu.VMEM((owners, 128), jnp.int32),
            pltpu.SMEM((owners, 128), jnp.int32),
            pltpu.SemaphoreType.DMA,
        ],
        compiler_params=pltpu.CompilerParams(vmem_limit_bytes=24 * 1024 * 1024),
        name="rows",
    )(received, *row_tables())
    return (
        result.reshape(2, LEAD, ROWS_DEV, TAIL).transpose(0, 2, 1, 3).reshape(2, ROWS_DEV, NG)
    )


def solution(mesh):
    placed = (
        P(("parts", "tile"), None, None),
        P(("parts", "tile"), None, None),
        P(("parts", "tile"), None),
        P(("parts", "tile")),
        P(("parts", "tile")),
        P(("parts", "tile"), None),
        P(("parts", "tile")),
        P(),
    )
    return jax.shard_map(
        shards,
        mesh=mesh,
        in_specs=placed,
        out_specs=P(None, ("parts", "tile"), None),
        check_vma=False,
    )
```

```python
import functools
import math

import jax
import jax.numpy as jnp
import ml_dtypes
import numpy as np
from jax import lax
from jax.experimental import pallas as pl
from jax.experimental.pallas import tpu as pltpu
from jax.sharding import PartitionSpec as P

VROWS = 128
SUB = 32
NG = 32768
ROWS_DEV = 8
LEAD = 256
TAIL = 128
GROUP = 8

SIN_TERMS = (4.442882920, -7.308245680, 3.606354030, -0.846110410, 0.109822040)
COS_TERMS = (1.414213500, -6.978850910, 5.739459580, -1.883552820, 0.310677860)


def halves(table):
    table = np.round(table, 12).astype(np.float32)
    high = table.astype(ml_dtypes.bfloat16)
    low = (table - high.astype(np.float32)).astype(ml_dtypes.bfloat16)
    return high, low


def root(numbers, length):
    angle = 2.0 * np.pi / length * (numbers % length)
    return np.cos(angle), -np.sin(angle)


def complex_left(re, im):
    return np.block([[re, -im], [im, re]])


@functools.cache
def image_tables():
    eight = np.arange(8)
    re, im = root(np.outer(eight, eight), 8)
    left = complex_left(np.kron(np.eye(GROUP), re), np.kron(np.eye(GROUP), im))
    lane = np.arange(128)
    twist = root(np.outer(eight, lane // SUB), SUB)
    four = 8 * np.outer(lane // SUB, lane // SUB) + np.outer(lane % SUB, lane % SUB)
    re, im = root(four, SUB)
    right = complex_left(re, im).T
    row_pos = ((4 * eight[:, None] + lane[None, :] // SUB) - SUB // 2) / SUB
    col_pos = np.broadcast_to((lane[None, :] % SUB - SUB // 2) / SUB, (8, 128))
    taper = (1 - 2 * row_pos**2) * (1 - 2 * col_pos**2) / SUB
    small = np.stack([taper, np.round(twist[0], 12), np.round(twist[1], 12)]).astype(np.float32)
    return (*halves(left), *halves(right), small)


@functools.cache
def row_tables():
    lead, tail = np.arange(LEAD), np.arange(TAIL)
    even = complex_left(*root(np.outer(tail, tail), TAIL))
    odd = complex_left(*root(np.outer(tail, 2 * tail + 1), LEAD))
    twist = np.stack(root(np.outer(lead, tail), NG)) / math.sqrt(NG)
    first = np.stack(halves(even) + halves(odd))
    return first, np.stack(halves(even)), np.round(twist, 12).astype(np.float32)


def split(value):
    high = value.astype(jnp.bfloat16)
    return high, (value - high.astype(jnp.float32)).astype(jnp.bfloat16)


def dot(left, right, transposed=False):
    dims = (((1,), (1 if transposed else 0,)), ((), ()))
    return lax.dot_general(left, right, dims, preferred_element_type=jnp.float32)


def polynomial(terms, z):
    value = z * terms[-1] + terms[-2]
    for term in terms[-3::-1]:
        value = value * z + term
    return value


def cos_sin(turns):
    whole = (turns + 12582912.0) - 12582912.0
    t = turns - whole
    z = t * t
    half_sin = t * polynomial(SIN_TERMS, z)
    half_cos = polynomial(COS_TERMS, z)
    return 1.0 - half_sin * half_sin, half_sin * half_cos


def send_layout(per_device, owners):
    cap = -(-per_device // (owners - SUB // ROWS_DEV + 1))
    tiles = 2 * cap + (2 * cap + 1 + 3) // 4
    return cap, tiles


def image_kernel(
    cap,
    tile_cols,
    *refs,
):
    me = lax.axis_index("tile")
    owners = lax.axis_size("tile")
    count_s, beams, args, refs = refs[0], refs[1], refs[2:13], refs[13:]
    slots, copied = refs[:owners], refs[owners : owners + 11]
    out, beam_buf, sky, ranks, sems, arg_sems = refs[owners + 11 :]
    copies = [
        pltpu.make_async_copy(arg, held, arg_sems.at[k])
        for k, (arg, held) in enumerate(zip(args, copied))
    ]
    for copy in copies:
        copy.start()
    owner_s, row_s, col_s, station_s, vis, coords = copied[:6]
    left_hi, left_lo, right_hi, right_lo, small = copied[6:]
    per_device = vis.shape[0] // 2
    out[...] = jnp.zeros_like(out)
    sky[...] = jnp.zeros_like(sky)
    for b in range(owners):
        ranks[b] = 0
    copies[3].wait()
    live = count_s[0]
    groups = (live + GROUP - 1) >> 3

    def fetch_beams(g):
        for j in range(GROUP):
            n = jnp.minimum(g, per_device // GROUP - 1) * GROUP + j
            for side in range(2):
                pltpu.make_async_copy(
                    beams.at[station_s[side, n]],
                    beam_buf.at[2 * (g * GROUP + j) + side],
                    sems.at[g],
                ).start()

    def await_beams(g):
        waited = beam_buf.at[pl.ds(g * 2 * GROUP, 2 * GROUP)]
        pltpu.make_async_copy(beams.at[pl.ds(0, 2 * GROUP)], waited, sems.at[g]).wait()

    for g in range(3):
        fetch_beams(g)
    copies[4].wait()
    copies[5].wait()
    copies[10].wait()
    taper = small[0]
    twist_re = jnp.concatenate([small[1]] * GROUP, axis=0)
    twist_im = jnp.concatenate([small[2]] * GROUP, axis=0)
    number = lax.broadcasted_iota(jnp.int32, (SUB, VROWS), 0)
    l_row = (4 * (number % 8) + number // 8 - SUB // 2).astype(jnp.float32) / SUB
    l_col = (number - SUB // 2).astype(jnp.float32) / SUB
    d_row = l_row * l_row
    d_col = l_col * l_col
    sublane = lax.broadcasted_iota(jnp.int32, (8, 128), 0)
    lane = lax.broadcasted_iota(jnp.int32, (8, 128), 1)
    lane_group = lane // SUB

    def images(g):
        for quad in range(GROUP // 4):
            x_hi, x_lo, columns = [], [], []
            for j in range(4):
                n = g * GROUP + quad * 4 + j
                u = coords[0, pl.ds(n, 1), :]
                v = coords[1, pl.ds(n, 1), :]
                w = coords[2, pl.ds(n, 1), :]
                vis_re = vis[pl.ds(2 * n, 1), :]
                vis_im = vis[pl.ds(2 * n + 1, 1), :]
                cos_row, sin_row = cos_sin(u * l_row + w * d_row)
                cos_col, sin_col = cos_sin(v * l_col + w * d_col)
                x = jnp.concatenate(
                    [
                        vis_re * cos_row - vis_im * sin_row,
                        vis_re * sin_row + vis_im * cos_row,
                    ],
                    axis=1,
                )
                hi, lo = split(x)
                x_hi.append(hi)
                x_lo.append(lo)
                columns.append(split(cos_col) + split(sin_col))
            c_hi, c_lo, s_hi, s_lo = zip(*columns)

            def matrix(c, s):
                real = [jnp.concatenate([a, -b], axis=1) for a, b in zip(c, s)]
                imag = [jnp.concatenate([b, a], axis=1) for a, b in zip(c, s)]
                return jnp.concatenate(real + imag, axis=0)

            lhs = jnp.concatenate(x_hi + x_lo, axis=0)
            both = dot(lhs, matrix(c_hi, s_hi), True)
            sums = both[:128] + both[128:] + dot(lhs[:128], matrix(c_lo, s_lo), True)
            for j in range(4):
                n = g * GROUP + quad * 4 + j
                flat = []
                for c in range(2):
                    value = None
                    for i in range(4):
                        piece = sums[32 * j + 8 * i : 32 * j + 8 * i + 8, 128 * c : 128 * c + 128]
                        if i != j:
                            piece = pltpu.roll(piece, (SUB * (i - j)) % 128, 1)
                        value = piece if value is None else jnp.where(lane_group == i, piece, value)
                    flat.append(value)
                one_re = beam_buf[2 * n, pl.ds(0, 8, stride=2), :]
                one_im = beam_buf[2 * n, pl.ds(1, 8, stride=2), :]
                two_re = beam_buf[2 * n + 1, pl.ds(0, 8, stride=2), :]
                two_im = beam_buf[2 * n + 1, pl.ds(1, 8, stride=2), :]
                beam_re = taper * (one_re * two_re + one_im * two_im)
                beam_im = taper * (one_im * two_re - one_re * two_im)
                sky_re = beam_re * flat[0] - beam_im * flat[1]
                sky_im = beam_re * flat[1] + beam_im * flat[0]
                in_use = n < live
                place = (quad * 4 + j) * 8
                sky[g & 1, place : place + 8, :] = jnp.where(in_use, sky_re, 0.0)
                sky[g & 1, place + 64 : place + 72, :] = jnp.where(in_use, sky_im, 0.0)

    label_tile = 2 * cap + (2 * cap) // 4
    label_lane = SUB * ((2 * cap) % 4)

    def slot_of(owner):
        return (owners - (owner ^ me)) & (owners - 1)

    def cells(g):
        hi, lo = split(sky[g & 1])
        left = jnp.concatenate([left_hi[...], left_lo[...], left_hi[...]], axis=1)
        z = dot(left, jnp.concatenate([hi, hi, lo], axis=0))
        z_re, z_im = z[:64], z[64:]
        y_re = z_re * twist_re - z_im * twist_im
        y_im = z_re * twist_im + z_im * twist_re
        hi, lo = split(jnp.concatenate([y_re, y_im], axis=1))
        right = jnp.concatenate([right_hi[...], right_hi[...], right_lo[...]], axis=0)
        result = dot(jnp.concatenate([hi, lo, hi], axis=1), right)
        for j in range(GROUP):
            n = g * GROUP + j
            band = row_s[n] >> 3
            shift = row_s[n] & 7
            rank = ranks[band]
            ranks[band] = rank + 1
            late = sublane < shift
            last = jnp.minimum(band + 4, owners - 1)
            for c in range(2):
                value = result[8 * j : 8 * j + 8, 128 * c : 128 * c + 128]
                value = pltpu.roll(value, shift, 0)
                next_value = pltpu.roll(value, SUB, 1)
                spread = jnp.where(late, jnp.where(lane_group == 0, 0.0, next_value), value)
                tile = 2 * rank + c
                for o in range(4):
                    pltpu.store(out.at[slot_of(band + o), tile], spread, mask=lane_group == o)
                part = tile & 3
                tail = pltpu.roll(value, SUB * (part + 1), 1)
                pltpu.store(
                    out.at[slot_of(last), 2 * cap + (tile >> 2)], tail, mask=late & (lane_group == part)
                )
            column = jnp.full((8, 128), owner_s[n] * tile_cols + col_s[n], jnp.float32)
            for o in range(5):
                here = (sublane == 0) & (lane == label_lane + o * cap + rank)
                if o == 4:
                    here = here & (sublane < shift)
                target = last if o == 4 else band + o
                pltpu.store(out.at[slot_of(target), label_tile], column, mask=here)

    await_beams(0)
    images(0)
    for copy in copies[6:10] + copies[:3]:
        copy.wait()

    @pl.loop(1, groups)
    def _(g):
        await_beams(g)
        fetch_beams(g + 2)
        cells(g - 1)
        images(g)

    cells(groups - 1)
    await_beams(groups)
    await_beams(groups + 1)
    for k, slot in enumerate(slots):
        slot[...] = out[k]


def row_kernel(
    cap,
    first,
    second,
    twist,
    *refs,
):
    sources = lax.axis_size("tile")
    slots = refs[:sources]
    out, received = refs[sources : sources + 2]
    grids, (label_v, label_s, sem) = refs[sources + 2 : sources + 4], refs[sources + 4 :]
    for k, slot in enumerate(slots):
        received[k] = slot[...]
    label_tile = 2 * cap + (2 * cap) // 4
    label_lane = SUB * ((2 * cap) % 4)
    label_v[...] = received[:, label_tile, 0, :].astype(jnp.int32)
    copy = pltpu.make_async_copy(label_v, label_s, sem)
    copy.start()
    for grid in grids:
        grid[...] = jnp.zeros_like(grid)
    lane = lax.broadcasted_iota(jnp.int32, (8, 128), 1)
    copy.wait()

    @pl.loop(0, sources)
    def _(source):
        for i in range(cap):
            for o in range(5):
                column = label_s[source, label_lane + o * cap + i]
                offset = column & 127
                here = pl.multiple_of((column >> 7) * 8, 8)
                place = lane - offset
                inside = (place >= 0) & (place < SUB)
                beyond = place < SUB - 128
                added = []
                for c in range(2):
                    if o < 4:
                        value, part = received[source, 2 * i + c], o
                    else:
                        value = received[source, 2 * cap + (2 * i + c) // 4]
                        part = (2 * i + c) % 4
                    value = pltpu.roll(value, (offset - SUB * part) & 127, 1)
                    added.append(jnp.where(inside, value, 0.0))
                    added.append(jnp.where(beyond, value, 0.0))
                held = [
                    grids[c][pl.ds(here + 8 * k, 8), :] for c in range(2) for k in range(2)
                ]
                for c in range(2):
                    for k in range(2):
                        grids[c][pl.ds(here + 8 * k, 8), :] = held[2 * c + k] + added[2 * c + k]

    for row in range(0, ROWS_DEV, 2):
        halves_of = []
        for e in range(2):
            rows = [pl.ds(ROWS_DEV * e + row + k, TAIL, stride=2 * ROWS_DEV) for k in range(2)]
            value = jnp.concatenate(
                [jnp.concatenate([grids[c][at, :] for at in rows], axis=1) for c in range(2)], 0
            )
            hi, lo = split(value)
            table_hi, table_lo = first[2 * e], first[2 * e + 1]
            table = jnp.concatenate([table_hi, table_lo, table_hi], axis=1)
            halves_of.append(dot(table, jnp.concatenate([hi, hi, lo], axis=0)))
        low, high = halves_of[0] + halves_of[1], halves_of[0] - halves_of[1]
        for k in range(2):
            b = []
            for e, a in enumerate((low, high)):
                a_re = a[:TAIL, 128 * k : 128 * k + 128]
                a_im = a[TAIL:, 128 * k : 128 * k + 128]
                turn_re = twist[0, TAIL * e : TAIL * e + TAIL]
                turn_im = twist[1, TAIL * e : TAIL * e + TAIL]
                b.append(
                    jnp.concatenate(
                        [a_re * turn_re - a_im * turn_im, a_re * turn_im + a_im * turn_re], axis=1
                    )
                )
            hi, lo = split(jnp.concatenate(b, axis=0))
            table = jnp.concatenate([second[0], second[1], second[0]], axis=1)
            result = dot(table, jnp.concatenate([hi, hi, lo], axis=1), True)
            for c in range(2):
                for h in range(2):
                    out[c, pl.ds(h * 8 + row + k, TAIL, stride=16), :] = result[
                        128 * c : 128 * c + 128, 128 * h : 128 * h + 128
                    ]


def shards(
    visibility, coords, block_owner, block_row, block_col, stations, block_count, beam_terms
):
    owners = lax.axis_size("tile")
    per_device = visibility.shape[0]
    tile_cols = NG // owners
    cap, tiles = send_layout(per_device, owners)
    stations_all = beam_terms.shape[0]
    vmem = pl.BlockSpec(memory_space=pltpu.VMEM)
    beams = (
        beam_terms.reshape(stations_all, 2, 8, 128)
        .transpose(0, 2, 1, 3)
        .reshape(stations_all, 16, 128)
    )
    labels = (
        block_owner.reshape(per_device),
        block_row,
        block_col,
        stations.T,
    )
    values = (
        visibility.reshape(per_device * 2, VROWS),
        coords.transpose(1, 0, 2),
        *image_tables(),
    )
    hbm = pl.BlockSpec(memory_space=pltpu.HBM)
    sent = pl.pallas_call(
        functools.partial(image_kernel, cap, tile_cols),
        out_shape=[jax.ShapeDtypeStruct((tiles, 8, 128), jnp.float32)] * owners,
        in_specs=[pl.BlockSpec(memory_space=pltpu.SMEM)] + [hbm] * (1 + len(labels) + len(values)),
        out_specs=[vmem] * owners,
        scratch_shapes=[
            *(pltpu.SMEM(label.shape, label.dtype) for label in labels),
            *(pltpu.VMEM(value.shape, value.dtype) for value in values),
            pltpu.VMEM((owners, tiles, 8, 128), jnp.float32),
            pltpu.VMEM((2 * (per_device + 2 * GROUP), 16, 128), jnp.float32),
            pltpu.VMEM((2, 128, 128), jnp.float32),
            pltpu.SMEM((owners,), jnp.int32),
            pltpu.SemaphoreType.DMA((per_device // GROUP + 2,)),
            pltpu.SemaphoreType.DMA((len(labels) + len(values),)),
        ],
        compiler_params=pltpu.CompilerParams(vmem_limit_bytes=24 * 1024 * 1024),
        name="image",
    )(
        block_count,
        *(pltpu.with_memory_space_constraint(x, pltpu.HBM) for x in (beams, *labels, *values)),
    )
    received = list(sent)
    for k in range(1, owners):
        received[k] = lax.ppermute(
            sent[k], "tile", [(source, source ^ (owners - k)) for source in range(owners)]
        )
    result = pl.pallas_call(
        functools.partial(row_kernel, cap),
        out_shape=jax.ShapeDtypeStruct((2, LEAD * ROWS_DEV, TAIL), jnp.float32),
        in_specs=[vmem] * (3 + owners),
        out_specs=vmem,
        scratch_shapes=[
            pltpu.VMEM((owners, tiles, 8, 128), jnp.float32),
            *(pltpu.VMEM(((LEAD + 1) * ROWS_DEV, TAIL), jnp.float32) for _ in range(2)),
            pltpu.VMEM((owners, 128), jnp.int32),
            pltpu.SMEM((owners, 128), jnp.int32),
            pltpu.SemaphoreType.DMA,
        ],
        compiler_params=pltpu.CompilerParams(vmem_limit_bytes=24 * 1024 * 1024),
        name="rows",
    )(*row_tables(), *received)
    return (
        result.reshape(2, LEAD, ROWS_DEV, TAIL).transpose(0, 2, 1, 3).reshape(2, ROWS_DEV, NG)
    )


def solution(mesh):
    placed = (
        P(("parts", "tile"), None, None),
        P(("parts", "tile"), None, None),
        P(("parts", "tile"), None),
        P(("parts", "tile")),
        P(("parts", "tile")),
        P(("parts", "tile"), None),
        P(("parts", "tile")),
        P(),
    )
    return jax.shard_map(
        shards,
        mesh=mesh,
        in_specs=placed,
        out_specs=P(None, ("parts", "tile"), None),
        check_vma=False,
    )
```

```python
import functools
import math

import jax
import jax.numpy as jnp
import ml_dtypes
import numpy as np
from jax import lax
from jax.experimental import pallas as pl
from jax.experimental.pallas import tpu as pltpu
from jax.sharding import PartitionSpec as P

VROWS = 128
SUB = 32
NG = 32768
ROWS_DEV = 8
LEAD = 256
TAIL = 128
GROUP = 8

SIN_TERMS = (4.442882920, -7.308245680, 3.606354030, -0.846110410, 0.109822040)
COS_TERMS = (1.414213500, -6.978850910, 5.739459580, -1.883552820, 0.310677860)


def halves(table):
    table = np.round(table, 12).astype(np.float32)
    high = table.astype(ml_dtypes.bfloat16)
    low = (table - high.astype(np.float32)).astype(ml_dtypes.bfloat16)
    return high, low


def root(numbers, length):
    angle = 2.0 * np.pi / length * (numbers % length)
    return np.cos(angle), -np.sin(angle)


def complex_left(re, im):
    return np.block([[re, -im], [im, re]])


@functools.cache
def image_tables():
    eight = np.arange(8)
    re, im = root(np.outer(eight, eight), 8)
    left = complex_left(np.kron(np.eye(GROUP), re), np.kron(np.eye(GROUP), im))
    lane = np.arange(128)
    twist = root(np.outer(eight, lane // SUB), SUB)
    four = 8 * np.outer(lane // SUB, lane // SUB) + np.outer(lane % SUB, lane % SUB)
    re, im = root(four, SUB)
    right = complex_left(re, im).T
    row_pos = ((4 * eight[:, None] + lane[None, :] // SUB) - SUB // 2) / SUB
    col_pos = np.broadcast_to((lane[None, :] % SUB - SUB // 2) / SUB, (8, 128))
    taper = (1 - 2 * row_pos**2) * (1 - 2 * col_pos**2) / SUB
    small = np.stack([taper, np.round(twist[0], 12), np.round(twist[1], 12)]).astype(np.float32)
    return (*halves(left), *halves(right), small)


@functools.cache
def row_tables():
    lead, tail = np.arange(LEAD), np.arange(TAIL)
    even = complex_left(*root(np.outer(tail, tail), TAIL))
    odd = complex_left(*root(np.outer(tail, 2 * tail + 1), LEAD))
    twist = np.stack(root(np.outer(lead, tail), NG)) / math.sqrt(NG)
    first = np.stack(halves(even) + halves(odd))
    return first, np.stack(halves(even)), np.round(twist, 12).astype(np.float32)


def split(value):
    high = value.astype(jnp.bfloat16)
    return high, (value - high.astype(jnp.float32)).astype(jnp.bfloat16)


def dot(left, right, transposed=False):
    dims = (((1,), (1 if transposed else 0,)), ((), ()))
    return lax.dot_general(left, right, dims, preferred_element_type=jnp.float32)


def polynomial(terms, z):
    value = z * terms[-1] + terms[-2]
    for term in terms[-3::-1]:
        value = value * z + term
    return value


def cos_sin(turns):
    whole = (turns + 12582912.0) - 12582912.0
    t = turns - whole
    z = t * t
    half_sin = t * polynomial(SIN_TERMS, z)
    half_cos = polynomial(COS_TERMS, z)
    return 1.0 - half_sin * half_sin, half_sin * half_cos


def send_layout(per_device, owners):
    cap = -(-per_device // (owners - SUB // ROWS_DEV + 1))
    tiles = 2 * cap + (2 * cap + 1 + 3) // 4
    return cap, tiles


def exchange_order(owners):
    half = owners // 2
    far = [k + part for k in range(half // 2) for part in (half + half // 2, half)]
    near = list(range(half - 1, 0, -1))
    order = [0] + far[:3]
    for k in range(3, half):
        order += near[: 1 if k < half - 1 else len(near)] + [far[k]]
        near = near[1:] if k < half - 1 else []
    return order


def image_kernel(
    cap,
    tile_cols,
    *refs,
):
    me = lax.axis_index("tile")
    owners = lax.axis_size("tile")
    count_s, beams, args, refs = refs[0], refs[1], refs[2:13], refs[13:]
    slots, copied = refs[:owners], refs[owners : owners + 11]
    out, beam_buf, sky, ranks, sems, arg_sems = refs[owners + 11 :]
    copies = [
        pltpu.make_async_copy(arg, held, arg_sems.at[k])
        for k, (arg, held) in enumerate(zip(args, copied))
    ]
    for copy in copies:
        copy.start()
    owner_s, row_s, col_s, station_s, vis, coords = copied[:6]
    left_hi, left_lo, right_hi, right_lo, small = copied[6:]
    per_device = vis.shape[0] // 2
    out[...] = jnp.zeros_like(out)
    sky[...] = jnp.zeros_like(sky)
    for b in range(owners):
        ranks[b] = 0
    copies[3].wait()
    live = count_s[0]
    groups = (live + GROUP - 1) >> 3

    def fetch_beams(g):
        for j in range(GROUP):
            n = jnp.minimum(g, per_device // GROUP - 1) * GROUP + j
            for side in range(2):
                pltpu.make_async_copy(
                    beams.at[station_s[side, n]],
                    beam_buf.at[2 * (g * GROUP + j) + side],
                    sems.at[g],
                ).start()

    def await_beams(g):
        waited = beam_buf.at[pl.ds(g * 2 * GROUP, 2 * GROUP)]
        pltpu.make_async_copy(beams.at[pl.ds(0, 2 * GROUP)], waited, sems.at[g]).wait()

    for g in range(3):
        fetch_beams(g)
    copies[4].wait()
    copies[5].wait()
    copies[10].wait()
    taper = small[0]
    twist_re = jnp.concatenate([small[1]] * GROUP, axis=0)
    twist_im = jnp.concatenate([small[2]] * GROUP, axis=0)
    number = lax.broadcasted_iota(jnp.int32, (SUB, VROWS), 0)
    l_row = (4 * (number % 8) + number // 8 - SUB // 2).astype(jnp.float32) / SUB
    l_col = (number - SUB // 2).astype(jnp.float32) / SUB
    d_row = l_row * l_row
    d_col = l_col * l_col
    sublane = lax.broadcasted_iota(jnp.int32, (8, 128), 0)
    lane = lax.broadcasted_iota(jnp.int32, (8, 128), 1)
    lane_group = lane // SUB

    def images(g):
        for quad in range(GROUP // 4):
            x_hi, x_lo, columns = [], [], []
            for j in range(4):
                n = g * GROUP + quad * 4 + j
                u = coords[0, pl.ds(n, 1), :]
                v = coords[1, pl.ds(n, 1), :]
                w = coords[2, pl.ds(n, 1), :]
                vis_re = vis[pl.ds(2 * n, 1), :]
                vis_im = vis[pl.ds(2 * n + 1, 1), :]
                cos_row, sin_row = cos_sin(u * l_row + w * d_row)
                cos_col, sin_col = cos_sin(v * l_col + w * d_col)
                x = jnp.concatenate(
                    [
                        vis_re * cos_row - vis_im * sin_row,
                        vis_re * sin_row + vis_im * cos_row,
                    ],
                    axis=1,
                )
                hi, lo = split(x)
                x_hi.append(hi)
                x_lo.append(lo)
                columns.append(split(cos_col) + split(sin_col))
            c_hi, c_lo, s_hi, s_lo = zip(*columns)

            def matrix(c, s):
                real = [jnp.concatenate([a, -b], axis=1) for a, b in zip(c, s)]
                imag = [jnp.concatenate([b, a], axis=1) for a, b in zip(c, s)]
                return jnp.concatenate(real + imag, axis=0)

            lhs = jnp.concatenate(x_hi + x_lo, axis=0)
            both = dot(lhs, matrix(c_hi, s_hi), True)
            sums = both[:128] + both[128:] + dot(lhs[:128], matrix(c_lo, s_lo), True)
            for j in range(4):
                n = g * GROUP + quad * 4 + j
                flat = []
                for c in range(2):
                    value = None
                    for i in range(4):
                        piece = sums[32 * j + 8 * i : 32 * j + 8 * i + 8, 128 * c : 128 * c + 128]
                        if i != j:
                            piece = pltpu.roll(piece, (SUB * (i - j)) % 128, 1)
                        value = piece if value is None else jnp.where(lane_group == i, piece, value)
                    flat.append(value)
                one_re = beam_buf[2 * n, pl.ds(0, 8, stride=2), :]
                one_im = beam_buf[2 * n, pl.ds(1, 8, stride=2), :]
                two_re = beam_buf[2 * n + 1, pl.ds(0, 8, stride=2), :]
                two_im = beam_buf[2 * n + 1, pl.ds(1, 8, stride=2), :]
                beam_re = taper * (one_re * two_re + one_im * two_im)
                beam_im = taper * (one_im * two_re - one_re * two_im)
                sky_re = beam_re * flat[0] - beam_im * flat[1]
                sky_im = beam_re * flat[1] + beam_im * flat[0]
                in_use = n < live
                place = (quad * 4 + j) * 8
                sky[g & 1, place : place + 8, :] = jnp.where(in_use, sky_re, 0.0)
                sky[g & 1, place + 64 : place + 72, :] = jnp.where(in_use, sky_im, 0.0)

    label_tile = 2 * cap + (2 * cap) // 4
    label_lane = SUB * ((2 * cap) % 4)

    def cells(g):
        hi, lo = split(sky[g & 1])
        left = jnp.concatenate([left_hi[...], left_lo[...], left_hi[...]], axis=1)
        z = dot(left, jnp.concatenate([hi, hi, lo], axis=0))
        z_re, z_im = z[:64], z[64:]
        y_re = z_re * twist_re - z_im * twist_im
        y_im = z_re * twist_im + z_im * twist_re
        hi, lo = split(jnp.concatenate([y_re, y_im], axis=1))
        right = jnp.concatenate([right_hi[...], right_hi[...], right_lo[...]], axis=0)
        result = dot(jnp.concatenate([hi, lo, hi], axis=1), right)
        for j in range(GROUP):
            n = g * GROUP + j
            band = row_s[n] >> 3
            shift = row_s[n] & 7
            rank = ranks[band]
            ranks[band] = rank + 1
            late = sublane < shift
            last = jnp.minimum(band + 4, owners - 1)
            for c in range(2):
                value = result[8 * j : 8 * j + 8, 128 * c : 128 * c + 128]
                value = pltpu.roll(value, shift, 0)
                next_value = pltpu.roll(value, SUB, 1)
                spread = jnp.where(late, jnp.where(lane_group == 0, 0.0, next_value), value)
                tile = 2 * rank + c
                for o in range(4):
                    pltpu.store(out.at[(band + o) ^ me, tile], spread, mask=lane_group == o)
                part = tile & 3
                tail = pltpu.roll(value, SUB * (part + 1), 1)
                pltpu.store(
                    out.at[last ^ me, 2 * cap + (tile >> 2)], tail, mask=late & (lane_group == part)
                )
            column = jnp.full((8, 128), owner_s[n] * tile_cols + col_s[n], jnp.float32)
            for o in range(5):
                here = (sublane == 0) & (lane == label_lane + o * cap + rank)
                if o == 4:
                    here = here & (sublane < shift)
                target = last if o == 4 else band + o
                pltpu.store(out.at[target ^ me, label_tile], column, mask=here)

    await_beams(0)
    images(0)
    for copy in copies[6:10] + copies[:3]:
        copy.wait()

    @pl.loop(1, groups)
    def _(g):
        await_beams(g)
        fetch_beams(g + 2)
        cells(g - 1)
        images(g)

    cells(groups - 1)
    await_beams(groups)
    await_beams(groups + 1)
    for slot, offset in zip(slots, exchange_order(owners)):
        slot[...] = out[offset]


def row_kernel(
    cap,
    first,
    second,
    twist,
    *refs,
):
    sources = lax.axis_size("tile")
    slots = refs[:sources]
    out, received = refs[sources : sources + 2]
    grids, (label_v, label_s, sem) = refs[sources + 2 : sources + 4], refs[sources + 4 :]
    for k, slot in enumerate(slots):
        received[k] = slot[...]
    label_tile = 2 * cap + (2 * cap) // 4
    label_lane = SUB * ((2 * cap) % 4)
    label_v[...] = received[:, label_tile, 0, :].astype(jnp.int32)
    copy = pltpu.make_async_copy(label_v, label_s, sem)
    copy.start()
    for grid in grids:
        grid[...] = jnp.zeros_like(grid)
    lane = lax.broadcasted_iota(jnp.int32, (8, 128), 1)
    copy.wait()

    @pl.loop(0, sources)
    def _(source):
        for i in range(cap):
            for o in range(5):
                column = label_s[source, label_lane + o * cap + i]
                offset = column & 127
                here = pl.multiple_of((column >> 7) * 8, 8)
                place = lane - offset
                inside = (place >= 0) & (place < SUB)
                beyond = place < SUB - 128
                added = []
                for c in range(2):
                    if o < 4:
                        value, part = received[source, 2 * i + c], o
                    else:
                        value = received[source, 2 * cap + (2 * i + c) // 4]
                        part = (2 * i + c) % 4
                    value = pltpu.roll(value, (offset - SUB * part) & 127, 1)
                    added.append(jnp.where(inside, value, 0.0))
                    added.append(jnp.where(beyond, value, 0.0))
                held = [
                    grids[c][pl.ds(here + 8 * k, 8), :] for c in range(2) for k in range(2)
                ]
                for c in range(2):
                    for k in range(2):
                        grids[c][pl.ds(here + 8 * k, 8), :] = held[2 * c + k] + added[2 * c + k]

    for row in range(0, ROWS_DEV, 2):
        halves_of = []
        for e in range(2):
            rows = [pl.ds(ROWS_DEV * e + row + k, TAIL, stride=2 * ROWS_DEV) for k in range(2)]
            value = jnp.concatenate(
                [jnp.concatenate([grids[c][at, :] for at in rows], axis=1) for c in range(2)], 0
            )
            hi, lo = split(value)
            table_hi, table_lo = first[2 * e], first[2 * e + 1]
            table = jnp.concatenate([table_hi, table_lo, table_hi], axis=1)
            halves_of.append(dot(table, jnp.concatenate([hi, hi, lo], axis=0)))
        low, high = halves_of[0] + halves_of[1], halves_of[0] - halves_of[1]
        for k in range(2):
            b = []
            for e, a in enumerate((low, high)):
                a_re = a[:TAIL, 128 * k : 128 * k + 128]
                a_im = a[TAIL:, 128 * k : 128 * k + 128]
                turn_re = twist[0, TAIL * e : TAIL * e + TAIL]
                turn_im = twist[1, TAIL * e : TAIL * e + TAIL]
                b.append(
                    jnp.concatenate(
                        [a_re * turn_re - a_im * turn_im, a_re * turn_im + a_im * turn_re], axis=1
                    )
                )
            hi, lo = split(jnp.concatenate(b, axis=0))
            table = jnp.concatenate([second[0], second[1], second[0]], axis=1)
            result = dot(table, jnp.concatenate([hi, hi, lo], axis=1), True)
            for c in range(2):
                for h in range(2):
                    out[c, pl.ds(h * 8 + row + k, TAIL, stride=16), :] = result[
                        128 * c : 128 * c + 128, 128 * h : 128 * h + 128
                    ]


def shards(
    visibility, coords, block_owner, block_row, block_col, stations, block_count, beam_terms
):
    owners = lax.axis_size("tile")
    per_device = visibility.shape[0]
    tile_cols = NG // owners
    cap, tiles = send_layout(per_device, owners)
    stations_all = beam_terms.shape[0]
    vmem = pl.BlockSpec(memory_space=pltpu.VMEM)
    beams = (
        beam_terms.reshape(stations_all, 2, 8, 128)
        .transpose(0, 2, 1, 3)
        .reshape(stations_all, 16, 128)
    )
    labels = (
        block_owner.reshape(per_device),
        block_row,
        block_col,
        stations.T,
    )
    values = (
        visibility.reshape(per_device * 2, VROWS),
        coords.transpose(1, 0, 2),
        *image_tables(),
    )
    hbm = pl.BlockSpec(memory_space=pltpu.HBM)
    sent = pl.pallas_call(
        functools.partial(image_kernel, cap, tile_cols),
        out_shape=[jax.ShapeDtypeStruct((tiles, 8, 128), jnp.float32)] * owners,
        in_specs=[pl.BlockSpec(memory_space=pltpu.SMEM)] + [hbm] * (1 + len(labels) + len(values)),
        out_specs=[vmem] * owners,
        scratch_shapes=[
            *(pltpu.SMEM(label.shape, label.dtype) for label in labels),
            *(pltpu.VMEM(value.shape, value.dtype) for value in values),
            pltpu.VMEM((owners, tiles, 8, 128), jnp.float32),
            pltpu.VMEM((2 * (per_device + 2 * GROUP), 16, 128), jnp.float32),
            pltpu.VMEM((2, 128, 128), jnp.float32),
            pltpu.SMEM((owners,), jnp.int32),
            pltpu.SemaphoreType.DMA((per_device // GROUP + 2,)),
            pltpu.SemaphoreType.DMA((len(labels) + len(values),)),
        ],
        compiler_params=pltpu.CompilerParams(vmem_limit_bytes=24 * 1024 * 1024),
        name="image",
    )(
        block_count,
        *(pltpu.with_memory_space_constraint(x, pltpu.HBM) for x in (beams, *labels, *values)),
    )
    received = [sent[0]] + [
        lax.ppermute(value, "tile", [(source, source ^ k) for source in range(owners)])
        for value, k in zip(sent[1:], exchange_order(owners)[1:])
    ]
    result = pl.pallas_call(
        functools.partial(row_kernel, cap),
        out_shape=jax.ShapeDtypeStruct((2, LEAD * ROWS_DEV, TAIL), jnp.float32),
        in_specs=[vmem] * (3 + owners),
        out_specs=vmem,
        scratch_shapes=[
            pltpu.VMEM((owners, tiles, 8, 128), jnp.float32),
            *(pltpu.VMEM(((LEAD + 1) * ROWS_DEV, TAIL), jnp.float32) for _ in range(2)),
            pltpu.VMEM((owners, 128), jnp.int32),
            pltpu.SMEM((owners, 128), jnp.int32),
            pltpu.SemaphoreType.DMA,
        ],
        compiler_params=pltpu.CompilerParams(vmem_limit_bytes=24 * 1024 * 1024),
        name="rows",
    )(*row_tables(), *received)
    return (
        result.reshape(2, LEAD, ROWS_DEV, TAIL).transpose(0, 2, 1, 3).reshape(2, ROWS_DEV, NG)
    )


def solution(mesh):
    placed = (
        P(("parts", "tile"), None, None),
        P(("parts", "tile"), None, None),
        P(("parts", "tile"), None),
        P(("parts", "tile")),
        P(("parts", "tile")),
        P(("parts", "tile"), None),
        P(("parts", "tile")),
        P(),
    )
    return jax.shard_map(
        shards,
        mesh=mesh,
        in_specs=placed,
        out_specs=P(None, ("parts", "tile"), None),
        check_vma=False,
    )
```

```python
import functools
import math

import jax
import jax.numpy as jnp
import ml_dtypes
import numpy as np
from jax import lax
from jax.experimental import pallas as pl
from jax.experimental.pallas import tpu as pltpu
from jax.sharding import PartitionSpec as P

VROWS = 128
SUB = 32
NG = 32768
ROWS_DEV = 8
LEAD = 256
TAIL = 128
GROUP = 8

SIN_TERMS = (4.442882920, -7.308245680, 3.606354030, -0.846110410, 0.109822040)
COS_TERMS = (1.414213500, -6.978850910, 5.739459580, -1.883552820, 0.310677860)


def halves(table):
    table = np.round(table, 12).astype(np.float32)
    high = table.astype(ml_dtypes.bfloat16)
    low = (table - high.astype(np.float32)).astype(ml_dtypes.bfloat16)
    return high, low


def root(numbers, length):
    angle = 2.0 * np.pi / length * (numbers % length)
    return np.cos(angle), -np.sin(angle)


def complex_left(re, im):
    return np.block([[re, -im], [im, re]])


@functools.cache
def image_tables():
    eight = np.arange(8)
    re, im = root(np.outer(eight, eight), 8)
    left = complex_left(np.kron(np.eye(GROUP), re), np.kron(np.eye(GROUP), im))
    lane = np.arange(128)
    twist = root(np.outer(eight, lane // SUB), SUB)
    four = 8 * np.outer(lane // SUB, lane // SUB) + np.outer(lane % SUB, lane % SUB)
    re, im = root(four, SUB)
    right = complex_left(re, im).T
    row_pos = ((4 * eight[:, None] + lane[None, :] // SUB) - SUB // 2) / SUB
    col_pos = np.broadcast_to((lane[None, :] % SUB - SUB // 2) / SUB, (8, 128))
    taper = (1 - 2 * row_pos**2) * (1 - 2 * col_pos**2) / SUB
    small = np.stack([taper, np.round(twist[0], 12), np.round(twist[1], 12)]).astype(np.float32)
    place = (np.arange(SUB) - SUB // 2) / SUB
    turn = [np.kron(np.eye(GROUP), power) for power in (place, place**2)]
    turns = np.concatenate(turn * 3).astype(ml_dtypes.bfloat16)
    return (*halves(left), *halves(right), small, turns)


@functools.cache
def row_tables():
    lead, tail = np.arange(LEAD), np.arange(TAIL)
    even = complex_left(*root(np.outer(tail, tail), TAIL))
    odd = complex_left(*root(np.outer(tail, 2 * tail + 1), LEAD))
    twist = np.stack(root(np.outer(lead, tail), NG)) / math.sqrt(NG)
    first = np.stack(halves(even) + halves(odd))
    return first, np.stack(halves(even)), np.round(twist, 12).astype(np.float32)


def split(value):
    high = value.astype(jnp.bfloat16)
    return high, (value - high.astype(jnp.float32)).astype(jnp.bfloat16)


def dot(left, right, transposed=False):
    dims = (((1,), (1 if transposed else 0,)), ((), ()))
    return lax.dot_general(left, right, dims, preferred_element_type=jnp.float32)


def polynomial(terms, z):
    value = z * terms[-1] + terms[-2]
    for term in terms[-3::-1]:
        value = value * z + term
    return value


def cos_sin(turns):
    whole = (turns + 12582912.0) - 12582912.0
    t = turns - whole
    z = t * t
    half_sin = t * polynomial(SIN_TERMS, z)
    half_cos = polynomial(COS_TERMS, z)
    return 1.0 - half_sin * half_sin, half_sin * half_cos


def send_layout(per_device, owners):
    cap = -(-per_device // (owners - SUB // ROWS_DEV + 1))
    tiles = 2 * cap + (2 * cap + 1 + 3) // 4
    return cap, tiles


def image_kernel(
    cap,
    tile_cols,
    *refs,
):
    count_s, beams, args, out, copied = refs[0], refs[1], refs[2:14], refs[14], refs[15:27]
    beam_buf, sky, ranks, sems, arg_sems = refs[27:]
    copies = [
        pltpu.make_async_copy(arg, held, arg_sems.at[k])
        for k, (arg, held) in enumerate(zip(args, copied))
    ]
    for copy in copies:
        copy.start()
    owner_s, row_s, col_s, station_s, vis, coords = copied[:6]
    left_hi, left_lo, right_hi, right_lo, small, turns = copied[6:]
    per_device = vis.shape[0] // 2
    owners = out.shape[0]
    out[...] = jnp.zeros_like(out)
    sky[...] = jnp.zeros_like(sky)
    for b in range(owners):
        ranks[b] = 0
    copies[3].wait()
    live = count_s[0]
    groups = (live + GROUP - 1) >> 3

    def fetch_beams(g):
        for j in range(GROUP):
            n = jnp.minimum(g, per_device // GROUP - 1) * GROUP + j
            for side in range(2):
                pltpu.make_async_copy(
                    beams.at[station_s[side, n]],
                    beam_buf.at[2 * (g * GROUP + j) + side],
                    sems.at[g],
                ).start()

    def await_beams(g):
        waited = beam_buf.at[pl.ds(g * 2 * GROUP, 2 * GROUP)]
        pltpu.make_async_copy(beams.at[pl.ds(0, 2 * GROUP)], waited, sems.at[g]).wait()

    for g in range(3):
        fetch_beams(g)
    copies[4].wait()
    copies[5].wait()
    copies[10].wait()
    copies[11].wait()
    taper = small[0]
    twist_re = jnp.concatenate([small[1]] * GROUP, axis=0)
    twist_im = jnp.concatenate([small[2]] * GROUP, axis=0)
    number = lax.broadcasted_iota(jnp.int32, (SUB, VROWS), 0)
    l_row = (4 * (number % 8) + number // 8 - SUB // 2).astype(jnp.float32) / SUB
    d_row = l_row * l_row
    sublane = lax.broadcasted_iota(jnp.int32, (8, 128), 0)
    lane = lax.broadcasted_iota(jnp.int32, (8, 128), 1)
    lane_group = lane // SUB

    def images(g, first=False):
        base = pl.multiple_of(g * GROUP, GROUP)
        rest = jnp.concatenate([coords[c, pl.ds(base, GROUP), :] for c in (1, 2)], axis=0)
        parts = []
        for _ in range(2):
            parts.append(rest.astype(jnp.bfloat16).astype(jnp.float32))
            rest = rest - parts[-1]
        parts = jnp.concatenate(parts + [rest], axis=0).T.astype(jnp.bfloat16)
        cos_col, sin_col = cos_sin(dot(parts, turns[...]))
        cos_col, sin_col = split(cos_col), split(sin_col)
        for quad in range(GROUP // 4):
            x_hi, x_lo = [], []
            for j in range(4):
                n = g * GROUP + quad * 4 + j
                u = coords[0, pl.ds(n, 1), :]
                w = coords[2, pl.ds(n, 1), :]
                vis_re = vis[pl.ds(2 * n, 1), :]
                vis_im = vis[pl.ds(2 * n + 1, 1), :]
                cos_row, sin_row = cos_sin(u * l_row + w * d_row)
                x = jnp.concatenate(
                    [
                        vis_re * cos_row - vis_im * sin_row,
                        vis_re * sin_row + vis_im * cos_row,
                    ],
                    axis=1,
                )
                hi, lo = split(x)
                x_hi.append(hi)
                x_lo.append(lo)

            def matrix(k):
                c = cos_col[k][:, 128 * quad : 128 * quad + 128]
                s = sin_col[k][:, 128 * quad : 128 * quad + 128]
                return jnp.concatenate(
                    [jnp.concatenate([c, s], axis=1), jnp.concatenate([-s, c], axis=1)], axis=0
                )

            lhs = jnp.concatenate(x_hi + x_lo, axis=0)
            both = dot(lhs, matrix(0))
            sums = both[:128] + both[128:] + dot(lhs[:128], matrix(1))
            if first and quad == 0:
                await_beams(g)
            for j in range(4):
                n = g * GROUP + quad * 4 + j
                flat = []
                for c in range(2):
                    value = None
                    for i in range(4):
                        piece = sums[32 * j + 8 * i : 32 * j + 8 * i + 8, 128 * c : 128 * c + 128]
                        if i != j:
                            piece = pltpu.roll(piece, (SUB * (i - j)) % 128, 1)
                        value = piece if value is None else jnp.where(lane_group == i, piece, value)
                    flat.append(value)
                one_re = beam_buf[2 * n, pl.ds(0, 8, stride=2), :]
                one_im = beam_buf[2 * n, pl.ds(1, 8, stride=2), :]
                two_re = beam_buf[2 * n + 1, pl.ds(0, 8, stride=2), :]
                two_im = beam_buf[2 * n + 1, pl.ds(1, 8, stride=2), :]
                beam_re = taper * (one_re * two_re + one_im * two_im)
                beam_im = taper * (one_im * two_re - one_re * two_im)
                sky_re = beam_re * flat[0] - beam_im * flat[1]
                sky_im = beam_re * flat[1] + beam_im * flat[0]
                in_use = n < live
                place = (quad * 4 + j) * 8
                sky[g & 1, place : place + 8, :] = jnp.where(in_use, sky_re, 0.0)
                sky[g & 1, place + 64 : place + 72, :] = jnp.where(in_use, sky_im, 0.0)

    label_tile = 2 * cap + (2 * cap) // 4
    label_lane = SUB * ((2 * cap) % 4)

    def cells(g):
        hi, lo = split(sky[g & 1])
        left = jnp.concatenate([left_hi[...], left_lo[...], left_hi[...]], axis=1)
        z = dot(left, jnp.concatenate([hi, hi, lo], axis=0))
        z_re, z_im = z[:64], z[64:]
        y_re = z_re * twist_re - z_im * twist_im
        y_im = z_re * twist_im + z_im * twist_re
        hi, lo = split(jnp.concatenate([y_re, y_im], axis=1))
        right = jnp.concatenate([right_hi[...], right_hi[...], right_lo[...]], axis=0)
        result = dot(jnp.concatenate([hi, lo, hi], axis=1), right)
        for j in range(GROUP):
            n = g * GROUP + j
            band = row_s[n] >> 3
            shift = row_s[n] & 7
            rank = ranks[band]
            ranks[band] = rank + 1
            late = sublane < shift
            last = jnp.minimum(band + 4, owners - 1)
            for c in range(2):
                value = result[8 * j : 8 * j + 8, 128 * c : 128 * c + 128]
                value = pltpu.roll(value, shift, 0)
                next_value = pltpu.roll(value, SUB, 1)
                spread = jnp.where(late, jnp.where(lane_group == 0, 0.0, next_value), value)
                tile = 2 * rank + c
                for o in range(4):
                    pltpu.store(out.at[band + o, tile], spread, mask=lane_group == o)
                part = tile & 3
                tail = pltpu.roll(value, SUB * (part + 1), 1)
                pltpu.store(
                    out.at[last, 2 * cap + (tile >> 2)], tail, mask=late & (lane_group == part)
                )
            column = jnp.full((8, 128), owner_s[n] * tile_cols + col_s[n], jnp.float32)
            for o in range(5):
                here = (sublane == 0) & (lane == label_lane + o * cap + rank)
                if o == 4:
                    here = here & (sublane < shift)
                target = last if o == 4 else band + o
                pltpu.store(out.at[target, label_tile], column, mask=here)

    images(0, True)
    for copy in copies[6:10] + copies[:3]:
        copy.wait()

    @pl.loop(1, groups)
    def _(g):
        await_beams(g)
        fetch_beams(g + 2)
        cells(g - 1)
        images(g)

    cells(groups - 1)
    await_beams(groups)
    await_beams(groups + 1)


def row_kernel(
    cap,
    received,
    first,
    second,
    twist,
    out,
    *scratch,
):
    grids, (label_v, label_s, sem) = scratch[:2], scratch[2:]
    sources = received.shape[0]
    label_tile = 2 * cap + (2 * cap) // 4
    label_lane = SUB * ((2 * cap) % 4)
    label_v[...] = received[:, label_tile, 0, :].astype(jnp.int32)
    copy = pltpu.make_async_copy(label_v, label_s, sem)
    copy.start()
    for grid in grids:
        grid[...] = jnp.zeros_like(grid)
    lane = lax.broadcasted_iota(jnp.int32, (8, 128), 1)
    copy.wait()

    @pl.loop(0, sources)
    def _(source):
        for i in range(cap):
            for o in range(5):
                column = label_s[source, label_lane + o * cap + i]
                offset = column & 127
                here = pl.multiple_of((column >> 7) * 8, 8)
                place = lane - offset
                inside = (place >= 0) & (place < SUB)
                beyond = place < SUB - 128
                added = []
                for c in range(2):
                    if o < 4:
                        value, part = received[source, 2 * i + c], o
                    else:
                        value = received[source, 2 * cap + (2 * i + c) // 4]
                        part = (2 * i + c) % 4
                    value = pltpu.roll(value, (offset - SUB * part) & 127, 1)
                    added.append(jnp.where(inside, value, 0.0))
                    added.append(jnp.where(beyond, value, 0.0))
                held = [
                    grids[c][pl.ds(here + 8 * k, 8), :] for c in range(2) for k in range(2)
                ]
                for c in range(2):
                    for k in range(2):
                        grids[c][pl.ds(here + 8 * k, 8), :] = held[2 * c + k] + added[2 * c + k]

    for row in range(0, ROWS_DEV, 2):
        halves_of = []
        for e in range(2):
            rows = [pl.ds(ROWS_DEV * e + row + k, TAIL, stride=2 * ROWS_DEV) for k in range(2)]
            value = jnp.concatenate(
                [jnp.concatenate([grids[c][at, :] for at in rows], axis=1) for c in range(2)], 0
            )
            hi, lo = split(value)
            table_hi, table_lo = first[2 * e], first[2 * e + 1]
            table = jnp.concatenate([table_hi, table_lo, table_hi], axis=1)
            halves_of.append(dot(table, jnp.concatenate([hi, hi, lo], axis=0)))
        low, high = halves_of[0] + halves_of[1], halves_of[0] - halves_of[1]
        for k in range(2):
            b = []
            for e, a in enumerate((low, high)):
                a_re = a[:TAIL, 128 * k : 128 * k + 128]
                a_im = a[TAIL:, 128 * k : 128 * k + 128]
                turn_re = twist[0, TAIL * e : TAIL * e + TAIL]
                turn_im = twist[1, TAIL * e : TAIL * e + TAIL]
                b.append(
                    jnp.concatenate(
                        [a_re * turn_re - a_im * turn_im, a_re * turn_im + a_im * turn_re], axis=1
                    )
                )
            hi, lo = split(jnp.concatenate(b, axis=0))
            table = jnp.concatenate([second[0], second[1], second[0]], axis=1)
            result = dot(table, jnp.concatenate([hi, hi, lo], axis=1), True)
            for c in range(2):
                for h in range(2):
                    out[c, pl.ds(h * 8 + row + k, TAIL, stride=16), :] = result[
                        128 * c : 128 * c + 128, 128 * h : 128 * h + 128
                    ]


def shards(
    visibility, coords, block_owner, block_row, block_col, stations, block_count, beam_terms
):
    owners = lax.axis_size("tile")
    per_device = visibility.shape[0]
    tile_cols = NG // owners
    cap, tiles = send_layout(per_device, owners)
    stations_all = beam_terms.shape[0]
    vmem = pl.BlockSpec(memory_space=pltpu.VMEM)
    beams = (
        beam_terms.reshape(stations_all, 2, 8, 128)
        .transpose(0, 2, 1, 3)
        .reshape(stations_all, 16, 128)
    )
    labels = (
        block_owner.reshape(per_device),
        block_row,
        block_col,
        stations.T,
    )
    values = (
        visibility.reshape(per_device * 2, VROWS),
        coords.transpose(1, 0, 2),
        *image_tables(),
    )
    hbm = pl.BlockSpec(memory_space=pltpu.HBM)
    sent = pl.pallas_call(
        functools.partial(image_kernel, cap, tile_cols),
        out_shape=jax.ShapeDtypeStruct((owners, tiles, 8, 128), jnp.float32),
        in_specs=[pl.BlockSpec(memory_space=pltpu.SMEM)] + [hbm] * (1 + len(labels) + len(values)),
        out_specs=vmem,
        scratch_shapes=[
            *(pltpu.SMEM(label.shape, label.dtype) for label in labels),
            *(pltpu.VMEM(value.shape, value.dtype) for value in values),
            pltpu.VMEM((2 * (per_device + 2 * GROUP), 16, 128), jnp.float32),
            pltpu.VMEM((2, 128, 128), jnp.float32),
            pltpu.SMEM((owners,), jnp.int32),
            pltpu.SemaphoreType.DMA((per_device // GROUP + 2,)),
            pltpu.SemaphoreType.DMA((len(labels) + len(values),)),
        ],
        compiler_params=pltpu.CompilerParams(vmem_limit_bytes=24 * 1024 * 1024),
        name="image",
    )(
        block_count,
        *(pltpu.with_memory_space_constraint(x, pltpu.HBM) for x in (beams, *labels, *values)),
    )
    received = lax.all_to_all(sent, "tile", split_axis=0, concat_axis=0, tiled=True)
    result = pl.pallas_call(
        functools.partial(row_kernel, cap),
        out_shape=jax.ShapeDtypeStruct((2, LEAD * ROWS_DEV, TAIL), jnp.float32),
        in_specs=[vmem] * 4,
        out_specs=vmem,
        scratch_shapes=[
            *(pltpu.VMEM(((LEAD + 1) * ROWS_DEV, TAIL), jnp.float32) for _ in range(2)),
            pltpu.VMEM((owners, 128), jnp.int32),
            pltpu.SMEM((owners, 128), jnp.int32),
            pltpu.SemaphoreType.DMA,
        ],
        compiler_params=pltpu.CompilerParams(vmem_limit_bytes=24 * 1024 * 1024),
        name="rows",
    )(received, *row_tables())
    return (
        result.reshape(2, LEAD, ROWS_DEV, TAIL).transpose(0, 2, 1, 3).reshape(2, ROWS_DEV, NG)
    )


def solution(mesh):
    placed = (
        P(("parts", "tile"), None, None),
        P(("parts", "tile"), None, None),
        P(("parts", "tile"), None),
        P(("parts", "tile")),
        P(("parts", "tile")),
        P(("parts", "tile"), None),
        P(("parts", "tile")),
        P(),
    )
    return jax.shard_map(
        shards,
        mesh=mesh,
        in_specs=placed,
        out_specs=P(None, ("parts", "tile"), None),
        check_vma=False,
    )
```

```python
import functools
import math

import jax
import jax.numpy as jnp
import ml_dtypes
import numpy as np
from jax import lax
from jax.experimental import pallas as pl
from jax.experimental.pallas import tpu as pltpu
from jax.sharding import PartitionSpec as P

VROWS = 128
SUB = 32
NG = 32768
ROWS_DEV = 8
LEAD = 256
TAIL = 128
GROUP = 16

SIN_TERMS = (4.442882920, -7.308245680, 3.606354030, -0.846110410, 0.109822040)
COS_TERMS = (1.414213500, -6.978850910, 5.739459580, -1.883552820, 0.310677860)


def halves(table):
    table = np.round(table, 12).astype(np.float32)
    high = table.astype(ml_dtypes.bfloat16)
    low = (table - high.astype(np.float32)).astype(ml_dtypes.bfloat16)
    return high, low


def root(numbers, length):
    angle = 2.0 * np.pi / length * (numbers % length)
    return np.cos(angle), -np.sin(angle)


def complex_left(re, im):
    return np.block([[re, -im], [im, re]])


@functools.cache
def image_tables():
    eight = np.arange(8)
    re, im = root(np.outer(eight, eight), 8)
    left = complex_left(np.kron(np.eye(GROUP), re), np.kron(np.eye(GROUP), im))
    lane = np.arange(128)
    twist = root(np.outer(eight, lane // SUB), SUB)
    four = 8 * np.outer(lane // SUB, lane // SUB) + np.outer(lane % SUB, lane % SUB)
    re, im = root(four, SUB)
    right = complex_left(re, im).T
    row_pos = ((4 * eight[:, None] + lane[None, :] // SUB) - SUB // 2) / SUB
    col_pos = np.broadcast_to((lane[None, :] % SUB - SUB // 2) / SUB, (8, 128))
    taper = (1 - 2 * row_pos**2) * (1 - 2 * col_pos**2) / SUB
    small = np.stack([taper, np.round(twist[0], 12), np.round(twist[1], 12)]).astype(np.float32)
    return (*halves(left), *halves(right), small)


@functools.cache
def row_tables():
    lead, tail = np.arange(LEAD), np.arange(TAIL)
    even = complex_left(*root(np.outer(tail, tail), TAIL))
    odd = complex_left(*root(np.outer(tail, 2 * tail + 1), LEAD))
    twist = np.stack(root(np.outer(lead, tail), NG)) / math.sqrt(NG)
    first = np.stack(halves(even) + halves(odd))
    return first, np.stack(halves(even)), np.round(twist, 12).astype(np.float32)


def split(value):
    high = value.astype(jnp.bfloat16)
    return high, (value - high.astype(jnp.float32)).astype(jnp.bfloat16)


def dot(left, right, transposed=False):
    dims = (((1,), (1 if transposed else 0,)), ((), ()))
    return lax.dot_general(left, right, dims, preferred_element_type=jnp.float32)


def polynomial(terms, z):
    value = z * terms[-1] + terms[-2]
    for term in terms[-3::-1]:
        value = value * z + term
    return value


def cos_sin(turns):
    whole = (turns + 12582912.0) - 12582912.0
    t = turns - whole
    z = t * t
    half_sin = t * polynomial(SIN_TERMS, z)
    half_cos = polynomial(COS_TERMS, z)
    return 1.0 - half_sin * half_sin, half_sin * half_cos


def send_layout(per_device, owners):
    cap = -(-per_device // (owners - SUB // ROWS_DEV + 1))
    tiles = 2 * cap + (2 * cap + 1 + 3) // 4
    return cap, tiles


def image_kernel(
    cap,
    tile_cols,
    *refs,
):
    count_s, beams, args, out, copied = refs[0], refs[1], refs[2:13], refs[13], refs[14:25]
    beam_buf, sky, ranks, sems, arg_sems = refs[25:]
    copies = [
        pltpu.make_async_copy(arg, held, arg_sems.at[k])
        for k, (arg, held) in enumerate(zip(args, copied))
    ]
    for copy in copies:
        copy.start()
    owner_s, row_s, col_s, station_s, vis, coords = copied[:6]
    left_hi, left_lo, right_hi, right_lo, small = copied[6:]
    per_device = vis.shape[0] // 2
    owners = out.shape[0]
    out[...] = jnp.zeros_like(out)
    sky[...] = jnp.zeros_like(sky)
    for b in range(owners):
        ranks[b] = 0
    copies[3].wait()
    live = count_s[0]
    groups = (live + GROUP - 1) >> (GROUP.bit_length() - 1)

    def fetch_beams(g):
        for j in range(GROUP):
            n = jnp.minimum(g, per_device // GROUP - 1) * GROUP + j
            for side in range(2):
                pltpu.make_async_copy(
                    beams.at[station_s[side, n]],
                    beam_buf.at[2 * (g * GROUP + j) + side],
                    sems.at[g],
                ).start()

    def await_beams(g):
        waited = beam_buf.at[pl.ds(g * 2 * GROUP, 2 * GROUP)]
        pltpu.make_async_copy(beams.at[pl.ds(0, 2 * GROUP)], waited, sems.at[g]).wait()

    for g in range(2):
        fetch_beams(g)
    copies[4].wait()
    copies[5].wait()
    copies[10].wait()
    taper = small[0]
    twist_re = jnp.concatenate([small[1]] * GROUP, axis=0)
    twist_im = jnp.concatenate([small[2]] * GROUP, axis=0)
    number = lax.broadcasted_iota(jnp.int32, (SUB, VROWS), 0)
    l_row = (4 * (number % 8) + number // 8 - SUB // 2).astype(jnp.float32) / SUB
    l_col = (number - SUB // 2).astype(jnp.float32) / SUB
    d_row = l_row * l_row
    d_col = l_col * l_col
    sublane = lax.broadcasted_iota(jnp.int32, (8, 128), 0)
    lane = lax.broadcasted_iota(jnp.int32, (8, 128), 1)
    lane_group = lane // SUB

    def images(g, first=False):
        for quad in range(GROUP // 4):
            x_hi, x_lo, columns = [], [], []
            for j in range(4):
                n = g * GROUP + quad * 4 + j
                u = coords[0, pl.ds(n, 1), :]
                v = coords[1, pl.ds(n, 1), :]
                w = coords[2, pl.ds(n, 1), :]
                vis_re = vis[pl.ds(2 * n, 1), :]
                vis_im = vis[pl.ds(2 * n + 1, 1), :]
                cos_row, sin_row = cos_sin(u * l_row + w * d_row)
                cos_col, sin_col = cos_sin(v * l_col + w * d_col)
                x = jnp.concatenate(
                    [
                        vis_re * cos_row - vis_im * sin_row,
                        vis_re * sin_row + vis_im * cos_row,
                    ],
                    axis=1,
                )
                hi, lo = split(x)
                x_hi.append(hi)
                x_lo.append(lo)
                columns.append(split(cos_col) + split(sin_col))
            c_hi, c_lo, s_hi, s_lo = zip(*columns)

            def matrix(c, s):
                real = [jnp.concatenate([a, -b], axis=1) for a, b in zip(c, s)]
                imag = [jnp.concatenate([b, a], axis=1) for a, b in zip(c, s)]
                return jnp.concatenate(real + imag, axis=0)

            lhs = jnp.concatenate(x_hi + x_lo, axis=0)
            both = dot(lhs, matrix(c_hi, s_hi), True)
            sums = both[:128] + both[128:] + dot(lhs[:128], matrix(c_lo, s_lo), True)
            if first and quad == 0:
                await_beams(g)
            for j in range(4):
                n = g * GROUP + quad * 4 + j
                flat = []
                for c in range(2):
                    value = None
                    for i in range(4):
                        piece = sums[32 * j + 8 * i : 32 * j + 8 * i + 8, 128 * c : 128 * c + 128]
                        if i != j:
                            piece = pltpu.roll(piece, (SUB * (i - j)) % 128, 1)
                        value = piece if value is None else jnp.where(lane_group == i, piece, value)
                    flat.append(value)
                one_re = beam_buf[2 * n, pl.ds(0, 8, stride=2), :]
                one_im = beam_buf[2 * n, pl.ds(1, 8, stride=2), :]
                two_re = beam_buf[2 * n + 1, pl.ds(0, 8, stride=2), :]
                two_im = beam_buf[2 * n + 1, pl.ds(1, 8, stride=2), :]
                beam_re = taper * (one_re * two_re + one_im * two_im)
                beam_im = taper * (one_im * two_re - one_re * two_im)
                sky_re = beam_re * flat[0] - beam_im * flat[1]
                sky_im = beam_re * flat[1] + beam_im * flat[0]
                in_use = n < live
                place = (quad * 4 + j) * 8
                sky[g & 1, place : place + 8, :] = jnp.where(in_use, sky_re, 0.0)
                sky[g & 1, place + 8 * GROUP : place + 8 * GROUP + 8, :] = jnp.where(in_use, sky_im, 0.0)

    label_tile = 2 * cap + (2 * cap) // 4
    label_lane = SUB * ((2 * cap) % 4)

    def cells(g):
        hi, lo = split(sky[g & 1])
        left = jnp.concatenate([left_hi[...], left_lo[...], left_hi[...]], axis=1)
        z = dot(left, jnp.concatenate([hi, hi, lo], axis=0))
        z_re, z_im = z[: 8 * GROUP], z[8 * GROUP :]
        y_re = z_re * twist_re - z_im * twist_im
        y_im = z_re * twist_im + z_im * twist_re
        hi, lo = split(jnp.concatenate([y_re, y_im], axis=1))
        right = jnp.concatenate([right_hi[...], right_hi[...], right_lo[...]], axis=0)
        result = dot(jnp.concatenate([hi, lo, hi], axis=1), right)
        for j in range(GROUP):
            n = g * GROUP + j
            band = row_s[n] >> 3
            shift = row_s[n] & 7
            rank = ranks[band]
            ranks[band] = rank + 1
            late = sublane < shift
            last = jnp.minimum(band + 4, owners - 1)
            for c in range(2):
                value = result[8 * j : 8 * j + 8, 128 * c : 128 * c + 128]
                value = pltpu.roll(value, shift, 0)
                next_value = pltpu.roll(value, SUB, 1)
                spread = jnp.where(late, jnp.where(lane_group == 0, 0.0, next_value), value)
                tile = 2 * rank + c
                for o in range(4):
                    pltpu.store(out.at[band + o, tile], spread, mask=lane_group == o)
                part = tile & 3
                tail = pltpu.roll(value, SUB * (part + 1), 1)
                pltpu.store(
                    out.at[last, 2 * cap + (tile >> 2)], tail, mask=late & (lane_group == part)
                )
            column = jnp.full((8, 128), owner_s[n] * tile_cols + col_s[n], jnp.float32)
            for o in range(5):
                here = (sublane == 0) & (lane == label_lane + o * cap + rank)
                if o == 4:
                    here = here & (sublane < shift)
                target = last if o == 4 else band + o
                pltpu.store(out.at[target, label_tile], column, mask=here)

    images(0, True)
    for copy in copies[6:10] + copies[:3]:
        copy.wait()

    @pl.loop(1, groups)
    def _(g):
        await_beams(g)
        fetch_beams(g + 1)
        cells(g - 1)
        images(g)

    cells(groups - 1)
    await_beams(groups)


def row_kernel(
    cap,
    received,
    first,
    second,
    twist,
    out,
    *scratch,
):
    grids, (label_v, label_s, sem) = scratch[:2], scratch[2:]
    sources = received.shape[0]
    label_tile = 2 * cap + (2 * cap) // 4
    label_lane = SUB * ((2 * cap) % 4)
    label_v[...] = received[:, label_tile, 0, :].astype(jnp.int32)
    copy = pltpu.make_async_copy(label_v, label_s, sem)
    copy.start()
    for grid in grids:
        grid[...] = jnp.zeros_like(grid)
    lane = lax.broadcasted_iota(jnp.int32, (8, 128), 1)
    copy.wait()

    @pl.loop(0, sources)
    def _(source):
        for i in range(cap):
            for o in range(5):
                column = label_s[source, label_lane + o * cap + i]
                offset = column & 127
                here = pl.multiple_of((column >> 7) * 8, 8)
                place = lane - offset
                inside = (place >= 0) & (place < SUB)
                beyond = place < SUB - 128
                added = []
                for c in range(2):
                    if o < 4:
                        value, part = received[source, 2 * i + c], o
                    else:
                        value = received[source, 2 * cap + (2 * i + c) // 4]
                        part = (2 * i + c) % 4
                    value = pltpu.roll(value, (offset - SUB * part) & 127, 1)
                    added.append(jnp.where(inside, value, 0.0))
                    added.append(jnp.where(beyond, value, 0.0))
                held = [
                    grids[c][pl.ds(here + 8 * k, 8), :] for c in range(2) for k in range(2)
                ]
                for c in range(2):
                    for k in range(2):
                        grids[c][pl.ds(here + 8 * k, 8), :] = held[2 * c + k] + added[2 * c + k]

    for row in range(0, ROWS_DEV, 2):
        halves_of = []
        for e in range(2):
            rows = [pl.ds(ROWS_DEV * e + row + k, TAIL, stride=2 * ROWS_DEV) for k in range(2)]
            value = jnp.concatenate(
                [jnp.concatenate([grids[c][at, :] for at in rows], axis=1) for c in range(2)], 0
            )
            hi, lo = split(value)
            table_hi, table_lo = first[2 * e], first[2 * e + 1]
            table = jnp.concatenate([table_hi, table_lo, table_hi], axis=1)
            halves_of.append(dot(table, jnp.concatenate([hi, hi, lo], axis=0)))
        low, high = halves_of[0] + halves_of[1], halves_of[0] - halves_of[1]
        for k in range(2):
            b = []
            for e, a in enumerate((low, high)):
                a_re = a[:TAIL, 128 * k : 128 * k + 128]
                a_im = a[TAIL:, 128 * k : 128 * k + 128]
                turn_re = twist[0, TAIL * e : TAIL * e + TAIL]
                turn_im = twist[1, TAIL * e : TAIL * e + TAIL]
                b.append(
                    jnp.concatenate(
                        [a_re * turn_re - a_im * turn_im, a_re * turn_im + a_im * turn_re], axis=1
                    )
                )
            hi, lo = split(jnp.concatenate(b, axis=0))
            table = jnp.concatenate([second[0], second[1], second[0]], axis=1)
            result = dot(table, jnp.concatenate([hi, hi, lo], axis=1), True)
            for c in range(2):
                for h in range(2):
                    out[c, pl.ds(h * 8 + row + k, TAIL, stride=16), :] = result[
                        128 * c : 128 * c + 128, 128 * h : 128 * h + 128
                    ]


def shards(
    visibility, coords, block_owner, block_row, block_col, stations, block_count, beam_terms
):
    owners = lax.axis_size("tile")
    per_device = visibility.shape[0]
    tile_cols = NG // owners
    cap, tiles = send_layout(per_device, owners)
    stations_all = beam_terms.shape[0]
    vmem = pl.BlockSpec(memory_space=pltpu.VMEM)
    beams = (
        beam_terms.reshape(stations_all, 2, 8, 128)
        .transpose(0, 2, 1, 3)
        .reshape(stations_all, 16, 128)
    )
    labels = (
        block_owner.reshape(per_device),
        block_row,
        block_col,
        stations.T,
    )
    values = (
        visibility.reshape(per_device * 2, VROWS),
        coords.transpose(1, 0, 2),
        *image_tables(),
    )
    hbm = pl.BlockSpec(memory_space=pltpu.HBM)
    sent = pl.pallas_call(
        functools.partial(image_kernel, cap, tile_cols),
        out_shape=jax.ShapeDtypeStruct((owners, tiles, 8, 128), jnp.float32),
        in_specs=[pl.BlockSpec(memory_space=pltpu.SMEM)] + [hbm] * (1 + len(labels) + len(values)),
        out_specs=vmem,
        scratch_shapes=[
            *(pltpu.SMEM(label.shape, label.dtype) for label in labels),
            *(pltpu.VMEM(value.shape, value.dtype) for value in values),
            pltpu.VMEM((2 * (per_device + GROUP), 16, 128), jnp.float32),
            pltpu.VMEM((2, 16 * GROUP, 128), jnp.float32),
            pltpu.SMEM((owners,), jnp.int32),
            pltpu.SemaphoreType.DMA((per_device // GROUP + 1,)),
            pltpu.SemaphoreType.DMA((len(labels) + len(values),)),
        ],
        compiler_params=pltpu.CompilerParams(vmem_limit_bytes=24 * 1024 * 1024),
        name="image",
    )(
        block_count,
        *(pltpu.with_memory_space_constraint(x, pltpu.HBM) for x in (beams, *labels, *values)),
    )
    received = lax.all_to_all(sent, "tile", split_axis=0, concat_axis=0, tiled=True)
    result = pl.pallas_call(
        functools.partial(row_kernel, cap),
        out_shape=jax.ShapeDtypeStruct((2, LEAD * ROWS_DEV, TAIL), jnp.float32),
        in_specs=[vmem] * 4,
        out_specs=vmem,
        scratch_shapes=[
            *(pltpu.VMEM(((LEAD + 1) * ROWS_DEV, TAIL), jnp.float32) for _ in range(2)),
            pltpu.VMEM((owners, 128), jnp.int32),
            pltpu.SMEM((owners, 128), jnp.int32),
            pltpu.SemaphoreType.DMA,
        ],
        compiler_params=pltpu.CompilerParams(vmem_limit_bytes=24 * 1024 * 1024),
        name="rows",
    )(received, *row_tables())
    return (
        result.reshape(2, LEAD, ROWS_DEV, TAIL).transpose(0, 2, 1, 3).reshape(2, ROWS_DEV, NG)
    )


def solution(mesh):
    placed = (
        P(("parts", "tile"), None, None),
        P(("parts", "tile"), None, None),
        P(("parts", "tile"), None),
        P(("parts", "tile")),
        P(("parts", "tile")),
        P(("parts", "tile"), None),
        P(("parts", "tile")),
        P(),
    )
    return jax.shard_map(
        shards,
        mesh=mesh,
        in_specs=placed,
        out_specs=P(None, ("parts", "tile"), None),
        check_vma=False,
    )
```

```python
import functools
import math

import jax
import jax.numpy as jnp
import ml_dtypes
import numpy as np
from jax import lax
from jax.experimental import pallas as pl
from jax.experimental.pallas import tpu as pltpu
from jax.sharding import PartitionSpec as P

VROWS = 128
SUB = 32
NG = 32768
ROWS_DEV = 8
LEAD = 256
TAIL = 128
GROUP = 16

SIN_TERMS = (4.442882920, -7.308245680, 3.606354030, -0.846110410, 0.109822040)
COS_TERMS = (1.414213500, -6.978850910, 5.739459580, -1.883552820, 0.310677860)


def halves(table):
    table = np.round(table, 12).astype(np.float32)
    high = table.astype(ml_dtypes.bfloat16)
    low = (table - high.astype(np.float32)).astype(ml_dtypes.bfloat16)
    return high, low


def root(numbers, length):
    angle = 2.0 * np.pi / length * (numbers % length)
    return np.cos(angle), -np.sin(angle)


def complex_left(re, im):
    return np.block([[re, -im], [im, re]])


@functools.cache
def image_tables():
    eight = np.arange(8)
    re, im = root(np.outer(eight, eight), 8)
    left = complex_left(np.kron(np.eye(GROUP), re), np.kron(np.eye(GROUP), im))
    lane = np.arange(128)
    twist = root(np.outer(eight, lane // SUB), SUB)
    four = 8 * np.outer(lane // SUB, lane // SUB) + np.outer(lane % SUB, lane % SUB)
    re, im = root(four, SUB)
    right = complex_left(re, im).T
    row_pos = ((4 * eight[:, None] + lane[None, :] // SUB) - SUB // 2) / SUB
    col_pos = np.broadcast_to((lane[None, :] % SUB - SUB // 2) / SUB, (8, 128))
    taper = (1 - 2 * row_pos**2) * (1 - 2 * col_pos**2) / SUB
    small = np.stack([taper, np.round(twist[0], 12), np.round(twist[1], 12)]).astype(np.float32)
    return (*halves(left), *halves(right), small)


@functools.cache
def row_tables():
    lead, tail = np.arange(LEAD), np.arange(TAIL)
    even = complex_left(*root(np.outer(tail, tail), TAIL))
    odd = complex_left(*root(np.outer(tail, 2 * tail + 1), LEAD))
    twist = np.stack(root(np.outer(lead, tail), NG)) / math.sqrt(NG)
    first = np.stack(halves(even) + halves(odd))
    return first, np.stack(halves(even)), np.round(twist, 12).astype(np.float32)


def split(value):
    high = value.astype(jnp.bfloat16)
    return high, (value - high.astype(jnp.float32)).astype(jnp.bfloat16)


def dot(left, right, transposed=False):
    dims = (((1,), (1 if transposed else 0,)), ((), ()))
    return lax.dot_general(left, right, dims, preferred_element_type=jnp.float32)


def table_times(table_hi, table_lo, hi, lo, transposed=False):
    rows = table_hi.shape[0]
    both = dot(jnp.concatenate([table_hi, table_lo], axis=0), hi, transposed)
    return both[:rows] + both[rows:] + dot(table_hi, lo, transposed)


def times_table(hi, lo, table_hi, table_lo):
    rows = hi.shape[0]
    both = dot(jnp.concatenate([hi, lo], axis=0), table_hi)
    return both[:rows] + both[rows:] + dot(hi, table_lo)


def polynomial(terms, z):
    value = z * terms[-1] + terms[-2]
    for term in terms[-3::-1]:
        value = value * z + term
    return value


def cos_sin(turns):
    whole = (turns + 12582912.0) - 12582912.0
    t = turns - whole
    z = t * t
    half_sin = t * polynomial(SIN_TERMS, z)
    half_cos = polynomial(COS_TERMS, z)
    return 1.0 - half_sin * half_sin, half_sin * half_cos


def send_layout(per_device, owners):
    cap = -(-per_device // (owners - SUB // ROWS_DEV + 1))
    tiles = 2 * cap + (2 * cap + 1 + 3) // 4
    return cap, tiles


def image_kernel(
    cap,
    tile_cols,
    *refs,
):
    count_s, beams, args, out, copied = refs[0], refs[1], refs[2:13], refs[13], refs[14:25]
    beam_buf, sky, ranks, sems, arg_sems = refs[25:]
    copies = [
        pltpu.make_async_copy(arg, held, arg_sems.at[k])
        for k, (arg, held) in enumerate(zip(args, copied))
    ]
    for copy in copies:
        copy.start()
    owner_s, row_s, col_s, station_s, vis, coords = copied[:6]
    left_hi, left_lo, right_hi, right_lo, small = copied[6:]
    per_device = vis.shape[0] // 2
    owners = out.shape[0]
    out[...] = jnp.zeros_like(out)
    sky[...] = jnp.zeros_like(sky)
    for b in range(owners):
        ranks[b] = 0
    copies[3].wait()
    live = count_s[0]
    groups = (live + GROUP - 1) >> (GROUP.bit_length() - 1)

    def fetch_beams(g):
        for j in range(GROUP):
            n = jnp.minimum(g, per_device // GROUP - 1) * GROUP + j
            for side in range(2):
                pltpu.make_async_copy(
                    beams.at[station_s[side, n]],
                    beam_buf.at[2 * (g * GROUP + j) + side],
                    sems.at[g],
                ).start()

    def await_beams(g):
        waited = beam_buf.at[pl.ds(g * 2 * GROUP, 2 * GROUP)]
        pltpu.make_async_copy(beams.at[pl.ds(0, 2 * GROUP)], waited, sems.at[g]).wait()

    for g in range(2):
        fetch_beams(g)
    copies[4].wait()
    copies[5].wait()
    copies[10].wait()
    taper = small[0]
    twist_re = jnp.concatenate([small[1]] * GROUP, axis=0)
    twist_im = jnp.concatenate([small[2]] * GROUP, axis=0)
    number = lax.broadcasted_iota(jnp.int32, (SUB, VROWS), 0)
    l_row = (4 * (number % 8) + number // 8 - SUB // 2).astype(jnp.float32) / SUB
    l_col = (number - SUB // 2).astype(jnp.float32) / SUB
    d_row = l_row * l_row
    d_col = l_col * l_col
    sublane = lax.broadcasted_iota(jnp.int32, (8, 128), 0)
    lane = lax.broadcasted_iota(jnp.int32, (8, 128), 1)
    lane_group = lane // SUB

    def images(g, first=False):
        for quad in range(GROUP // 4):
            x_hi, x_lo, columns = [], [], []
            for j in range(4):
                n = g * GROUP + quad * 4 + j
                u = coords[0, pl.ds(n, 1), :]
                v = coords[1, pl.ds(n, 1), :]
                w = coords[2, pl.ds(n, 1), :]
                vis_re = vis[pl.ds(2 * n, 1), :]
                vis_im = vis[pl.ds(2 * n + 1, 1), :]
                cos_row, sin_row = cos_sin(u * l_row + w * d_row)
                cos_col, sin_col = cos_sin(v * l_col + w * d_col)
                x = jnp.concatenate(
                    [
                        vis_re * cos_row - vis_im * sin_row,
                        vis_re * sin_row + vis_im * cos_row,
                    ],
                    axis=1,
                )
                hi, lo = split(x)
                x_hi.append(hi)
                x_lo.append(lo)
                columns.append(split(cos_col) + split(sin_col))
            c_hi, c_lo, s_hi, s_lo = zip(*columns)

            def matrix(c, s):
                real = [jnp.concatenate([a, -b], axis=1) for a, b in zip(c, s)]
                imag = [jnp.concatenate([b, a], axis=1) for a, b in zip(c, s)]
                return jnp.concatenate(real + imag, axis=0)

            lhs = jnp.concatenate(x_hi + x_lo, axis=0)
            both = dot(lhs, matrix(c_hi, s_hi), True)
            sums = both[:128] + both[128:] + dot(lhs[:128], matrix(c_lo, s_lo), True)
            if first and quad == 0:
                await_beams(g)
            for j in range(4):
                n = g * GROUP + quad * 4 + j
                flat = []
                for c in range(2):
                    value = None
                    for i in range(4):
                        piece = sums[32 * j + 8 * i : 32 * j + 8 * i + 8, 128 * c : 128 * c + 128]
                        if i != j:
                            piece = pltpu.roll(piece, (SUB * (i - j)) % 128, 1)
                        value = piece if value is None else jnp.where(lane_group == i, piece, value)
                    flat.append(value)
                one_re = beam_buf[2 * n, pl.ds(0, 8, stride=2), :]
                one_im = beam_buf[2 * n, pl.ds(1, 8, stride=2), :]
                two_re = beam_buf[2 * n + 1, pl.ds(0, 8, stride=2), :]
                two_im = beam_buf[2 * n + 1, pl.ds(1, 8, stride=2), :]
                beam_re = taper * (one_re * two_re + one_im * two_im)
                beam_im = taper * (one_im * two_re - one_re * two_im)
                sky_re = beam_re * flat[0] - beam_im * flat[1]
                sky_im = beam_re * flat[1] + beam_im * flat[0]
                in_use = n < live
                place = (quad * 4 + j) * 8
                sky[g & 1, place : place + 8, :] = jnp.where(in_use, sky_re, 0.0)
                sky[g & 1, place + 8 * GROUP : place + 8 * GROUP + 8, :] = jnp.where(in_use, sky_im, 0.0)

    label_tile = 2 * cap + (2 * cap) // 4
    label_lane = SUB * ((2 * cap) % 4)

    def cells(g):
        hi, lo = split(sky[g & 1])
        z = table_times(left_hi[...], left_lo[...], hi, lo)
        z_re, z_im = z[: 8 * GROUP], z[8 * GROUP :]
        y_re = z_re * twist_re - z_im * twist_im
        y_im = z_re * twist_im + z_im * twist_re
        hi, lo = split(jnp.concatenate([y_re, y_im], axis=1))
        result = times_table(hi, lo, right_hi[...], right_lo[...])
        for j in range(GROUP):
            n = g * GROUP + j
            band = row_s[n] >> 3
            shift = row_s[n] & 7
            rank = ranks[band]
            ranks[band] = rank + 1
            late = sublane < shift
            last = jnp.minimum(band + 4, owners - 1)
            for c in range(2):
                value = result[8 * j : 8 * j + 8, 128 * c : 128 * c + 128]
                value = pltpu.roll(value, shift, 0)
                next_value = pltpu.roll(value, SUB, 1)
                spread = jnp.where(late, jnp.where(lane_group == 0, 0.0, next_value), value)
                tile = 2 * rank + c
                for o in range(4):
                    pltpu.store(out.at[band + o, tile], spread, mask=lane_group == o)
                part = tile & 3
                tail = pltpu.roll(value, SUB * (part + 1), 1)
                pltpu.store(
                    out.at[last, 2 * cap + (tile >> 2)], tail, mask=late & (lane_group == part)
                )
            column = jnp.full((8, 128), owner_s[n] * tile_cols + col_s[n], jnp.float32)
            for o in range(5):
                here = (sublane == 0) & (lane == label_lane + o * cap + rank)
                if o == 4:
                    here = here & (sublane < shift)
                target = last if o == 4 else band + o
                pltpu.store(out.at[target, label_tile], column, mask=here)

    images(0, True)
    for copy in copies[6:10] + copies[:3]:
        copy.wait()

    @pl.loop(1, groups)
    def _(g):
        await_beams(g)
        fetch_beams(g + 1)
        cells(g - 1)
        images(g)

    cells(groups - 1)
    await_beams(groups)


def row_kernel(
    cap,
    received,
    first,
    second,
    twist,
    out,
    *scratch,
):
    grids, (label_v, label_s, sem) = scratch[:2], scratch[2:]
    sources = received.shape[0]
    label_tile = 2 * cap + (2 * cap) // 4
    label_lane = SUB * ((2 * cap) % 4)
    label_v[...] = received[:, label_tile, 0, :].astype(jnp.int32)
    copy = pltpu.make_async_copy(label_v, label_s, sem)
    copy.start()
    for grid in grids:
        grid[...] = jnp.zeros_like(grid)
    lane = lax.broadcasted_iota(jnp.int32, (8, 128), 1)
    copy.wait()

    @pl.loop(0, sources)
    def _(source):
        for i in range(cap):
            for o in range(5):
                column = label_s[source, label_lane + o * cap + i]
                offset = column & 127
                here = pl.multiple_of((column >> 7) * 8, 8)
                place = lane - offset
                inside = (place >= 0) & (place < SUB)
                beyond = place < SUB - 128
                added = []
                for c in range(2):
                    if o < 4:
                        value, part = received[source, 2 * i + c], o
                    else:
                        value = received[source, 2 * cap + (2 * i + c) // 4]
                        part = (2 * i + c) % 4
                    value = pltpu.roll(value, (offset - SUB * part) & 127, 1)
                    added.append(jnp.where(inside, value, 0.0))
                    added.append(jnp.where(beyond, value, 0.0))
                held = [
                    grids[c][pl.ds(here + 8 * k, 8), :] for c in range(2) for k in range(2)
                ]
                for c in range(2):
                    for k in range(2):
                        grids[c][pl.ds(here + 8 * k, 8), :] = held[2 * c + k] + added[2 * c + k]

    for row in range(0, ROWS_DEV, 2):
        halves_of = []
        for e in range(2):
            rows = [pl.ds(ROWS_DEV * e + row + k, TAIL, stride=2 * ROWS_DEV) for k in range(2)]
            value = jnp.concatenate(
                [jnp.concatenate([grids[c][at, :] for at in rows], axis=1) for c in range(2)], 0
            )
            hi, lo = split(value)
            halves_of.append(table_times(first[2 * e], first[2 * e + 1], hi, lo))
        low, high = halves_of[0] + halves_of[1], halves_of[0] - halves_of[1]
        for k in range(2):
            b = []
            for e, a in enumerate((low, high)):
                a_re = a[:TAIL, 128 * k : 128 * k + 128]
                a_im = a[TAIL:, 128 * k : 128 * k + 128]
                turn_re = twist[0, TAIL * e : TAIL * e + TAIL]
                turn_im = twist[1, TAIL * e : TAIL * e + TAIL]
                b.append(
                    jnp.concatenate(
                        [a_re * turn_re - a_im * turn_im, a_re * turn_im + a_im * turn_re], axis=1
                    )
                )
            hi, lo = split(jnp.concatenate(b, axis=0))
            result = table_times(second[0], second[1], hi, lo, True)
            for c in range(2):
                for h in range(2):
                    out[c, pl.ds(h * 8 + row + k, TAIL, stride=16), :] = result[
                        128 * c : 128 * c + 128, 128 * h : 128 * h + 128
                    ]


def shards(
    visibility, coords, block_owner, block_row, block_col, stations, block_count, beam_terms
):
    owners = lax.axis_size("tile")
    per_device = visibility.shape[0]
    tile_cols = NG // owners
    cap, tiles = send_layout(per_device, owners)
    stations_all = beam_terms.shape[0]
    vmem = pl.BlockSpec(memory_space=pltpu.VMEM)
    beams = (
        beam_terms.reshape(stations_all, 2, 8, 128)
        .transpose(0, 2, 1, 3)
        .reshape(stations_all, 16, 128)
    )
    labels = (
        block_owner.reshape(per_device),
        block_row,
        block_col,
        stations.T,
    )
    values = (
        visibility.reshape(per_device * 2, VROWS),
        coords.transpose(1, 0, 2),
        *image_tables(),
    )
    hbm = pl.BlockSpec(memory_space=pltpu.HBM)
    sent = pl.pallas_call(
        functools.partial(image_kernel, cap, tile_cols),
        out_shape=jax.ShapeDtypeStruct((owners, tiles, 8, 128), jnp.float32),
        in_specs=[pl.BlockSpec(memory_space=pltpu.SMEM)] + [hbm] * (1 + len(labels) + len(values)),
        out_specs=vmem,
        scratch_shapes=[
            *(pltpu.SMEM(label.shape, label.dtype) for label in labels),
            *(pltpu.VMEM(value.shape, value.dtype) for value in values),
            pltpu.VMEM((2 * (per_device + GROUP), 16, 128), jnp.float32),
            pltpu.VMEM((2, 16 * GROUP, 128), jnp.float32),
            pltpu.SMEM((owners,), jnp.int32),
            pltpu.SemaphoreType.DMA((per_device // GROUP + 1,)),
            pltpu.SemaphoreType.DMA((len(labels) + len(values),)),
        ],
        compiler_params=pltpu.CompilerParams(vmem_limit_bytes=24 * 1024 * 1024),
        name="image",
    )(
        block_count,
        *(pltpu.with_memory_space_constraint(x, pltpu.HBM) for x in (beams, *labels, *values)),
    )
    received = lax.all_to_all(sent, "tile", split_axis=0, concat_axis=0, tiled=True)
    result = pl.pallas_call(
        functools.partial(row_kernel, cap),
        out_shape=jax.ShapeDtypeStruct((2, LEAD * ROWS_DEV, TAIL), jnp.float32),
        in_specs=[vmem] * 4,
        out_specs=vmem,
        scratch_shapes=[
            *(pltpu.VMEM(((LEAD + 1) * ROWS_DEV, TAIL), jnp.float32) for _ in range(2)),
            pltpu.VMEM((owners, 128), jnp.int32),
            pltpu.SMEM((owners, 128), jnp.int32),
            pltpu.SemaphoreType.DMA,
        ],
        compiler_params=pltpu.CompilerParams(vmem_limit_bytes=24 * 1024 * 1024),
        name="rows",
    )(received, *row_tables())
    return (
        result.reshape(2, LEAD, ROWS_DEV, TAIL).transpose(0, 2, 1, 3).reshape(2, ROWS_DEV, NG)
    )


def solution(mesh):
    placed = (
        P(("parts", "tile"), None, None),
        P(("parts", "tile"), None, None),
        P(("parts", "tile"), None),
        P(("parts", "tile")),
        P(("parts", "tile")),
        P(("parts", "tile"), None),
        P(("parts", "tile")),
        P(),
    )
    return jax.shard_map(
        shards,
        mesh=mesh,
        in_specs=placed,
        out_specs=P(None, ("parts", "tile"), None),
        check_vma=False,
    )
```

```python
import functools
import math

import jax
import jax.numpy as jnp
import ml_dtypes
import numpy as np
from jax import lax
from jax.experimental import pallas as pl
from jax.experimental.pallas import tpu as pltpu
from jax.sharding import PartitionSpec as P

VROWS = 128
SUB = 32
NG = 32768
ROWS_DEV = 8
LEAD = 256
TAIL = 128
GROUP = 16

SIN_TERMS = (4.442882920, -7.308245680, 3.606354030, -0.846110410, 0.109822040)
COS_TERMS = (1.414213500, -6.978850910, 5.739459580, -1.883552820, 0.310677860)


def halves(table):
    table = np.round(table, 12).astype(np.float32)
    high = table.astype(ml_dtypes.bfloat16)
    low = (table - high.astype(np.float32)).astype(ml_dtypes.bfloat16)
    return high, low


def root(numbers, length):
    angle = 2.0 * np.pi / length * (numbers % length)
    return np.cos(angle), -np.sin(angle)


def complex_left(re, im):
    return np.block([[re, -im], [im, re]])


@functools.cache
def image_tables():
    eight = np.arange(8)
    turn_four = root(np.where(eight < 4, 0, eight - 4), 8)
    turn_two = root(np.where(eight & 2, eight & 1, 0), 4)
    turns = [np.broadcast_to(part[:, None], (8, 128)) for part in turn_four + turn_two]
    lane = np.arange(128)
    twist = root(np.outer(eight, lane // SUB), SUB)
    four = 8 * np.outer(lane // SUB, lane // SUB) + np.outer(lane % SUB, lane % SUB)
    re, im = root(four, SUB)
    right = complex_left(re, im).T
    row_pos = ((4 * eight[:, None] + lane[None, :] // SUB) - SUB // 2) / SUB
    col_pos = np.broadcast_to((lane[None, :] % SUB - SUB // 2) / SUB, (8, 128))
    taper = (1 - 2 * row_pos**2) * (1 - 2 * col_pos**2) / SUB
    small = np.stack([taper, *twist, *turns])
    return (*halves(right), np.round(small, 12).astype(np.float32))


@functools.cache
def row_tables():
    lead, tail = np.arange(LEAD), np.arange(TAIL)
    even = complex_left(*root(np.outer(tail, tail), TAIL))
    odd = complex_left(*root(np.outer(tail, 2 * tail + 1), LEAD))
    twist = np.stack(root(np.outer(lead, tail), NG)) / math.sqrt(NG)
    first = np.stack(halves(even) + halves(odd))
    return first, np.stack(halves(even)), np.round(twist, 12).astype(np.float32)


def split(value):
    high = value.astype(jnp.bfloat16)
    return high, (value - high.astype(jnp.float32)).astype(jnp.bfloat16)


def dot(left, right, transposed=False):
    dims = (((1,), (1 if transposed else 0,)), ((), ()))
    return lax.dot_general(left, right, dims, preferred_element_type=jnp.float32)


def table_times(table_hi, table_lo, hi, lo, transposed=False):
    rows = table_hi.shape[0]
    both = dot(jnp.concatenate([table_hi, table_lo], axis=0), hi, transposed)
    return both[:rows] + both[rows:] + dot(table_hi, lo, transposed)


def times_table(hi, lo, table_hi, table_lo):
    rows = hi.shape[0]
    both = dot(jnp.concatenate([hi, lo], axis=0), table_hi)
    return both[:rows] + both[rows:] + dot(hi, table_lo)


def polynomial(terms, z):
    value = z * terms[-1] + terms[-2]
    for term in terms[-3::-1]:
        value = value * z + term
    return value


def cos_sin(turns):
    whole = (turns + 12582912.0) - 12582912.0
    t = turns - whole
    z = t * t
    half_sin = t * polynomial(SIN_TERMS, z)
    half_cos = polynomial(COS_TERMS, z)
    return 1.0 - half_sin * half_sin, half_sin * half_cos


def send_layout(per_device, owners):
    cap = -(-per_device // (owners - SUB // ROWS_DEV + 1))
    tiles = 2 * cap + (2 * cap + 1 + 3) // 4
    return cap, tiles


def image_kernel(
    cap,
    tile_cols,
    *refs,
):
    count_s, beams, args, out, copied = refs[0], refs[1], refs[2:11], refs[11], refs[12:21]
    beam_buf, sky, ranks, sems, arg_sems = refs[21:]
    copies = [
        pltpu.make_async_copy(arg, held, arg_sems.at[k])
        for k, (arg, held) in enumerate(zip(args, copied))
    ]
    for copy in copies:
        copy.start()
    owner_s, row_s, col_s, station_s, vis, coords = copied[:6]
    right_hi, right_lo, small = copied[6:]
    per_device = vis.shape[0] // 2
    owners = out.shape[0]
    out[...] = jnp.zeros_like(out)
    sky[...] = jnp.zeros_like(sky)
    for b in range(owners):
        ranks[b] = 0
    copies[3].wait()
    live = count_s[0]
    groups = (live + GROUP - 1) >> (GROUP.bit_length() - 1)

    def fetch_beams(g):
        for j in range(GROUP):
            n = jnp.minimum(g, per_device // GROUP - 1) * GROUP + j
            for side in range(2):
                pltpu.make_async_copy(
                    beams.at[station_s[side, n]],
                    beam_buf.at[2 * (g * GROUP + j) + side],
                    sems.at[g],
                ).start()

    def await_beams(g):
        waited = beam_buf.at[pl.ds(g * 2 * GROUP, 2 * GROUP)]
        pltpu.make_async_copy(beams.at[pl.ds(0, 2 * GROUP)], waited, sems.at[g]).wait()

    for g in range(2):
        fetch_beams(g)
    copies[4].wait()
    copies[5].wait()
    copies[8].wait()
    taper = small[0]
    number = lax.broadcasted_iota(jnp.int32, (SUB, VROWS), 0)
    l_row = (4 * (number % 8) + number // 8 - SUB // 2).astype(jnp.float32) / SUB
    l_col = (number - SUB // 2).astype(jnp.float32) / SUB
    d_row = l_row * l_row
    d_col = l_col * l_col
    sublane = lax.broadcasted_iota(jnp.int32, (8, 128), 0)
    lane = lax.broadcasted_iota(jnp.int32, (8, 128), 1)
    lane_group = lane // SUB

    def partner(value, bit):
        if bit == 4:
            return pltpu.roll(value, 4, 0)
        return jnp.where((sublane & bit) == 0, pltpu.roll(value, 8 - bit, 0), pltpu.roll(value, bit, 0))

    def turned(pair, re, im):
        return pair[0] * re - pair[1] * im, pair[0] * im + pair[1] * re

    signs = {bit: jnp.where((sublane & bit) == 0, 1.0, -1.0) for bit in (4, 2, 1)}

    def eight_points(pair):
        for bit, turn in ((4, 3), (2, 5), (1, None)):
            pair = tuple(partner(part, bit) + signs[bit] * part for part in pair)
            if turn is not None:
                pair = turned(pair, small[turn], small[turn + 1])
        up = (sublane == 1) | (sublane == 3)
        down = (sublane == 4) | (sublane == 6)
        return tuple(
            jnp.where(up, pltpu.roll(part, 5, 0), jnp.where(down, pltpu.roll(part, 3, 0), part))
            for part in pair
        )

    def images(g, first=False):
        for quad in range(GROUP // 4):
            x_hi, x_lo, columns = [], [], []
            for j in range(4):
                n = g * GROUP + quad * 4 + j
                u = coords[0, pl.ds(n, 1), :]
                v = coords[1, pl.ds(n, 1), :]
                w = coords[2, pl.ds(n, 1), :]
                vis_re = vis[pl.ds(2 * n, 1), :]
                vis_im = vis[pl.ds(2 * n + 1, 1), :]
                cos_row, sin_row = cos_sin(u * l_row + w * d_row)
                cos_col, sin_col = cos_sin(v * l_col + w * d_col)
                x = jnp.concatenate(
                    [
                        vis_re * cos_row - vis_im * sin_row,
                        vis_re * sin_row + vis_im * cos_row,
                    ],
                    axis=1,
                )
                hi, lo = split(x)
                x_hi.append(hi)
                x_lo.append(lo)
                columns.append(split(cos_col) + split(sin_col))
            c_hi, c_lo, s_hi, s_lo = zip(*columns)

            def matrix(c, s):
                real = [jnp.concatenate([a, -b], axis=1) for a, b in zip(c, s)]
                imag = [jnp.concatenate([b, a], axis=1) for a, b in zip(c, s)]
                return jnp.concatenate(real + imag, axis=0)

            lhs = jnp.concatenate(x_hi + x_lo, axis=0)
            both = dot(lhs, matrix(c_hi, s_hi), True)
            sums = both[:128] + both[128:] + dot(lhs[:128], matrix(c_lo, s_lo), True)
            if first and quad == 0:
                await_beams(g)
            for j in range(4):
                n = g * GROUP + quad * 4 + j
                flat = []
                for c in range(2):
                    value = None
                    for i in range(4):
                        piece = sums[32 * j + 8 * i : 32 * j + 8 * i + 8, 128 * c : 128 * c + 128]
                        if i != j:
                            piece = pltpu.roll(piece, (SUB * (i - j)) % 128, 1)
                        value = piece if value is None else jnp.where(lane_group == i, piece, value)
                    flat.append(value)
                one_re = beam_buf[2 * n, pl.ds(0, 8, stride=2), :]
                one_im = beam_buf[2 * n, pl.ds(1, 8, stride=2), :]
                two_re = beam_buf[2 * n + 1, pl.ds(0, 8, stride=2), :]
                two_im = beam_buf[2 * n + 1, pl.ds(1, 8, stride=2), :]
                beam_re = taper * (one_re * two_re + one_im * two_im)
                beam_im = taper * (one_im * two_re - one_re * two_im)
                sky_re = beam_re * flat[0] - beam_im * flat[1]
                sky_im = beam_re * flat[1] + beam_im * flat[0]
                in_use = n < live
                pair = (jnp.where(in_use, sky_re, 0.0), jnp.where(in_use, sky_im, 0.0))
                pair = turned(eight_points(pair), small[1], small[2])
                place = (quad * 4 + j) * 8
                for c in range(2):
                    sky[g & 1, place : place + 8, 128 * c : 128 * c + 128] = pair[c]

    label_tile = 2 * cap + (2 * cap) // 4
    label_lane = SUB * ((2 * cap) % 4)

    def cells(g):
        hi, lo = split(sky[g & 1])
        result = times_table(hi, lo, right_hi[...], right_lo[...])
        for j in range(GROUP):
            n = g * GROUP + j
            band = row_s[n] >> 3
            shift = row_s[n] & 7
            rank = ranks[band]
            ranks[band] = rank + 1
            late = sublane < shift
            last = jnp.minimum(band + 4, owners - 1)
            for c in range(2):
                value = result[8 * j : 8 * j + 8, 128 * c : 128 * c + 128]
                value = pltpu.roll(value, shift, 0)
                next_value = pltpu.roll(value, SUB, 1)
                spread = jnp.where(late, jnp.where(lane_group == 0, 0.0, next_value), value)
                tile = 2 * rank + c
                for o in range(4):
                    pltpu.store(out.at[band + o, tile], spread, mask=lane_group == o)
                part = tile & 3
                tail = pltpu.roll(value, SUB * (part + 1), 1)
                pltpu.store(
                    out.at[last, 2 * cap + (tile >> 2)], tail, mask=late & (lane_group == part)
                )
            column = jnp.full((8, 128), owner_s[n] * tile_cols + col_s[n], jnp.float32)
            for o in range(5):
                here = (sublane == 0) & (lane == label_lane + o * cap + rank)
                if o == 4:
                    here = here & (sublane < shift)
                target = last if o == 4 else band + o
                pltpu.store(out.at[target, label_tile], column, mask=here)

    images(0, True)
    for copy in copies[6:8] + copies[:3]:
        copy.wait()

    @pl.loop(1, groups)
    def _(g):
        await_beams(g)
        fetch_beams(g + 1)
        cells(g - 1)
        images(g)

    cells(groups - 1)
    await_beams(groups)


def row_kernel(
    cap,
    received,
    first,
    second,
    twist,
    out,
    *scratch,
):
    grids, (label_v, label_s, sem, middle, held, out_sems) = scratch[:2], scratch[2:]
    sources = received.shape[0]
    label_tile = 2 * cap + (2 * cap) // 4
    label_lane = SUB * ((2 * cap) % 4)
    label_v[...] = received[:, label_tile, 0, :].astype(jnp.int32)
    copy = pltpu.make_async_copy(label_v, label_s, sem)
    copy.start()
    for grid in grids:
        grid[...] = jnp.zeros_like(grid)
    lane = lax.broadcasted_iota(jnp.int32, (8, 128), 1)
    copy.wait()

    @pl.loop(0, sources)
    def _(source):
        for i in range(cap):
            for o in range(5):
                column = label_s[source, label_lane + o * cap + i]
                offset = column & 127
                here = pl.multiple_of((column >> 7) * 8, 8)
                place = lane - offset
                inside = (place >= 0) & (place < SUB)
                beyond = place < SUB - 128
                added = []
                for c in range(2):
                    if o < 4:
                        value, part = received[source, 2 * i + c], o
                    else:
                        value = received[source, 2 * cap + (2 * i + c) // 4]
                        part = (2 * i + c) % 4
                    value = pltpu.roll(value, (offset - SUB * part) & 127, 1)
                    added.append(jnp.where(inside, value, 0.0))
                    added.append(jnp.where(beyond, value, 0.0))
                before = [
                    grids[c][pl.ds(here + 8 * k, 8), :] for c in range(2) for k in range(2)
                ]
                for c in range(2):
                    for k in range(2):
                        grids[c][pl.ds(here + 8 * k, 8), :] = before[2 * c + k] + added[2 * c + k]

    for pair in range(ROWS_DEV // 2):
        halves_of = []
        for e in range(2):
            rows = [
                pl.ds(ROWS_DEV * e + 2 * pair + k, TAIL, stride=2 * ROWS_DEV) for k in range(2)
            ]
            value = jnp.concatenate(
                [jnp.concatenate([grids[c][at, :] for at in rows], axis=1) for c in range(2)], 0
            )
            hi, lo = split(value)
            halves_of.append(table_times(first[2 * e], first[2 * e + 1], hi, lo))
        for h, a in enumerate((halves_of[0] + halves_of[1], halves_of[0] - halves_of[1])):
            turn_re = twist[0, TAIL * h : TAIL * h + TAIL]
            turn_im = twist[1, TAIL * h : TAIL * h + TAIL]
            for k in range(2):
                a_re = a[:TAIL, 128 * k : 128 * k + 128]
                a_im = a[TAIL:, 128 * k : 128 * k + 128]
                b = jnp.concatenate(
                    [a_re * turn_re - a_im * turn_im, a_re * turn_im + a_im * turn_re], axis=1
                )
                for part, value in enumerate(split(b)):
                    middle[h, pair, part, TAIL * k : TAIL * k + TAIL, :] = value

    copies = []
    for h in range(2):
        for pair in range(ROWS_DEV // 2):
            result = table_times(
                second[0], second[1], middle[h, pair, 0], middle[h, pair, 1], True
            )
            for c in range(2):
                for k in range(2):
                    held[h, c, pl.ds(2 * pair + k, TAIL, stride=ROWS_DEV), :] = result[
                        128 * c : 128 * c + 128, 128 * k : 128 * k + 128
                    ]
        for c in range(2):
            copies.append(
                pltpu.make_async_copy(
                    held.at[h, c].reshape(TAIL, ROWS_DEV, TAIL),
                    out.at[c, :, h],
                    out_sems.at[h, c],
                )
            )
            copies[-1].start()
    for copy in copies:
        copy.wait()


def shards(
    visibility, coords, block_owner, block_row, block_col, stations, block_count, beam_terms
):
    owners = lax.axis_size("tile")
    per_device = visibility.shape[0]
    tile_cols = NG // owners
    cap, tiles = send_layout(per_device, owners)
    stations_all = beam_terms.shape[0]
    vmem = pl.BlockSpec(memory_space=pltpu.VMEM)
    beams = (
        beam_terms.reshape(stations_all, 2, 8, 128)
        .transpose(0, 2, 1, 3)
        .reshape(stations_all, 16, 128)
    )
    labels = (
        block_owner.reshape(per_device),
        block_row,
        block_col,
        stations.T,
    )
    values = (
        visibility.reshape(per_device * 2, VROWS),
        coords.transpose(1, 0, 2),
        *image_tables(),
    )
    hbm = pl.BlockSpec(memory_space=pltpu.HBM)
    sent = pl.pallas_call(
        functools.partial(image_kernel, cap, tile_cols),
        out_shape=jax.ShapeDtypeStruct((owners, tiles, 8, 128), jnp.float32),
        in_specs=[pl.BlockSpec(memory_space=pltpu.SMEM)] + [hbm] * (1 + len(labels) + len(values)),
        out_specs=vmem,
        scratch_shapes=[
            *(pltpu.SMEM(label.shape, label.dtype) for label in labels),
            *(pltpu.VMEM(value.shape, value.dtype) for value in values),
            pltpu.VMEM((2 * (per_device + GROUP), 16, 128), jnp.float32),
            pltpu.VMEM((2, 8 * GROUP, 256), jnp.float32),
            pltpu.SMEM((owners,), jnp.int32),
            pltpu.SemaphoreType.DMA((per_device // GROUP + 1,)),
            pltpu.SemaphoreType.DMA((len(labels) + len(values),)),
        ],
        compiler_params=pltpu.CompilerParams(vmem_limit_bytes=24 * 1024 * 1024),
        name="image",
    )(
        block_count,
        *(pltpu.with_memory_space_constraint(x, pltpu.HBM) for x in (beams, *labels, *values)),
    )
    received = lax.all_to_all(sent, "tile", split_axis=0, concat_axis=0, tiled=True)
    result = pl.pallas_call(
        functools.partial(row_kernel, cap),
        out_shape=jax.ShapeDtypeStruct((2, TAIL, 2, ROWS_DEV, TAIL), jnp.float32),
        in_specs=[vmem] * 4,
        out_specs=pl.BlockSpec(memory_space=pl.ANY),
        scratch_shapes=[
            *(pltpu.VMEM(((LEAD + 1) * ROWS_DEV, TAIL), jnp.float32) for _ in range(2)),
            pltpu.VMEM((owners, 128), jnp.int32),
            pltpu.SMEM((owners, 128), jnp.int32),
            pltpu.SemaphoreType.DMA,
            pltpu.VMEM((2, ROWS_DEV // 2, 2, 2 * TAIL, 2 * TAIL), jnp.bfloat16),
            pltpu.VMEM((2, 2, TAIL * ROWS_DEV, TAIL), jnp.float32),
            pltpu.SemaphoreType.DMA((2, 2)),
        ],
        compiler_params=pltpu.CompilerParams(vmem_limit_bytes=24 * 1024 * 1024),
        name="rows",
    )(received, *row_tables())
    return (
        result.reshape(2, LEAD, ROWS_DEV, TAIL).transpose(0, 2, 1, 3).reshape(2, ROWS_DEV, NG)
    )


def solution(mesh):
    placed = (
        P(("parts", "tile"), None, None),
        P(("parts", "tile"), None, None),
        P(("parts", "tile"), None),
        P(("parts", "tile")),
        P(("parts", "tile")),
        P(("parts", "tile"), None),
        P(("parts", "tile")),
        P(),
    )
    return jax.shard_map(
        shards,
        mesh=mesh,
        in_specs=placed,
        out_specs=P(None, ("parts", "tile"), None),
        check_vma=False,
    )
```

```python
import functools
import math

import jax
import jax.numpy as jnp
import ml_dtypes
import numpy as np
from jax import lax
from jax.experimental import pallas as pl
from jax.experimental.pallas import tpu as pltpu
from jax.sharding import PartitionSpec as P

VROWS = 128
SUB = 32
NG = 32768
ROWS_DEV = 8
LEAD = 256
TAIL = 128
GROUP = 16

SIN_TERMS = (4.442882920, -7.308245680, 3.606354030, -0.846110410, 0.109822040)
COS_TERMS = (1.414213500, -6.978850910, 5.739459580, -1.883552820, 0.310677860)


def halves(table):
    table = np.round(table, 12).astype(np.float32)
    high = table.astype(ml_dtypes.bfloat16)
    low = (table - high.astype(np.float32)).astype(ml_dtypes.bfloat16)
    return high, low


def root(numbers, length):
    angle = 2.0 * np.pi / length * (numbers % length)
    return np.cos(angle), -np.sin(angle)


def complex_left(re, im):
    return np.block([[re, -im], [im, re]])


@functools.cache
def image_tables():
    eight = np.arange(8)
    re, im = root(np.outer(eight, eight), 8)
    left = complex_left(np.kron(np.eye(GROUP), re), np.kron(np.eye(GROUP), im))
    lane = np.arange(128)
    twist = root(np.outer(eight, lane // SUB), SUB)
    four = 8 * np.outer(lane // SUB, lane // SUB) + np.outer(lane % SUB, lane % SUB)
    re, im = root(four, SUB)
    right = complex_left(re, im).T
    row_pos = ((4 * eight[:, None] + lane[None, :] // SUB) - SUB // 2) / SUB
    col_pos = np.broadcast_to((lane[None, :] % SUB - SUB // 2) / SUB, (8, 128))
    taper = (1 - 2 * row_pos**2) * (1 - 2 * col_pos**2) / SUB
    small = np.stack([taper, np.round(twist[0], 12), np.round(twist[1], 12)]).astype(np.float32)
    return (*halves(left), *halves(right), small)


@functools.cache
def row_tables():
    lead, tail = np.arange(LEAD), np.arange(TAIL)
    even = complex_left(*root(np.outer(tail, tail), TAIL))
    odd = complex_left(*root(np.outer(tail, 2 * tail + 1), LEAD))
    twist = np.stack(root(np.outer(lead, tail), NG)) / math.sqrt(NG)
    first = np.stack(halves(even) + halves(odd))
    return first, np.stack(halves(even)), np.round(twist, 12).astype(np.float32)


def split(value):
    high = value.astype(jnp.bfloat16)
    return high, (value - high.astype(jnp.float32)).astype(jnp.bfloat16)


def dot(left, right, transposed=False):
    dims = (((1,), (1 if transposed else 0,)), ((), ()))
    return lax.dot_general(left, right, dims, preferred_element_type=jnp.float32)


def table_times(table_hi, table_lo, hi, lo, transposed=False):
    rows = table_hi.shape[0]
    both = dot(jnp.concatenate([table_hi, table_lo], axis=0), hi, transposed)
    return both[:rows] + both[rows:] + dot(table_hi, lo, transposed)


def times_table(hi, lo, table_hi, table_lo):
    rows = hi.shape[0]
    both = dot(jnp.concatenate([hi, lo], axis=0), table_hi)
    return both[:rows] + both[rows:] + dot(hi, table_lo)


def polynomial(terms, z):
    value = z * terms[-1] + terms[-2]
    for term in terms[-3::-1]:
        value = value * z + term
    return value


def cos_sin(turns):
    whole = (turns + 12582912.0) - 12582912.0
    t = turns - whole
    z = t * t
    half_sin = t * polynomial(SIN_TERMS, z)
    half_cos = polynomial(COS_TERMS, z)
    return 1.0 - half_sin * half_sin, half_sin * half_cos


def send_layout(per_device, owners):
    cap = -(-per_device // (owners - SUB // ROWS_DEV + 1))
    tiles = 2 * cap + (2 * cap + 1 + 3) // 4
    return cap, tiles


def image_kernel(
    cap,
    tile_cols,
    *refs,
):
    count_s, beams, args, out, copied = refs[0], refs[1], refs[2:13], refs[13], refs[14:25]
    beam_buf, sky, ranks, sems, arg_sems = refs[25:]
    copies = [
        pltpu.make_async_copy(arg, held, arg_sems.at[k])
        for k, (arg, held) in enumerate(zip(args, copied))
    ]
    for copy in copies:
        copy.start()
    owner_s, row_s, col_s, station_s, vis, coords = copied[:6]
    left_hi, left_lo, right_hi, right_lo, small = copied[6:]
    per_device = vis.shape[0] // 2
    owners = out.shape[0]
    out[...] = jnp.zeros_like(out)
    sky[...] = jnp.zeros_like(sky)
    for b in range(owners):
        ranks[b] = 0
    copies[3].wait()
    copies[1].wait()
    live = count_s[0]
    groups = (live + GROUP - 1) >> (GROUP.bit_length() - 1)

    def fetch_beams(g):
        for j in range(GROUP):
            n = jnp.minimum(g, per_device // GROUP - 1) * GROUP + j
            for side in range(2):
                pltpu.make_async_copy(
                    beams.at[station_s[side, n]],
                    beam_buf.at[2 * (g * GROUP + j) + side],
                    sems.at[g],
                ).start()

    def await_beams(g):
        waited = beam_buf.at[pl.ds(g * 2 * GROUP, 2 * GROUP)]
        pltpu.make_async_copy(beams.at[pl.ds(0, 2 * GROUP)], waited, sems.at[g]).wait()

    for g in range(2):
        fetch_beams(g)
    copies[4].wait()
    copies[5].wait()
    copies[10].wait()
    taper = small[0]
    twist_re = jnp.concatenate([small[1]] * GROUP, axis=0)
    twist_im = jnp.concatenate([small[2]] * GROUP, axis=0)
    number = lax.broadcasted_iota(jnp.int32, (SUB, VROWS), 0)
    l_row = (4 * (number % 8) + number // 8 - SUB // 2).astype(jnp.float32) / SUB
    l_col = (number - SUB // 2).astype(jnp.float32) / SUB
    d_row = l_row * l_row
    d_col = l_col * l_col
    sublane = lax.broadcasted_iota(jnp.int32, (8, 128), 0)
    lane = lax.broadcasted_iota(jnp.int32, (8, 128), 1)
    lane_group = lane // SUB

    def images(g, first=False):
        for quad in range(GROUP // 4):
            x_hi, x_lo, columns = [], [], []
            for j in range(4):
                n = g * GROUP + quad * 4 + j
                shift = row_s[n] & 7
                sign = (1 - 2 * (shift & 1)).astype(jnp.float32)
                u = coords[0, pl.ds(n, 1), :] + shift.astype(jnp.float32)
                v = coords[1, pl.ds(n, 1), :]
                w = coords[2, pl.ds(n, 1), :]
                vis_re = vis[pl.ds(2 * n, 1), :] * sign
                vis_im = vis[pl.ds(2 * n + 1, 1), :] * sign
                cos_row, sin_row = cos_sin(u * l_row + w * d_row)
                cos_col, sin_col = cos_sin(v * l_col + w * d_col)
                x = jnp.concatenate(
                    [
                        vis_re * cos_row - vis_im * sin_row,
                        vis_re * sin_row + vis_im * cos_row,
                    ],
                    axis=1,
                )
                hi, lo = split(x)
                x_hi.append(hi)
                x_lo.append(lo)
                columns.append(split(cos_col) + split(sin_col))
            c_hi, c_lo, s_hi, s_lo = zip(*columns)

            def matrix(c, s):
                real = [jnp.concatenate([a, -b], axis=1) for a, b in zip(c, s)]
                imag = [jnp.concatenate([b, a], axis=1) for a, b in zip(c, s)]
                return jnp.concatenate(real + imag, axis=0)

            lhs = jnp.concatenate(x_hi + x_lo, axis=0)
            both = dot(lhs, matrix(c_hi, s_hi), True)
            sums = both[:128] + both[128:] + dot(lhs[:128], matrix(c_lo, s_lo), True)
            if first and quad == 0:
                await_beams(g)
            flat = []
            for c in range(2):
                rolled = []
                for delta in range(4):
                    value = None
                    for j in range(4):
                        row = 32 * j + 8 * ((j + delta) % 4)
                        piece = sums[row : row + 8, 128 * c : 128 * c + 128]
                        value = piece if j == 0 else jnp.where(lane_group == j, piece, value)
                    rolled.append(pltpu.roll(value, SUB * delta, 1) if delta else value)
                for j in range(4):
                    value = rolled[-j % 4]
                    for i in range(1, 4):
                        value = jnp.where(lane_group == i, rolled[(i - j) % 4], value)
                    flat.append(value)
            for j in range(4):
                n = g * GROUP + quad * 4 + j
                one_re = beam_buf[2 * n, pl.ds(0, 8, stride=2), :]
                one_im = beam_buf[2 * n, pl.ds(1, 8, stride=2), :]
                two_re = beam_buf[2 * n + 1, pl.ds(0, 8, stride=2), :]
                two_im = beam_buf[2 * n + 1, pl.ds(1, 8, stride=2), :]
                beam_re = taper * (one_re * two_re + one_im * two_im)
                beam_im = taper * (one_im * two_re - one_re * two_im)
                sky_re = beam_re * flat[j] - beam_im * flat[4 + j]
                sky_im = beam_re * flat[4 + j] + beam_im * flat[j]
                in_use = n < live
                place = (quad * 4 + j) * 8
                sky[g & 1, place : place + 8, :] = jnp.where(in_use, sky_re, 0.0)
                sky[g & 1, place + 8 * GROUP : place + 8 * GROUP + 8, :] = jnp.where(in_use, sky_im, 0.0)

    label_tile = 2 * cap + (2 * cap) // 4
    label_lane = SUB * ((2 * cap) % 4)

    def cells(g):
        hi, lo = split(sky[g & 1])
        z = table_times(left_hi[...], left_lo[...], hi, lo)
        z_re, z_im = z[: 8 * GROUP], z[8 * GROUP :]
        y_re = z_re * twist_re - z_im * twist_im
        y_im = z_re * twist_im + z_im * twist_re
        hi, lo = split(jnp.concatenate([y_re, y_im], axis=1))
        result = times_table(hi, lo, right_hi[...], right_lo[...])
        for j in range(GROUP):
            n = g * GROUP + j
            band = row_s[n] >> 3
            shift = row_s[n] & 7
            rank = ranks[band]
            ranks[band] = rank + 1
            late = sublane < shift
            last = jnp.minimum(band + 4, owners - 1)
            for c in range(2):
                value = result[8 * j : 8 * j + 8, 128 * c : 128 * c + 128]
                spread = jnp.where(late & (lane_group == 0), 0.0, value)
                tile = 2 * rank + c
                for o in range(4):
                    pltpu.store(out.at[band + o, tile], spread, mask=lane_group == o)
                part = tile & 3
                tail = pltpu.roll(value, SUB * part, 1)
                pltpu.store(
                    out.at[last, 2 * cap + (tile >> 2)], tail, mask=late & (lane_group == part)
                )
            column = jnp.full((8, 128), owner_s[n] * tile_cols + col_s[n], jnp.float32)
            for o in range(5):
                here = (sublane == 0) & (lane == label_lane + o * cap + rank)
                if o == 4:
                    here = here & (sublane < shift)
                target = last if o == 4 else band + o
                pltpu.store(out.at[target, label_tile], column, mask=here)

    images(0, True)
    for copy in copies[6:10] + [copies[0], copies[2]]:
        copy.wait()

    @pl.loop(1, groups)
    def _(g):
        await_beams(g)
        fetch_beams(g + 1)
        cells(g - 1)
        images(g)

    cells(groups - 1)
    await_beams(groups)


def row_kernel(
    cap,
    received,
    first,
    second,
    twist,
    out,
    *scratch,
):
    grids, (label_v, label_s, sem, middle, held, out_sems) = scratch[:2], scratch[2:]
    sources = received.shape[0]
    label_tile = 2 * cap + (2 * cap) // 4
    label_lane = SUB * ((2 * cap) % 4)
    label_v[...] = received[:, label_tile, 0, :].astype(jnp.int32)
    copy = pltpu.make_async_copy(label_v, label_s, sem)
    copy.start()
    for grid in grids:
        grid[...] = jnp.zeros_like(grid)
    lane = lax.broadcasted_iota(jnp.int32, (8, 128), 1)
    copy.wait()

    @pl.loop(0, sources)
    def _(source):
        for i in range(cap):
            for o in range(5):
                column = label_s[source, label_lane + o * cap + i]
                offset = column & 127
                here = pl.multiple_of((column >> 7) * 8, 8)
                place = lane - offset
                inside = (place >= 0) & (place < SUB)
                beyond = place < SUB - 128
                added = []
                for c in range(2):
                    if o < 4:
                        value, part = received[source, 2 * i + c], o
                    else:
                        value = received[source, 2 * cap + (2 * i + c) // 4]
                        part = (2 * i + c) % 4
                    value = pltpu.roll(value, (offset - SUB * part) & 127, 1)
                    added.append(jnp.where(inside, value, 0.0))
                    added.append(jnp.where(beyond, value, 0.0))
                before = [
                    grids[c][pl.ds(here + 8 * k, 8), :] for c in range(2) for k in range(2)
                ]
                for c in range(2):
                    for k in range(2):
                        grids[c][pl.ds(here + 8 * k, 8), :] = before[2 * c + k] + added[2 * c + k]

    for pair in range(ROWS_DEV // 2):
        halves_of = []
        for e in range(2):
            rows = [
                pl.ds(ROWS_DEV * e + 2 * pair + k, TAIL, stride=2 * ROWS_DEV) for k in range(2)
            ]
            value = jnp.concatenate(
                [jnp.concatenate([grids[c][at, :] for at in rows], axis=1) for c in range(2)], 0
            )
            hi, lo = split(value)
            halves_of.append(table_times(first[2 * e], first[2 * e + 1], hi, lo))
        for h, a in enumerate((halves_of[0] + halves_of[1], halves_of[0] - halves_of[1])):
            turn_re = twist[0, TAIL * h : TAIL * h + TAIL]
            turn_im = twist[1, TAIL * h : TAIL * h + TAIL]
            for k in range(2):
                a_re = a[:TAIL, 128 * k : 128 * k + 128]
                a_im = a[TAIL:, 128 * k : 128 * k + 128]
                b = jnp.concatenate(
                    [a_re * turn_re - a_im * turn_im, a_re * turn_im + a_im * turn_re], axis=1
                )
                for part, value in enumerate(split(b)):
                    middle[h, pair, part, TAIL * k : TAIL * k + TAIL, :] = value

    copies = []
    for h in range(2):
        for pair in range(ROWS_DEV // 2):
            result = table_times(
                second[0], second[1], middle[h, pair, 0], middle[h, pair, 1], True
            )
            for c in range(2):
                for k in range(2):
                    held[h, c, pl.ds(2 * pair + k, TAIL, stride=ROWS_DEV), :] = result[
                        128 * c : 128 * c + 128, 128 * k : 128 * k + 128
                    ]
        for c in range(2):
            copies.append(
                pltpu.make_async_copy(
                    held.at[h, c].reshape(TAIL, ROWS_DEV, TAIL),
                    out.at[c, :, h],
                    out_sems.at[h, c],
                )
            )
            copies[-1].start()
    for copy in copies:
        copy.wait()


def shards(
    visibility, coords, block_owner, block_row, block_col, stations, block_count, beam_terms
):
    owners = lax.axis_size("tile")
    per_device = visibility.shape[0]
    tile_cols = NG // owners
    cap, tiles = send_layout(per_device, owners)
    stations_all = beam_terms.shape[0]
    vmem = pl.BlockSpec(memory_space=pltpu.VMEM)
    beams = (
        beam_terms.reshape(stations_all, 2, 8, 128)
        .transpose(0, 2, 1, 3)
        .reshape(stations_all, 16, 128)
    )
    labels = (
        block_owner.reshape(per_device),
        block_row,
        block_col,
        stations.T,
    )
    values = (
        visibility.reshape(per_device * 2, VROWS),
        coords.transpose(1, 0, 2),
        *image_tables(),
    )
    hbm = pl.BlockSpec(memory_space=pltpu.HBM)
    sent = pl.pallas_call(
        functools.partial(image_kernel, cap, tile_cols),
        out_shape=jax.ShapeDtypeStruct((owners, tiles, 8, 128), jnp.float32),
        in_specs=[pl.BlockSpec(memory_space=pltpu.SMEM)] + [hbm] * (1 + len(labels) + len(values)),
        out_specs=vmem,
        scratch_shapes=[
            *(pltpu.SMEM(label.shape, label.dtype) for label in labels),
            *(pltpu.VMEM(value.shape, value.dtype) for value in values),
            pltpu.VMEM((2 * (per_device + GROUP), 16, 128), jnp.float32),
            pltpu.VMEM((2, 16 * GROUP, 128), jnp.float32),
            pltpu.SMEM((owners,), jnp.int32),
            pltpu.SemaphoreType.DMA((per_device // GROUP + 1,)),
            pltpu.SemaphoreType.DMA((len(labels) + len(values),)),
        ],
        compiler_params=pltpu.CompilerParams(vmem_limit_bytes=24 * 1024 * 1024),
        name="image",
    )(
        block_count,
        *(pltpu.with_memory_space_constraint(x, pltpu.HBM) for x in (beams, *labels, *values)),
    )
    received = lax.all_to_all(sent, "tile", split_axis=0, concat_axis=0, tiled=True)
    result = pl.pallas_call(
        functools.partial(row_kernel, cap),
        out_shape=jax.ShapeDtypeStruct((2, TAIL, 2, ROWS_DEV, TAIL), jnp.float32),
        in_specs=[vmem] * 4,
        out_specs=pl.BlockSpec(memory_space=pl.ANY),
        scratch_shapes=[
            *(pltpu.VMEM(((LEAD + 1) * ROWS_DEV, TAIL), jnp.float32) for _ in range(2)),
            pltpu.VMEM((owners, 128), jnp.int32),
            pltpu.SMEM((owners, 128), jnp.int32),
            pltpu.SemaphoreType.DMA,
            pltpu.VMEM((2, ROWS_DEV // 2, 2, 2 * TAIL, 2 * TAIL), jnp.bfloat16),
            pltpu.VMEM((2, 2, TAIL * ROWS_DEV, TAIL), jnp.float32),
            pltpu.SemaphoreType.DMA((2, 2)),
        ],
        compiler_params=pltpu.CompilerParams(vmem_limit_bytes=24 * 1024 * 1024),
        name="rows",
    )(received, *row_tables())
    return (
        result.reshape(2, LEAD, ROWS_DEV, TAIL).transpose(0, 2, 1, 3).reshape(2, ROWS_DEV, NG)
    )


def solution(mesh):
    placed = (
        P(("parts", "tile"), None, None),
        P(("parts", "tile"), None, None),
        P(("parts", "tile"), None),
        P(("parts", "tile")),
        P(("parts", "tile")),
        P(("parts", "tile"), None),
        P(("parts", "tile")),
        P(),
    )
    return jax.shard_map(
        shards,
        mesh=mesh,
        in_specs=placed,
        out_specs=P(None, ("parts", "tile"), None),
        check_vma=False,
    )
```

```python
import functools
import math

import jax
import jax.numpy as jnp
import ml_dtypes
import numpy as np
from jax import lax
from jax.experimental import pallas as pl
from jax.experimental.pallas import tpu as pltpu
from jax.sharding import PartitionSpec as P

VROWS = 128
SUB = 32
NG = 32768
ROWS_DEV = 8
LEAD = 256
TAIL = 128
GROUP = 16

SIN_TERMS = (4.442882920, -7.308245680, 3.606354030, -0.846110410, 0.109822040)
COS_TERMS = (1.414213500, -6.978850910, 5.739459580, -1.883552820, 0.310677860)


def halves(table):
    table = np.round(table, 12).astype(np.float32)
    high = table.astype(ml_dtypes.bfloat16)
    low = (table - high.astype(np.float32)).astype(ml_dtypes.bfloat16)
    return high, low


def root(numbers, length):
    angle = 2.0 * np.pi / length * (numbers % length)
    return np.cos(angle), -np.sin(angle)


def complex_left(re, im):
    return np.block([[re, -im], [im, re]])


@functools.cache
def image_tables():
    eight = np.arange(8)
    re, im = root(np.outer(eight, eight), 8)
    left = complex_left(np.kron(np.eye(GROUP), re), np.kron(np.eye(GROUP), im))
    lane = np.arange(128)
    twist = root(np.outer(eight, lane // SUB), SUB)
    four = 8 * np.outer(lane // SUB, lane // SUB) + np.outer(lane % SUB, lane % SUB)
    re, im = root(four, SUB)
    right = complex_left(re, im).T
    row_pos = ((4 * eight[:, None] + lane[None, :] // SUB) - SUB // 2) / SUB
    col_pos = np.broadcast_to((lane[None, :] % SUB - SUB // 2) / SUB, (8, 128))
    taper = (1 - 2 * row_pos**2) * (1 - 2 * col_pos**2) / SUB
    small = np.stack([taper, np.round(twist[0], 12), np.round(twist[1], 12)]).astype(np.float32)
    return (*halves(left), *halves(right), small)


@functools.cache
def row_tables():
    lead, tail = np.arange(LEAD), np.arange(TAIL)
    even = complex_left(*root(np.outer(tail, tail), TAIL))
    odd = complex_left(*root(np.outer(tail, 2 * tail + 1), LEAD))
    twist = np.stack(root(np.outer(lead, tail), NG)) / math.sqrt(NG)
    first = np.stack(halves(even) + halves(odd))
    return first, np.stack(halves(even)), np.round(twist, 12).astype(np.float32)


def split(value):
    high = value.astype(jnp.bfloat16)
    return high, (value - high.astype(jnp.float32)).astype(jnp.bfloat16)


def dot(left, right, transposed=False):
    dims = (((1,), (1 if transposed else 0,)), ((), ()))
    return lax.dot_general(left, right, dims, preferred_element_type=jnp.float32)


def table_times(table_hi, table_lo, hi, lo, transposed=False):
    rows = table_hi.shape[0]
    both = dot(jnp.concatenate([table_hi, table_lo], axis=0), hi, transposed)
    return both[:rows] + both[rows:] + dot(table_hi, lo, transposed)


def times_table(hi, lo, table_hi, table_lo):
    rows = hi.shape[0]
    both = dot(jnp.concatenate([hi, lo], axis=0), table_hi)
    return both[:rows] + both[rows:] + dot(hi, table_lo)


def polynomial(terms, z):
    value = z * terms[-1] + terms[-2]
    for term in terms[-3::-1]:
        value = value * z + term
    return value


def cos_sin(turns):
    whole = (turns + 12582912.0) - 12582912.0
    t = turns - whole
    z = t * t
    half_sin = t * polynomial(SIN_TERMS, z)
    half_cos = polynomial(COS_TERMS, z)
    return 1.0 - half_sin * half_sin, half_sin * half_cos


def send_layout(per_device, owners):
    cap = -(-per_device // (owners - SUB // ROWS_DEV + 1))
    tiles = 2 * cap + (2 * cap + 1 + 3) // 4
    return cap, tiles


def image_kernel(
    cap,
    tile_cols,
    *refs,
):
    count_s, beams, args, out, copied = refs[0], refs[1], refs[2:13], refs[13], refs[14:25]
    beam_buf, sky, ranks, sems, arg_sems = refs[25:]
    copies = [
        pltpu.make_async_copy(arg, held, arg_sems.at[k])
        for k, (arg, held) in enumerate(zip(args, copied))
    ]
    for copy in copies:
        copy.start()
    owner_s, row_s, col_s, station_s, vis, coords = copied[:6]
    left_hi, left_lo, right_hi, right_lo, small = copied[6:]
    per_device = vis.shape[0] // 2
    owners = out.shape[0]
    out[...] = jnp.zeros_like(out)
    sky[...] = jnp.zeros_like(sky)
    for b in range(owners):
        ranks[b] = 0
    copies[3].wait()
    copies[1].wait()
    live = count_s[0]
    groups = (live + GROUP - 1) >> (GROUP.bit_length() - 1)

    def fetch_beams(g):
        for j in range(GROUP):
            n = jnp.minimum(g, per_device // GROUP - 1) * GROUP + j
            for side in range(2):
                pltpu.make_async_copy(
                    beams.at[station_s[side, n]],
                    beam_buf.at[2 * (g * GROUP + j) + side],
                    sems.at[g],
                ).start()

    def await_beams(g):
        waited = beam_buf.at[pl.ds(g * 2 * GROUP, 2 * GROUP)]
        pltpu.make_async_copy(beams.at[pl.ds(0, 2 * GROUP)], waited, sems.at[g]).wait()

    for g in range(2):
        fetch_beams(g)
    copies[4].wait()
    copies[5].wait()
    copies[10].wait()
    taper = small[0]
    twist_re = jnp.concatenate([small[1]] * GROUP, axis=0)
    twist_im = jnp.concatenate([small[2]] * GROUP, axis=0)
    number = lax.broadcasted_iota(jnp.int32, (SUB, VROWS), 0)
    l_row = (4 * (number % 8) + number // 8 - SUB // 2).astype(jnp.float32) / SUB
    l_col = (number - SUB // 2).astype(jnp.float32) / SUB
    d_row = l_row * l_row
    d_col = l_col * l_col
    sublane = lax.broadcasted_iota(jnp.int32, (8, 128), 0)
    lane = lax.broadcasted_iota(jnp.int32, (8, 128), 1)
    lane_group = lane // SUB

    def images(g, first=False):
        for quad in range(GROUP // 4):
            x_hi, x_lo, columns = [], [], []
            for j in range(4):
                n = g * GROUP + quad * 4 + j
                shift = row_s[n] & 7
                sign = (1 - 2 * (shift & 1)).astype(jnp.float32)
                u = coords[0, pl.ds(n, 1), :] + shift.astype(jnp.float32)
                v = coords[1, pl.ds(n, 1), :]
                w = coords[2, pl.ds(n, 1), :]
                vis_re = vis[pl.ds(2 * n, 1), :] * sign
                vis_im = vis[pl.ds(2 * n + 1, 1), :] * sign
                cos_row, sin_row = cos_sin(u * l_row + w * d_row)
                cos_col, sin_col = cos_sin(v * l_col + w * d_col)
                x = jnp.concatenate(
                    [
                        vis_re * cos_row - vis_im * sin_row,
                        vis_re * sin_row + vis_im * cos_row,
                    ],
                    axis=1,
                )
                hi, lo = split(x)
                x_hi.append(hi)
                x_lo.append(lo)
                columns.append(split(cos_col) + split(sin_col))
            c_hi, c_lo, s_hi, s_lo = zip(*columns)

            def matrix(c, s):
                real = [jnp.concatenate([a, -b], axis=1) for a, b in zip(c, s)]
                imag = [jnp.concatenate([b, a], axis=1) for a, b in zip(c, s)]
                return jnp.concatenate(real + imag, axis=0)

            lhs = jnp.concatenate(x_hi + x_lo, axis=0)
            both = dot(lhs, matrix(c_hi, s_hi), True)
            sums = both[:128] + both[128:] + dot(lhs[:128], matrix(c_lo, s_lo), True)
            if first and quad == 0:
                await_beams(g)
            for j in range(4):
                n = g * GROUP + quad * 4 + j
                flat = []
                for c in range(2):
                    value = None
                    for i in range(4):
                        piece = sums[32 * j + 8 * i : 32 * j + 8 * i + 8, 128 * c : 128 * c + 128]
                        if i != j:
                            piece = pltpu.roll(piece, (SUB * (i - j)) % 128, 1)
                        value = piece if value is None else jnp.where(lane_group == i, piece, value)
                    flat.append(value)
                one_re = beam_buf[2 * n, pl.ds(0, 8, stride=2), :]
                one_im = beam_buf[2 * n, pl.ds(1, 8, stride=2), :]
                two_re = beam_buf[2 * n + 1, pl.ds(0, 8, stride=2), :]
                two_im = beam_buf[2 * n + 1, pl.ds(1, 8, stride=2), :]
                beam_re = taper * (one_re * two_re + one_im * two_im)
                beam_im = taper * (one_im * two_re - one_re * two_im)
                sky_re = beam_re * flat[0] - beam_im * flat[1]
                sky_im = beam_re * flat[1] + beam_im * flat[0]
                in_use = n < live
                place = (quad * 4 + j) * 8
                sky[g & 1, place : place + 8, :] = jnp.where(in_use, sky_re, 0.0)
                sky[g & 1, place + 8 * GROUP : place + 8 * GROUP + 8, :] = jnp.where(in_use, sky_im, 0.0)

    label_tile = 2 * cap + (2 * cap) // 4
    label_lane = SUB * ((2 * cap) % 4)

    def cells(g):
        hi, lo = split(sky[g & 1])
        z = table_times(left_hi[...], left_lo[...], hi, lo)
        z_re, z_im = z[: 8 * GROUP], z[8 * GROUP :]
        y_re = z_re * twist_re - z_im * twist_im
        y_im = z_re * twist_im + z_im * twist_re
        hi, lo = split(jnp.concatenate([y_re, y_im], axis=1))
        result = times_table(hi, lo, right_hi[...], right_lo[...])
        for j in range(GROUP):
            n = g * GROUP + j
            band = row_s[n] >> 3
            shift = row_s[n] & 7
            rank = ranks[band]
            ranks[band] = rank + 1
            late = sublane < shift
            last = jnp.minimum(band + 4, owners - 1)
            for c in range(2):
                value = result[8 * j : 8 * j + 8, 128 * c : 128 * c + 128]
                spread = jnp.where(late & (lane_group == 0), 0.0, value)
                tile = 2 * rank + c
                for o in range(4):
                    pltpu.store(out.at[band + o, tile], spread, mask=lane_group == o)
                part = tile & 3
                tail = pltpu.roll(value, SUB * part, 1)
                pltpu.store(
                    out.at[last, 2 * cap + (tile >> 2)], tail, mask=late & (lane_group == part)
                )
            column = jnp.full((8, 128), owner_s[n] * tile_cols + col_s[n], jnp.float32)
            for o in range(5):
                here = (sublane == 0) & (lane == label_lane + o * cap + rank)
                if o == 4:
                    here = here & (sublane < shift)
                target = last if o == 4 else band + o
                pltpu.store(out.at[target, label_tile], column, mask=here)

    images(0, True)
    for copy in copies[6:10] + [copies[0], copies[2]]:
        copy.wait()

    @pl.loop(1, groups)
    def _(g):
        await_beams(g)
        fetch_beams(g + 1)
        cells(g - 1)
        images(g)

    cells(groups - 1)
    await_beams(groups)


def row_kernel(
    cap,
    received,
    first,
    second,
    twist,
    out,
    *scratch,
):
    grids, (label_v, label_s, sem, middle, held, out_sems) = scratch[:2], scratch[2:]
    sources = received.shape[0]
    label_tile = 2 * cap + (2 * cap) // 4
    label_lane = SUB * ((2 * cap) % 4)
    label_v[...] = received[:, label_tile, 0, :].astype(jnp.int32)
    copy = pltpu.make_async_copy(label_v, label_s, sem)
    copy.start()
    for grid in grids:
        grid[...] = jnp.zeros_like(grid)
    lane = lax.broadcasted_iota(jnp.int32, (8, 128), 1)
    copy.wait()

    @pl.loop(0, sources)
    def _(source):
        for i in range(cap):
            for o in range(5):
                column = label_s[source, label_lane + o * cap + i]
                offset = column & 127
                here = pl.multiple_of((column >> 7) * 8, 8)
                place = lane - offset
                inside = (place >= 0) & (place < SUB)
                beyond = place < SUB - 128
                added = []
                for c in range(2):
                    if o < 4:
                        value, part = received[source, 2 * i + c], o
                    else:
                        value = received[source, 2 * cap + (2 * i + c) // 4]
                        part = (2 * i + c) % 4
                    value = pltpu.roll(value, (offset - SUB * part) & 127, 1)
                    added.append(jnp.where(inside, value, 0.0))
                    added.append(jnp.where(beyond, value, 0.0))
                before = [
                    grids[c][pl.ds(here + 8 * k, 8), :] for c in range(2) for k in range(2)
                ]
                for c in range(2):
                    for k in range(2):
                        grids[c][pl.ds(here + 8 * k, 8), :] = before[2 * c + k] + added[2 * c + k]

    for pair in range(ROWS_DEV // 2):
        halves_of = []
        for e in range(2):
            rows = [
                pl.ds(ROWS_DEV * e + 2 * pair + k, TAIL, stride=2 * ROWS_DEV) for k in range(2)
            ]
            value = jnp.concatenate(
                [jnp.concatenate([grids[c][at, :] for at in rows], axis=1) for c in range(2)], 0
            )
            hi, lo = split(value)
            halves_of.append(table_times(first[2 * e], first[2 * e + 1], hi, lo))
        for h, a in enumerate((halves_of[0] + halves_of[1], halves_of[0] - halves_of[1])):
            turn_re = twist[0, TAIL * h : TAIL * h + TAIL]
            turn_im = twist[1, TAIL * h : TAIL * h + TAIL]
            for k in range(2):
                a_re = a[:TAIL, 128 * k : 128 * k + 128]
                a_im = a[TAIL:, 128 * k : 128 * k + 128]
                b = jnp.concatenate(
                    [a_re * turn_re - a_im * turn_im, a_re * turn_im + a_im * turn_re], axis=1
                )
                for part, value in enumerate(split(b)):
                    middle[h, pair, part, TAIL * k : TAIL * k + TAIL, :] = value

    copies = []
    for h in range(2):
        for pair in range(ROWS_DEV // 2):
            result = table_times(
                second[0], second[1], middle[h, pair, 0], middle[h, pair, 1], True
            )
            for c in range(2):
                for k in range(2):
                    held[h, c, pl.ds(2 * pair + k, TAIL, stride=ROWS_DEV), :] = result[
                        128 * c : 128 * c + 128, 128 * k : 128 * k + 128
                    ]
        for c in range(2):
            copies.append(
                pltpu.make_async_copy(
                    held.at[h, c].reshape(TAIL, ROWS_DEV, TAIL),
                    out.at[c, :, h],
                    out_sems.at[h, c],
                )
            )
            copies[-1].start()
    for copy in copies:
        copy.wait()


def shards(
    visibility, coords, block_owner, block_row, block_col, stations, block_count, beam_terms
):
    owners = lax.axis_size("tile")
    per_device = visibility.shape[0]
    tile_cols = NG // owners
    cap, tiles = send_layout(per_device, owners)
    stations_all = beam_terms.shape[0]
    vmem = pl.BlockSpec(memory_space=pltpu.VMEM)
    beams = (
        beam_terms.reshape(stations_all, 2, 8, 128)
        .transpose(0, 2, 1, 3)
        .reshape(stations_all, 16, 128)
    )
    labels = (
        block_owner.reshape(per_device),
        block_row,
        block_col,
        stations.T,
    )
    values = (
        visibility.reshape(per_device * 2, VROWS),
        coords.transpose(1, 0, 2),
        *image_tables(),
    )
    hbm = pl.BlockSpec(memory_space=pltpu.HBM)
    sent = pl.pallas_call(
        functools.partial(image_kernel, cap, tile_cols),
        out_shape=jax.ShapeDtypeStruct((owners, tiles, 8, 128), jnp.float32),
        in_specs=[pl.BlockSpec(memory_space=pltpu.SMEM)] + [hbm] * (1 + len(labels) + len(values)),
        out_specs=vmem,
        scratch_shapes=[
            *(pltpu.SMEM(label.shape, label.dtype) for label in labels),
            *(pltpu.VMEM(value.shape, value.dtype) for value in values),
            pltpu.VMEM((2 * (per_device + GROUP), 16, 128), jnp.float32),
            pltpu.VMEM((2, 16 * GROUP, 128), jnp.float32),
            pltpu.SMEM((owners,), jnp.int32),
            pltpu.SemaphoreType.DMA((per_device // GROUP + 1,)),
            pltpu.SemaphoreType.DMA((len(labels) + len(values),)),
        ],
        compiler_params=pltpu.CompilerParams(vmem_limit_bytes=24 * 1024 * 1024),
        name="image",
    )(
        block_count,
        *(pltpu.with_memory_space_constraint(x, pltpu.HBM) for x in (beams, *labels, *values)),
    )
    received = lax.all_to_all(sent, "tile", split_axis=0, concat_axis=0, tiled=True)
    result = pl.pallas_call(
        functools.partial(row_kernel, cap),
        out_shape=jax.ShapeDtypeStruct((2, TAIL, 2, ROWS_DEV, TAIL), jnp.float32),
        in_specs=[vmem] * 4,
        out_specs=pl.BlockSpec(memory_space=pl.ANY),
        scratch_shapes=[
            *(pltpu.VMEM(((LEAD + 1) * ROWS_DEV, TAIL), jnp.float32) for _ in range(2)),
            pltpu.VMEM((owners, 128), jnp.int32),
            pltpu.SMEM((owners, 128), jnp.int32),
            pltpu.SemaphoreType.DMA,
            pltpu.VMEM((2, ROWS_DEV // 2, 2, 2 * TAIL, 2 * TAIL), jnp.bfloat16),
            pltpu.VMEM((2, 2, TAIL * ROWS_DEV, TAIL), jnp.float32),
            pltpu.SemaphoreType.DMA((2, 2)),
        ],
        compiler_params=pltpu.CompilerParams(vmem_limit_bytes=24 * 1024 * 1024),
        name="rows",
    )(received, *row_tables())
    return (
        result.reshape(2, LEAD, ROWS_DEV, TAIL).transpose(0, 2, 1, 3).reshape(2, ROWS_DEV, NG)
    )


def solution(mesh):
    placed = (
        P(("parts", "tile"), None, None),
        P(("parts", "tile"), None, None),
        P(("parts", "tile"), None),
        P(("parts", "tile")),
        P(("parts", "tile")),
        P(("parts", "tile"), None),
        P(("parts", "tile")),
        P(),
    )
    return jax.shard_map(
        shards,
        mesh=mesh,
        in_specs=placed,
        out_specs=P(None, ("parts", "tile"), None),
        check_vma=False,
    )
```

```python
import functools
import math

import jax
import jax.numpy as jnp
import ml_dtypes
import numpy as np
from jax import lax
from jax.experimental import pallas as pl
from jax.experimental.pallas import tpu as pltpu
from jax.sharding import PartitionSpec as P

VROWS = 128
SUB = 32
NG = 32768
ROWS_DEV = 8
LEAD = 256
TAIL = 128
GROUP = 16

SIN_TERMS = (4.442882920, -7.308245680, 3.606354030, -0.846110410, 0.109822040)
COS_TERMS = (1.414213500, -6.978850910, 5.739459580, -1.883552820, 0.310677860)


def halves(table):
    table = np.round(table, 12).astype(np.float32)
    high = table.astype(ml_dtypes.bfloat16)
    low = (table - high.astype(np.float32)).astype(ml_dtypes.bfloat16)
    return high, low


def root(numbers, length):
    angle = 2.0 * np.pi / length * (numbers % length)
    return np.cos(angle), -np.sin(angle)


def complex_left(re, im):
    return np.block([[re, -im], [im, re]])


@functools.cache
def image_tables():
    eight = np.arange(8)
    re, im = root(np.outer(eight, eight), 8)
    left = complex_left(np.kron(np.eye(GROUP), re), np.kron(np.eye(GROUP), im))
    lane = np.arange(128)
    twist = root(np.outer(eight, lane // SUB), SUB)
    four = 8 * np.outer(lane // SUB, lane // SUB) + np.outer(lane % SUB, lane % SUB)
    re, im = root(four, SUB)
    right = complex_left(re, im).T
    row_pos = ((4 * eight[:, None] + lane[None, :] // SUB) - SUB // 2) / SUB
    col_pos = np.broadcast_to((lane[None, :] % SUB - SUB // 2) / SUB, (8, 128))
    taper = (1 - 2 * row_pos**2) * (1 - 2 * col_pos**2) / SUB
    small = np.stack([taper, np.round(twist[0], 12), np.round(twist[1], 12)]).astype(np.float32)
    return (*halves(left), *halves(right), small)


@functools.cache
def row_tables():
    lead, tail = np.arange(LEAD), np.arange(TAIL)
    even = complex_left(*root(np.outer(tail, tail), TAIL))
    odd = complex_left(*root(np.outer(tail, 2 * tail + 1), LEAD))
    twist = np.stack(root(np.outer(lead, tail), NG)) / math.sqrt(NG)
    first = np.stack(halves(even) + halves(odd))
    return first, np.stack(halves(even)), np.round(twist, 12).astype(np.float32)


def split(value):
    high = value.astype(jnp.bfloat16)
    return high, (value - high.astype(jnp.float32)).astype(jnp.bfloat16)


def dot(left, right, transposed=False):
    dims = (((1,), (1 if transposed else 0,)), ((), ()))
    return lax.dot_general(left, right, dims, preferred_element_type=jnp.float32)


def table_times(table_hi, table_lo, hi, lo, transposed=False):
    rows = table_hi.shape[0]
    both = dot(jnp.concatenate([table_hi, table_lo], axis=0), hi, transposed)
    return both[:rows] + both[rows:] + dot(table_hi, lo, transposed)


def times_table(hi, lo, table_hi, table_lo):
    rows = hi.shape[0]
    both = dot(jnp.concatenate([hi, lo], axis=0), table_hi)
    return both[:rows] + both[rows:] + dot(hi, table_lo)


def polynomial(terms, z):
    value = z * terms[-1] + terms[-2]
    for term in terms[-3::-1]:
        value = value * z + term
    return value


def cos_sin(turns):
    whole = (turns + 12582912.0) - 12582912.0
    t = turns - whole
    z = t * t
    half_sin = t * polynomial(SIN_TERMS, z)
    half_cos = polynomial(COS_TERMS, z)
    return 1.0 - half_sin * half_sin, half_sin * half_cos


def send_layout(per_device, owners):
    cap = -(-per_device // (owners - SUB // ROWS_DEV + 1))
    tiles = 2 * cap + (2 * cap + 1 + 3) // 4
    return cap, tiles


def image_kernel(
    cap,
    tile_cols,
    *refs,
):
    count_s, beams, args, out, copied = refs[0], refs[1], refs[2:13], refs[13], refs[14:25]
    beam_buf, sky, ranks, sems, arg_sems = refs[25:]
    copies = [
        pltpu.make_async_copy(arg, held, arg_sems.at[k])
        for k, (arg, held) in enumerate(zip(args, copied))
    ]
    for copy in copies:
        copy.start()
    owner_s, row_s, col_s, station_s, vis, coords = copied[:6]
    left_hi, left_lo, right_hi, right_lo, small = copied[6:]
    per_device = vis.shape[0] // 2
    owners = out.shape[0]
    out[...] = jnp.zeros_like(out)
    sky[...] = jnp.zeros_like(sky)
    for b in range(owners):
        ranks[b] = 0
    copies[3].wait()
    copies[1].wait()
    live = count_s[0]
    groups = (live + GROUP - 1) >> (GROUP.bit_length() - 1)

    def fetch_beams(g):
        for j in range(GROUP):
            n = jnp.minimum(g, per_device // GROUP - 1) * GROUP + j
            for side in range(2):
                pltpu.make_async_copy(
                    beams.at[station_s[side, n]],
                    beam_buf.at[2 * (g * GROUP + j) + side],
                    sems.at[g],
                ).start()

    def await_beams(g):
        waited = beam_buf.at[pl.ds(g * 2 * GROUP, 2 * GROUP)]
        pltpu.make_async_copy(beams.at[pl.ds(0, 2 * GROUP)], waited, sems.at[g]).wait()

    for g in range(2):
        fetch_beams(g)
    copies[4].wait()
    copies[5].wait()
    copies[10].wait()

    @pl.loop(0, groups * (GROUP // 8))
    def _(g):
        for j in range(8):
            n = g * 8 + j
            shift = row_s[n] & 7
            coords[0, pl.ds(n, 1), :] += shift.astype(jnp.float32)
            vis[pl.ds(2 * n, 2), :] *= (1 - 2 * (shift & 1)).astype(jnp.float32)

    taper = small[0]
    twist_re = jnp.concatenate([small[1]] * GROUP, axis=0)
    twist_im = jnp.concatenate([small[2]] * GROUP, axis=0)
    number = lax.broadcasted_iota(jnp.int32, (SUB, VROWS), 0)
    l_row = (4 * (number % 8) + number // 8 - SUB // 2).astype(jnp.float32) / SUB
    l_col = (number - SUB // 2).astype(jnp.float32) / SUB
    d_row = l_row * l_row
    d_col = l_col * l_col
    sublane = lax.broadcasted_iota(jnp.int32, (8, 128), 0)
    lane = lax.broadcasted_iota(jnp.int32, (8, 128), 1)
    lane_group = lane // SUB

    def images(g, first=False):
        for quad in range(GROUP // 4):
            x_hi, x_lo, columns = [], [], []
            for j in range(4):
                n = g * GROUP + quad * 4 + j
                u = coords[0, pl.ds(n, 1), :]
                v = coords[1, pl.ds(n, 1), :]
                w = coords[2, pl.ds(n, 1), :]
                vis_re = vis[pl.ds(2 * n, 1), :]
                vis_im = vis[pl.ds(2 * n + 1, 1), :]
                cos_row, sin_row = cos_sin(u * l_row + w * d_row)
                cos_col, sin_col = cos_sin(v * l_col + w * d_col)
                x = jnp.concatenate(
                    [
                        vis_re * cos_row - vis_im * sin_row,
                        vis_re * sin_row + vis_im * cos_row,
                    ],
                    axis=1,
                )
                hi, lo = split(x)
                x_hi.append(hi)
                x_lo.append(lo)
                columns.append(split(cos_col) + split(sin_col))
            c_hi, c_lo, s_hi, s_lo = zip(*columns)

            def matrix(c, s):
                real = [jnp.concatenate([a, -b], axis=1) for a, b in zip(c, s)]
                imag = [jnp.concatenate([b, a], axis=1) for a, b in zip(c, s)]
                return jnp.concatenate(real + imag, axis=0)

            lhs = jnp.concatenate(x_hi + x_lo, axis=0)
            both = dot(lhs, matrix(c_hi, s_hi), True)
            sums = both[:128] + both[128:] + dot(lhs[:128], matrix(c_lo, s_lo), True)
            if first and quad == 0:
                await_beams(g)
            for j in range(4):
                n = g * GROUP + quad * 4 + j
                flat = []
                for c in range(2):
                    value = None
                    for i in range(4):
                        piece = sums[32 * j + 8 * i : 32 * j + 8 * i + 8, 128 * c : 128 * c + 128]
                        if i != j:
                            piece = pltpu.roll(piece, (SUB * (i - j)) % 128, 1)
                        value = piece if value is None else jnp.where(lane_group == i, piece, value)
                    flat.append(value)
                one_re = beam_buf[2 * n, pl.ds(0, 8, stride=2), :]
                one_im = beam_buf[2 * n, pl.ds(1, 8, stride=2), :]
                two_re = beam_buf[2 * n + 1, pl.ds(0, 8, stride=2), :]
                two_im = beam_buf[2 * n + 1, pl.ds(1, 8, stride=2), :]
                beam_re = taper * (one_re * two_re + one_im * two_im)
                beam_im = taper * (one_im * two_re - one_re * two_im)
                sky_re = beam_re * flat[0] - beam_im * flat[1]
                sky_im = beam_re * flat[1] + beam_im * flat[0]
                in_use = n < live
                place = (quad * 4 + j) * 8
                sky[g & 1, place : place + 8, :] = jnp.where(in_use, sky_re, 0.0)
                sky[g & 1, place + 8 * GROUP : place + 8 * GROUP + 8, :] = jnp.where(in_use, sky_im, 0.0)

    label_tile = 2 * cap + (2 * cap) // 4
    label_lane = SUB * ((2 * cap) % 4)

    def cells(g):
        hi, lo = split(sky[g & 1])
        z = table_times(left_hi[...], left_lo[...], hi, lo)
        z_re, z_im = z[: 8 * GROUP], z[8 * GROUP :]
        y_re = z_re * twist_re - z_im * twist_im
        y_im = z_re * twist_im + z_im * twist_re
        hi, lo = split(jnp.concatenate([y_re, y_im], axis=1))
        result = times_table(hi, lo, right_hi[...], right_lo[...])
        for j in range(GROUP):
            n = g * GROUP + j
            band = row_s[n] >> 3
            shift = row_s[n] & 7
            rank = ranks[band]
            ranks[band] = rank + 1
            late = sublane < shift
            last = jnp.minimum(band + 4, owners - 1)
            for c in range(2):
                value = result[8 * j : 8 * j + 8, 128 * c : 128 * c + 128]
                spread = jnp.where(late & (lane_group == 0), 0.0, value)
                tile = 2 * rank + c
                for o in range(4):
                    pltpu.store(out.at[band + o, tile], spread, mask=lane_group == o)
                part = tile & 3
                tail = pltpu.roll(value, SUB * part, 1)
                pltpu.store(
                    out.at[last, 2 * cap + (tile >> 2)], tail, mask=late & (lane_group == part)
                )
            column = jnp.full((8, 128), owner_s[n] * tile_cols + col_s[n], jnp.float32)
            for o in range(5):
                here = (sublane == 0) & (lane == label_lane + o * cap + rank)
                if o == 4:
                    here = here & (sublane < shift)
                target = last if o == 4 else band + o
                pltpu.store(out.at[target, label_tile], column, mask=here)

    images(0, True)
    for copy in copies[6:10] + [copies[0], copies[2]]:
        copy.wait()

    @pl.loop(1, groups)
    def _(g):
        await_beams(g)
        fetch_beams(g + 1)
        cells(g - 1)
        images(g)

    cells(groups - 1)
    await_beams(groups)


def row_kernel(
    cap,
    received,
    first,
    second,
    twist,
    out,
    *scratch,
):
    grids, (label_v, label_s, sem, middle, held, out_sems) = scratch[:2], scratch[2:]
    sources = received.shape[0]
    label_tile = 2 * cap + (2 * cap) // 4
    label_lane = SUB * ((2 * cap) % 4)
    label_v[...] = received[:, label_tile, 0, :].astype(jnp.int32)
    copy = pltpu.make_async_copy(label_v, label_s, sem)
    copy.start()
    for grid in grids:
        grid[...] = jnp.zeros_like(grid)
    lane = lax.broadcasted_iota(jnp.int32, (8, 128), 1)
    copy.wait()

    @pl.loop(0, sources)
    def _(source):
        for i in range(cap):
            for o in range(5):
                column = label_s[source, label_lane + o * cap + i]
                offset = column & 127
                here = pl.multiple_of((column >> 7) * 8, 8)
                place = lane - offset
                inside = (place >= 0) & (place < SUB)
                beyond = place < SUB - 128
                added = []
                for c in range(2):
                    if o < 4:
                        value, part = received[source, 2 * i + c], o
                    else:
                        value = received[source, 2 * cap + (2 * i + c) // 4]
                        part = (2 * i + c) % 4
                    value = pltpu.roll(value, (offset - SUB * part) & 127, 1)
                    added.append(jnp.where(inside, value, 0.0))
                    added.append(jnp.where(beyond, value, 0.0))
                before = [
                    grids[c][pl.ds(here + 8 * k, 8), :] for c in range(2) for k in range(2)
                ]
                for c in range(2):
                    for k in range(2):
                        grids[c][pl.ds(here + 8 * k, 8), :] = before[2 * c + k] + added[2 * c + k]

    for pair in range(ROWS_DEV // 2):
        halves_of = []
        for e in range(2):
            rows = [
                pl.ds(ROWS_DEV * e + 2 * pair + k, TAIL, stride=2 * ROWS_DEV) for k in range(2)
            ]
            value = jnp.concatenate(
                [jnp.concatenate([grids[c][at, :] for at in rows], axis=1) for c in range(2)], 0
            )
            hi, lo = split(value)
            halves_of.append(table_times(first[2 * e], first[2 * e + 1], hi, lo))
        for h, a in enumerate((halves_of[0] + halves_of[1], halves_of[0] - halves_of[1])):
            turn_re = twist[0, TAIL * h : TAIL * h + TAIL]
            turn_im = twist[1, TAIL * h : TAIL * h + TAIL]
            for k in range(2):
                a_re = a[:TAIL, 128 * k : 128 * k + 128]
                a_im = a[TAIL:, 128 * k : 128 * k + 128]
                b = jnp.concatenate(
                    [a_re * turn_re - a_im * turn_im, a_re * turn_im + a_im * turn_re], axis=1
                )
                for part, value in enumerate(split(b)):
                    middle[h, pair, part, TAIL * k : TAIL * k + TAIL, :] = value

    copies = []
    for h in range(2):
        for pair in range(ROWS_DEV // 2):
            result = table_times(
                second[0], second[1], middle[h, pair, 0], middle[h, pair, 1], True
            )
            for c in range(2):
                for k in range(2):
                    held[h, c, pl.ds(2 * pair + k, TAIL, stride=ROWS_DEV), :] = result[
                        128 * c : 128 * c + 128, 128 * k : 128 * k + 128
                    ]
        for c in range(2):
            copies.append(
                pltpu.make_async_copy(
                    held.at[h, c].reshape(TAIL, ROWS_DEV, TAIL),
                    out.at[c, :, h],
                    out_sems.at[h, c],
                )
            )
            copies[-1].start()
    for copy in copies:
        copy.wait()


def shards(
    visibility, coords, block_owner, block_row, block_col, stations, block_count, beam_terms
):
    owners = lax.axis_size("tile")
    per_device = visibility.shape[0]
    tile_cols = NG // owners
    cap, tiles = send_layout(per_device, owners)
    stations_all = beam_terms.shape[0]
    vmem = pl.BlockSpec(memory_space=pltpu.VMEM)
    beams = (
        beam_terms.reshape(stations_all, 2, 8, 128)
        .transpose(0, 2, 1, 3)
        .reshape(stations_all, 16, 128)
    )
    labels = (
        block_owner.reshape(per_device),
        block_row,
        block_col,
        stations.T,
    )
    values = (
        visibility.reshape(per_device * 2, VROWS),
        coords.transpose(1, 0, 2),
        *image_tables(),
    )
    hbm = pl.BlockSpec(memory_space=pltpu.HBM)
    sent = pl.pallas_call(
        functools.partial(image_kernel, cap, tile_cols),
        out_shape=jax.ShapeDtypeStruct((owners, tiles, 8, 128), jnp.float32),
        in_specs=[pl.BlockSpec(memory_space=pltpu.SMEM)] + [hbm] * (1 + len(labels) + len(values)),
        out_specs=vmem,
        scratch_shapes=[
            *(pltpu.SMEM(label.shape, label.dtype) for label in labels),
            *(pltpu.VMEM(value.shape, value.dtype) for value in values),
            pltpu.VMEM((2 * (per_device + GROUP), 16, 128), jnp.float32),
            pltpu.VMEM((2, 16 * GROUP, 128), jnp.float32),
            pltpu.SMEM((owners,), jnp.int32),
            pltpu.SemaphoreType.DMA((per_device // GROUP + 1,)),
            pltpu.SemaphoreType.DMA((len(labels) + len(values),)),
        ],
        compiler_params=pltpu.CompilerParams(vmem_limit_bytes=24 * 1024 * 1024),
        name="image",
    )(
        block_count,
        *(pltpu.with_memory_space_constraint(x, pltpu.HBM) for x in (beams, *labels, *values)),
    )
    received = lax.all_to_all(sent, "tile", split_axis=0, concat_axis=0, tiled=True)
    result = pl.pallas_call(
        functools.partial(row_kernel, cap),
        out_shape=jax.ShapeDtypeStruct((2, TAIL, 2, ROWS_DEV, TAIL), jnp.float32),
        in_specs=[vmem] * 4,
        out_specs=pl.BlockSpec(memory_space=pl.ANY),
        scratch_shapes=[
            *(pltpu.VMEM(((LEAD + 1) * ROWS_DEV, TAIL), jnp.float32) for _ in range(2)),
            pltpu.VMEM((owners, 128), jnp.int32),
            pltpu.SMEM((owners, 128), jnp.int32),
            pltpu.SemaphoreType.DMA,
            pltpu.VMEM((2, ROWS_DEV // 2, 2, 2 * TAIL, 2 * TAIL), jnp.bfloat16),
            pltpu.VMEM((2, 2, TAIL * ROWS_DEV, TAIL), jnp.float32),
            pltpu.SemaphoreType.DMA((2, 2)),
        ],
        compiler_params=pltpu.CompilerParams(vmem_limit_bytes=24 * 1024 * 1024),
        name="rows",
    )(received, *row_tables())
    return (
        result.reshape(2, LEAD, ROWS_DEV, TAIL).transpose(0, 2, 1, 3).reshape(2, ROWS_DEV, NG)
    )


def solution(mesh):
    placed = (
        P(("parts", "tile"), None, None),
        P(("parts", "tile"), None, None),
        P(("parts", "tile"), None),
        P(("parts", "tile")),
        P(("parts", "tile")),
        P(("parts", "tile"), None),
        P(("parts", "tile")),
        P(),
    )
    return jax.shard_map(
        shards,
        mesh=mesh,
        in_specs=placed,
        out_specs=P(None, ("parts", "tile"), None),
        check_vma=False,
    )
```

```python
import functools
import math

import jax
import jax.numpy as jnp
import ml_dtypes
import numpy as np
from jax import lax
from jax.experimental import pallas as pl
from jax.experimental.pallas import tpu as pltpu
from jax.sharding import PartitionSpec as P

VROWS = 128
SUB = 32
NG = 32768
ROWS_DEV = 8
LEAD = 256
TAIL = 128
GROUP = 16

SIN_TERMS = (4.442879549, -7.307815317, 3.597759608, -0.791160565)
COS_TERMS = (1.414213500, -6.978850910, 5.739459580, -1.883552820, 0.310677860)


def halves(table):
    table = np.round(table, 12).astype(np.float32)
    high = table.astype(ml_dtypes.bfloat16)
    low = (table - high.astype(np.float32)).astype(ml_dtypes.bfloat16)
    return high, low


def root(numbers, length):
    angle = 2.0 * np.pi / length * (numbers % length)
    return np.cos(angle), -np.sin(angle)


def complex_left(re, im):
    return np.block([[re, -im], [im, re]])


@functools.cache
def image_tables():
    eight = np.arange(8)
    re, im = root(np.outer(eight, eight), 8)
    left = complex_left(np.kron(np.eye(GROUP), re), np.kron(np.eye(GROUP), im))
    lane = np.arange(128)
    twist = root(np.outer(eight, lane // SUB), SUB)
    four = 8 * np.outer(lane // SUB, lane // SUB) + np.outer(lane % SUB, lane % SUB)
    re, im = root(four, SUB)
    right = complex_left(re, im).T
    row_pos = ((4 * eight[:, None] + lane[None, :] // SUB) - SUB // 2) / SUB
    col_pos = np.broadcast_to((lane[None, :] % SUB - SUB // 2) / SUB, (8, 128))
    taper = (1 - 2 * row_pos**2) * (1 - 2 * col_pos**2) / SUB
    small = np.stack([taper, np.round(twist[0], 12), np.round(twist[1], 12)]).astype(np.float32)
    return (*halves(left), *halves(right), small)


@functools.cache
def row_tables():
    lead, tail = np.arange(LEAD), np.arange(TAIL)
    even = complex_left(*root(np.outer(tail, tail), TAIL))
    odd = complex_left(*root(np.outer(tail, 2 * tail + 1), LEAD))
    twist = np.stack(root(np.outer(lead, tail), NG)) / math.sqrt(NG)
    first = np.stack(halves(even) + halves(odd))
    return first, np.stack(halves(even)), np.round(twist, 12).astype(np.float32)


def split(value):
    high = value.astype(jnp.bfloat16)
    return high, (value - high.astype(jnp.float32)).astype(jnp.bfloat16)


def dot(left, right, transposed=False):
    dims = (((1,), (1 if transposed else 0,)), ((), ()))
    return lax.dot_general(left, right, dims, preferred_element_type=jnp.float32)


def table_times(table_hi, table_lo, hi, lo, transposed=False):
    rows = table_hi.shape[0]
    both = dot(jnp.concatenate([table_hi, table_lo], axis=0), hi, transposed)
    return both[:rows] + both[rows:] + dot(table_hi, lo, transposed)


def times_table(hi, lo, table_hi, table_lo):
    rows = hi.shape[0]
    both = dot(jnp.concatenate([hi, lo], axis=0), table_hi)
    return both[:rows] + both[rows:] + dot(hi, table_lo)


def polynomial(terms, z):
    value = z * terms[-1] + terms[-2]
    for term in terms[-3::-1]:
        value = value * z + term
    return value


def cos_sin(turns):
    whole = (turns + 12582912.0) - 12582912.0
    t = turns - whole
    z = t * t
    half_sin = t * polynomial(SIN_TERMS, z)
    half_cos = polynomial(COS_TERMS, z)
    return 1.0 - half_sin * half_sin, half_sin * half_cos


def send_layout(per_device, owners):
    cap = -(-per_device // (owners - SUB // ROWS_DEV + 1))
    tiles = 2 * cap + (2 * cap + 1 + 3) // 4
    return cap, tiles


def image_kernel(
    cap,
    tile_cols,
    *refs,
):
    count_s, beams, args, out, copied = refs[0], refs[1], refs[2:13], refs[13], refs[14:25]
    beam_buf, sky, ranks, sems, arg_sems = refs[25:]
    copies = [
        pltpu.make_async_copy(arg, held, arg_sems.at[k])
        for k, (arg, held) in enumerate(zip(args, copied))
    ]
    for copy in copies:
        copy.start()
    owner_s, row_s, col_s, station_s, vis, coords = copied[:6]
    left_hi, left_lo, right_hi, right_lo, small = copied[6:]
    per_device = vis.shape[0] // 2
    owners = out.shape[0]
    label_tile = 2 * cap + (2 * cap) // 4
    label_lane = SUB * ((2 * cap) % 4)
    sublane = lax.broadcasted_iota(jnp.int32, (8, 128), 0)
    lane = lax.broadcasted_iota(jnp.int32, (8, 128), 1)
    lane_group = lane // SUB
    out[...] = jnp.zeros_like(out)
    spread_columns = ((lane - label_lane) * (NG // SUB)).astype(jnp.float32)
    is_label = (sublane == 0) & (lane >= label_lane) & (lane < label_lane + SUB)
    for d in range(owners):
        out[d, label_tile] = jnp.where(is_label, spread_columns, 0.0)
    sky[...] = jnp.zeros_like(sky)
    for b in range(owners):
        ranks[b] = 0
    copies[3].wait()
    copies[1].wait()
    live = count_s[0]
    groups = (live + GROUP - 1) >> (GROUP.bit_length() - 1)

    def fetch_beams(g):
        for j in range(GROUP):
            n = jnp.minimum(g, per_device // GROUP - 1) * GROUP + j
            for side in range(2):
                pltpu.make_async_copy(
                    beams.at[station_s[side, n]],
                    beam_buf.at[2 * (g * GROUP + j) + side],
                    sems.at[g],
                ).start()

    def await_beams(g):
        waited = beam_buf.at[pl.ds(g * 2 * GROUP, 2 * GROUP)]
        pltpu.make_async_copy(beams.at[pl.ds(0, 2 * GROUP)], waited, sems.at[g]).wait()

    for g in range(2):
        fetch_beams(g)
    copies[4].wait()
    copies[5].wait()
    copies[10].wait()

    @pl.loop(0, groups * (GROUP // 8))
    def _(g):
        for j in range(8):
            n = g * 8 + j
            shift = row_s[n] & 7
            coords[0, pl.ds(n, 1), :] += shift.astype(jnp.float32)
            vis[pl.ds(2 * n, 2), :] *= (1 - 2 * (shift & 1)).astype(jnp.float32)

    taper = small[0]
    twist_re = jnp.concatenate([small[1]] * GROUP, axis=0)
    twist_im = jnp.concatenate([small[2]] * GROUP, axis=0)
    number = lax.broadcasted_iota(jnp.int32, (SUB, VROWS), 0)
    l_row = (4 * (number % 8) + number // 8 - SUB // 2).astype(jnp.float32) / SUB
    l_col = (number - SUB // 2).astype(jnp.float32) / SUB
    d_row = l_row * l_row
    d_col = l_col * l_col

    def images(g, first=False):
        for quad in range(GROUP // 4):
            x_hi, x_lo, columns = [], [], []
            for j in range(4):
                n = g * GROUP + quad * 4 + j
                u = coords[0, pl.ds(n, 1), :]
                v = coords[1, pl.ds(n, 1), :]
                w = coords[2, pl.ds(n, 1), :]
                vis_re = vis[pl.ds(2 * n, 1), :]
                vis_im = vis[pl.ds(2 * n + 1, 1), :]
                cos_row, sin_row = cos_sin(u * l_row + w * d_row)
                cos_col, sin_col = cos_sin(v * l_col + w * d_col)
                x = jnp.concatenate(
                    [
                        vis_re * cos_row - vis_im * sin_row,
                        vis_re * sin_row + vis_im * cos_row,
                    ],
                    axis=1,
                )
                hi, lo = split(x)
                x_hi.append(hi)
                x_lo.append(lo)
                columns.append(split(cos_col) + split(sin_col))
            c_hi, c_lo, s_hi, s_lo = zip(*columns)

            def matrix(c, s):
                real = [jnp.concatenate([a, -b], axis=1) for a, b in zip(c, s)]
                imag = [jnp.concatenate([b, a], axis=1) for a, b in zip(c, s)]
                return jnp.concatenate(real + imag, axis=0)

            lhs = jnp.concatenate(x_hi + x_lo, axis=0)
            both = dot(lhs, matrix(c_hi, s_hi), True)
            sums = both[:128] + both[128:] + dot(lhs[:128], matrix(c_lo, s_lo), True)
            if first and quad == 0:
                await_beams(g)
            for j in range(4):
                n = g * GROUP + quad * 4 + j
                flat = []
                for c in range(2):
                    value = None
                    for i in range(4):
                        piece = sums[32 * j + 8 * i : 32 * j + 8 * i + 8, 128 * c : 128 * c + 128]
                        if i != j:
                            piece = pltpu.roll(piece, (SUB * (i - j)) % 128, 1)
                        value = piece if value is None else jnp.where(lane_group == i, piece, value)
                    flat.append(value)
                one_re = beam_buf[2 * n, pl.ds(0, 8, stride=2), :]
                one_im = beam_buf[2 * n, pl.ds(1, 8, stride=2), :]
                two_re = beam_buf[2 * n + 1, pl.ds(0, 8, stride=2), :]
                two_im = beam_buf[2 * n + 1, pl.ds(1, 8, stride=2), :]
                beam_re = taper * (one_re * two_re + one_im * two_im)
                beam_im = taper * (one_im * two_re - one_re * two_im)
                sky_re = beam_re * flat[0] - beam_im * flat[1]
                sky_im = beam_re * flat[1] + beam_im * flat[0]
                in_use = n < live
                place = (quad * 4 + j) * 8
                sky[g & 1, place : place + 8, :] = jnp.where(in_use, sky_re, 0.0)
                sky[g & 1, place + 8 * GROUP : place + 8 * GROUP + 8, :] = jnp.where(in_use, sky_im, 0.0)

    def cells(g):
        hi, lo = split(sky[g & 1])
        z = table_times(left_hi[...], left_lo[...], hi, lo)
        z_re, z_im = z[: 8 * GROUP], z[8 * GROUP :]
        y_re = z_re * twist_re - z_im * twist_im
        y_im = z_re * twist_im + z_im * twist_re
        hi, lo = split(jnp.concatenate([y_re, y_im], axis=1))
        result = times_table(hi, lo, right_hi[...], right_lo[...])
        for j in range(GROUP):
            n = g * GROUP + j
            band = row_s[n] >> 3
            shift = row_s[n] & 7
            rank = ranks[band]
            ranks[band] = rank + 1
            late = sublane < shift
            last = jnp.minimum(band + 4, owners - 1)
            for c in range(2):
                value = result[8 * j : 8 * j + 8, 128 * c : 128 * c + 128]
                spread = jnp.where(late & (lane_group == 0), 0.0, value)
                tile = 2 * rank + c
                for o in range(4):
                    pltpu.store(out.at[band + o, tile], spread, mask=lane_group == o)
                part = tile & 3
                tail = pltpu.roll(value, SUB * part, 1)
                pltpu.store(
                    out.at[last, 2 * cap + (tile >> 2)], tail, mask=late & (lane_group == part)
                )
            column = jnp.full((8, 128), owner_s[n] * tile_cols + col_s[n], jnp.float32)
            for o in range(5):
                here = (sublane == 0) & (lane == label_lane + o * cap + rank)
                if o == 4:
                    here = here & (sublane < shift)
                target = last if o == 4 else band + o
                pltpu.store(out.at[target, label_tile], column, mask=here)

    images(0, True)
    for copy in copies[6:10] + [copies[0], copies[2]]:
        copy.wait()

    @pl.loop(1, groups)
    def _(g):
        await_beams(g)
        fetch_beams(g + 1)
        cells(g - 1)
        images(g)

    cells(groups - 1)
    await_beams(groups)


def row_kernel(
    cap,
    received,
    first,
    second,
    twist,
    out,
    *scratch,
):
    grids, (label_v, label_s, sem, middle, held, out_sems) = scratch[:2], scratch[2:]
    sources = received.shape[0]
    label_tile = 2 * cap + (2 * cap) // 4
    label_lane = SUB * ((2 * cap) % 4)
    label_v[...] = received[:, label_tile, 0, :].astype(jnp.int32)
    copy = pltpu.make_async_copy(label_v, label_s, sem)
    copy.start()
    for grid in grids:
        grid[...] = jnp.zeros_like(grid)
    lane = lax.broadcasted_iota(jnp.int32, (8, 128), 1)
    copy.wait()

    @pl.loop(0, sources)
    def _(source):
        for i in range(cap):
            for o in range(5):
                column = label_s[source, label_lane + o * cap + i]
                offset = column & 127
                here = pl.multiple_of((column >> 7) * 8, 8)
                place = lane - offset
                inside = (place >= 0) & (place < SUB)
                beyond = place < SUB - 128
                added = []
                for c in range(2):
                    if o < 4:
                        value, part = received[source, 2 * i + c], o
                    else:
                        value = received[source, 2 * cap + (2 * i + c) // 4]
                        part = (2 * i + c) % 4
                    value = pltpu.roll(value, (offset - SUB * part) & 127, 1)
                    added.append(jnp.where(inside, value, 0.0))
                    added.append(jnp.where(beyond, value, 0.0))
                before = [
                    grids[c][pl.ds(here + 8 * k, 8), :] for c in range(2) for k in range(2)
                ]
                for c in range(2):
                    for k in range(2):
                        grids[c][pl.ds(here + 8 * k, 8), :] = before[2 * c + k] + added[2 * c + k]

    for pair in range(ROWS_DEV // 2):
        halves_of = []
        for e in range(2):
            rows = [
                pl.ds(ROWS_DEV * e + 2 * pair + k, TAIL, stride=2 * ROWS_DEV) for k in range(2)
            ]
            value = jnp.concatenate(
                [jnp.concatenate([grids[c][at, :] for at in rows], axis=1) for c in range(2)], 0
            )
            hi, lo = split(value)
            halves_of.append(table_times(first[2 * e], first[2 * e + 1], hi, lo))
        for h, a in enumerate((halves_of[0] + halves_of[1], halves_of[0] - halves_of[1])):
            turn_re = twist[0, TAIL * h : TAIL * h + TAIL]
            turn_im = twist[1, TAIL * h : TAIL * h + TAIL]
            for k in range(2):
                a_re = a[:TAIL, 128 * k : 128 * k + 128]
                a_im = a[TAIL:, 128 * k : 128 * k + 128]
                b = jnp.concatenate(
                    [a_re * turn_re - a_im * turn_im, a_re * turn_im + a_im * turn_re], axis=1
                )
                for part, value in enumerate(split(b)):
                    middle[h, pair, part, TAIL * k : TAIL * k + TAIL, :] = value

    copies = []
    for h in range(2):
        for pair in range(ROWS_DEV // 2):
            result = table_times(
                second[0], second[1], middle[h, pair, 0], middle[h, pair, 1], True
            )
            for c in range(2):
                for k in range(2):
                    held[h, c, pl.ds(2 * pair + k, TAIL, stride=ROWS_DEV), :] = result[
                        128 * c : 128 * c + 128, 128 * k : 128 * k + 128
                    ]
        for c in range(2):
            copies.append(
                pltpu.make_async_copy(
                    held.at[h, c].reshape(TAIL, ROWS_DEV, TAIL),
                    out.at[c, :, h],
                    out_sems.at[h, c],
                )
            )
            copies[-1].start()
    for copy in copies:
        copy.wait()


def shards(
    visibility, coords, block_owner, block_row, block_col, stations, block_count, beam_terms
):
    owners = lax.axis_size("tile")
    per_device = visibility.shape[0]
    tile_cols = NG // owners
    cap, tiles = send_layout(per_device, owners)
    stations_all = beam_terms.shape[0]
    vmem = pl.BlockSpec(memory_space=pltpu.VMEM)
    beams = (
        beam_terms.reshape(stations_all, 2, 8, 128)
        .transpose(0, 2, 1, 3)
        .reshape(stations_all, 16, 128)
    )
    labels = (
        block_owner.reshape(per_device),
        block_row,
        block_col,
        stations.T,
    )
    values = (
        visibility.reshape(per_device * 2, VROWS),
        coords.transpose(1, 0, 2),
        *image_tables(),
    )
    hbm = pl.BlockSpec(memory_space=pltpu.HBM)
    sent = pl.pallas_call(
        functools.partial(image_kernel, cap, tile_cols),
        out_shape=jax.ShapeDtypeStruct((owners, tiles, 8, 128), jnp.float32),
        in_specs=[pl.BlockSpec(memory_space=pltpu.SMEM)] + [hbm] * (1 + len(labels) + len(values)),
        out_specs=vmem,
        scratch_shapes=[
            *(pltpu.SMEM(label.shape, label.dtype) for label in labels),
            *(pltpu.VMEM(value.shape, value.dtype) for value in values),
            pltpu.VMEM((2 * (per_device + GROUP), 16, 128), jnp.float32),
            pltpu.VMEM((2, 16 * GROUP, 128), jnp.float32),
            pltpu.SMEM((owners,), jnp.int32),
            pltpu.SemaphoreType.DMA((per_device // GROUP + 1,)),
            pltpu.SemaphoreType.DMA((len(labels) + len(values),)),
        ],
        compiler_params=pltpu.CompilerParams(vmem_limit_bytes=24 * 1024 * 1024),
        name="image",
    )(
        block_count,
        *(pltpu.with_memory_space_constraint(x, pltpu.HBM) for x in (beams, *labels, *values)),
    )
    received = lax.all_to_all(sent, "tile", split_axis=0, concat_axis=0, tiled=True)
    result = pl.pallas_call(
        functools.partial(row_kernel, cap),
        out_shape=jax.ShapeDtypeStruct((2, TAIL, 2, ROWS_DEV, TAIL), jnp.float32),
        in_specs=[vmem] * 4,
        out_specs=pl.BlockSpec(memory_space=pl.ANY),
        scratch_shapes=[
            *(pltpu.VMEM(((LEAD + 1) * ROWS_DEV, TAIL), jnp.float32) for _ in range(2)),
            pltpu.VMEM((owners, 128), jnp.int32),
            pltpu.SMEM((owners, 128), jnp.int32),
            pltpu.SemaphoreType.DMA,
            pltpu.VMEM((2, ROWS_DEV // 2, 2, 2 * TAIL, 2 * TAIL), jnp.bfloat16),
            pltpu.VMEM((2, 2, TAIL * ROWS_DEV, TAIL), jnp.float32),
            pltpu.SemaphoreType.DMA((2, 2)),
        ],
        compiler_params=pltpu.CompilerParams(vmem_limit_bytes=24 * 1024 * 1024),
        name="rows",
    )(received, *row_tables())
    return (
        result.reshape(2, LEAD, ROWS_DEV, TAIL).transpose(0, 2, 1, 3).reshape(2, ROWS_DEV, NG)
    )


def solution(mesh):
    placed = (
        P(("parts", "tile"), None, None),
        P(("parts", "tile"), None, None),
        P(("parts", "tile"), None),
        P(("parts", "tile")),
        P(("parts", "tile")),
        P(("parts", "tile"), None),
        P(("parts", "tile")),
        P(),
    )
    return jax.shard_map(
        shards,
        mesh=mesh,
        in_specs=placed,
        out_specs=P(None, ("parts", "tile"), None),
        check_vma=False,
    )
```

```python
import functools
import math

import jax
import jax.numpy as jnp
import ml_dtypes
import numpy as np
from jax import lax
from jax.experimental import pallas as pl
from jax.experimental.pallas import tpu as pltpu
from jax.sharding import PartitionSpec as P

VROWS = 128
SUB = 32
NG = 32768
ROWS_DEV = 8
LEAD = 256
TAIL = 128
GROUP = 16

SIN_TERMS = (4.442879549, -7.307815317, 3.597759608, -0.791160565)
COS_TERMS = (1.414213500, -6.978850910, 5.739459580, -1.883552820, 0.310677860)


def halves(table):
    table = np.round(table, 12).astype(np.float32)
    high = table.astype(ml_dtypes.bfloat16)
    low = (table - high.astype(np.float32)).astype(ml_dtypes.bfloat16)
    return high, low


def root(numbers, length):
    angle = 2.0 * np.pi / length * (numbers % length)
    return np.cos(angle), -np.sin(angle)


def complex_left(re, im):
    return np.block([[re, -im], [im, re]])


@functools.cache
def image_tables():
    eight = np.arange(8)
    re, im = root(np.outer(eight, eight), 8)
    left = complex_left(np.kron(np.eye(GROUP), re), np.kron(np.eye(GROUP), im))
    lane = np.arange(128)
    twist = root(np.outer(eight, lane // SUB), SUB)
    four = 8 * np.outer(lane // SUB, lane // SUB) + np.outer(lane % SUB, lane % SUB)
    re, im = root(four, SUB)
    right = complex_left(re, im).T
    row_pos = ((4 * eight[:, None] + lane[None, :] // SUB) - SUB // 2) / SUB
    col_pos = np.broadcast_to((lane[None, :] % SUB - SUB // 2) / SUB, (8, 128))
    taper = (1 - 2 * row_pos**2) * (1 - 2 * col_pos**2) / SUB
    small = np.stack([taper, np.round(twist[0], 12), np.round(twist[1], 12)]).astype(np.float32)
    return (*halves(left), *halves(right), small)


@functools.cache
def row_tables():
    lead, tail = np.arange(LEAD), np.arange(TAIL)
    even = complex_left(*root(np.outer(tail, tail), TAIL))
    odd = complex_left(*root(np.outer(tail, 2 * tail + 1), LEAD))
    twist = np.stack(root(np.outer(lead, tail), NG)) / math.sqrt(NG)
    first = np.stack(halves(even) + halves(odd))
    return first, np.stack(halves(even)), np.round(twist, 12).astype(np.float32)


def split(value):
    high = value.astype(jnp.bfloat16)
    return high, (value - high.astype(jnp.float32)).astype(jnp.bfloat16)


def dot(left, right, transposed=False):
    dims = (((1,), (1 if transposed else 0,)), ((), ()))
    return lax.dot_general(left, right, dims, preferred_element_type=jnp.float32)


def table_times(table_hi, table_lo, hi, lo, transposed=False):
    rows = table_hi.shape[0]
    both = dot(jnp.concatenate([table_hi, table_lo], axis=0), hi, transposed)
    return both[:rows] + both[rows:] + dot(table_hi, lo, transposed)


def times_table(hi, lo, table_hi, table_lo):
    rows = hi.shape[0]
    both = dot(jnp.concatenate([hi, lo], axis=0), table_hi)
    return both[:rows] + both[rows:] + dot(hi, table_lo)


def polynomial(terms, z):
    value = z * terms[-1] + terms[-2]
    for term in terms[-3::-1]:
        value = value * z + term
    return value


def cos_sin(turns):
    whole = (turns + 12582912.0) - 12582912.0
    t = turns - whole
    z = t * t
    half_sin = t * polynomial(SIN_TERMS, z)
    half_cos = polynomial(COS_TERMS, z)
    return 1.0 - half_sin * half_sin, half_sin * half_cos


def send_layout(per_device, owners):
    cap = -(-per_device // (owners - SUB // ROWS_DEV + 1))
    tiles = 2 * cap + (2 * cap + 1 + 3) // 4
    return cap, tiles


def exchange_order(chips):
    quarter = chips // 4
    far = [k + part for k in range(quarter) for part in (3 * quarter, 2 * quarter)]
    near = list(range(chips // 2 - 1, 0, -1))
    return [0] + far[:3] + near[:1] + far[3:] + near[1:]


def image_kernel(
    cap,
    tile_cols,
    *refs,
):
    me = lax.axis_index("tile")
    owners = lax.axis_size("tile")
    count_s, beams, args, keep, give = refs[0], refs[1], refs[2:13], refs[13], refs[14]
    copied, (out, beam_buf, sky, ranks, sems, arg_sems) = refs[15:26], refs[26:]
    copies = [
        pltpu.make_async_copy(arg, held, arg_sems.at[k])
        for k, (arg, held) in enumerate(zip(args, copied))
    ]
    for copy in copies:
        copy.start()
    owner_s, row_s, col_s, station_s, vis, coords = copied[:6]
    left_hi, left_lo, right_hi, right_lo, small = copied[6:]
    per_device = vis.shape[0] // 2
    label_tile = 2 * cap + (2 * cap) // 4
    label_lane = SUB * ((2 * cap) % 4)
    sublane = lax.broadcasted_iota(jnp.int32, (8, 128), 0)
    lane = lax.broadcasted_iota(jnp.int32, (8, 128), 1)
    lane_group = lane // SUB
    out[...] = jnp.zeros_like(out)
    spread_columns = ((lane - label_lane) * (NG // SUB)).astype(jnp.float32)
    is_label = (sublane == 0) & (lane >= label_lane) & (lane < label_lane + SUB)
    for d in range(owners):
        out[d, label_tile] = jnp.where(is_label, spread_columns, 0.0)
    sky[...] = jnp.zeros_like(sky)
    for b in range(owners):
        ranks[b] = 0
    copies[3].wait()
    copies[1].wait()
    live = count_s[0]
    groups = (live + GROUP - 1) >> (GROUP.bit_length() - 1)

    def fetch_beams(g):
        for j in range(GROUP):
            n = jnp.minimum(g, per_device // GROUP - 1) * GROUP + j
            for side in range(2):
                pltpu.make_async_copy(
                    beams.at[station_s[side, n]],
                    beam_buf.at[2 * (g * GROUP + j) + side],
                    sems.at[g],
                ).start()

    def await_beams(g):
        waited = beam_buf.at[pl.ds(g * 2 * GROUP, 2 * GROUP)]
        pltpu.make_async_copy(beams.at[pl.ds(0, 2 * GROUP)], waited, sems.at[g]).wait()

    for g in range(2):
        fetch_beams(g)
    copies[4].wait()
    copies[5].wait()
    copies[10].wait()

    @pl.loop(0, groups * (GROUP // 8))
    def _(g):
        for j in range(8):
            n = g * 8 + j
            shift = row_s[n] & 7
            coords[0, pl.ds(n, 1), :] += shift.astype(jnp.float32)
            vis[pl.ds(2 * n, 2), :] *= (1 - 2 * (shift & 1)).astype(jnp.float32)

    taper = small[0]
    twist_re = jnp.concatenate([small[1]] * GROUP, axis=0)
    twist_im = jnp.concatenate([small[2]] * GROUP, axis=0)
    number = lax.broadcasted_iota(jnp.int32, (SUB, VROWS), 0)
    l_row = (4 * (number % 8) + number // 8 - SUB // 2).astype(jnp.float32) / SUB
    l_col = (number - SUB // 2).astype(jnp.float32) / SUB
    d_row = l_row * l_row
    d_col = l_col * l_col

    def images(g, first=False):
        for quad in range(GROUP // 4):
            x_hi, x_lo, columns = [], [], []
            for j in range(4):
                n = g * GROUP + quad * 4 + j
                u = coords[0, pl.ds(n, 1), :]
                v = coords[1, pl.ds(n, 1), :]
                w = coords[2, pl.ds(n, 1), :]
                vis_re = vis[pl.ds(2 * n, 1), :]
                vis_im = vis[pl.ds(2 * n + 1, 1), :]
                cos_row, sin_row = cos_sin(u * l_row + w * d_row)
                cos_col, sin_col = cos_sin(v * l_col + w * d_col)
                x = jnp.concatenate(
                    [
                        vis_re * cos_row - vis_im * sin_row,
                        vis_re * sin_row + vis_im * cos_row,
                    ],
                    axis=1,
                )
                hi, lo = split(x)
                x_hi.append(hi)
                x_lo.append(lo)
                columns.append(split(cos_col) + split(sin_col))
            c_hi, c_lo, s_hi, s_lo = zip(*columns)

            def matrix(c, s):
                real = [jnp.concatenate([a, -b], axis=1) for a, b in zip(c, s)]
                imag = [jnp.concatenate([b, a], axis=1) for a, b in zip(c, s)]
                return jnp.concatenate(real + imag, axis=0)

            lhs = jnp.concatenate(x_hi + x_lo, axis=0)
            both = dot(lhs, matrix(c_hi, s_hi), True)
            sums = both[:128] + both[128:] + dot(lhs[:128], matrix(c_lo, s_lo), True)
            if first and quad == 0:
                await_beams(g)
            for j in range(4):
                n = g * GROUP + quad * 4 + j
                flat = []
                for c in range(2):
                    value = None
                    for i in range(4):
                        piece = sums[32 * j + 8 * i : 32 * j + 8 * i + 8, 128 * c : 128 * c + 128]
                        if i != j:
                            piece = pltpu.roll(piece, (SUB * (i - j)) % 128, 1)
                        value = piece if value is None else jnp.where(lane_group == i, piece, value)
                    flat.append(value)
                one_re = beam_buf[2 * n, pl.ds(0, 8, stride=2), :]
                one_im = beam_buf[2 * n, pl.ds(1, 8, stride=2), :]
                two_re = beam_buf[2 * n + 1, pl.ds(0, 8, stride=2), :]
                two_im = beam_buf[2 * n + 1, pl.ds(1, 8, stride=2), :]
                beam_re = taper * (one_re * two_re + one_im * two_im)
                beam_im = taper * (one_im * two_re - one_re * two_im)
                sky_re = beam_re * flat[0] - beam_im * flat[1]
                sky_im = beam_re * flat[1] + beam_im * flat[0]
                in_use = n < live
                place = (quad * 4 + j) * 8
                sky[g & 1, place : place + 8, :] = jnp.where(in_use, sky_re, 0.0)
                sky[g & 1, place + 8 * GROUP : place + 8 * GROUP + 8, :] = jnp.where(in_use, sky_im, 0.0)

    def cells(g):
        hi, lo = split(sky[g & 1])
        z = table_times(left_hi[...], left_lo[...], hi, lo)
        z_re, z_im = z[: 8 * GROUP], z[8 * GROUP :]
        y_re = z_re * twist_re - z_im * twist_im
        y_im = z_re * twist_im + z_im * twist_re
        hi, lo = split(jnp.concatenate([y_re, y_im], axis=1))
        result = times_table(hi, lo, right_hi[...], right_lo[...])
        for j in range(GROUP):
            n = g * GROUP + j
            band = row_s[n] >> 3
            shift = row_s[n] & 7
            rank = ranks[band]
            ranks[band] = rank + 1
            late = sublane < shift
            last = jnp.minimum(band + 4, owners - 1)
            for c in range(2):
                value = result[8 * j : 8 * j + 8, 128 * c : 128 * c + 128]
                spread = jnp.where(late & (lane_group == 0), 0.0, value)
                tile = 2 * rank + c
                for o in range(4):
                    pltpu.store(out.at[(band + o) ^ me, tile], spread, mask=lane_group == o)
                part = tile & 3
                tail = pltpu.roll(value, SUB * part, 1)
                pltpu.store(
                    out.at[last ^ me, 2 * cap + (tile >> 2)], tail, mask=late & (lane_group == part)
                )
            column = jnp.full((8, 128), owner_s[n] * tile_cols + col_s[n], jnp.float32)
            for o in range(5):
                here = (sublane == 0) & (lane == label_lane + o * cap + rank)
                if o == 4:
                    here = here & (sublane < shift)
                target = last if o == 4 else band + o
                pltpu.store(out.at[target ^ me, label_tile], column, mask=here)

    images(0, True)
    for copy in copies[6:10] + [copies[0], copies[2]]:
        copy.wait()

    @pl.loop(1, groups)
    def _(g):
        await_beams(g)
        fetch_beams(g + 1)
        cells(g - 1)
        images(g)

    cells(groups - 1)
    await_beams(groups)
    for k in range(owners // 2):
        keep[k] = out[2 * k]
        give[k] = out[2 * k + 1]


def merge_kernel(keep, got, *messages):
    for k, message in zip(exchange_order(keep.shape[0]), messages):
        message[0] = keep[k]
        message[1] = got[k]


def row_kernel(
    cap,
    first,
    second,
    twist,
    *refs,
):
    sources = lax.axis_size("tile")
    messages, out, received = refs[: sources // 2], refs[sources // 2], refs[sources // 2 + 1]
    scratch = refs[sources // 2 + 2 :]
    grids, (label_v, label_s, sem, middle, held, out_sems) = scratch[:2], scratch[2:]
    for k, message in enumerate(messages):
        received[2 * k] = message[0]
        received[2 * k + 1] = message[1]
    label_tile = 2 * cap + (2 * cap) // 4
    label_lane = SUB * ((2 * cap) % 4)
    label_v[...] = received[:, label_tile, 0, :].astype(jnp.int32)
    copy = pltpu.make_async_copy(label_v, label_s, sem)
    copy.start()
    for grid in grids:
        grid[...] = jnp.zeros_like(grid)
    lane = lax.broadcasted_iota(jnp.int32, (8, 128), 1)
    copy.wait()

    @pl.loop(0, sources)
    def _(source):
        for i in range(cap):
            for o in range(5):
                column = label_s[source, label_lane + o * cap + i]
                offset = column & 127
                here = pl.multiple_of((column >> 7) * 8, 8)
                place = lane - offset
                inside = (place >= 0) & (place < SUB)
                beyond = place < SUB - 128
                added = []
                for c in range(2):
                    if o < 4:
                        value, part = received[source, 2 * i + c], o
                    else:
                        value = received[source, 2 * cap + (2 * i + c) // 4]
                        part = (2 * i + c) % 4
                    value = pltpu.roll(value, (offset - SUB * part) & 127, 1)
                    added.append(jnp.where(inside, value, 0.0))
                    added.append(jnp.where(beyond, value, 0.0))
                before = [
                    grids[c][pl.ds(here + 8 * k, 8), :] for c in range(2) for k in range(2)
                ]
                for c in range(2):
                    for k in range(2):
                        grids[c][pl.ds(here + 8 * k, 8), :] = before[2 * c + k] + added[2 * c + k]

    for pair in range(ROWS_DEV // 2):
        halves_of = []
        for e in range(2):
            rows = [
                pl.ds(ROWS_DEV * e + 2 * pair + k, TAIL, stride=2 * ROWS_DEV) for k in range(2)
            ]
            value = jnp.concatenate(
                [jnp.concatenate([grids[c][at, :] for at in rows], axis=1) for c in range(2)], 0
            )
            hi, lo = split(value)
            halves_of.append(table_times(first[2 * e], first[2 * e + 1], hi, lo))
        for h, a in enumerate((halves_of[0] + halves_of[1], halves_of[0] - halves_of[1])):
            turn_re = twist[0, TAIL * h : TAIL * h + TAIL]
            turn_im = twist[1, TAIL * h : TAIL * h + TAIL]
            for k in range(2):
                a_re = a[:TAIL, 128 * k : 128 * k + 128]
                a_im = a[TAIL:, 128 * k : 128 * k + 128]
                b = jnp.concatenate(
                    [a_re * turn_re - a_im * turn_im, a_re * turn_im + a_im * turn_re], axis=1
                )
                for part, value in enumerate(split(b)):
                    middle[h, pair, part, TAIL * k : TAIL * k + TAIL, :] = value

    copies = []
    for h in range(2):
        for pair in range(ROWS_DEV // 2):
            result = table_times(
                second[0], second[1], middle[h, pair, 0], middle[h, pair, 1], True
            )
            for c in range(2):
                for k in range(2):
                    held[h, c, pl.ds(2 * pair + k, TAIL, stride=ROWS_DEV), :] = result[
                        128 * c : 128 * c + 128, 128 * k : 128 * k + 128
                    ]
        for c in range(2):
            copies.append(
                pltpu.make_async_copy(
                    held.at[h, c].reshape(TAIL, ROWS_DEV, TAIL),
                    out.at[c, :, h],
                    out_sems.at[h, c],
                )
            )
            copies[-1].start()
    for copy in copies:
        copy.wait()


def shards(
    visibility, coords, block_owner, block_row, block_col, stations, block_count, beam_terms
):
    owners = lax.axis_size("tile")
    per_device = visibility.shape[0]
    tile_cols = NG // owners
    cap, tiles = send_layout(per_device, owners)
    stations_all = beam_terms.shape[0]
    vmem = pl.BlockSpec(memory_space=pltpu.VMEM)
    beams = (
        beam_terms.reshape(stations_all, 2, 8, 128)
        .transpose(0, 2, 1, 3)
        .reshape(stations_all, 16, 128)
    )
    labels = (
        block_owner.reshape(per_device),
        block_row,
        block_col,
        stations.T,
    )
    values = (
        visibility.reshape(per_device * 2, VROWS),
        coords.transpose(1, 0, 2),
        *image_tables(),
    )
    hbm = pl.BlockSpec(memory_space=pltpu.HBM)
    half = jax.ShapeDtypeStruct((owners // 2, tiles, 8, 128), jnp.float32)
    keep, give = pl.pallas_call(
        functools.partial(image_kernel, cap, tile_cols),
        out_shape=[half] * 2,
        in_specs=[pl.BlockSpec(memory_space=pltpu.SMEM)] + [hbm] * (1 + len(labels) + len(values)),
        out_specs=[vmem] * 2,
        scratch_shapes=[
            *(pltpu.SMEM(label.shape, label.dtype) for label in labels),
            *(pltpu.VMEM(value.shape, value.dtype) for value in values),
            pltpu.VMEM((owners, tiles, 8, 128), jnp.float32),
            pltpu.VMEM((2 * (per_device + GROUP), 16, 128), jnp.float32),
            pltpu.VMEM((2, 16 * GROUP, 128), jnp.float32),
            pltpu.SMEM((owners,), jnp.int32),
            pltpu.SemaphoreType.DMA((per_device // GROUP + 1,)),
            pltpu.SemaphoreType.DMA((len(labels) + len(values),)),
        ],
        compiler_params=pltpu.CompilerParams(vmem_limit_bytes=24 * 1024 * 1024),
        name="image",
    )(
        block_count,
        *(pltpu.with_memory_space_constraint(x, pltpu.HBM) for x in (beams, *labels, *values)),
    )
    got = lax.ppermute(give, "tile", [(source, source ^ 1) for source in range(owners)])
    messages = pl.pallas_call(
        merge_kernel,
        out_shape=[jax.ShapeDtypeStruct((2, tiles, 8, 128), jnp.float32)] * (owners // 2),
        in_specs=[vmem] * 2,
        out_specs=[vmem] * (owners // 2),
        compiler_params=pltpu.CompilerParams(vmem_limit_bytes=24 * 1024 * 1024),
        name="merge",
    )(keep, got)
    received = [messages[0]] + [
        lax.ppermute(message, "tile", [(source, source ^ (2 * k)) for source in range(owners)])
        for message, k in zip(messages[1:], exchange_order(owners // 2)[1:])
    ]
    result = pl.pallas_call(
        functools.partial(row_kernel, cap),
        out_shape=jax.ShapeDtypeStruct((2, TAIL, 2, ROWS_DEV, TAIL), jnp.float32),
        in_specs=[vmem] * (3 + owners // 2),
        out_specs=pl.BlockSpec(memory_space=pl.ANY),
        scratch_shapes=[
            pltpu.VMEM((owners, tiles, 8, 128), jnp.float32),
            *(pltpu.VMEM(((LEAD + 1) * ROWS_DEV, TAIL), jnp.float32) for _ in range(2)),
            pltpu.VMEM((owners, 128), jnp.int32),
            pltpu.SMEM((owners, 128), jnp.int32),
            pltpu.SemaphoreType.DMA,
            pltpu.VMEM((2, ROWS_DEV // 2, 2, 2 * TAIL, 2 * TAIL), jnp.bfloat16),
            pltpu.VMEM((2, 2, TAIL * ROWS_DEV, TAIL), jnp.float32),
            pltpu.SemaphoreType.DMA((2, 2)),
        ],
        compiler_params=pltpu.CompilerParams(vmem_limit_bytes=24 * 1024 * 1024),
        name="rows",
    )(*row_tables(), *received)
    return (
        result.reshape(2, LEAD, ROWS_DEV, TAIL).transpose(0, 2, 1, 3).reshape(2, ROWS_DEV, NG)
    )


def solution(mesh):
    placed = (
        P(("parts", "tile"), None, None),
        P(("parts", "tile"), None, None),
        P(("parts", "tile"), None),
        P(("parts", "tile")),
        P(("parts", "tile")),
        P(("parts", "tile"), None),
        P(("parts", "tile")),
        P(),
    )
    return jax.shard_map(
        shards,
        mesh=mesh,
        in_specs=placed,
        out_specs=P(None, ("parts", "tile"), None),
        check_vma=False,
    )
```

```python
import functools
import math

import jax
import jax.numpy as jnp
import ml_dtypes
import numpy as np
from jax import lax
from jax.experimental import pallas as pl
from jax.experimental.pallas import tpu as pltpu
from jax.sharding import PartitionSpec as P

VROWS = 128
SUB = 32
NG = 32768
ROWS_DEV = 8
LEAD = 256
TAIL = 128
GROUP = 16

SIN_TERMS = (4.442879549, -7.307815317, 3.597759608, -0.791160565)
COS_TERMS = (1.414213500, -6.978850910, 5.739459580, -1.883552820, 0.310677860)


def halves(table):
    table = np.round(table, 12).astype(np.float32)
    high = table.astype(ml_dtypes.bfloat16)
    low = (table - high.astype(np.float32)).astype(ml_dtypes.bfloat16)
    return high, low


def root(numbers, length):
    angle = 2.0 * np.pi / length * (numbers % length)
    return np.cos(angle), -np.sin(angle)


def complex_left(re, im):
    return np.block([[re, -im], [im, re]])


@functools.cache
def image_tables():
    eight = np.arange(8)
    re, im = root(np.outer(eight, eight), 8)
    left = complex_left(np.kron(np.eye(GROUP), re), np.kron(np.eye(GROUP), im))
    lane = np.arange(128)
    twist = root(np.outer(eight, lane // SUB), SUB)
    four = 8 * np.outer(lane // SUB, lane // SUB) + np.outer(lane % SUB, lane % SUB)
    re, im = root(four, SUB)
    right = complex_left(re, im).T
    row_pos = ((4 * eight[:, None] + lane[None, :] // SUB) - SUB // 2) / SUB
    col_pos = np.broadcast_to((lane[None, :] % SUB - SUB // 2) / SUB, (8, 128))
    taper = (1 - 2 * row_pos**2) * (1 - 2 * col_pos**2) / SUB
    small = np.stack([taper, np.round(twist[0], 12), np.round(twist[1], 12)]).astype(np.float32)
    return (*halves(left), *halves(right), small)


@functools.cache
def row_tables():
    lead, tail = np.arange(LEAD), np.arange(TAIL)
    even = complex_left(*root(np.outer(tail, tail), TAIL))
    odd = complex_left(*root(np.outer(tail, 2 * tail + 1), LEAD))
    twist = np.stack(root(np.outer(lead, tail), NG)) / math.sqrt(NG)
    first = np.stack(halves(even) + halves(odd))
    return first, np.stack(halves(even)), np.round(twist, 12).astype(np.float32)


def split(value):
    high = value.astype(jnp.bfloat16)
    return high, (value - high.astype(jnp.float32)).astype(jnp.bfloat16)


def dot(left, right, transposed=False):
    dims = (((1,), (1 if transposed else 0,)), ((), ()))
    return lax.dot_general(left, right, dims, preferred_element_type=jnp.float32)


def table_times(table_hi, table_lo, hi, lo, transposed=False):
    rows = table_hi.shape[0]
    both = dot(jnp.concatenate([table_hi, table_lo], axis=0), hi, transposed)
    return both[:rows] + both[rows:] + dot(table_hi, lo, transposed)


def times_table(hi, lo, table_hi, table_lo):
    rows = hi.shape[0]
    both = dot(jnp.concatenate([hi, lo], axis=0), table_hi)
    return both[:rows] + both[rows:] + dot(hi, table_lo)


def polynomial(terms, z):
    value = z * terms[-1] + terms[-2]
    for term in terms[-3::-1]:
        value = value * z + term
    return value


def cos_sin(turns):
    whole = (turns + 12582912.0) - 12582912.0
    t = turns - whole
    z = t * t
    half_sin = t * polynomial(SIN_TERMS, z)
    half_cos = polynomial(COS_TERMS, z)
    return 1.0 - half_sin * half_sin, half_sin * half_cos


def send_layout(per_device, owners):
    cap = -(-per_device // (owners - SUB // ROWS_DEV + 1))
    tiles = 2 * cap + (2 * cap + 1 + 3) // 4
    return cap, tiles


def exchange_order(chips):
    quarter = chips // 4
    far = [k + part for k in range(quarter) for part in (3 * quarter, 2 * quarter)]
    near = list(range(chips // 2 - 1, 0, -1))
    return [0] + far[:3] + near[:1] + far[3:] + near[1:]


def image_kernel(
    cap,
    tile_cols,
    *refs,
):
    me = lax.axis_index("tile")
    owners = lax.axis_size("tile")
    count_s, beams, args, keep, give = refs[0], refs[1], refs[2:13], refs[13], refs[14]
    copied, (out, beam_buf, sky, ranks, sems, arg_sems) = refs[15:26], refs[26:]
    copies = [
        pltpu.make_async_copy(arg, held, arg_sems.at[k])
        for k, (arg, held) in enumerate(zip(args, copied))
    ]
    for copy in copies:
        copy.start()
    owner_s, row_s, col_s, station_s, vis, coords = copied[:6]
    left_hi, left_lo, right_hi, right_lo, small = copied[6:]
    per_device = vis.shape[0] // 2
    label_tile = 2 * cap + (2 * cap) // 4
    label_lane = SUB * ((2 * cap) % 4)
    sublane = lax.broadcasted_iota(jnp.int32, (8, 128), 0)
    lane = lax.broadcasted_iota(jnp.int32, (8, 128), 1)
    lane_group = lane // SUB
    out[...] = jnp.zeros_like(out)
    spread_columns = ((lane - label_lane) * (NG // SUB)).astype(jnp.float32)
    is_label = (sublane == 0) & (lane >= label_lane) & (lane < label_lane + SUB)
    for d in range(owners):
        out[d, label_tile] = jnp.where(is_label, spread_columns, 0.0)
    sky[...] = jnp.zeros_like(sky)
    for b in range(owners):
        ranks[b] = 0
    copies[3].wait()
    copies[1].wait()
    live = count_s[0]
    groups = (live + GROUP - 1) >> (GROUP.bit_length() - 1)

    def fetch_beams(g):
        for j in range(GROUP):
            n = jnp.minimum(g, per_device // GROUP - 1) * GROUP + j
            for side in range(2):
                pltpu.make_async_copy(
                    beams.at[station_s[side, n]],
                    beam_buf.at[2 * (g * GROUP + j) + side],
                    sems.at[g],
                ).start()

    def await_beams(g):
        waited = beam_buf.at[pl.ds(g * 2 * GROUP, 2 * GROUP)]
        pltpu.make_async_copy(beams.at[pl.ds(0, 2 * GROUP)], waited, sems.at[g]).wait()

    for g in range(2):
        fetch_beams(g)
    copies[4].wait()
    copies[5].wait()
    copies[10].wait()

    @pl.loop(0, groups * (GROUP // 8))
    def _(g):
        for j in range(8):
            n = g * 8 + j
            shift = row_s[n] & 7
            coords[0, pl.ds(n, 1), :] += shift.astype(jnp.float32)
            vis[pl.ds(2 * n, 2), :] *= (1 - 2 * (shift & 1)).astype(jnp.float32)

    taper = small[0]
    twist_re = jnp.concatenate([small[1]] * GROUP, axis=0)
    twist_im = jnp.concatenate([small[2]] * GROUP, axis=0)
    number = lax.broadcasted_iota(jnp.int32, (SUB, VROWS), 0)
    l_row = (4 * (number % 8) + number // 8 - SUB // 2).astype(jnp.float32) / SUB
    l_col = (number - SUB // 2).astype(jnp.float32) / SUB
    d_row = l_row * l_row
    d_col = l_col * l_col

    def images(g, first=False):
        for quad in range(GROUP // 4):
            x_hi, x_lo, columns = [], [], []
            for j in range(4):
                n = g * GROUP + quad * 4 + j
                u = coords[0, pl.ds(n, 1), :]
                v = coords[1, pl.ds(n, 1), :]
                w = coords[2, pl.ds(n, 1), :]
                vis_re = vis[pl.ds(2 * n, 1), :]
                vis_im = vis[pl.ds(2 * n + 1, 1), :]
                cos_row, sin_row = cos_sin(u * l_row + w * d_row)
                cos_col, sin_col = cos_sin(v * l_col + w * d_col)
                x = jnp.concatenate(
                    [
                        vis_re * cos_row - vis_im * sin_row,
                        vis_re * sin_row + vis_im * cos_row,
                    ],
                    axis=1,
                )
                hi, lo = split(x)
                x_hi.append(hi)
                x_lo.append(lo)
                columns.append(split(cos_col) + split(sin_col))
            c_hi, c_lo, s_hi, s_lo = zip(*columns)

            def matrix(c, s):
                real = [jnp.concatenate([a, -b], axis=1) for a, b in zip(c, s)]
                imag = [jnp.concatenate([b, a], axis=1) for a, b in zip(c, s)]
                return jnp.concatenate(real + imag, axis=0)

            lhs = jnp.concatenate(x_hi + x_lo, axis=0)
            both = dot(lhs, matrix(c_hi, s_hi), True)
            sums = both[:128] + both[128:] + dot(lhs[:128], matrix(c_lo, s_lo), True)
            if first and quad == 0:
                await_beams(g)
            for j in range(4):
                n = g * GROUP + quad * 4 + j
                flat = []
                for c in range(2):
                    value = None
                    for i in range(4):
                        piece = sums[32 * j + 8 * i : 32 * j + 8 * i + 8, 128 * c : 128 * c + 128]
                        if i != j:
                            piece = pltpu.roll(piece, (SUB * (i - j)) % 128, 1)
                        value = piece if value is None else jnp.where(lane_group == i, piece, value)
                    flat.append(value)
                one_re = beam_buf[2 * n, pl.ds(0, 8, stride=2), :]
                one_im = beam_buf[2 * n, pl.ds(1, 8, stride=2), :]
                two_re = beam_buf[2 * n + 1, pl.ds(0, 8, stride=2), :]
                two_im = beam_buf[2 * n + 1, pl.ds(1, 8, stride=2), :]
                beam_re = taper * (one_re * two_re + one_im * two_im)
                beam_im = taper * (one_im * two_re - one_re * two_im)
                sky_re = beam_re * flat[0] - beam_im * flat[1]
                sky_im = beam_re * flat[1] + beam_im * flat[0]
                in_use = n < live
                place = (quad * 4 + j) * 8
                sky[g & 1, place : place + 8, :] = jnp.where(in_use, sky_re, 0.0)
                sky[g & 1, place + 8 * GROUP : place + 8 * GROUP + 8, :] = jnp.where(in_use, sky_im, 0.0)

    def cells(g):
        hi, lo = split(sky[g & 1])
        z = table_times(left_hi[...], left_lo[...], hi, lo)
        z_re, z_im = z[: 8 * GROUP], z[8 * GROUP :]
        y_re = z_re * twist_re - z_im * twist_im
        y_im = z_re * twist_im + z_im * twist_re
        hi, lo = split(jnp.concatenate([y_re, y_im], axis=1))
        result = times_table(hi, lo, right_hi[...], right_lo[...])
        for j in range(GROUP):
            n = g * GROUP + j
            band = row_s[n] >> 3
            shift = row_s[n] & 7
            rank = ranks[band]
            ranks[band] = rank + 1
            late = sublane < shift
            last = jnp.minimum(band + 4, owners - 1)
            for c in range(2):
                value = result[8 * j : 8 * j + 8, 128 * c : 128 * c + 128]
                spread = jnp.where(late & (lane_group == 0), 0.0, value)
                tile = 2 * rank + c
                for o in range(4):
                    pltpu.store(out.at[(band + o) ^ me, tile], spread, mask=lane_group == o)
                part = tile & 3
                tail = pltpu.roll(value, SUB * part, 1)
                pltpu.store(
                    out.at[last ^ me, 2 * cap + (tile >> 2)], tail, mask=late & (lane_group == part)
                )
            column = jnp.full((8, 128), owner_s[n] * tile_cols + col_s[n], jnp.float32)
            for o in range(5):
                here = (sublane == 0) & (lane == label_lane + o * cap + rank)
                if o == 4:
                    here = here & (sublane < shift)
                target = last if o == 4 else band + o
                pltpu.store(out.at[target ^ me, label_tile], column, mask=here)

    images(0, True)
    for copy in copies[6:10] + [copies[0], copies[2]]:
        copy.wait()

    @pl.loop(1, groups)
    def _(g):
        await_beams(g)
        fetch_beams(g + 1)
        cells(g - 1)
        images(g)

    cells(groups - 1)
    await_beams(groups)
    for k in range(owners // 2):
        keep[k] = out[2 * k]
        give[k] = out[2 * k + 1]


def merge_kernel(keep, got, *messages):
    for k, message in zip(exchange_order(keep.shape[0]), messages):
        message[0] = keep[k]
        message[1] = got[k]


def place_slabs(cap, messages, grids, scratch, earlier=None):
    received, label_v, label_s, sem = scratch
    sources = 2 * len(messages)
    for k, message in enumerate(messages):
        received[2 * k] = message[0]
        received[2 * k + 1] = message[1]
    label_tile = 2 * cap + (2 * cap) // 4
    label_lane = SUB * ((2 * cap) % 4)
    label_v[:sources] = received[:sources, label_tile, 0, :].astype(jnp.int32)
    copy = pltpu.make_async_copy(label_v, label_s, sem)
    copy.start()
    for c, grid in enumerate(grids):
        grid[...] = earlier[c][...] if earlier else jnp.zeros_like(grid)
    lane = lax.broadcasted_iota(jnp.int32, (8, 128), 1)
    copy.wait()

    @pl.loop(0, sources)
    def _(source):
        for i in range(cap):
            for o in range(5):
                column = label_s[source, label_lane + o * cap + i]
                offset = column & 127
                here = pl.multiple_of((column >> 7) * 8, 8)
                place = lane - offset
                inside = (place >= 0) & (place < SUB)
                beyond = place < SUB - 128
                added = []
                for c in range(2):
                    if o < 4:
                        value, part = received[source, 2 * i + c], o
                    else:
                        value = received[source, 2 * cap + (2 * i + c) // 4]
                        part = (2 * i + c) % 4
                    value = pltpu.roll(value, (offset - SUB * part) & 127, 1)
                    added.append(jnp.where(inside, value, 0.0))
                    added.append(jnp.where(beyond, value, 0.0))
                before = [
                    grids[c][pl.ds(here + 8 * k, 8), :] for c in range(2) for k in range(2)
                ]
                for c in range(2):
                    for k in range(2):
                        grids[c][pl.ds(here + 8 * k, 8), :] = before[2 * c + k] + added[2 * c + k]


def early_kernel(cap, count, *refs):
    place_slabs(cap, refs[:count], refs[count : count + 2], refs[count + 2 :])


def row_kernel(
    cap,
    count,
    first,
    second,
    twist,
    *refs,
):
    earlier, messages, out = refs[:2], refs[2 : 2 + count], refs[2 + count]
    grids, scratch = refs[3 + count : 5 + count], refs[5 + count :]
    middle, held, out_sems = scratch[4:]
    place_slabs(cap, messages, grids, scratch[:4], earlier)

    for pair in range(ROWS_DEV // 2):
        halves_of = []
        for e in range(2):
            rows = [
                pl.ds(ROWS_DEV * e + 2 * pair + k, TAIL, stride=2 * ROWS_DEV) for k in range(2)
            ]
            value = jnp.concatenate(
                [jnp.concatenate([grids[c][at, :] for at in rows], axis=1) for c in range(2)], 0
            )
            hi, lo = split(value)
            halves_of.append(table_times(first[2 * e], first[2 * e + 1], hi, lo))
        for h, a in enumerate((halves_of[0] + halves_of[1], halves_of[0] - halves_of[1])):
            turn_re = twist[0, TAIL * h : TAIL * h + TAIL]
            turn_im = twist[1, TAIL * h : TAIL * h + TAIL]
            for k in range(2):
                a_re = a[:TAIL, 128 * k : 128 * k + 128]
                a_im = a[TAIL:, 128 * k : 128 * k + 128]
                b = jnp.concatenate(
                    [a_re * turn_re - a_im * turn_im, a_re * turn_im + a_im * turn_re], axis=1
                )
                for part, value in enumerate(split(b)):
                    middle[h, pair, part, TAIL * k : TAIL * k + TAIL, :] = value

    copies = []
    for h in range(2):
        for pair in range(ROWS_DEV // 2):
            result = table_times(
                second[0], second[1], middle[h, pair, 0], middle[h, pair, 1], True
            )
            for c in range(2):
                for k in range(2):
                    held[h, c, pl.ds(2 * pair + k, TAIL, stride=ROWS_DEV), :] = result[
                        128 * c : 128 * c + 128, 128 * k : 128 * k + 128
                    ]
        for c in range(2):
            copies.append(
                pltpu.make_async_copy(
                    held.at[h, c].reshape(TAIL, ROWS_DEV, TAIL),
                    out.at[c, :, h],
                    out_sems.at[h, c],
                )
            )
            copies[-1].start()
    for copy in copies:
        copy.wait()


def shards(
    visibility, coords, block_owner, block_row, block_col, stations, block_count, beam_terms
):
    owners = lax.axis_size("tile")
    per_device = visibility.shape[0]
    tile_cols = NG // owners
    cap, tiles = send_layout(per_device, owners)
    stations_all = beam_terms.shape[0]
    vmem = pl.BlockSpec(memory_space=pltpu.VMEM)
    beams = (
        beam_terms.reshape(stations_all, 2, 8, 128)
        .transpose(0, 2, 1, 3)
        .reshape(stations_all, 16, 128)
    )
    labels = (
        block_owner.reshape(per_device),
        block_row,
        block_col,
        stations.T,
    )
    values = (
        visibility.reshape(per_device * 2, VROWS),
        coords.transpose(1, 0, 2),
        *image_tables(),
    )
    hbm = pl.BlockSpec(memory_space=pltpu.HBM)
    half = jax.ShapeDtypeStruct((owners // 2, tiles, 8, 128), jnp.float32)
    keep, give = pl.pallas_call(
        functools.partial(image_kernel, cap, tile_cols),
        out_shape=[half] * 2,
        in_specs=[pl.BlockSpec(memory_space=pltpu.SMEM)] + [hbm] * (1 + len(labels) + len(values)),
        out_specs=[vmem] * 2,
        scratch_shapes=[
            *(pltpu.SMEM(label.shape, label.dtype) for label in labels),
            *(pltpu.VMEM(value.shape, value.dtype) for value in values),
            pltpu.VMEM((owners, tiles, 8, 128), jnp.float32),
            pltpu.VMEM((2 * (per_device + GROUP), 16, 128), jnp.float32),
            pltpu.VMEM((2, 16 * GROUP, 128), jnp.float32),
            pltpu.SMEM((owners,), jnp.int32),
            pltpu.SemaphoreType.DMA((per_device // GROUP + 1,)),
            pltpu.SemaphoreType.DMA((len(labels) + len(values),)),
        ],
        compiler_params=pltpu.CompilerParams(vmem_limit_bytes=24 * 1024 * 1024),
        name="image",
    )(
        block_count,
        *(pltpu.with_memory_space_constraint(x, pltpu.HBM) for x in (beams, *labels, *values)),
    )
    got = lax.ppermute(give, "tile", [(source, source ^ 1) for source in range(owners)])
    messages = pl.pallas_call(
        merge_kernel,
        out_shape=[jax.ShapeDtypeStruct((2, tiles, 8, 128), jnp.float32)] * (owners // 2),
        in_specs=[vmem] * 2,
        out_specs=[vmem] * (owners // 2),
        compiler_params=pltpu.CompilerParams(vmem_limit_bytes=24 * 1024 * 1024),
        name="merge",
    )(keep, got)
    received = [messages[0]] + [
        lax.ppermute(message, "tile", [(source, source ^ (2 * k)) for source in range(owners)])
        for message, k in zip(messages[1:], exchange_order(owners // 2)[1:])
    ]
    early = min(5, owners // 2)
    late = owners // 2 - early
    grid = jax.ShapeDtypeStruct(((LEAD + 1) * ROWS_DEV, TAIL), jnp.float32)
    placing = [
        pltpu.VMEM((owners, tiles, 8, 128), jnp.float32),
        pltpu.VMEM((owners, 128), jnp.int32),
        pltpu.SMEM((owners, 128), jnp.int32),
        pltpu.SemaphoreType.DMA,
    ]
    grids = pl.pallas_call(
        functools.partial(early_kernel, cap, early),
        out_shape=[grid] * 2,
        in_specs=[vmem] * early,
        out_specs=[vmem] * 2,
        scratch_shapes=placing,
        cost_estimate=pl.CostEstimate(flops=3 * 10**9, bytes_accessed=10**7, transcendentals=0),
        compiler_params=pltpu.CompilerParams(vmem_limit_bytes=24 * 1024 * 1024),
        name="early",
    )(*received[:early])
    result = pl.pallas_call(
        functools.partial(row_kernel, cap, late),
        out_shape=jax.ShapeDtypeStruct((2, TAIL, 2, ROWS_DEV, TAIL), jnp.float32),
        in_specs=[vmem] * (5 + late),
        out_specs=pl.BlockSpec(memory_space=pl.ANY),
        scratch_shapes=[
            *(pltpu.VMEM(grid.shape, grid.dtype) for _ in range(2)),
            *placing,
            pltpu.VMEM((2, ROWS_DEV // 2, 2, 2 * TAIL, 2 * TAIL), jnp.bfloat16),
            pltpu.VMEM((2, 2, TAIL * ROWS_DEV, TAIL), jnp.float32),
            pltpu.SemaphoreType.DMA((2, 2)),
        ],
        compiler_params=pltpu.CompilerParams(vmem_limit_bytes=24 * 1024 * 1024),
        name="rows",
    )(*row_tables(), *grids, *received[early:])
    return (
        result.reshape(2, LEAD, ROWS_DEV, TAIL).transpose(0, 2, 1, 3).reshape(2, ROWS_DEV, NG)
    )


def solution(mesh):
    placed = (
        P(("parts", "tile"), None, None),
        P(("parts", "tile"), None, None),
        P(("parts", "tile"), None),
        P(("parts", "tile")),
        P(("parts", "tile")),
        P(("parts", "tile"), None),
        P(("parts", "tile")),
        P(),
    )
    return jax.shard_map(
        shards,
        mesh=mesh,
        in_specs=placed,
        out_specs=P(None, ("parts", "tile"), None),
        check_vma=False,
    )
```

```python
import functools
import math

import jax
import jax.numpy as jnp
import ml_dtypes
import numpy as np
from jax import lax
from jax.experimental import pallas as pl
from jax.experimental.pallas import tpu as pltpu
from jax.sharding import PartitionSpec as P

VROWS = 128
SUB = 32
NG = 32768
ROWS_DEV = 8
LEAD = 256
TAIL = 128
GROUP = 16

SIN_TERMS = (4.442879549, -7.307815317, 3.597759608, -0.791160565)
COS_TERMS = (1.414213500, -6.978850910, 5.739459580, -1.883552820, 0.310677860)


def halves(table):
    table = np.round(table, 12).astype(np.float32)
    high = table.astype(ml_dtypes.bfloat16)
    low = (table - high.astype(np.float32)).astype(ml_dtypes.bfloat16)
    return high, low


def root(numbers, length):
    angle = 2.0 * np.pi / length * (numbers % length)
    return np.cos(angle), -np.sin(angle)


def complex_left(re, im):
    return np.block([[re, -im], [im, re]])


@functools.cache
def image_tables():
    eight = np.arange(8)
    re, im = root(np.outer(eight, eight), 8)
    left = complex_left(np.kron(np.eye(GROUP), re), np.kron(np.eye(GROUP), im))
    lane = np.arange(128)
    twist = root(np.outer(eight, lane // SUB), SUB)
    four = 8 * np.outer(lane // SUB, lane // SUB) + np.outer(lane % SUB, lane % SUB)
    re, im = root(four, SUB)
    right = complex_left(re, im).T
    row_pos = ((4 * eight[:, None] + lane[None, :] // SUB) - SUB // 2) / SUB
    col_pos = np.broadcast_to((lane[None, :] % SUB - SUB // 2) / SUB, (8, 128))
    taper = (1 - 2 * row_pos**2) * (1 - 2 * col_pos**2) / SUB
    small = np.stack([taper, np.round(twist[0], 12), np.round(twist[1], 12)]).astype(np.float32)
    return (*halves(left), *halves(right), small)


@functools.cache
def row_tables():
    lead, tail = np.arange(LEAD), np.arange(TAIL)
    even = complex_left(*root(np.outer(tail, tail), TAIL))
    odd = complex_left(*root(np.outer(tail, 2 * tail + 1), LEAD))
    twist = np.stack(root(np.outer(lead, tail), NG)) / math.sqrt(NG)
    first = np.stack(halves(even) + halves(odd))
    return first, np.stack(halves(even)), np.round(twist, 12).astype(np.float32)


def split(value):
    high = value.astype(jnp.bfloat16)
    return high, (value - high.astype(jnp.float32)).astype(jnp.bfloat16)


def dot(left, right, transposed=False):
    dims = (((1,), (1 if transposed else 0,)), ((), ()))
    return lax.dot_general(left, right, dims, preferred_element_type=jnp.float32)


def table_times(table_hi, table_lo, hi, lo, transposed=False):
    rows = table_hi.shape[0]
    both = dot(jnp.concatenate([table_hi, table_lo], axis=0), hi, transposed)
    return both[:rows] + both[rows:] + dot(table_hi, lo, transposed)


def times_table(hi, lo, table_hi, table_lo):
    rows = hi.shape[0]
    both = dot(jnp.concatenate([hi, lo], axis=0), table_hi)
    return both[:rows] + both[rows:] + dot(hi, table_lo)


def polynomial(terms, z):
    value = z * terms[-1] + terms[-2]
    for term in terms[-3::-1]:
        value = value * z + term
    return value


def cos_sin(turns):
    whole = (turns + 12582912.0) - 12582912.0
    t = turns - whole
    z = t * t
    half_sin = t * polynomial(SIN_TERMS, z)
    half_cos = polynomial(COS_TERMS, z)
    return 1.0 - half_sin * half_sin, half_sin * half_cos


def send_layout(per_device, owners):
    cap = -(-per_device // (owners - SUB // ROWS_DEV + 1))
    tiles = 2 * cap + (2 * cap + 1 + 3) // 4
    return cap, tiles


def exchange_order(chips):
    quarter = chips // 4
    far = [k + part for k in range(quarter) for part in (3 * quarter, 2 * quarter)]
    near = list(range(chips // 2 - 1, 0, -1))
    return [0] + near[:1] + far + near[1:]


def image_kernel(
    cap,
    tile_cols,
    *refs,
):
    me = lax.axis_index("tile")
    owners = lax.axis_size("tile")
    count_s, beams, args, keep, give = refs[0], refs[1], refs[2:13], refs[13], refs[14]
    copied, (out, beam_buf, sky, ranks, sems, arg_sems) = refs[15:26], refs[26:]
    copies = [
        pltpu.make_async_copy(arg, held, arg_sems.at[k])
        for k, (arg, held) in enumerate(zip(args, copied))
    ]
    for copy in copies:
        copy.start()
    owner_s, row_s, col_s, station_s, vis, coords = copied[:6]
    left_hi, left_lo, right_hi, right_lo, small = copied[6:]
    per_device = vis.shape[0] // 2
    label_tile = 2 * cap + (2 * cap) // 4
    label_lane = SUB * ((2 * cap) % 4)
    sublane = lax.broadcasted_iota(jnp.int32, (8, 128), 0)
    lane = lax.broadcasted_iota(jnp.int32, (8, 128), 1)
    lane_group = lane // SUB
    out[...] = jnp.zeros_like(out)
    spread_columns = ((lane - label_lane) * (NG // SUB)).astype(jnp.float32)
    is_label = (sublane == 0) & (lane >= label_lane) & (lane < label_lane + SUB)
    for d in range(owners):
        out[d, label_tile] = jnp.where(is_label, spread_columns, 0.0)
    sky[...] = jnp.zeros_like(sky)
    for b in range(owners):
        ranks[b] = 0
    copies[3].wait()
    copies[1].wait()
    live = count_s[0]
    groups = (live + GROUP - 1) >> (GROUP.bit_length() - 1)

    def fetch_beams(g):
        for j in range(GROUP):
            n = jnp.minimum(g, per_device // GROUP - 1) * GROUP + j
            for side in range(2):
                pltpu.make_async_copy(
                    beams.at[station_s[side, n]],
                    beam_buf.at[2 * (g * GROUP + j) + side],
                    sems.at[g],
                ).start()

    def await_beams(g):
        waited = beam_buf.at[pl.ds(g * 2 * GROUP, 2 * GROUP)]
        pltpu.make_async_copy(beams.at[pl.ds(0, 2 * GROUP)], waited, sems.at[g]).wait()

    for g in range(2):
        fetch_beams(g)
    copies[4].wait()
    copies[5].wait()
    copies[10].wait()

    @pl.loop(0, groups * (GROUP // 8))
    def _(g):
        for j in range(8):
            n = g * 8 + j
            shift = row_s[n] & 7
            coords[0, pl.ds(n, 1), :] += shift.astype(jnp.float32)
            vis[pl.ds(2 * n, 2), :] *= (1 - 2 * (shift & 1)).astype(jnp.float32)

    taper = small[0]
    twist_re = jnp.concatenate([small[1]] * GROUP, axis=0)
    twist_im = jnp.concatenate([small[2]] * GROUP, axis=0)
    number = lax.broadcasted_iota(jnp.int32, (SUB, VROWS), 0)
    l_row = (4 * (number % 8) + number // 8 - SUB // 2).astype(jnp.float32) / SUB
    l_col = (number - SUB // 2).astype(jnp.float32) / SUB
    d_row = l_row * l_row
    d_col = l_col * l_col

    def images(g, first=False):
        for quad in range(GROUP // 4):
            x_hi, x_lo, columns = [], [], []
            for j in range(4):
                n = g * GROUP + quad * 4 + j
                u = coords[0, pl.ds(n, 1), :]
                v = coords[1, pl.ds(n, 1), :]
                w = coords[2, pl.ds(n, 1), :]
                vis_re = vis[pl.ds(2 * n, 1), :]
                vis_im = vis[pl.ds(2 * n + 1, 1), :]
                cos_row, sin_row = cos_sin(u * l_row + w * d_row)
                cos_col, sin_col = cos_sin(v * l_col + w * d_col)
                x = jnp.concatenate(
                    [
                        vis_re * cos_row - vis_im * sin_row,
                        vis_re * sin_row + vis_im * cos_row,
                    ],
                    axis=1,
                )
                hi, lo = split(x)
                x_hi.append(hi)
                x_lo.append(lo)
                columns.append(split(cos_col) + split(sin_col))
            c_hi, c_lo, s_hi, s_lo = zip(*columns)

            def matrix(c, s):
                real = [jnp.concatenate([a, -b], axis=1) for a, b in zip(c, s)]
                imag = [jnp.concatenate([b, a], axis=1) for a, b in zip(c, s)]
                return jnp.concatenate(real + imag, axis=0)

            lhs = jnp.concatenate(x_hi + x_lo, axis=0)
            both = dot(lhs, matrix(c_hi, s_hi), True)
            sums = both[:128] + both[128:] + dot(lhs[:128], matrix(c_lo, s_lo), True)
            if first and quad == 0:
                await_beams(g)
            for j in range(4):
                n = g * GROUP + quad * 4 + j
                flat = []
                for c in range(2):
                    value = None
                    for i in range(4):
                        piece = sums[32 * j + 8 * i : 32 * j + 8 * i + 8, 128 * c : 128 * c + 128]
                        if i != j:
                            piece = pltpu.roll(piece, (SUB * (i - j)) % 128, 1)
                        value = piece if value is None else jnp.where(lane_group == i, piece, value)
                    flat.append(value)
                one_re = beam_buf[2 * n, pl.ds(0, 8, stride=2), :]
                one_im = beam_buf[2 * n, pl.ds(1, 8, stride=2), :]
                two_re = beam_buf[2 * n + 1, pl.ds(0, 8, stride=2), :]
                two_im = beam_buf[2 * n + 1, pl.ds(1, 8, stride=2), :]
                beam_re = taper * (one_re * two_re + one_im * two_im)
                beam_im = taper * (one_im * two_re - one_re * two_im)
                sky_re = beam_re * flat[0] - beam_im * flat[1]
                sky_im = beam_re * flat[1] + beam_im * flat[0]
                in_use = n < live
                place = (quad * 4 + j) * 8
                sky[g & 1, place : place + 8, :] = jnp.where(in_use, sky_re, 0.0)
                sky[g & 1, place + 8 * GROUP : place + 8 * GROUP + 8, :] = jnp.where(in_use, sky_im, 0.0)

    def cells(g):
        hi, lo = split(sky[g & 1])
        z = table_times(left_hi[...], left_lo[...], hi, lo)
        z_re, z_im = z[: 8 * GROUP], z[8 * GROUP :]
        y_re = z_re * twist_re - z_im * twist_im
        y_im = z_re * twist_im + z_im * twist_re
        hi, lo = split(jnp.concatenate([y_re, y_im], axis=1))
        result = times_table(hi, lo, right_hi[...], right_lo[...])
        for j in range(GROUP):
            n = g * GROUP + j
            band = row_s[n] >> 3
            shift = row_s[n] & 7
            rank = ranks[band]
            ranks[band] = rank + 1
            late = sublane < shift
            last = jnp.minimum(band + 4, owners - 1)
            for c in range(2):
                value = result[8 * j : 8 * j + 8, 128 * c : 128 * c + 128]
                spread = jnp.where(late & (lane_group == 0), 0.0, value)
                tile = 2 * rank + c
                for o in range(4):
                    pltpu.store(out.at[(band + o) ^ me, tile], spread, mask=lane_group == o)
                part = tile & 3
                tail = pltpu.roll(value, SUB * part, 1)
                pltpu.store(
                    out.at[last ^ me, 2 * cap + (tile >> 2)], tail, mask=late & (lane_group == part)
                )
            column = jnp.full((8, 128), owner_s[n] * tile_cols + col_s[n], jnp.float32)
            for o in range(5):
                here = (sublane == 0) & (lane == label_lane + o * cap + rank)
                if o == 4:
                    here = here & (sublane < shift)
                target = last if o == 4 else band + o
                pltpu.store(out.at[target ^ me, label_tile], column, mask=here)

    images(0, True)
    for copy in copies[6:10] + [copies[0], copies[2]]:
        copy.wait()

    @pl.loop(1, groups)
    def _(g):
        await_beams(g)
        fetch_beams(g + 1)
        cells(g - 1)
        images(g)

    cells(groups - 1)
    await_beams(groups)
    for k in range(owners // 2):
        keep[k] = out[2 * k]
        give[k] = out[2 * k + 1]


def merge_kernel(keep, got, *messages):
    for k, message in zip(exchange_order(keep.shape[0]), messages):
        message[0] = keep[k]
        message[1] = got[k]


def place_slabs(cap, messages, grids, scratch, earlier=None):
    received, label_v, label_s, sem = scratch
    sources = 2 * len(messages)
    for k, message in enumerate(messages):
        received[2 * k] = message[0]
        received[2 * k + 1] = message[1]
    label_tile = 2 * cap + (2 * cap) // 4
    label_lane = SUB * ((2 * cap) % 4)
    label_v[:sources] = received[:sources, label_tile, 0, :].astype(jnp.int32)
    copy = pltpu.make_async_copy(label_v, label_s, sem)
    copy.start()
    for c, grid in enumerate(grids):
        grid[...] = earlier[c][...] if earlier else jnp.zeros_like(grid)
    lane = lax.broadcasted_iota(jnp.int32, (8, 128), 1)
    copy.wait()

    @pl.loop(0, sources)
    def _(source):
        for i in range(cap):
            for o in range(5):
                column = label_s[source, label_lane + o * cap + i]
                offset = column & 127
                here = pl.multiple_of((column >> 7) * 8, 8)
                place = lane - offset
                inside = (place >= 0) & (place < SUB)
                beyond = place < SUB - 128
                added = []
                for c in range(2):
                    if o < 4:
                        value, part = received[source, 2 * i + c], o
                    else:
                        value = received[source, 2 * cap + (2 * i + c) // 4]
                        part = (2 * i + c) % 4
                    value = pltpu.roll(value, (offset - SUB * part) & 127, 1)
                    added.append(jnp.where(inside, value, 0.0))
                    added.append(jnp.where(beyond, value, 0.0))
                before = [
                    grids[c][pl.ds(here + 8 * k, 8), :] for c in range(2) for k in range(2)
                ]
                for c in range(2):
                    for k in range(2):
                        grids[c][pl.ds(here + 8 * k, 8), :] = before[2 * c + k] + added[2 * c + k]


def early_kernel(cap, count, started, *refs):
    earlier, refs = refs[: 2 * started], refs[2 * started :]
    place_slabs(cap, refs[:count], refs[count : count + 2], refs[count + 2 :], earlier)


def row_kernel(
    cap,
    count,
    first,
    second,
    twist,
    *refs,
):
    earlier, messages, out = refs[:2], refs[2 : 2 + count], refs[2 + count]
    grids, scratch = refs[3 + count : 5 + count], refs[5 + count :]
    middle, held, out_sems = scratch[4:]
    place_slabs(cap, messages, grids, scratch[:4], earlier)

    for pair in range(ROWS_DEV // 2):
        halves_of = []
        for e in range(2):
            rows = [
                pl.ds(ROWS_DEV * e + 2 * pair + k, TAIL, stride=2 * ROWS_DEV) for k in range(2)
            ]
            value = jnp.concatenate(
                [jnp.concatenate([grids[c][at, :] for at in rows], axis=1) for c in range(2)], 0
            )
            hi, lo = split(value)
            halves_of.append(table_times(first[2 * e], first[2 * e + 1], hi, lo))
        for h, a in enumerate((halves_of[0] + halves_of[1], halves_of[0] - halves_of[1])):
            turn_re = twist[0, TAIL * h : TAIL * h + TAIL]
            turn_im = twist[1, TAIL * h : TAIL * h + TAIL]
            for k in range(2):
                a_re = a[:TAIL, 128 * k : 128 * k + 128]
                a_im = a[TAIL:, 128 * k : 128 * k + 128]
                b = jnp.concatenate(
                    [a_re * turn_re - a_im * turn_im, a_re * turn_im + a_im * turn_re], axis=1
                )
                for part, value in enumerate(split(b)):
                    middle[h, pair, part, TAIL * k : TAIL * k + TAIL, :] = value

    copies = []
    for h in range(2):
        for pair in range(ROWS_DEV // 2):
            result = table_times(
                second[0], second[1], middle[h, pair, 0], middle[h, pair, 1], True
            )
            for c in range(2):
                for k in range(2):
                    held[h, c, pl.ds(2 * pair + k, TAIL, stride=ROWS_DEV), :] = result[
                        128 * c : 128 * c + 128, 128 * k : 128 * k + 128
                    ]
        for c in range(2):
            copies.append(
                pltpu.make_async_copy(
                    held.at[h, c].reshape(TAIL, ROWS_DEV, TAIL),
                    out.at[c, :, h],
                    out_sems.at[h, c],
                )
            )
            copies[-1].start()
    for copy in copies:
        copy.wait()


def shards(
    visibility, coords, block_owner, block_row, block_col, stations, block_count, beam_terms
):
    owners = lax.axis_size("tile")
    per_device = visibility.shape[0]
    tile_cols = NG // owners
    cap, tiles = send_layout(per_device, owners)
    stations_all = beam_terms.shape[0]
    vmem = pl.BlockSpec(memory_space=pltpu.VMEM)
    beams = (
        beam_terms.reshape(stations_all, 2, 8, 128)
        .transpose(0, 2, 1, 3)
        .reshape(stations_all, 16, 128)
    )
    labels = (
        block_owner.reshape(per_device),
        block_row,
        block_col,
        stations.T,
    )
    values = (
        visibility.reshape(per_device * 2, VROWS),
        coords.transpose(1, 0, 2),
        *image_tables(),
    )
    hbm = pl.BlockSpec(memory_space=pltpu.HBM)
    half = jax.ShapeDtypeStruct((owners // 2, tiles, 8, 128), jnp.float32)
    keep, give = pl.pallas_call(
        functools.partial(image_kernel, cap, tile_cols),
        out_shape=[half] * 2,
        in_specs=[pl.BlockSpec(memory_space=pltpu.SMEM)] + [hbm] * (1 + len(labels) + len(values)),
        out_specs=[vmem] * 2,
        scratch_shapes=[
            *(pltpu.SMEM(label.shape, label.dtype) for label in labels),
            *(pltpu.VMEM(value.shape, value.dtype) for value in values),
            pltpu.VMEM((owners, tiles, 8, 128), jnp.float32),
            pltpu.VMEM((2 * (per_device + GROUP), 16, 128), jnp.float32),
            pltpu.VMEM((2, 16 * GROUP, 128), jnp.float32),
            pltpu.SMEM((owners,), jnp.int32),
            pltpu.SemaphoreType.DMA((per_device // GROUP + 1,)),
            pltpu.SemaphoreType.DMA((len(labels) + len(values),)),
        ],
        compiler_params=pltpu.CompilerParams(vmem_limit_bytes=24 * 1024 * 1024),
        name="image",
    )(
        block_count,
        *(pltpu.with_memory_space_constraint(x, pltpu.HBM) for x in (beams, *labels, *values)),
    )
    got = lax.ppermute(give, "tile", [(source, source ^ 1) for source in range(owners)])
    messages = pl.pallas_call(
        merge_kernel,
        out_shape=[jax.ShapeDtypeStruct((2, tiles, 8, 128), jnp.float32)] * (owners // 2),
        in_specs=[vmem] * 2,
        out_specs=[vmem] * (owners // 2),
        compiler_params=pltpu.CompilerParams(vmem_limit_bytes=24 * 1024 * 1024),
        name="merge",
    )(keep, got)
    order = exchange_order(owners // 2)

    def exchange(k, message):
        pairs = [(source, source ^ (2 * k)) for source in range(owners)]
        return lax.ppermute(message, "tile", pairs) if k else message

    received = [exchange(k, message) for k, message in zip(order, messages)]
    last = 1 + owners // 4
    grid = jax.ShapeDtypeStruct(((LEAD + 1) * ROWS_DEV, TAIL), jnp.float32)
    placing = [
        pltpu.VMEM((owners, tiles, 8, 128), jnp.float32),
        pltpu.VMEM((owners, 128), jnp.int32),
        pltpu.SMEM((owners, 128), jnp.int32),
        pltpu.SemaphoreType.DMA,
    ]

    def place_early(grids, stage):
        return pl.pallas_call(
            functools.partial(early_kernel, cap, len(stage), len(grids) // 2),
            out_shape=[grid] * 2,
            in_specs=[vmem] * (len(grids) + len(stage)),
            out_specs=[vmem] * 2,
            scratch_shapes=placing,
            cost_estimate=pl.CostEstimate(flops=3 * 10**9, bytes_accessed=10**7, transcendentals=0),
            compiler_params=pltpu.CompilerParams(vmem_limit_bytes=24 * 1024 * 1024),
            name="early",
        )(*grids, *stage)

    grids = place_early(place_early([], received[:3]), received[3:last])
    result = pl.pallas_call(
        functools.partial(row_kernel, cap, owners // 2 - last),
        out_shape=jax.ShapeDtypeStruct((2, TAIL, 2, ROWS_DEV, TAIL), jnp.float32),
        in_specs=[vmem] * (5 + owners // 2 - last),
        out_specs=pl.BlockSpec(memory_space=pl.ANY),
        scratch_shapes=[
            *(pltpu.VMEM(grid.shape, grid.dtype) for _ in range(2)),
            *placing,
            pltpu.VMEM((2, ROWS_DEV // 2, 2, 2 * TAIL, 2 * TAIL), jnp.bfloat16),
            pltpu.VMEM((2, 2, TAIL * ROWS_DEV, TAIL), jnp.float32),
            pltpu.SemaphoreType.DMA((2, 2)),
        ],
        compiler_params=pltpu.CompilerParams(vmem_limit_bytes=24 * 1024 * 1024),
        name="rows",
    )(*row_tables(), *grids, *received[last:])
    return (
        result.reshape(2, LEAD, ROWS_DEV, TAIL).transpose(0, 2, 1, 3).reshape(2, ROWS_DEV, NG)
    )


def solution(mesh):
    placed = (
        P(("parts", "tile"), None, None),
        P(("parts", "tile"), None, None),
        P(("parts", "tile"), None),
        P(("parts", "tile")),
        P(("parts", "tile")),
        P(("parts", "tile"), None),
        P(("parts", "tile")),
        P(),
    )
    return jax.shard_map(
        shards,
        mesh=mesh,
        in_specs=placed,
        out_specs=P(None, ("parts", "tile"), None),
        check_vma=False,
    )
```

```python
import functools
import math

import jax
import jax.numpy as jnp
import ml_dtypes
import numpy as np
from jax import lax
from jax.experimental import pallas as pl
from jax.experimental.pallas import tpu as pltpu
from jax.sharding import PartitionSpec as P

VROWS = 128
SUB = 32
NG = 32768
ROWS_DEV = 8
LEAD = 256
TAIL = 128
GROUP = 16

SIN_TERMS = (4.442879549, -7.307815317, 3.597759608, -0.791160565)
COS_TERMS = (1.414213500, -6.978850910, 5.739459580, -1.883552820, 0.310677860)


def halves(table):
    table = np.round(table, 12).astype(np.float32)
    high = table.astype(ml_dtypes.bfloat16)
    low = (table - high.astype(np.float32)).astype(ml_dtypes.bfloat16)
    return high, low


def root(numbers, length):
    angle = 2.0 * np.pi / length * (numbers % length)
    return np.cos(angle), -np.sin(angle)


def complex_left(re, im):
    return np.block([[re, -im], [im, re]])


@functools.cache
def image_tables():
    eight = np.arange(8)
    re, im = root(np.outer(eight, eight), 8)
    left = complex_left(np.kron(np.eye(GROUP), re), np.kron(np.eye(GROUP), im))
    lane = np.arange(128)
    twist = root(np.outer(eight, lane // SUB), SUB)
    four = 8 * np.outer(lane // SUB, lane // SUB) + np.outer(lane % SUB, lane % SUB)
    re, im = root(four, SUB)
    right = complex_left(re, im).T
    row_pos = ((4 * eight[:, None] + lane[None, :] // SUB) - SUB // 2) / SUB
    col_pos = np.broadcast_to((lane[None, :] % SUB - SUB // 2) / SUB, (8, 128))
    taper = (1 - 2 * row_pos**2) * (1 - 2 * col_pos**2) / SUB
    small = np.stack([taper, np.round(twist[0], 12), np.round(twist[1], 12)]).astype(np.float32)
    return (*halves(left), *halves(right), small)


@functools.cache
def row_tables():
    lead, tail = np.arange(LEAD), np.arange(TAIL)
    even = complex_left(*root(np.outer(tail, tail), TAIL))
    odd = complex_left(*root(np.outer(tail, 2 * tail + 1), LEAD))
    twist = np.stack(root(np.outer(lead, tail), NG)) / math.sqrt(NG)
    first = np.stack(halves(even) + halves(odd))
    return first, np.stack(halves(even)), np.round(twist, 12).astype(np.float32)


def split(value):
    high = value.astype(jnp.bfloat16)
    return high, (value - high.astype(jnp.float32)).astype(jnp.bfloat16)


def dot(left, right, transposed=False):
    dims = (((1,), (1 if transposed else 0,)), ((), ()))
    return lax.dot_general(left, right, dims, preferred_element_type=jnp.float32)


def table_times(table_hi, table_lo, hi, lo, transposed=False):
    rows = table_hi.shape[0]
    both = dot(jnp.concatenate([table_hi, table_lo], axis=0), hi, transposed)
    return both[:rows] + both[rows:] + dot(table_hi, lo, transposed)


def times_table(hi, lo, table_hi, table_lo):
    rows = hi.shape[0]
    both = dot(jnp.concatenate([hi, lo], axis=0), table_hi)
    return both[:rows] + both[rows:] + dot(hi, table_lo)


def polynomial(terms, z):
    value = z * terms[-1] + terms[-2]
    for term in terms[-3::-1]:
        value = value * z + term
    return value


def cos_sin(turns):
    whole = (turns + 12582912.0) - 12582912.0
    t = turns - whole
    z = t * t
    half_sin = t * polynomial(SIN_TERMS, z)
    half_cos = polynomial(COS_TERMS, z)
    return 1.0 - half_sin * half_sin, half_sin * half_cos


def send_layout(per_device, owners):
    cap = -(-per_device // (owners - SUB // ROWS_DEV + 1))
    tiles = 2 * cap + (2 * cap + 3) // 4
    return cap, tiles


def merge_halves(cap):
    return cap % 2


def exchange_order(chips):
    quarter = chips // 4
    far = [k + part for k in range(quarter) for part in (3 * quarter, 2 * quarter)]
    near = list(range(chips // 2 - 1, 0, -1))
    return [0] + near[:1] + far + near[1:]


def image_kernel(
    cap,
    tile_cols,
    *refs,
):
    me = lax.axis_index("tile")
    owners = lax.axis_size("tile")
    count_s, beams, args, keep, give = refs[0], refs[1], refs[2:13], refs[13], refs[14]
    copied, (out, beam_buf, sky, ranks, sems, arg_sems) = refs[15:26], refs[26:]
    copies = [
        pltpu.make_async_copy(arg, held, arg_sems.at[k])
        for k, (arg, held) in enumerate(zip(args, copied))
    ]
    for copy in copies:
        copy.start()
    owner_s, row_s, col_s, station_s, vis, coords = copied[:6]
    left_hi, left_lo, right_hi, right_lo, small = copied[6:]
    per_device = vis.shape[0] // 2
    label_tile = 2 * cap
    sublane = lax.broadcasted_iota(jnp.int32, (8, 128), 0)
    lane = lax.broadcasted_iota(jnp.int32, (8, 128), 1)
    lane_group = lane // SUB
    out[...] = jnp.zeros_like(out)
    spread_columns = (lane * (NG // SUB)).astype(jnp.float32)
    is_label = (sublane == 7) & (lane < 5 * cap)
    for d in range(owners):
        out[d, label_tile] = jnp.where(is_label, spread_columns, 0.0)
    sky[...] = jnp.zeros_like(sky)
    for b in range(owners):
        ranks[b] = 0
    copies[3].wait()
    copies[1].wait()
    live = count_s[0]
    groups = (live + GROUP - 1) >> (GROUP.bit_length() - 1)

    def fetch_beams(g):
        for j in range(GROUP):
            n = jnp.minimum(g, per_device // GROUP - 1) * GROUP + j
            for side in range(2):
                pltpu.make_async_copy(
                    beams.at[station_s[side, n]],
                    beam_buf.at[2 * (g * GROUP + j) + side],
                    sems.at[g],
                ).start()

    def await_beams(g):
        waited = beam_buf.at[pl.ds(g * 2 * GROUP, 2 * GROUP)]
        pltpu.make_async_copy(beams.at[pl.ds(0, 2 * GROUP)], waited, sems.at[g]).wait()

    for g in range(2):
        fetch_beams(g)
    copies[4].wait()
    copies[5].wait()
    copies[10].wait()

    @pl.loop(0, groups * (GROUP // 8))
    def _(g):
        for j in range(8):
            n = g * 8 + j
            shift = row_s[n] & 7
            coords[0, pl.ds(n, 1), :] += shift.astype(jnp.float32)
            vis[pl.ds(2 * n, 2), :] *= (1 - 2 * (shift & 1)).astype(jnp.float32)

    taper = small[0]
    twist_re = jnp.concatenate([small[1]] * GROUP, axis=0)
    twist_im = jnp.concatenate([small[2]] * GROUP, axis=0)
    number = lax.broadcasted_iota(jnp.int32, (SUB, VROWS), 0)
    l_row = (4 * (number % 8) + number // 8 - SUB // 2).astype(jnp.float32) / SUB
    l_col = (number - SUB // 2).astype(jnp.float32) / SUB
    d_row = l_row * l_row
    d_col = l_col * l_col

    def images(g, first=False):
        for quad in range(GROUP // 4):
            x_hi, x_lo, columns = [], [], []
            for j in range(4):
                n = g * GROUP + quad * 4 + j
                u = coords[0, pl.ds(n, 1), :]
                v = coords[1, pl.ds(n, 1), :]
                w = coords[2, pl.ds(n, 1), :]
                vis_re = vis[pl.ds(2 * n, 1), :]
                vis_im = vis[pl.ds(2 * n + 1, 1), :]
                cos_row, sin_row = cos_sin(u * l_row + w * d_row)
                cos_col, sin_col = cos_sin(v * l_col + w * d_col)
                x = jnp.concatenate(
                    [
                        vis_re * cos_row - vis_im * sin_row,
                        vis_re * sin_row + vis_im * cos_row,
                    ],
                    axis=1,
                )
                hi, lo = split(x)
                x_hi.append(hi)
                x_lo.append(lo)
                columns.append(split(cos_col) + split(sin_col))
            c_hi, c_lo, s_hi, s_lo = zip(*columns)

            def matrix(c, s):
                real = [jnp.concatenate([a, -b], axis=1) for a, b in zip(c, s)]
                imag = [jnp.concatenate([b, a], axis=1) for a, b in zip(c, s)]
                return jnp.concatenate(real + imag, axis=0)

            lhs = jnp.concatenate(x_hi + x_lo, axis=0)
            both = dot(lhs, matrix(c_hi, s_hi), True)
            sums = both[:128] + both[128:] + dot(lhs[:128], matrix(c_lo, s_lo), True)
            if first and quad == 0:
                await_beams(g)
            for j in range(4):
                n = g * GROUP + quad * 4 + j
                flat = []
                for c in range(2):
                    value = None
                    for i in range(4):
                        piece = sums[32 * j + 8 * i : 32 * j + 8 * i + 8, 128 * c : 128 * c + 128]
                        if i != j:
                            piece = pltpu.roll(piece, (SUB * (i - j)) % 128, 1)
                        value = piece if value is None else jnp.where(lane_group == i, piece, value)
                    flat.append(value)
                one_re = beam_buf[2 * n, pl.ds(0, 8, stride=2), :]
                one_im = beam_buf[2 * n, pl.ds(1, 8, stride=2), :]
                two_re = beam_buf[2 * n + 1, pl.ds(0, 8, stride=2), :]
                two_im = beam_buf[2 * n + 1, pl.ds(1, 8, stride=2), :]
                beam_re = taper * (one_re * two_re + one_im * two_im)
                beam_im = taper * (one_im * two_re - one_re * two_im)
                sky_re = beam_re * flat[0] - beam_im * flat[1]
                sky_im = beam_re * flat[1] + beam_im * flat[0]
                in_use = n < live
                place = (quad * 4 + j) * 8
                sky[g & 1, place : place + 8, :] = jnp.where(in_use, sky_re, 0.0)
                sky[g & 1, place + 8 * GROUP : place + 8 * GROUP + 8, :] = jnp.where(in_use, sky_im, 0.0)

    def cells(g):
        hi, lo = split(sky[g & 1])
        z = table_times(left_hi[...], left_lo[...], hi, lo)
        z_re, z_im = z[: 8 * GROUP], z[8 * GROUP :]
        y_re = z_re * twist_re - z_im * twist_im
        y_im = z_re * twist_im + z_im * twist_re
        hi, lo = split(jnp.concatenate([y_re, y_im], axis=1))
        result = times_table(hi, lo, right_hi[...], right_lo[...])
        for j in range(GROUP):
            n = g * GROUP + j
            band = row_s[n] >> 3
            shift = row_s[n] & 7
            rank = ranks[band]
            ranks[band] = rank + 1
            late = sublane < shift
            last = jnp.minimum(band + 4, owners - 1)
            for c in range(2):
                value = result[8 * j : 8 * j + 8, 128 * c : 128 * c + 128]
                spread = jnp.where(late & (lane_group == 0), 0.0, value)
                tile = 2 * rank + c
                for o in range(4):
                    pltpu.store(out.at[(band + o) ^ me, tile], spread, mask=lane_group == o)
                part = tile & 3
                tail = pltpu.roll(value, SUB * part, 1)
                pltpu.store(
                    out.at[last ^ me, 2 * cap + (tile >> 2)], tail, mask=late & (lane_group == part)
                )
            column = jnp.full((8, 128), owner_s[n] * tile_cols + col_s[n], jnp.float32)
            for o in range(5):
                here = (sublane == 7) & (lane == o * cap + rank)
                if o == 4:
                    here = here & (sublane - 7 < shift)
                target = last if o == 4 else band + o
                pltpu.store(out.at[target ^ me, label_tile], column, mask=here)

    images(0, True)
    for copy in copies[6:10] + [copies[0], copies[2]]:
        copy.wait()

    @pl.loop(1, groups)
    def _(g):
        await_beams(g)
        fetch_beams(g + 1)
        cells(g - 1)
        images(g)

    cells(groups - 1)
    await_beams(groups)
    for k in range(owners // 2):
        keep[k] = out[2 * k]
        give[k] = out[2 * k + 1]


def merge_kernel(cap, keep, got, *messages):
    tiles = keep.shape[1]
    whole = tiles - merge_halves(cap)
    lane = lax.broadcasted_iota(jnp.int32, (8, 128), 1)
    for k, message in zip(exchange_order(keep.shape[0]), messages):
        message[:whole] = keep[k, :whole]
        message[whole : 2 * whole] = got[k, :whole]
        if whole < tiles:
            message[2 * whole] = jnp.where(
                lane < 64, keep[k, whole], pltpu.roll(got[k, whole], 64, 1)
            )


def place_slabs(cap, messages, grids, scratch, earlier=None):
    received, label_v, label_s, sem = scratch
    sources = 2 * len(messages)
    whole = received.shape[1] - merge_halves(cap)
    for k, message in enumerate(messages):
        received[2 * k, :whole] = message[:whole]
        received[2 * k + 1, :whole] = message[whole : 2 * whole]
        if merge_halves(cap):
            received[2 * k, whole] = message[2 * whole]
            received[2 * k + 1, whole] = pltpu.roll(message[2 * whole], 64, 1)
    label_v[:sources] = received[:sources, 2 * cap, 7, :].astype(jnp.int32)
    copy = pltpu.make_async_copy(label_v, label_s, sem)
    copy.start()
    for c, grid in enumerate(grids):
        grid[...] = earlier[c][...] if earlier else jnp.zeros_like(grid)
    lane = lax.broadcasted_iota(jnp.int32, (8, 128), 1)
    not_label = lax.broadcasted_iota(jnp.int32, (8, 128), 0) < 7
    copy.wait()

    @pl.loop(0, sources)
    def _(source):
        for i in range(cap):
            for o in range(5):
                column = label_s[source, o * cap + i]
                offset = column & 127
                here = pl.multiple_of((column >> 7) * 8, 8)
                place = lane - offset
                inside = (place >= 0) & (place < SUB)
                beyond = place < SUB - 128
                if o == 4:
                    inside, beyond = inside & not_label, beyond & not_label
                added = []
                for c in range(2):
                    if o < 4:
                        value, part = received[source, 2 * i + c], o
                    else:
                        value = received[source, 2 * cap + (2 * i + c) // 4]
                        part = (2 * i + c) % 4
                    value = pltpu.roll(value, (offset - SUB * part) & 127, 1)
                    added.append(jnp.where(inside, value, 0.0))
                    added.append(jnp.where(beyond, value, 0.0))
                before = [
                    grids[c][pl.ds(here + 8 * k, 8), :] for c in range(2) for k in range(2)
                ]
                for c in range(2):
                    for k in range(2):
                        grids[c][pl.ds(here + 8 * k, 8), :] = before[2 * c + k] + added[2 * c + k]


def early_kernel(cap, count, started, *refs):
    earlier, refs = refs[: 2 * started], refs[2 * started :]
    place_slabs(cap, refs[:count], refs[count : count + 2], refs[count + 2 :], earlier)


def row_kernel(
    cap,
    count,
    first,
    second,
    twist,
    *refs,
):
    earlier, messages, out = refs[:2], refs[2 : 2 + count], refs[2 + count]
    grids, scratch = refs[3 + count : 5 + count], refs[5 + count :]
    middle, held, out_sems = scratch[4:]
    place_slabs(cap, messages, grids, scratch[:4], earlier)

    for pair in range(ROWS_DEV // 2):
        halves_of = []
        for e in range(2):
            rows = [
                pl.ds(ROWS_DEV * e + 2 * pair + k, TAIL, stride=2 * ROWS_DEV) for k in range(2)
            ]
            value = jnp.concatenate(
                [jnp.concatenate([grids[c][at, :] for at in rows], axis=1) for c in range(2)], 0
            )
            hi, lo = split(value)
            halves_of.append(table_times(first[2 * e], first[2 * e + 1], hi, lo))
        for h, a in enumerate((halves_of[0] + halves_of[1], halves_of[0] - halves_of[1])):
            turn_re = twist[0, TAIL * h : TAIL * h + TAIL]
            turn_im = twist[1, TAIL * h : TAIL * h + TAIL]
            for k in range(2):
                a_re = a[:TAIL, 128 * k : 128 * k + 128]
                a_im = a[TAIL:, 128 * k : 128 * k + 128]
                b = jnp.concatenate(
                    [a_re * turn_re - a_im * turn_im, a_re * turn_im + a_im * turn_re], axis=1
                )
                for part, value in enumerate(split(b)):
                    middle[h, pair, part, TAIL * k : TAIL * k + TAIL, :] = value

    copies = []
    for h in range(2):
        for pair in range(ROWS_DEV // 2):
            result = table_times(
                second[0], second[1], middle[h, pair, 0], middle[h, pair, 1], True
            )
            for c in range(2):
                for k in range(2):
                    held[h, c, pl.ds(2 * pair + k, TAIL, stride=ROWS_DEV), :] = result[
                        128 * c : 128 * c + 128, 128 * k : 128 * k + 128
                    ]
        for c in range(2):
            copies.append(
                pltpu.make_async_copy(
                    held.at[h, c].reshape(TAIL, ROWS_DEV, TAIL),
                    out.at[c, :, h],
                    out_sems.at[h, c],
                )
            )
            copies[-1].start()
    for copy in copies:
        copy.wait()


def shards(
    visibility, coords, block_owner, block_row, block_col, stations, block_count, beam_terms
):
    owners = lax.axis_size("tile")
    per_device = visibility.shape[0]
    tile_cols = NG // owners
    cap, tiles = send_layout(per_device, owners)
    stations_all = beam_terms.shape[0]
    vmem = pl.BlockSpec(memory_space=pltpu.VMEM)
    beams = (
        beam_terms.reshape(stations_all, 2, 8, 128)
        .transpose(0, 2, 1, 3)
        .reshape(stations_all, 16, 128)
    )
    labels = (
        block_owner.reshape(per_device),
        block_row,
        block_col,
        stations.T,
    )
    values = (
        visibility.reshape(per_device * 2, VROWS),
        coords.transpose(1, 0, 2),
        *image_tables(),
    )
    hbm = pl.BlockSpec(memory_space=pltpu.HBM)
    half = jax.ShapeDtypeStruct((owners // 2, tiles, 8, 128), jnp.float32)
    keep, give = pl.pallas_call(
        functools.partial(image_kernel, cap, tile_cols),
        out_shape=[half] * 2,
        in_specs=[pl.BlockSpec(memory_space=pltpu.SMEM)] + [hbm] * (1 + len(labels) + len(values)),
        out_specs=[vmem] * 2,
        scratch_shapes=[
            *(pltpu.SMEM(label.shape, label.dtype) for label in labels),
            *(pltpu.VMEM(value.shape, value.dtype) for value in values),
            pltpu.VMEM((owners, tiles, 8, 128), jnp.float32),
            pltpu.VMEM((2 * (per_device + GROUP), 16, 128), jnp.float32),
            pltpu.VMEM((2, 16 * GROUP, 128), jnp.float32),
            pltpu.SMEM((owners,), jnp.int32),
            pltpu.SemaphoreType.DMA((per_device // GROUP + 1,)),
            pltpu.SemaphoreType.DMA((len(labels) + len(values),)),
        ],
        compiler_params=pltpu.CompilerParams(vmem_limit_bytes=24 * 1024 * 1024),
        name="image",
    )(
        block_count,
        *(pltpu.with_memory_space_constraint(x, pltpu.HBM) for x in (beams, *labels, *values)),
    )
    got = lax.ppermute(give, "tile", [(source, source ^ 1) for source in range(owners)])
    messages = pl.pallas_call(
        functools.partial(merge_kernel, cap),
        out_shape=[jax.ShapeDtypeStruct((2 * tiles - merge_halves(cap), 8, 128), jnp.float32)]
        * (owners // 2),
        in_specs=[vmem] * 2,
        out_specs=[vmem] * (owners // 2),
        compiler_params=pltpu.CompilerParams(vmem_limit_bytes=24 * 1024 * 1024),
        name="merge",
    )(keep, got)
    order = exchange_order(owners // 2)

    def exchange(k, message):
        pairs = [(source, source ^ (2 * k)) for source in range(owners)]
        return lax.ppermute(message, "tile", pairs) if k else message

    received = [exchange(k, message) for k, message in zip(order, messages)]
    last = 1 + owners // 4
    grid = jax.ShapeDtypeStruct(((LEAD + 1) * ROWS_DEV, TAIL), jnp.float32)
    placing = [
        pltpu.VMEM((owners, tiles, 8, 128), jnp.float32),
        pltpu.VMEM((owners, 128), jnp.int32),
        pltpu.SMEM((owners, 128), jnp.int32),
        pltpu.SemaphoreType.DMA,
    ]

    def place_early(grids, stage):
        return pl.pallas_call(
            functools.partial(early_kernel, cap, len(stage), len(grids) // 2),
            out_shape=[grid] * 2,
            in_specs=[vmem] * (len(grids) + len(stage)),
            out_specs=[vmem] * 2,
            scratch_shapes=placing,
            cost_estimate=pl.CostEstimate(flops=3 * 10**9, bytes_accessed=10**7, transcendentals=0),
            compiler_params=pltpu.CompilerParams(vmem_limit_bytes=24 * 1024 * 1024),
            name="early",
        )(*grids, *stage)

    grids = place_early(place_early([], received[:3]), received[3:last])
    result = pl.pallas_call(
        functools.partial(row_kernel, cap, owners // 2 - last),
        out_shape=jax.ShapeDtypeStruct((2, TAIL, 2, ROWS_DEV, TAIL), jnp.float32),
        in_specs=[vmem] * (5 + owners // 2 - last),
        out_specs=pl.BlockSpec(memory_space=pl.ANY),
        scratch_shapes=[
            *(pltpu.VMEM(grid.shape, grid.dtype) for _ in range(2)),
            *placing,
            pltpu.VMEM((2, ROWS_DEV // 2, 2, 2 * TAIL, 2 * TAIL), jnp.bfloat16),
            pltpu.VMEM((2, 2, TAIL * ROWS_DEV, TAIL), jnp.float32),
            pltpu.SemaphoreType.DMA((2, 2)),
        ],
        compiler_params=pltpu.CompilerParams(vmem_limit_bytes=24 * 1024 * 1024),
        name="rows",
    )(*row_tables(), *grids, *received[last:])
    return (
        result.reshape(2, LEAD, ROWS_DEV, TAIL).transpose(0, 2, 1, 3).reshape(2, ROWS_DEV, NG)
    )


def solution(mesh):
    placed = (
        P(("parts", "tile"), None, None),
        P(("parts", "tile"), None, None),
        P(("parts", "tile"), None),
        P(("parts", "tile")),
        P(("parts", "tile")),
        P(("parts", "tile"), None),
        P(("parts", "tile")),
        P(),
    )
    return jax.shard_map(
        shards,
        mesh=mesh,
        in_specs=placed,
        out_specs=P(None, ("parts", "tile"), None),
        check_vma=False,
    )
```

```python
import functools
import math

import jax
import jax.numpy as jnp
import ml_dtypes
import numpy as np
from jax import lax
from jax.experimental import pallas as pl
from jax.experimental.pallas import tpu as pltpu
from jax.sharding import PartitionSpec as P

VROWS = 128
SUB = 32
NG = 32768
ROWS_DEV = 8
LEAD = 256
TAIL = 128
GROUP = 16

SIN_TERMS = (4.442879549, -7.307815317, 3.597759608, -0.791160565)
COS_TERMS = (1.414213500, -6.978850910, 5.739459580, -1.883552820, 0.310677860)


def halves(table):
    table = np.round(table, 12).astype(np.float32)
    high = table.astype(ml_dtypes.bfloat16)
    low = (table - high.astype(np.float32)).astype(ml_dtypes.bfloat16)
    return high, low


def root(numbers, length):
    angle = 2.0 * np.pi / length * (numbers % length)
    return np.cos(angle), -np.sin(angle)


def complex_left(re, im):
    return np.block([[re, -im], [im, re]])


@functools.cache
def image_tables():
    eight = np.arange(8)
    re, im = root(np.outer(eight, eight), 8)
    left = complex_left(np.kron(np.eye(GROUP), re), np.kron(np.eye(GROUP), im))
    lane = np.arange(128)
    twist = root(np.outer(eight, lane // SUB), SUB)
    four = 8 * np.outer(lane // SUB, lane // SUB) + np.outer(lane % SUB, lane % SUB)
    re, im = root(four, SUB)
    right = complex_left(re, im).T
    row_pos = ((4 * eight[:, None] + lane[None, :] // SUB) - SUB // 2) / SUB
    col_pos = np.broadcast_to((lane[None, :] % SUB - SUB // 2) / SUB, (8, 128))
    taper = (1 - 2 * row_pos**2) * (1 - 2 * col_pos**2) / SUB
    small = np.stack([taper, np.round(twist[0], 12), np.round(twist[1], 12)]).astype(np.float32)
    return (*halves(left), *halves(right), small)


@functools.cache
def row_tables():
    lead, tail = np.arange(LEAD), np.arange(TAIL)
    even = complex_left(*root(np.outer(tail, tail), TAIL))
    odd = complex_left(*root(np.outer(tail, 2 * tail + 1), LEAD))
    twist = np.stack(root(np.outer(lead, tail), NG)) / math.sqrt(NG)
    first = np.stack(halves(even) + halves(odd))
    return first, np.stack(halves(even)), np.round(twist, 12).astype(np.float32)


def split(value):
    high = value.astype(jnp.bfloat16)
    return high, (value - high.astype(jnp.float32)).astype(jnp.bfloat16)


def dot(left, right, transposed=False):
    dims = (((1,), (1 if transposed else 0,)), ((), ()))
    return lax.dot_general(left, right, dims, preferred_element_type=jnp.float32)


def table_times(table_hi, table_lo, hi, lo, transposed=False):
    rows = table_hi.shape[0]
    both = dot(jnp.concatenate([table_hi, table_lo], axis=0), hi, transposed)
    return both[:rows] + both[rows:] + dot(table_hi, lo, transposed)


def times_table(hi, lo, table_hi, table_lo):
    rows = hi.shape[0]
    both = dot(jnp.concatenate([hi, lo], axis=0), table_hi)
    return both[:rows] + both[rows:] + dot(hi, table_lo)


def polynomial(terms, z):
    value = z * terms[-1] + terms[-2]
    for term in terms[-3::-1]:
        value = value * z + term
    return value


def cos_sin(turns):
    whole = (turns + 12582912.0) - 12582912.0
    t = turns - whole
    z = t * t
    half_sin = t * polynomial(SIN_TERMS, z)
    half_cos = polynomial(COS_TERMS, z)
    return 1.0 - half_sin * half_sin, half_sin * half_cos


def send_layout(per_device, owners):
    cap = -(-per_device // (owners - SUB // ROWS_DEV + 1))
    tiles = 2 * cap + (2 * cap + 3) // 4
    return cap, tiles


def merge_halves(cap):
    return cap % 2


def exchange_order(chips):
    quarter = chips // 4
    far = [k + part for k in range(quarter) for part in (3 * quarter, 2 * quarter)]
    near = list(range(chips // 2 - 1, 0, -1))
    return [0] + far[:1] + near[:1] + far[1:] + near[1:]


def image_kernel(
    cap,
    tile_cols,
    *refs,
):
    me = lax.axis_index("tile")
    owners = lax.axis_size("tile")
    count_s, beams, args, keep, give = refs[0], refs[1], refs[2:13], refs[13], refs[14]
    copied, (out, beam_buf, sky, ranks, sems, arg_sems) = refs[15:26], refs[26:]
    copies = [
        pltpu.make_async_copy(arg, held, arg_sems.at[k])
        for k, (arg, held) in enumerate(zip(args, copied))
    ]
    for copy in copies:
        copy.start()
    owner_s, row_s, col_s, station_s, vis, coords = copied[:6]
    left_hi, left_lo, right_hi, right_lo, small = copied[6:]
    per_device = vis.shape[0] // 2
    label_tile = 2 * cap
    sublane = lax.broadcasted_iota(jnp.int32, (8, 128), 0)
    lane = lax.broadcasted_iota(jnp.int32, (8, 128), 1)
    lane_group = lane // SUB
    out[...] = jnp.zeros_like(out)
    spread_columns = (lane * (NG // SUB)).astype(jnp.float32)
    is_label = (sublane == 7) & (lane < 5 * cap)
    for d in range(owners):
        out[d, label_tile] = jnp.where(is_label, spread_columns, 0.0)
    sky[...] = jnp.zeros_like(sky)
    for b in range(owners):
        ranks[b] = 0
    copies[3].wait()
    copies[1].wait()
    live = count_s[0]
    groups = (live + GROUP - 1) >> (GROUP.bit_length() - 1)

    def fetch_beams(g):
        for j in range(GROUP):
            n = jnp.minimum(g, per_device // GROUP - 1) * GROUP + j
            for side in range(2):
                pltpu.make_async_copy(
                    beams.at[station_s[side, n]],
                    beam_buf.at[2 * (g * GROUP + j) + side],
                    sems.at[g],
                ).start()

    def await_beams(g):
        waited = beam_buf.at[pl.ds(g * 2 * GROUP, 2 * GROUP)]
        pltpu.make_async_copy(beams.at[pl.ds(0, 2 * GROUP)], waited, sems.at[g]).wait()

    for g in range(2):
        fetch_beams(g)
    copies[4].wait()
    copies[5].wait()
    copies[10].wait()

    @pl.loop(0, groups * (GROUP // 8))
    def _(g):
        for j in range(8):
            n = g * 8 + j
            shift = row_s[n] & 7
            coords[0, pl.ds(n, 1), :] += shift.astype(jnp.float32)
            vis[pl.ds(2 * n, 2), :] *= (1 - 2 * (shift & 1)).astype(jnp.float32)

    taper = small[0]
    twist_re = jnp.concatenate([small[1]] * GROUP, axis=0)
    twist_im = jnp.concatenate([small[2]] * GROUP, axis=0)
    number = lax.broadcasted_iota(jnp.int32, (SUB, VROWS), 0)
    l_row = (4 * (number % 8) + number // 8 - SUB // 2).astype(jnp.float32) / SUB
    l_col = (number - SUB // 2).astype(jnp.float32) / SUB
    d_row = l_row * l_row
    d_col = l_col * l_col

    def images(g, first=False):
        for quad in range(GROUP // 4):
            x_hi, x_lo, columns = [], [], []
            for j in range(4):
                n = g * GROUP + quad * 4 + j
                u = coords[0, pl.ds(n, 1), :]
                v = coords[1, pl.ds(n, 1), :]
                w = coords[2, pl.ds(n, 1), :]
                vis_re = vis[pl.ds(2 * n, 1), :]
                vis_im = vis[pl.ds(2 * n + 1, 1), :]
                cos_row, sin_row = cos_sin(u * l_row + w * d_row)
                cos_col, sin_col = cos_sin(v * l_col + w * d_col)
                x = jnp.concatenate(
                    [
                        vis_re * cos_row - vis_im * sin_row,
                        vis_re * sin_row + vis_im * cos_row,
                    ],
                    axis=1,
                )
                hi, lo = split(x)
                x_hi.append(hi)
                x_lo.append(lo)
                columns.append(split(cos_col) + split(sin_col))
            c_hi, c_lo, s_hi, s_lo = zip(*columns)

            def matrix(c, s):
                real = [jnp.concatenate([a, -b], axis=1) for a, b in zip(c, s)]
                imag = [jnp.concatenate([b, a], axis=1) for a, b in zip(c, s)]
                return jnp.concatenate(real + imag, axis=0)

            lhs = jnp.concatenate(x_hi + x_lo, axis=0)
            both = dot(lhs, matrix(c_hi, s_hi), True)
            sums = both[:128] + both[128:] + dot(lhs[:128], matrix(c_lo, s_lo), True)
            if first and quad == 0:
                await_beams(g)
            for j in range(4):
                n = g * GROUP + quad * 4 + j
                flat = []
                for c in range(2):
                    value = None
                    for i in range(4):
                        piece = sums[32 * j + 8 * i : 32 * j + 8 * i + 8, 128 * c : 128 * c + 128]
                        if i != j:
                            piece = pltpu.roll(piece, (SUB * (i - j)) % 128, 1)
                        value = piece if value is None else jnp.where(lane_group == i, piece, value)
                    flat.append(value)
                one_re = beam_buf[2 * n, pl.ds(0, 8, stride=2), :]
                one_im = beam_buf[2 * n, pl.ds(1, 8, stride=2), :]
                two_re = beam_buf[2 * n + 1, pl.ds(0, 8, stride=2), :]
                two_im = beam_buf[2 * n + 1, pl.ds(1, 8, stride=2), :]
                beam_re = taper * (one_re * two_re + one_im * two_im)
                beam_im = taper * (one_im * two_re - one_re * two_im)
                sky_re = beam_re * flat[0] - beam_im * flat[1]
                sky_im = beam_re * flat[1] + beam_im * flat[0]
                in_use = n < live
                place = (quad * 4 + j) * 8
                sky[g & 1, place : place + 8, :] = jnp.where(in_use, sky_re, 0.0)
                sky[g & 1, place + 8 * GROUP : place + 8 * GROUP + 8, :] = jnp.where(in_use, sky_im, 0.0)

    def cells(g):
        hi, lo = split(sky[g & 1])
        z = table_times(left_hi[...], left_lo[...], hi, lo)
        z_re, z_im = z[: 8 * GROUP], z[8 * GROUP :]
        y_re = z_re * twist_re - z_im * twist_im
        y_im = z_re * twist_im + z_im * twist_re
        hi, lo = split(jnp.concatenate([y_re, y_im], axis=1))
        result = times_table(hi, lo, right_hi[...], right_lo[...])
        for j in range(GROUP):
            n = g * GROUP + j
            band = row_s[n] >> 3
            shift = row_s[n] & 7
            rank = ranks[band]
            ranks[band] = rank + 1
            late = sublane < shift
            last = jnp.minimum(band + 4, owners - 1)
            for c in range(2):
                value = result[8 * j : 8 * j + 8, 128 * c : 128 * c + 128]
                spread = jnp.where(late & (lane_group == 0), 0.0, value)
                tile = 2 * rank + c
                for o in range(4):
                    pltpu.store(out.at[(band + o) ^ me, tile], spread, mask=lane_group == o)
                part = tile & 3
                tail = pltpu.roll(value, SUB * part, 1)
                pltpu.store(
                    out.at[last ^ me, 2 * cap + (tile >> 2)], tail, mask=late & (lane_group == part)
                )
            column = jnp.full((8, 128), owner_s[n] * tile_cols + col_s[n], jnp.float32)
            for o in range(5):
                here = (sublane == 7) & (lane == o * cap + rank)
                if o == 4:
                    here = here & (sublane - 7 < shift)
                target = last if o == 4 else band + o
                pltpu.store(out.at[target ^ me, label_tile], column, mask=here)

    images(0, True)
    for copy in copies[6:10] + [copies[0], copies[2]]:
        copy.wait()

    @pl.loop(1, groups)
    def _(g):
        await_beams(g)
        fetch_beams(g + 1)
        cells(g - 1)
        images(g)

    cells(groups - 1)
    await_beams(groups)
    for k in range(owners // 2):
        keep[k] = out[2 * k]
        give[k] = out[2 * k + 1]


def merge_kernel(cap, keep, got, *messages):
    tiles = keep.shape[1]
    whole = tiles - merge_halves(cap)
    lane = lax.broadcasted_iota(jnp.int32, (8, 128), 1)
    for k, message in zip(exchange_order(keep.shape[0]), messages):
        message[:whole] = keep[k, :whole]
        message[whole : 2 * whole] = got[k, :whole]
        if whole < tiles:
            message[2 * whole] = jnp.where(
                lane < 64, keep[k, whole], pltpu.roll(got[k, whole], 64, 1)
            )


def place_slabs(cap, messages, grids, scratch, earlier=None):
    received, label_v, label_s, sem = scratch
    sources = 2 * len(messages)
    whole = received.shape[1] - merge_halves(cap)
    for k, message in enumerate(messages):
        received[2 * k, :whole] = message[:whole]
        received[2 * k + 1, :whole] = message[whole : 2 * whole]
        if merge_halves(cap):
            received[2 * k, whole] = message[2 * whole]
            received[2 * k + 1, whole] = pltpu.roll(message[2 * whole], 64, 1)
    label_v[:sources] = received[:sources, 2 * cap, 7, :].astype(jnp.int32)
    copy = pltpu.make_async_copy(label_v, label_s, sem)
    copy.start()
    for c, grid in enumerate(grids):
        grid[...] = earlier[c][...] if earlier else jnp.zeros_like(grid)
    lane = lax.broadcasted_iota(jnp.int32, (8, 128), 1)
    not_label = lax.broadcasted_iota(jnp.int32, (8, 128), 0) < 7
    copy.wait()

    @pl.loop(0, sources)
    def _(source):
        for i in range(cap):
            for o in range(5):
                column = label_s[source, o * cap + i]
                offset = column & 127
                here = pl.multiple_of((column >> 7) * 8, 8)
                place = lane - offset
                inside = (place >= 0) & (place < SUB)
                beyond = place < SUB - 128
                if o == 4:
                    inside, beyond = inside & not_label, beyond & not_label
                added = []
                for c in range(2):
                    if o < 4:
                        value, part = received[source, 2 * i + c], o
                    else:
                        value = received[source, 2 * cap + (2 * i + c) // 4]
                        part = (2 * i + c) % 4
                    value = pltpu.roll(value, (offset - SUB * part) & 127, 1)
                    added.append(jnp.where(inside, value, 0.0))
                    added.append(jnp.where(beyond, value, 0.0))
                before = [
                    grids[c][pl.ds(here + 8 * k, 8), :] for c in range(2) for k in range(2)
                ]
                for c in range(2):
                    for k in range(2):
                        grids[c][pl.ds(here + 8 * k, 8), :] = before[2 * c + k] + added[2 * c + k]


def early_kernel(cap, count, started, *refs):
    earlier, refs = refs[: 2 * started], refs[2 * started :]
    place_slabs(cap, refs[:count], refs[count : count + 2], refs[count + 2 :], earlier)


def row_kernel(
    cap,
    count,
    first,
    second,
    twist,
    *refs,
):
    earlier, messages, out = refs[:2], refs[2 : 2 + count], refs[2 + count]
    grids, scratch = refs[3 + count : 5 + count], refs[5 + count :]
    middle, held, out_sems = scratch[4:]
    place_slabs(cap, messages, grids, scratch[:4], earlier)

    for pair in range(ROWS_DEV // 2):
        halves_of = []
        for e in range(2):
            rows = [
                pl.ds(ROWS_DEV * e + 2 * pair + k, TAIL, stride=2 * ROWS_DEV) for k in range(2)
            ]
            value = jnp.concatenate(
                [jnp.concatenate([grids[c][at, :] for at in rows], axis=1) for c in range(2)], 0
            )
            hi, lo = split(value)
            halves_of.append(table_times(first[2 * e], first[2 * e + 1], hi, lo))
        for h, a in enumerate((halves_of[0] + halves_of[1], halves_of[0] - halves_of[1])):
            turn_re = twist[0, TAIL * h : TAIL * h + TAIL]
            turn_im = twist[1, TAIL * h : TAIL * h + TAIL]
            for k in range(2):
                a_re = a[:TAIL, 128 * k : 128 * k + 128]
                a_im = a[TAIL:, 128 * k : 128 * k + 128]
                b = jnp.concatenate(
                    [a_re * turn_re - a_im * turn_im, a_re * turn_im + a_im * turn_re], axis=1
                )
                for part, value in enumerate(split(b)):
                    middle[h, pair, part, TAIL * k : TAIL * k + TAIL, :] = value

    copies = []
    for h in range(2):
        for pair in range(ROWS_DEV // 2):
            result = table_times(
                second[0], second[1], middle[h, pair, 0], middle[h, pair, 1], True
            )
            for c in range(2):
                for k in range(2):
                    held[h, c, pl.ds(2 * pair + k, TAIL, stride=ROWS_DEV), :] = result[
                        128 * c : 128 * c + 128, 128 * k : 128 * k + 128
                    ]
        for c in range(2):
            copies.append(
                pltpu.make_async_copy(
                    held.at[h, c].reshape(TAIL, ROWS_DEV, TAIL),
                    out.at[c, :, h],
                    out_sems.at[h, c],
                )
            )
            copies[-1].start()
    for copy in copies:
        copy.wait()


def shards(
    visibility, coords, block_owner, block_row, block_col, stations, block_count, beam_terms
):
    owners = lax.axis_size("tile")
    per_device = visibility.shape[0]
    tile_cols = NG // owners
    cap, tiles = send_layout(per_device, owners)
    stations_all = beam_terms.shape[0]
    vmem = pl.BlockSpec(memory_space=pltpu.VMEM)
    beams = (
        beam_terms.reshape(stations_all, 2, 8, 128)
        .transpose(0, 2, 1, 3)
        .reshape(stations_all, 16, 128)
    )
    labels = (
        block_owner.reshape(per_device),
        block_row,
        block_col,
        stations.T,
    )
    values = (
        visibility.reshape(per_device * 2, VROWS),
        coords.transpose(1, 0, 2),
        *image_tables(),
    )
    hbm = pl.BlockSpec(memory_space=pltpu.HBM)
    half = jax.ShapeDtypeStruct((owners // 2, tiles, 8, 128), jnp.float32)
    keep, give = pl.pallas_call(
        functools.partial(image_kernel, cap, tile_cols),
        out_shape=[half] * 2,
        in_specs=[pl.BlockSpec(memory_space=pltpu.SMEM)] + [hbm] * (1 + len(labels) + len(values)),
        out_specs=[vmem] * 2,
        scratch_shapes=[
            *(pltpu.SMEM(label.shape, label.dtype) for label in labels),
            *(pltpu.VMEM(value.shape, value.dtype) for value in values),
            pltpu.VMEM((owners, tiles, 8, 128), jnp.float32),
            pltpu.VMEM((2 * (per_device + GROUP), 16, 128), jnp.float32),
            pltpu.VMEM((2, 16 * GROUP, 128), jnp.float32),
            pltpu.SMEM((owners,), jnp.int32),
            pltpu.SemaphoreType.DMA((per_device // GROUP + 1,)),
            pltpu.SemaphoreType.DMA((len(labels) + len(values),)),
        ],
        compiler_params=pltpu.CompilerParams(vmem_limit_bytes=24 * 1024 * 1024),
        name="image",
    )(
        block_count,
        *(pltpu.with_memory_space_constraint(x, pltpu.HBM) for x in (beams, *labels, *values)),
    )
    got = lax.ppermute(give, "tile", [(source, source ^ 1) for source in range(owners)])
    messages = pl.pallas_call(
        functools.partial(merge_kernel, cap),
        out_shape=[jax.ShapeDtypeStruct((2 * tiles - merge_halves(cap), 8, 128), jnp.float32)]
        * (owners // 2),
        in_specs=[vmem] * 2,
        out_specs=[vmem] * (owners // 2),
        compiler_params=pltpu.CompilerParams(vmem_limit_bytes=24 * 1024 * 1024),
        name="merge",
    )(keep, got)
    order = exchange_order(owners // 2)

    def exchange(k, message):
        pairs = [(source, source ^ (2 * k)) for source in range(owners)]
        return lax.ppermute(message, "tile", pairs) if k else message

    received = [exchange(k, message) for k, message in zip(order, messages)]
    last = 1 + owners // 4
    grid = jax.ShapeDtypeStruct(((LEAD + 1) * ROWS_DEV, TAIL), jnp.float32)
    placing = [
        pltpu.VMEM((owners, tiles, 8, 128), jnp.float32),
        pltpu.VMEM((owners, 128), jnp.int32),
        pltpu.SMEM((owners, 128), jnp.int32),
        pltpu.SemaphoreType.DMA,
    ]

    def place_early(grids, stage):
        return pl.pallas_call(
            functools.partial(early_kernel, cap, len(stage), len(grids) // 2),
            out_shape=[grid] * 2,
            in_specs=[vmem] * (len(grids) + len(stage)),
            out_specs=[vmem] * 2,
            scratch_shapes=placing,
            cost_estimate=pl.CostEstimate(flops=3 * 10**9, bytes_accessed=10**7, transcendentals=0),
            compiler_params=pltpu.CompilerParams(vmem_limit_bytes=24 * 1024 * 1024),
            name="early",
        )(*grids, *stage)

    grids = place_early(place_early([], received[:3]), received[3:last])
    result = pl.pallas_call(
        functools.partial(row_kernel, cap, owners // 2 - last),
        out_shape=jax.ShapeDtypeStruct((2, TAIL, 2, ROWS_DEV, TAIL), jnp.float32),
        in_specs=[vmem] * (5 + owners // 2 - last),
        out_specs=pl.BlockSpec(memory_space=pl.ANY),
        scratch_shapes=[
            *(pltpu.VMEM(grid.shape, grid.dtype) for _ in range(2)),
            *placing,
            pltpu.VMEM((2, ROWS_DEV // 2, 2, 2 * TAIL, 2 * TAIL), jnp.bfloat16),
            pltpu.VMEM((2, 2, TAIL * ROWS_DEV, TAIL), jnp.float32),
            pltpu.SemaphoreType.DMA((2, 2)),
        ],
        compiler_params=pltpu.CompilerParams(vmem_limit_bytes=24 * 1024 * 1024),
        name="rows",
    )(*row_tables(), *grids, *received[last:])
    return (
        result.reshape(2, LEAD, ROWS_DEV, TAIL).transpose(0, 2, 1, 3).reshape(2, ROWS_DEV, NG)
    )


def solution(mesh):
    placed = (
        P(("parts", "tile"), None, None),
        P(("parts", "tile"), None, None),
        P(("parts", "tile"), None),
        P(("parts", "tile")),
        P(("parts", "tile")),
        P(("parts", "tile"), None),
        P(("parts", "tile")),
        P(),
    )
    return jax.shard_map(
        shards,
        mesh=mesh,
        in_specs=placed,
        out_specs=P(None, ("parts", "tile"), None),
        check_vma=False,
    )
```

```python
import functools
import math

import jax
import jax.numpy as jnp
import ml_dtypes
import numpy as np
from jax import lax
from jax.experimental import pallas as pl
from jax.experimental.pallas import tpu as pltpu
from jax.sharding import PartitionSpec as P

VROWS = 128
SUB = 32
NG = 32768
ROWS_DEV = 8
LEAD = 256
TAIL = 128
GROUP = 16

SIN_TERMS = (4.442879549, -7.307815317, 3.597759608, -0.791160565)
COS_TERMS = (1.414213500, -6.978850910, 5.739459580, -1.883552820, 0.310677860)


def halves(table):
    table = np.round(table, 12).astype(np.float32)
    high = table.astype(ml_dtypes.bfloat16)
    low = (table - high.astype(np.float32)).astype(ml_dtypes.bfloat16)
    return high, low


def root(numbers, length):
    angle = 2.0 * np.pi / length * (numbers % length)
    return np.cos(angle), -np.sin(angle)


def complex_left(re, im):
    return np.block([[re, -im], [im, re]])


@functools.cache
def image_tables():
    eight = np.arange(8)
    re, im = root(np.outer(eight, eight), 8)
    left = complex_left(np.kron(np.eye(GROUP), re), np.kron(np.eye(GROUP), im))
    lane = np.arange(128)
    twist = root(np.outer(eight, lane // SUB), SUB)
    four = 8 * np.outer(lane // SUB, lane // SUB) + np.outer(lane % SUB, lane % SUB)
    re, im = root(four, SUB)
    right = complex_left(re, im).T
    row_pos = ((4 * eight[:, None] + lane[None, :] // SUB) - SUB // 2) / SUB
    col_pos = np.broadcast_to((lane[None, :] % SUB - SUB // 2) / SUB, (8, 128))
    taper = (1 - 2 * row_pos**2) * (1 - 2 * col_pos**2) / SUB
    small = np.stack([taper, np.round(twist[0], 12), np.round(twist[1], 12)]).astype(np.float32)
    return (*halves(left), *halves(right), small)


@functools.cache
def row_tables():
    lead, tail = np.arange(LEAD), np.arange(TAIL)
    even = complex_left(*root(np.outer(tail, tail), TAIL))
    odd = complex_left(*root(np.outer(tail, 2 * tail + 1), LEAD))
    twist = np.stack(root(np.outer(lead, tail), NG)) / math.sqrt(NG)
    first = np.stack(halves(even) + halves(odd))
    return first, np.stack(halves(even)), np.round(twist, 12).astype(np.float32)


def split(value):
    high = value.astype(jnp.bfloat16)
    return high, (value - high.astype(jnp.float32)).astype(jnp.bfloat16)


def dot(left, right, transposed=False):
    dims = (((1,), (1 if transposed else 0,)), ((), ()))
    return lax.dot_general(left, right, dims, preferred_element_type=jnp.float32)


def table_times(table_hi, table_lo, hi, lo, transposed=False):
    rows = table_hi.shape[0]
    both = dot(jnp.concatenate([table_hi, table_lo], axis=0), hi, transposed)
    return both[:rows] + both[rows:] + dot(table_hi, lo, transposed)


def times_table(hi, lo, table_hi, table_lo):
    rows = hi.shape[0]
    both = dot(jnp.concatenate([hi, lo], axis=0), table_hi)
    return both[:rows] + both[rows:] + dot(hi, table_lo)


def polynomial(terms, z):
    value = z * terms[-1] + terms[-2]
    for term in terms[-3::-1]:
        value = value * z + term
    return value


def cos_sin(turns):
    whole = (turns + 12582912.0) - 12582912.0
    t = turns - whole
    z = t * t
    half_sin = t * polynomial(SIN_TERMS, z)
    half_cos = polynomial(COS_TERMS, z)
    return 1.0 - half_sin * half_sin, half_sin * half_cos


def send_layout(per_device, owners):
    cap = -(-per_device // (owners - SUB // ROWS_DEV + 1))
    tiles = 2 * cap + (2 * cap + 3) // 4
    return cap, tiles


def merge_halves(cap):
    return cap % 2


def exchange_order(chips):
    quarter = chips // 4
    far = [k + part for k in range(quarter) for part in (3 * quarter, 2 * quarter)]
    near = [1] + list(range(chips // 2 - 1, 1, -1))
    return [0] + far[:1] + near[:1] + far[1:] + near[1:]


def image_kernel(
    cap,
    tile_cols,
    *refs,
):
    me = lax.axis_index("tile")
    owners = lax.axis_size("tile")
    count_s, beams, args, keep, give = refs[0], refs[1], refs[2:13], refs[13], refs[14]
    copied, (out, beam_buf, sky, ranks, sems, arg_sems) = refs[15:26], refs[26:]
    copies = [
        pltpu.make_async_copy(arg, held, arg_sems.at[k])
        for k, (arg, held) in enumerate(zip(args, copied))
    ]
    for copy in copies:
        copy.start()
    owner_s, row_s, col_s, station_s, vis, coords = copied[:6]
    left_hi, left_lo, right_hi, right_lo, small = copied[6:]
    per_device = vis.shape[0] // 2
    label_tile = 2 * cap
    sublane = lax.broadcasted_iota(jnp.int32, (8, 128), 0)
    lane = lax.broadcasted_iota(jnp.int32, (8, 128), 1)
    lane_group = lane // SUB
    out[...] = jnp.zeros_like(out)
    spread_columns = (lane * (NG // SUB)).astype(jnp.float32)
    is_label = (sublane == 7) & (lane < 5 * cap)
    for d in range(owners):
        out[d, label_tile] = jnp.where(is_label, spread_columns, 0.0)
    sky[...] = jnp.zeros_like(sky)
    for b in range(owners):
        ranks[b] = 0
    copies[3].wait()
    copies[1].wait()
    live = count_s[0]
    groups = (live + GROUP - 1) >> (GROUP.bit_length() - 1)

    def fetch_beams(g):
        for j in range(GROUP):
            n = jnp.minimum(g, per_device // GROUP - 1) * GROUP + j
            for side in range(2):
                pltpu.make_async_copy(
                    beams.at[station_s[side, n]],
                    beam_buf.at[2 * (g * GROUP + j) + side],
                    sems.at[g],
                ).start()

    def await_beams(g):
        waited = beam_buf.at[pl.ds(g * 2 * GROUP, 2 * GROUP)]
        pltpu.make_async_copy(beams.at[pl.ds(0, 2 * GROUP)], waited, sems.at[g]).wait()

    for g in range(2):
        fetch_beams(g)
    copies[4].wait()
    copies[5].wait()
    copies[10].wait()

    @pl.loop(0, groups * (GROUP // 8))
    def _(g):
        for j in range(8):
            n = g * 8 + j
            shift = row_s[n] & 7
            coords[0, pl.ds(n, 1), :] += shift.astype(jnp.float32)
            vis[pl.ds(2 * n, 2), :] *= (1 - 2 * (shift & 1)).astype(jnp.float32)

    taper = small[0]
    twist_re = jnp.concatenate([small[1]] * GROUP, axis=0)
    twist_im = jnp.concatenate([small[2]] * GROUP, axis=0)
    number = lax.broadcasted_iota(jnp.int32, (SUB, VROWS), 0)
    l_row = (4 * (number % 8) + number // 8 - SUB // 2).astype(jnp.float32) / SUB
    l_col = (number - SUB // 2).astype(jnp.float32) / SUB
    d_row = l_row * l_row
    d_col = l_col * l_col

    def images(g, first=False):
        for quad in range(GROUP // 4):
            x_hi, x_lo, columns = [], [], []
            for j in range(4):
                n = g * GROUP + quad * 4 + j
                u = coords[0, pl.ds(n, 1), :]
                v = coords[1, pl.ds(n, 1), :]
                w = coords[2, pl.ds(n, 1), :]
                vis_re = vis[pl.ds(2 * n, 1), :]
                vis_im = vis[pl.ds(2 * n + 1, 1), :]
                cos_row, sin_row = cos_sin(u * l_row + w * d_row)
                cos_col, sin_col = cos_sin(v * l_col + w * d_col)
                x = jnp.concatenate(
                    [
                        vis_re * cos_row - vis_im * sin_row,
                        vis_re * sin_row + vis_im * cos_row,
                    ],
                    axis=1,
                )
                hi, lo = split(x)
                x_hi.append(hi)
                x_lo.append(lo)
                columns.append(split(cos_col) + split(sin_col))
            c_hi, c_lo, s_hi, s_lo = zip(*columns)

            def matrix(c, s):
                real = [jnp.concatenate([a, -b], axis=1) for a, b in zip(c, s)]
                imag = [jnp.concatenate([b, a], axis=1) for a, b in zip(c, s)]
                return jnp.concatenate(real + imag, axis=0)

            lhs = jnp.concatenate(x_hi + x_lo, axis=0)
            both = dot(lhs, matrix(c_hi, s_hi), True)
            sums = both[:128] + both[128:] + dot(lhs[:128], matrix(c_lo, s_lo), True)
            if first and quad == 0:
                await_beams(g)
            for j in range(4):
                n = g * GROUP + quad * 4 + j
                flat = []
                for c in range(2):
                    value = None
                    for i in range(4):
                        piece = sums[32 * j + 8 * i : 32 * j + 8 * i + 8, 128 * c : 128 * c + 128]
                        if i != j:
                            piece = pltpu.roll(piece, (SUB * (i - j)) % 128, 1)
                        value = piece if value is None else jnp.where(lane_group == i, piece, value)
                    flat.append(value)
                one_re = beam_buf[2 * n, pl.ds(0, 8, stride=2), :]
                one_im = beam_buf[2 * n, pl.ds(1, 8, stride=2), :]
                two_re = beam_buf[2 * n + 1, pl.ds(0, 8, stride=2), :]
                two_im = beam_buf[2 * n + 1, pl.ds(1, 8, stride=2), :]
                beam_re = taper * (one_re * two_re + one_im * two_im)
                beam_im = taper * (one_im * two_re - one_re * two_im)
                sky_re = beam_re * flat[0] - beam_im * flat[1]
                sky_im = beam_re * flat[1] + beam_im * flat[0]
                in_use = n < live
                place = (quad * 4 + j) * 8
                sky[g & 1, place : place + 8, :] = jnp.where(in_use, sky_re, 0.0)
                sky[g & 1, place + 8 * GROUP : place + 8 * GROUP + 8, :] = jnp.where(in_use, sky_im, 0.0)

    def cells(g):
        hi, lo = split(sky[g & 1])
        z = table_times(left_hi[...], left_lo[...], hi, lo)
        z_re, z_im = z[: 8 * GROUP], z[8 * GROUP :]
        y_re = z_re * twist_re - z_im * twist_im
        y_im = z_re * twist_im + z_im * twist_re
        hi, lo = split(jnp.concatenate([y_re, y_im], axis=1))
        result = times_table(hi, lo, right_hi[...], right_lo[...])
        for j in range(GROUP):
            n = g * GROUP + j
            band = row_s[n] >> 3
            shift = row_s[n] & 7
            rank = ranks[band]
            ranks[band] = rank + 1
            late = sublane < shift
            last = jnp.minimum(band + 4, owners - 1)
            for c in range(2):
                value = result[8 * j : 8 * j + 8, 128 * c : 128 * c + 128]
                spread = jnp.where(late & (lane_group == 0), 0.0, value)
                tile = 2 * rank + c
                for o in range(4):
                    pltpu.store(out.at[(band + o) ^ me, tile], spread, mask=lane_group == o)
                part = tile & 3
                tail = pltpu.roll(value, SUB * part, 1)
                pltpu.store(
                    out.at[last ^ me, 2 * cap + (tile >> 2)], tail, mask=late & (lane_group == part)
                )
            column = jnp.full((8, 128), owner_s[n] * tile_cols + col_s[n], jnp.float32)
            for o in range(5):
                here = (sublane == 7) & (lane == o * cap + rank)
                if o == 4:
                    here = here & (sublane - 7 < shift)
                target = last if o == 4 else band + o
                pltpu.store(out.at[target ^ me, label_tile], column, mask=here)

    images(0, True)
    for copy in copies[6:10] + [copies[0], copies[2]]:
        copy.wait()

    @pl.loop(1, groups)
    def _(g):
        await_beams(g)
        fetch_beams(g + 1)
        cells(g - 1)
        images(g)

    cells(groups - 1)
    await_beams(groups)
    for k in range(owners // 2):
        keep[k] = out[2 * k]
        give[k] = out[2 * k + 1]


def merge_kernel(cap, keep, got, *messages):
    tiles = keep.shape[1]
    whole = tiles - merge_halves(cap)
    lane = lax.broadcasted_iota(jnp.int32, (8, 128), 1)
    for k, message in zip(exchange_order(keep.shape[0]), messages):
        message[:whole] = keep[k, :whole]
        message[whole : 2 * whole] = got[k, :whole]
        if whole < tiles:
            message[2 * whole] = jnp.where(
                lane < 64, keep[k, whole], pltpu.roll(got[k, whole], 64, 1)
            )


def place_slabs(cap, messages, grids, scratch, earlier=None):
    received, label_v, label_s, sem = scratch
    sources = 2 * len(messages)
    whole = received.shape[1] - merge_halves(cap)
    for k, message in enumerate(messages):
        received[2 * k, :whole] = message[:whole]
        received[2 * k + 1, :whole] = message[whole : 2 * whole]
        if merge_halves(cap):
            received[2 * k, whole] = message[2 * whole]
            received[2 * k + 1, whole] = pltpu.roll(message[2 * whole], 64, 1)
    label_v[:sources] = received[:sources, 2 * cap, 7, :].astype(jnp.int32)
    copy = pltpu.make_async_copy(label_v, label_s, sem)
    copy.start()
    for c, grid in enumerate(grids):
        grid[...] = earlier[c][...] if earlier else jnp.zeros_like(grid)
    lane = lax.broadcasted_iota(jnp.int32, (8, 128), 1)
    not_label = lax.broadcasted_iota(jnp.int32, (8, 128), 0) < 7
    copy.wait()

    @pl.loop(0, sources)
    def _(source):
        for i in range(cap):
            for o in range(5):
                column = label_s[source, o * cap + i]
                offset = column & 127
                here = pl.multiple_of((column >> 7) * 8, 8)
                place = lane - offset
                inside = (place >= 0) & (place < SUB)
                beyond = place < SUB - 128
                if o == 4:
                    inside, beyond = inside & not_label, beyond & not_label
                added = []
                for c in range(2):
                    if o < 4:
                        value, part = received[source, 2 * i + c], o
                    else:
                        value = received[source, 2 * cap + (2 * i + c) // 4]
                        part = (2 * i + c) % 4
                    value = pltpu.roll(value, (offset - SUB * part) & 127, 1)
                    added.append(jnp.where(inside, value, 0.0))
                    added.append(jnp.where(beyond, value, 0.0))
                before = [
                    grids[c][pl.ds(here + 8 * k, 8), :] for c in range(2) for k in range(2)
                ]
                for c in range(2):
                    for k in range(2):
                        grids[c][pl.ds(here + 8 * k, 8), :] = before[2 * c + k] + added[2 * c + k]


def early_kernel(cap, count, started, *refs):
    earlier, refs = refs[: 2 * started], refs[2 * started :]
    place_slabs(cap, refs[:count], refs[count : count + 2], refs[count + 2 :], earlier)


def row_kernel(
    cap,
    count,
    first,
    second,
    twist,
    *refs,
):
    earlier, messages, out = refs[:2], refs[2 : 2 + count], refs[2 + count]
    grids, scratch = refs[3 + count : 5 + count], refs[5 + count :]
    middle, held, out_sems = scratch[4:]
    place_slabs(cap, messages, grids, scratch[:4], earlier)

    for pair in range(ROWS_DEV // 2):
        halves_of = []
        for e in range(2):
            rows = [
                pl.ds(ROWS_DEV * e + 2 * pair + k, TAIL, stride=2 * ROWS_DEV) for k in range(2)
            ]
            value = jnp.concatenate(
                [jnp.concatenate([grids[c][at, :] for at in rows], axis=1) for c in range(2)], 0
            )
            hi, lo = split(value)
            halves_of.append(table_times(first[2 * e], first[2 * e + 1], hi, lo))
        for h, a in enumerate((halves_of[0] + halves_of[1], halves_of[0] - halves_of[1])):
            turn_re = twist[0, TAIL * h : TAIL * h + TAIL]
            turn_im = twist[1, TAIL * h : TAIL * h + TAIL]
            for k in range(2):
                a_re = a[:TAIL, 128 * k : 128 * k + 128]
                a_im = a[TAIL:, 128 * k : 128 * k + 128]
                b = jnp.concatenate(
                    [a_re * turn_re - a_im * turn_im, a_re * turn_im + a_im * turn_re], axis=1
                )
                for part, value in enumerate(split(b)):
                    middle[h, pair, part, TAIL * k : TAIL * k + TAIL, :] = value

    copies = []
    for h in range(2):
        for pair in range(ROWS_DEV // 2):
            result = table_times(
                second[0], second[1], middle[h, pair, 0], middle[h, pair, 1], True
            )
            for c in range(2):
                for k in range(2):
                    held[h, c, pl.ds(2 * pair + k, TAIL, stride=ROWS_DEV), :] = result[
                        128 * c : 128 * c + 128, 128 * k : 128 * k + 128
                    ]
        for c in range(2):
            copies.append(
                pltpu.make_async_copy(
                    held.at[h, c].reshape(TAIL, ROWS_DEV, TAIL),
                    out.at[c, :, h],
                    out_sems.at[h, c],
                )
            )
            copies[-1].start()
    for copy in copies:
        copy.wait()


def shards(
    visibility, coords, block_owner, block_row, block_col, stations, block_count, beam_terms
):
    owners = lax.axis_size("tile")
    per_device = visibility.shape[0]
    tile_cols = NG // owners
    cap, tiles = send_layout(per_device, owners)
    stations_all = beam_terms.shape[0]
    vmem = pl.BlockSpec(memory_space=pltpu.VMEM)
    beams = (
        beam_terms.reshape(stations_all, 2, 8, 128)
        .transpose(0, 2, 1, 3)
        .reshape(stations_all, 16, 128)
    )
    labels = (
        block_owner.reshape(per_device),
        block_row,
        block_col,
        stations.T,
    )
    values = (
        visibility.reshape(per_device * 2, VROWS),
        coords.transpose(1, 0, 2),
        *image_tables(),
    )
    hbm = pl.BlockSpec(memory_space=pltpu.HBM)
    half = jax.ShapeDtypeStruct((owners // 2, tiles, 8, 128), jnp.float32)
    keep, give = pl.pallas_call(
        functools.partial(image_kernel, cap, tile_cols),
        out_shape=[half] * 2,
        in_specs=[pl.BlockSpec(memory_space=pltpu.SMEM)] + [hbm] * (1 + len(labels) + len(values)),
        out_specs=[vmem] * 2,
        scratch_shapes=[
            *(pltpu.SMEM(label.shape, label.dtype) for label in labels),
            *(pltpu.VMEM(value.shape, value.dtype) for value in values),
            pltpu.VMEM((owners, tiles, 8, 128), jnp.float32),
            pltpu.VMEM((2 * (per_device + GROUP), 16, 128), jnp.float32),
            pltpu.VMEM((2, 16 * GROUP, 128), jnp.float32),
            pltpu.SMEM((owners,), jnp.int32),
            pltpu.SemaphoreType.DMA((per_device // GROUP + 1,)),
            pltpu.SemaphoreType.DMA((len(labels) + len(values),)),
        ],
        compiler_params=pltpu.CompilerParams(vmem_limit_bytes=24 * 1024 * 1024),
        name="image",
    )(
        block_count,
        *(pltpu.with_memory_space_constraint(x, pltpu.HBM) for x in (beams, *labels, *values)),
    )
    got = lax.ppermute(give, "tile", [(source, source ^ 1) for source in range(owners)])
    messages = pl.pallas_call(
        functools.partial(merge_kernel, cap),
        out_shape=[jax.ShapeDtypeStruct((2 * tiles - merge_halves(cap), 8, 128), jnp.float32)]
        * (owners // 2),
        in_specs=[vmem] * 2,
        out_specs=[vmem] * (owners // 2),
        compiler_params=pltpu.CompilerParams(vmem_limit_bytes=24 * 1024 * 1024),
        name="merge",
    )(keep, got)
    order = exchange_order(owners // 2)

    def exchange(k, message):
        pairs = [(source, source ^ (2 * k)) for source in range(owners)]
        return lax.ppermute(message, "tile", pairs) if k else message

    received = [exchange(k, message) for k, message in zip(order, messages)]
    last = 1 + owners // 4
    grid = jax.ShapeDtypeStruct(((LEAD + 1) * ROWS_DEV, TAIL), jnp.float32)
    placing = [
        pltpu.VMEM((owners, tiles, 8, 128), jnp.float32),
        pltpu.VMEM((owners, 128), jnp.int32),
        pltpu.SMEM((owners, 128), jnp.int32),
        pltpu.SemaphoreType.DMA,
    ]

    def place_early(grids, stage):
        return pl.pallas_call(
            functools.partial(early_kernel, cap, len(stage), len(grids) // 2),
            out_shape=[grid] * 2,
            in_specs=[vmem] * (len(grids) + len(stage)),
            out_specs=[vmem] * 2,
            scratch_shapes=placing,
            cost_estimate=pl.CostEstimate(flops=3 * 10**9, bytes_accessed=10**7, transcendentals=0),
            compiler_params=pltpu.CompilerParams(vmem_limit_bytes=24 * 1024 * 1024),
            name="early",
        )(*grids, *stage)

    grids = place_early(place_early([], received[:3]), received[3:last])
    result = pl.pallas_call(
        functools.partial(row_kernel, cap, owners // 2 - last),
        out_shape=jax.ShapeDtypeStruct((2, TAIL, 2, ROWS_DEV, TAIL), jnp.float32),
        in_specs=[vmem] * (5 + owners // 2 - last),
        out_specs=pl.BlockSpec(memory_space=pl.ANY),
        scratch_shapes=[
            *(pltpu.VMEM(grid.shape, grid.dtype) for _ in range(2)),
            *placing,
            pltpu.VMEM((2, ROWS_DEV // 2, 2, 2 * TAIL, 2 * TAIL), jnp.bfloat16),
            pltpu.VMEM((2, 2, TAIL * ROWS_DEV, TAIL), jnp.float32),
            pltpu.SemaphoreType.DMA((2, 2)),
        ],
        compiler_params=pltpu.CompilerParams(vmem_limit_bytes=24 * 1024 * 1024),
        name="rows",
    )(*row_tables(), *grids, *received[last:])
    return (
        result.reshape(2, LEAD, ROWS_DEV, TAIL).transpose(0, 2, 1, 3).reshape(2, ROWS_DEV, NG)
    )


def solution(mesh):
    placed = (
        P(("parts", "tile"), None, None),
        P(("parts", "tile"), None, None),
        P(("parts", "tile"), None),
        P(("parts", "tile")),
        P(("parts", "tile")),
        P(("parts", "tile"), None),
        P(("parts", "tile")),
        P(),
    )
    return jax.shard_map(
        shards,
        mesh=mesh,
        in_specs=placed,
        out_specs=P(None, ("parts", "tile"), None),
        check_vma=False,
    )
```
